32 devices in a mesh: dp: 8 (over y, x, core), tensor: 4 (over z).
Axes of the slice: x: 2, y: 2, z: 4, core: 2. Of those that a mesh axis runs over, the one named last changes fastest.
Arguments:
- tokens: bfloat16 [8192, 1280], P(('dp', 'tensor')), may hold values from -6 to 6
- cotangent: bfloat16 [8192, 1280], P(('dp', 'tensor')), may hold values from -6 to 6
- slot: int32 [8192], replicated, may hold values from 0 to 8191, as said below
- lengths: int32 [16, 4], replicated, may hold values from 1 to 256, 512 in all within a row
- w_query: bfloat16 [1, 1280, 1280], P(None, 'dp', 'tensor'), may hold values from -0.15625 to 0.15625
- w_key: bfloat16 [1, 1280, 1280], P(None, 'dp', 'tensor'), may hold values from -0.15625 to 0.15625
- w_value: bfloat16 [1, 1280, 1280], P(None, 'dp', 'tensor'), may hold values from -0.15625 to 0.15625
- w_out: bfloat16 [1, 1280, 1280], P(None, 'dp', 'tensor'), may hold values from -0.15625 to 0.15625
- w_up: bfloat16 [1, 1280, 5120], P(None, 'dp', 'tensor'), may hold values from -0.15625 to 0.15625
- w_gate: bfloat16 [1, 1280, 5120], P(None, 'dp', 'tensor'), may hold values from -0.15625 to 0.15625
- w_down: bfloat16 [1, 1280, 5120], P(None, 'dp', 'tensor'), may hold values from -0.078125 to 0.078125
- scale_qk: float32 [1, 1280], P(None, 'tensor'), may hold values from 0.1 to 1.9
- scale_up: float32 [1, 5120], P(None, 'tensor'), may hold values from 0.1 to 1.9
- scale_gate: float32 [1, 5120], P(None, 'tensor'), may hold values from 0.1 to 1.9
- rate_attn: float32 [1, 1280], replicated, may hold values from 0.1 to 0.9
- rate_mlp: float32 [1, 1280], replicated, may hold values from 0.1 to 0.9
Outputs:
- out_hidden: float32 [8192, 1280], P(('dp', 'tensor'))
- in_grad: float32 [8192, 1280], P(('dp', 'tensor'))
- grad_query: float32 [1, 1280, 1280], P(None, 'dp', 'tensor')
- grad_key: float32 [1, 1280, 1280], P(None, 'dp', 'tensor')
- grad_value: float32 [1, 1280, 1280], P(None, 'dp', 'tensor')
- grad_out: float32 [1, 1280, 1280], P(None, 'dp', 'tensor')
- grad_up: float32 [1, 1280, 5120], P(None, 'dp', 'tensor')
- grad_gate: float32 [1, 1280, 5120], P(None, 'dp', 'tensor')
- grad_down: float32 [1, 1280, 5120], P(None, 'dp', 'tensor')
- grad_scale_qk: float32 [1, 1280], P(None, 'tensor')
- grad_scale_up: float32 [1, 5120], P(None, 'tensor')
- grad_scale_gate: float32 [1, 5120], P(None, 'tensor')
- grad_rate_attn: float32 [1, 1280], replicated
- grad_rate_mlp: float32 [1, 1280], replicated
The draws below stay inside these ranges and needn't reach their ends.
Inputs may be any that keep to these rules, and one draw needn't show every extreme that they name: slot is a permutation of all rows; each device's 256 rows of the arrival order send exactly 8 rows to the owner rows of every device (owner rows d * 256 to (d + 1) * 256 - 1 of device d = dp index times 4 plus tensor index). `lengths`: each row sums to 512, and its largest entry is 256.
All inputs are finite; a program needn't handle non-finite values.
Results may differ from the reference program's by a relative error of at most 0.015.
Values may be sent and summed in bfloat16 or wider, within the bound.
A program may use at most 192 MiB of HBM per device.

```python
import math
import jax
import jax.numpy as jnp
import numpy as np
from jax import lax

D = 1280
HEADS = 20
HEAD_DIM = 64
FF = 5120
LAYERS = 1
MB = 2
MB_TOK = 512
SEQ_B = 4
MOST_LEN = 256
ROWS_DEV = 256
CAP = 8
TOKENS = 8192
NBLK = 16
N_DP = 8
N_TENSOR = 4


def draw_slot(key, part):
    device_count = TOKENS // ROWS_DEV
    first_key, second_key = jax.random.split(key)
    owner_keys = jax.random.split(first_key, device_count)
    spread = jax.vmap(lambda subkey: jax.random.permutation(subkey, ROWS_DEV))(owner_keys).astype(jnp.int32)
    spread = spread + (jnp.arange(device_count, dtype=jnp.int32) * ROWS_DEV)[:, None]
    spread = spread.reshape(device_count, device_count, CAP).transpose(1, 0, 2).reshape(device_count, ROWS_DEV)
    mix_keys = jax.random.split(second_key, device_count)
    mixed = jax.vmap(lambda subkey, row_vals: jax.random.permutation(subkey, row_vals))(mix_keys, spread)
    return mixed.reshape(TOKENS).astype(jnp.int32)


def block_levels(key, dims, shards, low, top_value):
    gain = 1.0
    for axis_at, parts in shards:
        steps = jax.random.uniform(jax.random.fold_in(jax.random.fold_in(key, 6), axis_at), (parts,), jnp.float32, low / len(shards), top_value / len(shards))
        gain = gain * jnp.repeat(jnp.exp(steps), dims[axis_at] // parts).reshape((-1,) + (1,) * (len(dims) - 1 - axis_at))
    return gain


def profile(amount, total, reach, slope):
    portions = [(1 << 20) // math.isqrt(standing ** slope) + 1 for standing in range(2, amount + 1)]
    surplus, counts = total - reach - (amount - 1), [1] * (amount - 1)
    while surplus > 0:
        candidates = [i for i in range(amount - 1) if counts[i] < reach]
        pool, budget = sum([portions[i] for i in candidates]), surplus
        for i in candidates:
            more = min(reach - counts[i], max(1, budget * portions[i] // pool), surplus)
            counts[i] = counts[i] + more
            surplus = surplus - more
    return np.array([reach] + counts)


def uneven_parts(stream_key, count, total, limit, lean):
    if count == 2:
        one = jax.random.randint(stream_key, (), max(1, total - limit), min(limit, total - 1) + 1)
        return jnp.stack([one, total - one])
    sizes = jnp.asarray(profile(count, total, limit, lean), jnp.int32)
    pairs = (count - 1) // 2
    source_of, sink = sizes[1:1 + 2 * pairs:2], sizes[2:2 + 2 * pairs:2]
    slack = jnp.minimum(source_of - 1, limit - sink)
    shifted = jax.random.randint(jax.random.fold_in(stream_key, 1), (pairs,), 0, 1 << 20) % (slack + 1)
    sizes = sizes.at[1:1 + 2 * pairs:2].set(source_of - shifted).at[2:2 + 2 * pairs:2].set(sink + shifted)
    return sizes[jax.random.permutation(jax.random.fold_in(stream_key, 2), count)]


def normal_values(rng, extent, width, reach, shards=(), kind=jnp.bfloat16):
    entries = width * jax.random.normal(rng, extent, jnp.float32)
    if shards:
        entries = entries * block_levels(rng, extent, shards, -0.22, 0.18)
    return jnp.clip(entries, -reach, reach).astype(kind)


def setup_inputs(seed: int = 0) -> dict:
    seeds = jax.random.split(jax.random.key(seed), 17)
    return {
        "tokens": normal_values(seeds[0], (TOKENS, D), 1.0, 6.0, ((0, 32),)),
        "cotangent": normal_values(seeds[1], (TOKENS, D), 1.0, 6.0, ((0, 32),)),
        "slot": draw_slot(jax.random.fold_in(seeds[16], 71), 0),
        "lengths": jax.vmap(lambda own: uneven_parts(own, SEQ_B, MB_TOK, MOST_LEN, 2))(jax.random.split(seeds[3], NBLK)).reshape((NBLK, SEQ_B)).astype(jnp.int32),
        "w_query": normal_values(seeds[4], (LAYERS, D, D), D ** -0.5, 0.15625, ((1, 8), (2, 4))),
        "w_key": normal_values(seeds[5], (LAYERS, D, D), D ** -0.5, 0.15625, ((1, 8), (2, 4))),
        "w_value": normal_values(seeds[6], (LAYERS, D, D), D ** -0.5, 0.15625, ((1, 8), (2, 4))),
        "w_out": normal_values(seeds[7], (LAYERS, D, D), D ** -0.5, 0.15625, ((1, 8), (2, 4))),
        "w_up": normal_values(seeds[8], (LAYERS, D, FF), D ** -0.5, 0.15625, ((1, 8), (2, 4))),
        "w_gate": normal_values(seeds[9], (LAYERS, D, FF), D ** -0.5, 0.15625, ((1, 8), (2, 4))),
        "w_down": normal_values(seeds[10], (LAYERS, D, FF), FF ** -0.5, 0.078125, ((1, 8), (2, 4))),
        "scale_qk": jnp.clip(1.0 + 0.18 * jax.random.normal(seeds[11], (LAYERS, D), jnp.float32), 0.1, 1.9),
        "scale_up": jnp.clip(1.0 + 0.18 * jax.random.normal(seeds[12], (LAYERS, FF), jnp.float32), 0.1, 1.9),
        "scale_gate": jnp.clip(1.0 + 0.18 * jax.random.normal(seeds[13], (LAYERS, FF), jnp.float32), 0.1, 1.9),
        "rate_attn": jnp.clip(jnp.exp(jax.random.uniform(seeds[14], (LAYERS, D), jnp.float32, math.log(0.1), math.log(0.9))), 0.1, 0.9),
        "rate_mlp": jnp.clip(jnp.exp(jax.random.uniform(seeds[15], (LAYERS, D), jnp.float32, math.log(0.1), math.log(0.9))), 0.1, 0.9),
    }


EPSILON = 1e-06
MASKED = -1e+30
HIGHEST = lax.Precision.HIGHEST

@jax.custom_vjp
def low(v):
    return lax.optimization_barrier(v.astype(jnp.bfloat16)).astype(jnp.float32)

@jax.custom_vjp
def low_back(v):
    return v

def low_keep(v):
    return (low(v), None)

def low_pass(kept, grad):
    return (grad,)

def back_keep(v):
    return (v, None)

def back_low(kept, grad):
    return (low(grad),)
low.defvjp(low_keep, low_pass)
low_back.defvjp(back_keep, back_low)

def rms_norm(values_in):
    return values_in * lax.rsqrt(lax.optimization_barrier(jnp.mean(values_in * values_in, axis=-1, keepdims=True)) + EPSILON)

def matmul(operand, weight_mat):
    return jnp.dot(operand, weight_mat, precision=HIGHEST, preferred_element_type=jnp.float32)

def doc_allowed(lengths_row):
    doc_ends = jnp.cumsum(lengths_row)
    places = jnp.arange(MB_TOK, dtype=jnp.int32)
    segment = lax.optimization_barrier(jnp.sum((places[:, None] >= doc_ends[None, :]).astype(jnp.int32), axis=1))
    return (segment[:, None] == segment[None, :]) & (places[None, :] <= places[:, None])

def one_layer(hidden, allowed, layer_params):
    wquery, wkey, wvalue, wout, wup, wgate, wdown, sqk, sup, sgate, rattn, rmlp = layer_params
    hidden_b = low(hidden)
    query_raw = low_back(matmul(hidden_b, wquery)).reshape(MB_TOK, HEADS, HEAD_DIM)
    keys_raw = low_back(matmul(hidden_b, wkey)).reshape(MB_TOK, HEADS, HEAD_DIM)
    values_b = low(low_back(matmul(hidden_b, wvalue))).reshape(MB_TOK, HEADS, HEAD_DIM)
    scale_grid = sqk.reshape(HEADS, HEAD_DIM)
    query_b = low(scale_grid * rms_norm(query_raw))
    keys_b = low(scale_grid * rms_norm(keys_raw))
    scores = low_back(jnp.einsum('qhd,khd->hqk', query_b, keys_b, precision=HIGHEST) * HEAD_DIM ** (-0.5))
    scores = jnp.where(allowed[None], scores, MASKED)
    probs_b = low(jax.nn.softmax(scores, axis=-1))
    mixed_b = low(low_back(jnp.einsum('hqk,khd->qhd', probs_b, values_b, precision=HIGHEST))).reshape(MB_TOK, D)
    branch = low_back(jnp.einsum('qj,dj->qd', mixed_b, wout, precision=HIGHEST))
    middle = rms_norm(hidden + rattn * (rms_norm(branch) - hidden))
    middle_b = low(middle)
    up_raw = low_back(matmul(middle_b, wup))
    gate_raw = low_back(matmul(middle_b, wgate))
    act_b = low(jax.nn.silu(sgate * gate_raw) * (sup * up_raw))
    branch_mlp = low_back(jnp.einsum('qf,df->qd', act_b, wdown, precision=HIGHEST))
    return rms_norm(middle + rmlp * (rms_norm(branch_mlp) - middle))

def block_fn(params_in, inputs_in, lengths_row):
    allowed = doc_allowed(lengths_row)
    hidden = inputs_in
    for layer in range(LAYERS):
        hidden = one_layer(hidden, allowed, tuple((param[layer] for param in params_in)))
    return hidden

def reference(tokens, cotangent, slot, lengths, w_query, w_key, w_value, w_out, w_up, w_gate, w_down, scale_qk, scale_up, scale_gate, rate_attn, rate_mlp):
    row_count = MB_TOK // N_TENSOR

    def to_blocks(rows_in):
        owned = jnp.zeros_like(rows_in).at[slot].set(rows_in)
        owned = owned.reshape(N_DP, N_TENSOR, MB, row_count, D).transpose(0, 2, 1, 3, 4)
        return owned.reshape(N_DP * MB, MB_TOK, D)

    def from_blocks(blocks):
        owned = blocks.reshape(N_DP, MB, N_TENSOR, row_count, D).transpose(0, 2, 1, 3, 4).reshape(TOKENS, D)
        return owned[slot]
    params = tuple((param.astype(jnp.float32) for param in (w_query, w_key, w_value, w_out, w_up, w_gate, w_down, scale_qk, scale_up, scale_gate, rate_attn, rate_mlp)))
    inputs = to_blocks(tokens.astype(jnp.float32))
    checked = jax.checkpoint(block_fn)

    def forward(inputs_in, params_in):
        return lax.map(lambda block_item: checked(params_in, block_item[0], block_item[1]), (inputs_in, lengths))
    outputs, pull = jax.vjp(forward, inputs, params)
    grad_inputs, grad_params = pull(to_blocks(cotangent.astype(jnp.float32)))
    grad_wq, grad_wk, grad_wv, grad_wo, grad_wu, grad_wg, grad_wd, grad_sqk, grad_sup, grad_sgate, grad_rattn, grad_rmlp = grad_params
    return (from_blocks(outputs), from_blocks(grad_inputs), grad_wq, grad_wk, grad_wv, grad_wo, grad_wu, grad_wg, grad_wd, grad_sqk, grad_sup, grad_sgate, grad_rattn, grad_rmlp)
```

```python
import jax
import jax.numpy as jnp
from jax import lax
from jax.experimental import pallas as pl
from jax.experimental.pallas import tpu as pltpu
from jax.sharding import PartitionSpec as P

HEAD_DIM = 64
MB = 2
LANES = 128

EPSILON = 1e-06
MASKED = -1e30
BF = jnp.bfloat16
F32 = jnp.float32
MESH = pl.DeviceIdType.MESH


class Place:
    def __init__(self):
        self.n_t = lax.axis_size("tensor")
        self.n_dp = lax.axis_size("dp")
        self.n_p = self.n_t
        self.n_r = self.n_dp // self.n_p
        self.n_dev = self.n_dp * self.n_t
        dp = lax.axis_index("dp")
        self.t = lax.axis_index("tensor")
        self.p = dp // self.n_r
        self.r = dp % self.n_r
        self.me = dp * self.n_t + self.t

    def dev(self, p, r, t):
        return (p * self.n_r + r, t)

    def flat(self, j):
        return (j // self.n_t, j % self.n_t)


def width3(p, t):
    return (p + t) % 2 == 0


def src_tile(p, t):
    return 5 * (p // 2) + (p % 2) * (3 - t % 2)


def dst_tile(p, t):
    return 5 * (t // 2) + (t % 2) * (3 - p % 2)


def lanes(tile, count):
    return pl.ds(pl.multiple_of(tile * LANES, LANES), count * LANES)


class Move:
    def __init__(self, src, dst, send, recv, dev, landing, landed):
        self.going = (src, dst, send, recv, dev)
        self.coming = (landing, landing, send, landed, dev)

    @staticmethod
    def copy(args):
        src, dst, send, recv, dev = args
        return pltpu.make_async_remote_copy(
            src_ref=src, dst_ref=dst, send_sem=send, recv_sem=recv, device_id=dev, device_id_type=MESH
        )

    def start(self):
        self.copy(self.going).start()

    def wait_recv(self):
        self.copy(self.coming).wait_recv()

    def wait_send(self):
        self.copy(self.going).wait_send()


def others(k_count, own):
    return [(own + k) % k_count for k in range(1, k_count)]


class Deal:
    groups = ("all",)
    aliases = {}

    def __init__(self, pc, x):
        self.ins = [x]
        self.outs = [jax.ShapeDtypeStruct(x.shape, x.dtype)]
        self.sems = [pc.n_dev, pc.n_dev, 1]

    def run(self, pc, ins, outs, sems):
        (x,), (y,), (ss, rs, ls) = ins, outs, sems

        def move(i):
            j = (pc.me + i) % pc.n_dev
            k = (pc.me + pc.n_dev - i) % pc.n_dev
            return Move(x.at[j], y.at[pc.me], ss.at[j], rs.at[pc.me], pc.flat(j), y.at[k], rs.at[k])

        def start(i, carry):
            move(i).start()
            return carry

        def finish(i, carry):
            m = move(i)
            m.wait_recv()
            m.wait_send()
            return carry

        lax.fori_loop(1, pc.n_dev, start, 0)
        own = pltpu.make_async_copy(x.at[pc.me], y.at[pc.me], ls.at[0])
        own.start()
        yield
        own.wait()
        lax.fori_loop(1, pc.n_dev, finish, 0)


class PlaneGather:
    groups = ("plane",)
    aliases = {}

    def __init__(self, pc, x):
        self.ins = [x]
        self.outs = [jax.ShapeDtypeStruct((x.shape[0], pc.n_p) + x.shape[1:], x.dtype)]
        self.sems = [pc.n_p, pc.n_p, 1]

    def run(self, pc, ins, outs, sems):
        (x,), (y,), (ss, rs, ls) = ins, outs, sems
        moves = [
            Move(x, y.at[:, pc.p], ss.at[q], rs.at[pc.p], pc.dev(q, pc.r, pc.t), y.at[:, q], rs.at[q])
            for q in others(pc.n_p, pc.p)
        ]
        for m in moves:
            m.start()
        own = pltpu.make_async_copy(x, y.at[:, pc.p], ls.at[0])
        own.start()
        yield
        own.wait()
        for m in moves:
            m.wait_recv()
            m.wait_send()


class PlaneScatter:
    groups = ("plane",)
    aliases = {}

    def __init__(self, pc, x):
        self.ins = [x]
        self.outs = [jax.ShapeDtypeStruct((pc.n_p, x.shape[0]) + x.shape[2:], x.dtype)]
        self.sems = [pc.n_p, pc.n_p, 1]

    def run(self, pc, ins, outs, sems):
        (x,), (y,), (ss, rs, ls) = ins, outs, sems
        moves = [
            Move(x.at[:, q], y.at[pc.p], ss.at[q], rs.at[pc.p], pc.dev(q, pc.r, pc.t), y.at[q], rs.at[q])
            for q in others(pc.n_p, pc.p)
        ]
        for m in moves:
            m.start()
        own = pltpu.make_async_copy(x.at[:, pc.p], y.at[pc.p], ls.at[0])
        own.start()
        yield
        own.wait()
        for m in moves:
            m.wait_recv()
            m.wait_send()


class TallScatter:
    groups = ("tall",)
    aliases = {}

    def __init__(self, pc, x):
        self.ins = [x]
        self.outs = [jax.ShapeDtypeStruct(x.shape, x.dtype)]
        self.sems = [pc.n_t, pc.n_t, 1]

    def run(self, pc, ins, outs, sems):
        (x,), (y,), (ss, rs, ls) = ins, outs, sems
        moves = [
            Move(x.at[q], y.at[pc.t], ss.at[q], rs.at[pc.t], pc.dev(pc.p, pc.r, q), y.at[q], rs.at[q])
            for q in others(pc.n_t, pc.t)
        ]
        for m in moves:
            m.start()
        own = pltpu.make_async_copy(x.at[pc.t], y.at[pc.t], ls.at[0])
        own.start()
        yield
        own.wait()
        for m in moves:
            m.wait_recv()
            m.wait_send()


class HeadWeights:
    groups = ("plane", "tall", "near")
    aliases = {}

    def __init__(self, pc, x):
        mats, rows, cols = x.shape
        self.ins = [x]
        self.outs = [
            jax.ShapeDtypeStruct((pc.n_t,) + x.shape, x.dtype),
            jax.ShapeDtypeStruct((mats, pc.n_p, pc.n_r, rows, cols), x.dtype),
        ]
        self.sems = [pc.n_t, pc.n_t, pc.n_p, pc.n_p, pc.n_r, pc.n_r, 2]

    def run(self, pc, ins, outs, sems):
        (x,), (a, f) = ins, outs
        s1, r1, s2, r2, s3, r3, ls = sems
        first = [
            Move(x, a.at[pc.t], s1.at[q], r1.at[pc.t], pc.dev(pc.p, pc.r, q), a.at[q], r1.at[q])
            for q in others(pc.n_t, pc.t)
        ]
        for m in first:
            m.start()
        own = pltpu.make_async_copy(x, a.at[pc.t], ls.at[0])
        own.start()
        yield
        own.wait()
        for m in first:
            m.wait_recv()
        second = [
            Move(
                a.at[q], f.at[:, pc.p, pc.r], s2.at[q], r2.at[pc.p], pc.dev(q, pc.r, pc.t), f.at[:, q, pc.r], r2.at[q]
            )
            for q in others(pc.n_p, pc.p)
        ]
        for m in second:
            m.start()
        own = pltpu.make_async_copy(a.at[pc.p], f.at[:, pc.p, pc.r], ls.at[1])
        own.start()
        yield
        own.wait()
        for m in second:
            m.wait_recv()
        third = [
            Move(
                f.at[:, :, pc.r], f.at[:, :, pc.r], s3.at[q], r3.at[pc.r], pc.dev(pc.p, q, pc.t), f.at[:, :, q], r3.at[q]
            )
            for q in others(pc.n_r, pc.r)
        ]
        for m in third:
            m.start()
        yield
        for m in third:
            m.wait_recv()
        for m in first + second + third:
            m.wait_send()


class HiddenSplit:
    groups = ("plane",)
    aliases = {}

    def __init__(self, pc, x):
        self.ins = [x]
        self.outs = [jax.ShapeDtypeStruct((pc.n_p, pc.n_r) + x.shape, x.dtype)]
        self.sems = [pc.n_p, pc.n_p, pc.n_p, pc.n_p, 2]

    def run(self, pc, ins, outs, sems):
        (x,), (g,), (s1, r1, s2, r2, ls) = ins, outs, sems

        def pieces(q):
            two = Move(
                x.at[:, lanes(src_tile(q, pc.t), 2)],
                g.at[pc.p, pc.r, :, lanes(dst_tile(q, pc.t), 2)],
                s1.at[q],
                r1.at[pc.p],
                pc.dev(q, pc.r, pc.t),
                g.at[q, pc.r, :, lanes(dst_tile(pc.p, pc.t), 2)],
                r1.at[q],
            )
            one = Move(
                x.at[:, lanes(src_tile(q, pc.t) + 2, 1)],
                g.at[pc.p, pc.r, :, lanes(dst_tile(q, pc.t) + 2, 1)],
                s2.at[q],
                r2.at[pc.p],
                pc.dev(q, pc.r, pc.t),
                g.at[q, pc.r, :, lanes(dst_tile(pc.p, pc.t) + 2, 1)],
                r2.at[q],
            )
            return two, one

        for q in others(pc.n_p, pc.p):
            two, one = pieces(q)
            two.start()
            pl.when(width3(q, pc.t))(one.start)
        own2 = pltpu.make_async_copy(
            x.at[:, lanes(src_tile(pc.p, pc.t), 2)],
            g.at[pc.p, pc.r, :, lanes(dst_tile(pc.p, pc.t), 2)],
            ls.at[0],
        )
        own1 = pltpu.make_async_copy(
            x.at[:, lanes(src_tile(pc.p, pc.t) + 2, 1)],
            g.at[pc.p, pc.r, :, lanes(dst_tile(pc.p, pc.t) + 2, 1)],
            ls.at[1],
        )
        own2.start()
        pl.when(width3(pc.p, pc.t))(own1.start)
        yield
        own2.wait()
        pl.when(width3(pc.p, pc.t))(own1.wait)
        for q in others(pc.n_p, pc.p):
            two, one = pieces(q)
            two.wait_recv()
            two.wait_send()
            pl.when(width3(pc.p, pc.t))(one.wait_recv)
            pl.when(width3(q, pc.t))(one.wait_send)


class HiddenGather:
    groups = ("tall", "near")
    aliases = {0: 0}

    def __init__(self, pc, x):
        self.ins = [x]
        self.outs = [jax.ShapeDtypeStruct(x.shape, x.dtype)]
        self.sems = [pc.n_t, pc.n_t, pc.n_t, pc.n_t, pc.n_r, pc.n_r]

    def run(self, pc, ins, outs, sems):
        (g,), (s1, r1, s2, r2, s3, r3) = outs, sems

        def pieces(q):
            here = dst_tile(pc.p, pc.t)
            there = dst_tile(pc.p, q)
            dev = pc.dev(pc.p, pc.r, q)
            two = Move(
                g.at[:, pc.r, :, lanes(here, 2)],
                g.at[:, pc.r, :, lanes(here, 2)],
                s1.at[q],
                r1.at[pc.t],
                dev,
                g.at[:, pc.r, :, lanes(there, 2)],
                r1.at[q],
            )
            one = Move(
                g.at[:, pc.r, :, lanes(here + 2, 1)],
                g.at[:, pc.r, :, lanes(here + 2, 1)],
                s2.at[q],
                r2.at[pc.t],
                dev,
                g.at[:, pc.r, :, lanes(there + 2, 1)],
                r2.at[q],
            )
            return two, one

        for q in others(pc.n_t, pc.t):
            two, one = pieces(q)
            two.start()
            pl.when(width3(pc.p, pc.t))(one.start)
        yield
        for q in others(pc.n_t, pc.t):
            two, one = pieces(q)
            two.wait_recv()
            pl.when(width3(pc.p, q))(one.wait_recv)
        third = [
            Move(g.at[:, pc.r], g.at[:, pc.r], s3.at[q], r3.at[pc.r], pc.dev(pc.p, q, pc.t), g.at[:, q], r3.at[q])
            for q in others(pc.n_r, pc.r)
        ]
        for m in third:
            m.start()
        yield
        for m in third:
            m.wait_recv()
            m.wait_send()
        for q in others(pc.n_t, pc.t):
            two, one = pieces(q)
            two.wait_send()
            pl.when(width3(pc.p, pc.t))(one.wait_send)


class NearScatter:
    groups = ("near",)
    aliases = {}

    def __init__(self, pc, x):
        self.ins = [x]
        self.outs = [jax.ShapeDtypeStruct((pc.n_r, x.shape[0]) + x.shape[2:], x.dtype)]
        self.sems = [pc.n_r, pc.n_r, 1]

    def run(self, pc, ins, outs, sems):
        (x,), (y,), (ss, rs, ls) = ins, outs, sems
        moves = [
            Move(x.at[:, q], y.at[pc.r], ss.at[q], rs.at[pc.r], pc.dev(pc.p, q, pc.t), y.at[q], rs.at[q])
            for q in others(pc.n_r, pc.r)
        ]
        for m in moves:
            m.start()
        own = pltpu.make_async_copy(x.at[:, pc.r], y.at[pc.r], ls.at[0])
        own.start()
        yield
        own.wait()
        for m in moves:
            m.wait_recv()
            m.wait_send()


class HiddenTall:
    groups = ("tall",)
    aliases = {}

    def __init__(self, pc, x):
        n_p, rows, _ = x.shape
        self.ins = [x]
        self.outs = [jax.ShapeDtypeStruct((pc.n_t, n_p, rows, 3 * LANES), x.dtype)]
        self.sems = [pc.n_t, pc.n_t, pc.n_t, pc.n_t, 2]

    def run(self, pc, ins, outs, sems):
        (x,), (y,), (s1, r1, s2, r2, ls) = ins, outs, sems

        def pieces(q):
            there = dst_tile(pc.p, q)
            dev = pc.dev(pc.p, pc.r, q)
            two = Move(
                x.at[:, :, lanes(there, 2)],
                y.at[pc.t, :, :, pl.ds(0, 2 * LANES)],
                s1.at[q],
                r1.at[pc.t],
                dev,
                y.at[q, :, :, pl.ds(0, 2 * LANES)],
                r1.at[q],
            )
            one = Move(
                x.at[:, :, lanes(there + 2, 1)],
                y.at[pc.t, :, :, pl.ds(2 * LANES, LANES)],
                s2.at[q],
                r2.at[pc.t],
                dev,
                y.at[q, :, :, pl.ds(2 * LANES, LANES)],
                r2.at[q],
            )
            return two, one

        for q in others(pc.n_t, pc.t):
            two, one = pieces(q)
            two.start()
            pl.when(width3(pc.p, q))(one.start)
        here = dst_tile(pc.p, pc.t)
        own2 = pltpu.make_async_copy(x.at[:, :, lanes(here, 2)], y.at[pc.t, :, :, pl.ds(0, 2 * LANES)], ls.at[0])
        own1 = pltpu.make_async_copy(
            x.at[:, :, lanes(here + 2, 1)], y.at[pc.t, :, :, pl.ds(2 * LANES, LANES)], ls.at[1]
        )
        own2.start()
        pl.when(width3(pc.p, pc.t))(own1.start)
        yield
        own2.wait()
        pl.when(width3(pc.p, pc.t))(own1.wait)
        for q in others(pc.n_t, pc.t):
            two, one = pieces(q)
            two.wait_recv()
            two.wait_send()
            pl.when(width3(pc.p, pc.t))(one.wait_recv)
            pl.when(width3(pc.p, q))(one.wait_send)


class HiddenPlane:
    groups = ("plane",)
    aliases = {}

    def __init__(self, pc, x, hidden):
        self.ins = [x]
        self.outs = [jax.ShapeDtypeStruct((x.shape[1], hidden), x.dtype)]
        self.sems = [pc.n_p, pc.n_p, pc.n_p, pc.n_p, 2]

    def run(self, pc, ins, outs, sems):
        (x,), (y,), (s1, r1, s2, r2, ls) = ins, outs, sems
        here = src_tile(pc.p, pc.t)

        def pieces(q):
            there = src_tile(q, pc.t)
            dev = pc.dev(q, pc.r, pc.t)
            two = Move(
                x.at[q, :, pl.ds(0, 2 * LANES)],
                y.at[:, lanes(here, 2)],
                s1.at[q],
                r1.at[pc.p],
                dev,
                y.at[:, lanes(there, 2)],
                r1.at[q],
            )
            one = Move(
                x.at[q, :, pl.ds(2 * LANES, LANES)],
                y.at[:, lanes(here + 2, 1)],
                s2.at[q],
                r2.at[pc.p],
                dev,
                y.at[:, lanes(there + 2, 1)],
                r2.at[q],
            )
            return two, one

        for q in others(pc.n_p, pc.p):
            two, one = pieces(q)
            two.start()
            pl.when(width3(pc.p, pc.t))(one.start)
        own2 = pltpu.make_async_copy(x.at[pc.p, :, pl.ds(0, 2 * LANES)], y.at[:, lanes(here, 2)], ls.at[0])
        own1 = pltpu.make_async_copy(
            x.at[pc.p, :, pl.ds(2 * LANES, LANES)], y.at[:, lanes(here + 2, 1)], ls.at[1]
        )
        own2.start()
        pl.when(width3(pc.p, pc.t))(own1.start)
        yield
        own2.wait()
        pl.when(width3(pc.p, pc.t))(own1.wait)
        for q in others(pc.n_p, pc.p):
            two, one = pieces(q)
            two.wait_recv()
            two.wait_send()
            pl.when(width3(q, pc.t))(one.wait_recv)
            pl.when(width3(pc.p, pc.t))(one.wait_send)


def greet(pc, groups):
    barrier = pltpu.get_barrier_semaphore()

    def signal(dev):
        pl.semaphore_signal(barrier, inc=1, device_id=dev, device_id_type=MESH)

    if "all" in groups:

        def step(i, carry):
            signal(pc.flat((pc.me + i) % pc.n_dev))
            return carry

        lax.fori_loop(1, pc.n_dev, step, 0)
        count = pc.n_dev - 1
    else:
        devs = []
        if "plane" in groups:
            devs += [pc.dev(q, pc.r, pc.t) for q in others(pc.n_p, pc.p)]
        if "tall" in groups:
            devs += [pc.dev(pc.p, pc.r, q) for q in others(pc.n_t, pc.t)]
        if "near" in groups:
            devs += [pc.dev(pc.p, q, pc.t) for q in others(pc.n_r, pc.r)]
        for dev in devs:
            signal(dev)
        count = len(devs)
    pl.semaphore_wait(barrier, count)


def exchange(collective_id, tasks):
    ins = [x for task in tasks for x in task.ins]
    outs = [y for task in tasks for y in task.outs]
    sems = [n for task in tasks for n in task.sems]
    aliases = {}
    at_in = at_out = 0
    for task in tasks:
        for i, o in task.aliases.items():
            aliases[at_in + i] = at_out + o
        at_in += len(task.ins)
        at_out += len(task.outs)
    groups = sorted({g for task in tasks for g in task.groups})

    def kernel(*refs):
        pc = Place()
        in_refs = list(refs[: len(ins)])
        out_refs = list(refs[len(ins) : len(ins) + len(outs)])
        sem_refs = list(refs[len(ins) + len(outs) :])
        greet(pc, groups)
        live = []
        for task in tasks:
            args = [[refs_.pop(0) for _ in range(n)] for refs_, n in (
                (in_refs, len(task.ins)),
                (out_refs, len(task.outs)),
                (sem_refs, len(task.sems)),
            )]
            live.append(task.run(pc, *args))
        while live:
            still = []
            for gen in live:
                try:
                    next(gen)
                    still.append(gen)
                except StopIteration:
                    pass
            live = still

    results = pl.pallas_call(
        kernel,
        out_shape=tuple(outs),
        in_specs=[pl.BlockSpec(memory_space=pl.ANY)] * len(ins),
        out_specs=tuple([pl.BlockSpec(memory_space=pl.ANY)] * len(outs)),
        scratch_shapes=[pltpu.SemaphoreType.DMA((n,)) for n in sems],
        input_output_aliases=aliases,
        compiler_params=pltpu.CompilerParams(collective_id=collective_id, has_side_effects=True),
    )(*ins)
    results = list(results)
    return [[results.pop(0) for _ in task.outs] for task in tasks]


def rms_norm(values_in):
    return values_in * lax.rsqrt(jnp.mean(values_in * values_in, axis=-1, keepdims=True) + EPSILON)


def residual_step(hidden, branch, rate):
    return rms_norm(hidden + rate * (rms_norm(branch) - hidden))


def head_norm(query_raw, keys_raw, scale_grid):
    return (scale_grid * rms_norm(query_raw), scale_grid * rms_norm(keys_raw))


def swiglu(up_raw, gate_raw, scale_upper, scale_gating):
    return jax.nn.silu(scale_gating * gate_raw) * (scale_upper * up_raw)


def mm(a, b):
    return jnp.dot(a, b, preferred_element_type=F32)


def times_rows(operand, weight_mat):
    return lax.dot_general(operand, weight_mat, (((1,), (1,)), ((), ())), preferred_element_type=F32)


def times_cols(operand, other_mat):
    return lax.dot_general(operand, other_mat, (((0,), (0,)), ((), ())), preferred_element_type=F32)


def doc_allowed(lengths_row, tok_count):
    count = lengths_row.shape[0]
    upto = jnp.arange(count)[:, None] >= jnp.arange(count)[None, :]
    doc_ends = jnp.sum(jnp.where(upto, lengths_row[None, :], 0), axis=1)
    places = jnp.arange(tok_count, dtype=jnp.int32)
    segment = jnp.sum((places[:, None] >= doc_ends[None, :]).astype(jnp.int32), axis=1)
    return (segment[:, None] == segment[None, :]) & (places[None, :] <= places[:, None])


def body(
    tokens,
    cotangent,
    slot,
    lengths,
    w_query,
    w_key,
    w_value,
    w_out,
    w_up,
    w_gate,
    w_down,
    scale_qk,
    scale_up,
    scale_gate,
    rate_attn,
    rate_mlp,
):
    pc = Place()
    n_p, n_r, n_t, n_dev = pc.n_p, pc.n_r, pc.n_t, pc.n_dev
    rows_dev, width = tokens.shape
    part = rows_dev // MB
    tok_count = part * n_p
    all_tok = MB * tok_count
    cap = rows_dev // n_dev
    w_rows = w_query.shape[1]
    head_cols = w_query.shape[2]
    heads = head_cols // HEAD_DIM
    hid = w_up.shape[2]
    group = pc.r * n_t + pc.t
    owner = group * n_p + pc.p

    table = slot.reshape(n_dev, rows_dev)
    own_slots = lax.dynamic_index_in_dim(table, pc.me, 0, keepdims=False)
    d = own_slots // rows_dev
    to_dev = ((d % n_p) * n_r + (d // n_p) // n_t) * n_t + (d // n_p) % n_t
    places = jnp.arange(rows_dev, dtype=jnp.int32)
    before = (d[:, None] == d[None, :]) & (places[None, :] < places[:, None])
    rank = jnp.sum(before.astype(jnp.int32), axis=1)
    send_at = to_dev * cap + rank
    send_hot = (places[:, None] == send_at[None, :]).astype(BF)

    sel = table // rows_dev == owner
    tri = (places[:, None] < places[None, :]).astype(BF)
    ranks = mm(sel.astype(BF), tri).astype(jnp.int32)
    kth = sel[:, None, :] & (ranks[:, None, :] == jnp.arange(cap, dtype=jnp.int32)[None, :, None])
    owner_rows = jnp.sum(jnp.where(kth, (table - owner * rows_dev)[:, None, :], 0), axis=2).reshape(rows_dev)
    recv_hot = (places[:, None] == owner_rows[None, :]).astype(BF)

    sent = jnp.concatenate(
        [
            mm(send_hot, tokens).astype(BF).reshape(n_dev, cap, width),
            mm(send_hot, cotangent).astype(BF).reshape(n_dev, cap, width),
        ],
        axis=1,
    )
    w4 = jnp.concatenate([w_query, w_key, w_value, w_out], axis=0)
    (arrived,), (_, wh), (gu,), (gg,), (gd,) = exchange(
        0,
        [
            Deal(pc, sent),
            HeadWeights(pc, w4),
            HiddenSplit(pc, w_up[0]),
            HiddenSplit(pc, w_gate[0]),
            HiddenSplit(pc, w_down[0]),
        ],
    )
    wh = wh.reshape(4, width, head_cols)
    tok_b = mm(recv_hot, arrived[:, :cap].reshape(rows_dev, width)).astype(BF)
    grad_in = mm(recv_hot, arrived[:, cap:].reshape(rows_dev, width))
    hidden = tok_b.astype(F32)

    small = jnp.concatenate([scale_qk[0], scale_up[0], scale_gate[0]])
    small = lax.all_gather(small, "tensor", axis=0)
    sqk = lax.dynamic_index_in_dim(small[:, :head_cols], pc.p, 0, keepdims=False).reshape(heads, HEAD_DIM)
    tiles = hid // LANES
    t_all = jnp.arange(n_t * tiles, dtype=jnp.int32) // tiles
    tile_all = jnp.arange(n_t * tiles, dtype=jnp.int32) % tiles
    first = src_tile(pc.p, t_all)
    count = 2 + width3(pc.p, t_all).astype(jnp.int32)
    mine = (tile_all >= first) & (tile_all < first + count)
    spot = jnp.where(mine, dst_tile(pc.p, t_all) + tile_all - first, -1)
    hot = spot[None, :] == jnp.arange(tiles, dtype=jnp.int32)[:, None]

    def take_tiles(x):
        return jnp.sum(jnp.where(hot[:, :, None], x.reshape(1, n_t * tiles, LANES), 0.0), axis=1).reshape(hid)

    def put_tiles(x):
        return jnp.sum(jnp.where(hot[:, :, None], x.reshape(tiles, 1, LANES), 0.0), axis=0).reshape(n_t * hid)

    sup = take_tiles(small[:, head_cols : head_cols + hid])
    sgate = take_tiles(small[:, head_cols + hid :])
    rattn, rmlp = rate_attn[0], rate_mlp[0]

    (hb,), (gu,) = exchange(1, [PlaneGather(pc, tok_b.reshape(MB, part, width)), HiddenGather(pc, gu)])
    hb = hb.reshape(all_tok, width)
    wup = gu.reshape(width, hid)
    grid = (MB, tok_count, heads, HEAD_DIM)
    q_raw = mm(hb, wh[0]).reshape(grid)
    k_raw = mm(hb, wh[1]).reshape(grid)
    v_b = mm(hb, wh[2]).astype(BF).reshape(grid)
    q_hat, k_hat = head_norm(q_raw, k_raw, sqk)
    q_b, k_b = q_hat.astype(BF), k_hat.astype(BF)
    own_lengths = lax.dynamic_slice_in_dim(lengths, group * MB, MB, 0)
    allowed = jnp.stack([doc_allowed(own_lengths[m], tok_count) for m in range(MB)])

    def scores_of():
        s = jnp.einsum("mqhd,mkhd->mhqk", q_b, k_b, preferred_element_type=F32) * HEAD_DIM ** (-0.5)
        return jnp.where(allowed[:, None], s, MASKED)

    scores = scores_of()
    row_max = jnp.max(scores, axis=-1, keepdims=True)
    lse = row_max + jnp.log(jnp.sum(jnp.exp(scores - row_max), axis=-1, keepdims=True))
    probs_b = jnp.exp(scores - lse).astype(BF)
    o_b = jnp.einsum("mhqk,mkhd->mqhd", probs_b, v_b, preferred_element_type=F32).astype(BF).reshape(all_tok, head_cols)
    part_a = times_rows(o_b, wh[3]).astype(BF).reshape(MB, n_p, part, width)
    (got_a,), (gg,) = exchange(2, [PlaneScatter(pc, part_a), HiddenGather(pc, gg)])
    wgate = gg.reshape(width, hid)
    branch = jnp.sum(got_a.astype(F32), axis=0).reshape(rows_dev, width)
    middle, pull_attn = jax.vjp(residual_step, hidden, branch, rattn)

    (hb1,), (gd,) = exchange(3, [PlaneGather(pc, middle.astype(BF).reshape(MB, part, width)), HiddenGather(pc, gd)])
    hb1 = hb1.reshape(all_tok, width)
    wdown = gd.reshape(width, hid)
    up_raw = mm(hb1, wup)
    gate_raw = mm(hb1, wgate)
    act, pull_glu = jax.vjp(swiglu, up_raw, gate_raw, sup, sgate)
    act_b = act.astype(BF)
    part_c = times_rows(act_b, wdown).astype(BF).reshape(MB, n_p, part, width)
    ((got_c,),) = exchange(4, [PlaneScatter(pc, part_c)])
    branch_mlp = jnp.sum(got_c.astype(F32), axis=0).reshape(rows_dev, width)
    output, pull_mlp = jax.vjp(residual_step, middle, branch_mlp, rmlp)

    def to_arrival(x):
        return times_cols(recv_hot, x.astype(BF)).astype(BF).reshape(n_dev, cap, width)

    grad_middle, grad_c, grad_rmlp = pull_mlp(grad_in)
    (dcb,), (back_out,) = exchange(
        5, [PlaneGather(pc, grad_c.astype(BF).reshape(MB, part, width)), Deal(pc, to_arrival(output))]
    )
    dcb = dcb.reshape(all_tok, width)
    d_act = mm(dcb, wdown)
    d_up, d_gate, grad_sup, grad_sgate = pull_glu(d_act)
    dub, dgb = d_up.astype(BF), d_gate.astype(BF)
    part_h1 = (times_rows(dub, wup) + times_rows(dgb, wgate)).astype(BF).reshape(MB, n_p, part, width)
    split = (n_p, n_r, w_rows, hid)
    g_down = times_cols(dcb, act_b).astype(BF).reshape(split)
    g_up = times_cols(hb1, dub).astype(BF).reshape(split)
    g_gate = times_cols(hb1, dgb).astype(BF).reshape(split)

    def near_sum(x):
        return jnp.sum(x.astype(F32), axis=0).astype(BF)

    (got_h1,), (n_down,), (n_up,), (n_gate,) = exchange(
        6,
        [PlaneScatter(pc, part_h1), NearScatter(pc, g_down), NearScatter(pc, g_up), NearScatter(pc, g_gate)],
    )
    grad_middle = grad_middle + jnp.sum(got_h1.astype(F32), axis=0).reshape(rows_dev, width)
    grad_hidden, grad_a, grad_rattn = pull_attn(grad_middle)
    (dab,), (t_down,) = exchange(
        7, [PlaneGather(pc, grad_a.astype(BF).reshape(MB, part, width)), HiddenTall(pc, near_sum(n_down))]
    )

    def tall_sum(x):
        valid = jnp.arange(3 * LANES) < jnp.where(width3(pc.p, pc.t), 3, 2) * LANES
        return jnp.sum(jnp.where(valid, x, 0).astype(F32), axis=0).astype(BF)

    dab = dab.reshape(all_tok, width)
    do_b = mm(dab, wh[3]).astype(BF).reshape(grid)
    probs = jnp.exp(scores_of() - lse)
    probs_b2 = probs.astype(BF)
    d_probs = jnp.einsum("mqhd,mkhd->mhqk", do_b, v_b, preferred_element_type=F32)
    dvb = jnp.einsum("mhqk,mqhd->mkhd", probs_b2, do_b, preferred_element_type=F32).astype(BF).reshape(all_tok, head_cols)
    inner = jnp.sum(probs * d_probs, axis=-1, keepdims=True)
    d_s = (probs * (d_probs - inner)).astype(BF)
    d_qhat = jnp.einsum("mhqk,mkhd->mqhd", d_s, k_b, preferred_element_type=F32) * HEAD_DIM ** (-0.5)
    d_khat = jnp.einsum("mhqk,mqhd->mkhd", d_s, q_b, preferred_element_type=F32) * HEAD_DIM ** (-0.5)
    _, pull_norm = jax.vjp(head_norm, q_raw, k_raw, sqk)
    d_q, d_k, grad_sqk = pull_norm((d_qhat, d_khat))
    dqb = d_q.astype(BF).reshape(all_tok, head_cols)
    dkb = d_k.astype(BF).reshape(all_tok, head_cols)
    part_h = (times_rows(dqb, wh[0]) + times_rows(dkb, wh[1]) + times_rows(dvb, wh[2])).astype(BF)
    part_h = part_h.reshape(MB, n_p, part, width)
    g_heads = jnp.stack([times_cols(hb, dqb), times_cols(hb, dkb), times_cols(hb, dvb), times_cols(dab, o_b)])
    g_heads = g_heads.astype(BF).reshape(4 * n_p, n_r, w_rows, head_cols)
    (got_h,), (n_heads,), (t_up,), (f_down,) = exchange(
        8,
        [
            PlaneScatter(pc, part_h),
            NearScatter(pc, g_heads),
            HiddenTall(pc, near_sum(n_up)),
            HiddenPlane(pc, tall_sum(t_down), hid),
        ],
    )
    grad_hidden = grad_hidden + jnp.sum(got_h.astype(F32), axis=0).reshape(rows_dev, width)
    s_heads = near_sum(n_heads).reshape(4, n_p, w_rows, head_cols)
    (back_grad,), (t_gate,), (f_up,), (p_heads,) = exchange(
        9,
        [
            Deal(pc, to_arrival(grad_hidden)),
            HiddenTall(pc, near_sum(n_gate)),
            HiddenPlane(pc, tall_sum(t_up), hid),
            PlaneScatter(pc, s_heads),
        ],
    )
    (z_heads,), (f_gate,) = exchange(10, [TallScatter(pc, p_heads), HiddenPlane(pc, tall_sum(t_gate), hid)])
    w_out_all = jnp.sum(z_heads.astype(F32), axis=0)[:, None]

    qk_full = lax.dynamic_update_slice(jnp.zeros((n_t * head_cols,), F32), grad_sqk.reshape(-1), (pc.p * head_cols,))
    vec = jnp.concatenate([qk_full, put_tiles(grad_sup), put_tiles(grad_sgate), grad_rattn, grad_rmlp])
    vec = lax.psum(vec, ("dp", "tensor"))
    at = n_t * head_cols
    out_sqk = lax.dynamic_slice_in_dim(vec[:at], pc.t * head_cols, head_cols)[None]
    out_sup = lax.dynamic_slice_in_dim(vec[at : at + n_t * hid], pc.t * hid, hid)[None]
    out_sgate = lax.dynamic_slice_in_dim(vec[at + n_t * hid : at + 2 * n_t * hid], pc.t * hid, hid)[None]
    at = at + 2 * n_t * hid
    out_rattn = vec[at : at + width][None]
    out_rmlp = vec[at + width :][None]

    def from_back(x):
        return times_cols(send_hot, x.reshape(rows_dev, width))

    return (
        from_back(back_out),
        from_back(back_grad),
        w_out_all[0],
        w_out_all[1],
        w_out_all[2],
        w_out_all[3],
        f_up.astype(F32)[None],
        f_gate.astype(F32)[None],
        f_down.astype(F32)[None],
        out_sqk,
        out_sup,
        out_sgate,
        out_rattn,
        out_rmlp,
    )


def solution(mesh):
    tok = P(("dp", "tensor"), None)
    mat = P(None, "dp", "tensor")
    vec = P(None, "tensor")
    in_specs = (tok, tok, P(), P()) + (mat,) * 7 + (vec,) * 3 + (P(), P())
    out_specs = (tok, tok) + (mat,) * 7 + (vec,) * 3 + (P(), P())
    return jax.shard_map(body, mesh=mesh, in_specs=in_specs, out_specs=out_specs, check_vma=False)
```

```python
import jax
import jax.numpy as jnp
from jax import lax
from jax.experimental import pallas as pl
from jax.experimental.pallas import tpu as pltpu
from jax.sharding import PartitionSpec as P

HEAD_DIM = 64
MB = 2
LANES = 128

EPSILON = 1e-06
MASKED = -1e30
BF = jnp.bfloat16
F32 = jnp.float32
MESH = pl.DeviceIdType.MESH


class Place:
    def __init__(self):
        self.n_t = lax.axis_size("tensor")
        self.n_dp = lax.axis_size("dp")
        self.n_p = self.n_t
        self.n_r = self.n_dp // self.n_p
        self.n_dev = self.n_dp * self.n_t
        dp = lax.axis_index("dp")
        self.t = lax.axis_index("tensor")
        self.p = dp // self.n_r
        self.r = dp % self.n_r
        self.me = dp * self.n_t + self.t

    def dev(self, p, r, t):
        return (p * self.n_r + r, t)

    def flat(self, j):
        return (j // self.n_t, j % self.n_t)


def width3(p, t):
    return (p + t) % 2 == 0


def src_tile(p, t):
    return 5 * (p // 2) + (p % 2) * (3 - t % 2)


def dst_tile(p, t):
    return 5 * (t // 2) + (t % 2) * (3 - p % 2)


def lanes(tile, count):
    return pl.ds(pl.multiple_of(tile * LANES, LANES), count * LANES)


class Move:
    def __init__(self, src, dst, send, recv, dev, landing, landed):
        self.going = (src, dst, send, recv, dev)
        self.coming = (landing, landing, send, landed, dev)

    @staticmethod
    def copy(args):
        src, dst, send, recv, dev = args
        return pltpu.make_async_remote_copy(
            src_ref=src, dst_ref=dst, send_sem=send, recv_sem=recv, device_id=dev, device_id_type=MESH
        )

    def start(self):
        self.copy(self.going).start()

    def wait_recv(self):
        self.copy(self.coming).wait_recv()

    def wait_send(self):
        self.copy(self.going).wait_send()


def others(k_count, own):
    return [(own + k) % k_count for k in range(1, k_count)]


class Deal:
    groups = ("all",)
    aliases = {}

    def __init__(self, pc, x):
        self.ins = [x]
        self.outs = [jax.ShapeDtypeStruct(x.shape, x.dtype)]
        self.sems = [pc.n_dev, pc.n_dev, 1]

    def run(self, pc, ins, outs, sems):
        (x,), (y,), (ss, rs, ls) = ins, outs, sems

        def move(i):
            j = (pc.me + i) % pc.n_dev
            k = (pc.me + pc.n_dev - i) % pc.n_dev
            return Move(x.at[j], y.at[pc.me], ss.at[j], rs.at[pc.me], pc.flat(j), y.at[k], rs.at[k])

        def start(i, carry):
            move(i).start()
            return carry

        def finish(i, carry):
            m = move(i)
            m.wait_recv()
            m.wait_send()
            return carry

        lax.fori_loop(1, pc.n_dev, start, 0)
        own = pltpu.make_async_copy(x.at[pc.me], y.at[pc.me], ls.at[0])
        own.start()
        yield
        own.wait()
        lax.fori_loop(1, pc.n_dev, finish, 0)


class PlaneGather:
    groups = ("plane",)
    aliases = {}

    def __init__(self, pc, x):
        self.ins = [x]
        self.outs = [jax.ShapeDtypeStruct((x.shape[0], pc.n_p) + x.shape[1:], x.dtype)]
        self.sems = [pc.n_p, pc.n_p, 1]

    def run(self, pc, ins, outs, sems):
        (x,), (y,), (ss, rs, ls) = ins, outs, sems
        moves = [
            Move(x, y.at[:, pc.p], ss.at[q], rs.at[pc.p], pc.dev(q, pc.r, pc.t), y.at[:, q], rs.at[q])
            for q in others(pc.n_p, pc.p)
        ]
        for m in moves:
            m.start()
        own = pltpu.make_async_copy(x, y.at[:, pc.p], ls.at[0])
        own.start()
        yield
        own.wait()
        for m in moves:
            m.wait_recv()
            m.wait_send()


class PlaneScatter:
    groups = ("plane",)
    aliases = {}

    def __init__(self, pc, x):
        self.ins = [x]
        self.outs = [jax.ShapeDtypeStruct((pc.n_p, x.shape[0]) + x.shape[2:], x.dtype)]
        self.sems = [pc.n_p, pc.n_p]

    def run(self, pc, ins, outs, sems):
        (x,), (y,), (ss, rs) = ins, outs, sems
        moves = [
            Move(x.at[:, q], y.at[pc.p], ss.at[q], rs.at[pc.p], pc.dev(q, pc.r, pc.t), y.at[q], rs.at[q])
            for q in others(pc.n_p, pc.p)
        ]
        for m in moves:
            m.start()
        yield
        for m in moves:
            m.wait_recv()
            m.wait_send()


class TallScatter:
    groups = ("tall",)
    aliases = {}

    def __init__(self, pc, x):
        self.ins = [x]
        self.outs = [jax.ShapeDtypeStruct(x.shape, x.dtype)]
        self.sems = [pc.n_t, pc.n_t]

    def run(self, pc, ins, outs, sems):
        (x,), (y,), (ss, rs) = ins, outs, sems
        moves = [
            Move(x.at[q], y.at[pc.t], ss.at[q], rs.at[pc.t], pc.dev(pc.p, pc.r, q), y.at[q], rs.at[q])
            for q in others(pc.n_t, pc.t)
        ]
        for m in moves:
            m.start()
        yield
        for m in moves:
            m.wait_recv()
            m.wait_send()


class TallGather:
    groups = ("tall",)
    aliases = {}

    def __init__(self, pc, x):
        self.ins = [x]
        self.outs = [jax.ShapeDtypeStruct((pc.n_t,) + x.shape, x.dtype)]
        self.sems = [pc.n_t, pc.n_t, 1]

    def run(self, pc, ins, outs, sems):
        (x,), (y,), (ss, rs, ls) = ins, outs, sems
        moves = [
            Move(x, y.at[pc.t], ss.at[q], rs.at[pc.t], pc.dev(pc.p, pc.r, q), y.at[q], rs.at[q])
            for q in others(pc.n_t, pc.t)
        ]
        for m in moves:
            m.start()
        own = pltpu.make_async_copy(x, y.at[pc.t], ls.at[0])
        own.start()
        yield
        own.wait()
        for m in moves:
            m.wait_recv()
            m.wait_send()


class Spread:
    groups = ("all",)
    aliases = {}

    def __init__(self, pc, x):
        self.ins = [x]
        self.outs = [jax.ShapeDtypeStruct((pc.n_dev,) + x.shape, x.dtype)]
        self.sems = [pc.n_dev, pc.n_dev, 1]

    def run(self, pc, ins, outs, sems):
        (x,), (y,), (ss, rs, ls) = ins, outs, sems

        def move(i):
            j = (pc.me + i) % pc.n_dev
            k = (pc.me + pc.n_dev - i) % pc.n_dev
            return Move(x, y.at[pc.me], ss.at[j], rs.at[pc.me], pc.flat(j), y.at[k], rs.at[k])

        def start(i, carry):
            move(i).start()
            return carry

        def finish(i, carry):
            m = move(i)
            m.wait_recv()
            m.wait_send()
            return carry

        lax.fori_loop(1, pc.n_dev, start, 0)
        own = pltpu.make_async_copy(x, y.at[pc.me], ls.at[0])
        own.start()
        yield
        own.wait()
        lax.fori_loop(1, pc.n_dev, finish, 0)


class HeadWeights:
    groups = ("plane", "tall", "near")
    aliases = {}

    def __init__(self, pc, x):
        mats, rows, cols = x.shape
        self.ins = [x]
        self.outs = [
            jax.ShapeDtypeStruct((pc.n_t,) + x.shape, x.dtype),
            jax.ShapeDtypeStruct((mats, pc.n_p, pc.n_r, rows, cols), x.dtype),
        ]
        self.sems = [pc.n_t, pc.n_t, pc.n_p, pc.n_p, pc.n_r, pc.n_r, 2]

    def run(self, pc, ins, outs, sems):
        (x,), (a, f) = ins, outs
        s1, r1, s2, r2, s3, r3, ls = sems
        first = [
            Move(x, a.at[pc.t], s1.at[q], r1.at[pc.t], pc.dev(pc.p, pc.r, q), a.at[q], r1.at[q])
            for q in others(pc.n_t, pc.t)
        ]
        for m in first:
            m.start()
        own = pltpu.make_async_copy(x, a.at[pc.t], ls.at[0])
        own.start()
        yield
        own.wait()
        for m in first:
            m.wait_recv()
        second = [
            Move(
                a.at[q], f.at[:, pc.p, pc.r], s2.at[q], r2.at[pc.p], pc.dev(q, pc.r, pc.t), f.at[:, q, pc.r], r2.at[q]
            )
            for q in others(pc.n_p, pc.p)
        ]
        for m in second:
            m.start()
        own = pltpu.make_async_copy(a.at[pc.p], f.at[:, pc.p, pc.r], ls.at[1])
        own.start()
        yield
        own.wait()
        for m in second:
            m.wait_recv()
        third = [
            Move(
                f.at[:, :, pc.r], f.at[:, :, pc.r], s3.at[q], r3.at[pc.r], pc.dev(pc.p, q, pc.t), f.at[:, :, q], r3.at[q]
            )
            for q in others(pc.n_r, pc.r)
        ]
        for m in third:
            m.start()
        yield
        for m in third:
            m.wait_recv()
        for m in first + second + third:
            m.wait_send()


class HiddenSplit:
    groups = ("plane",)
    aliases = {}

    def __init__(self, pc, x):
        self.ins = [x]
        self.outs = [jax.ShapeDtypeStruct((pc.n_p, pc.n_r) + x.shape, x.dtype)]
        self.sems = [pc.n_p, pc.n_p, pc.n_p, pc.n_p, 2]

    def run(self, pc, ins, outs, sems):
        (x,), (g,), (s1, r1, s2, r2, ls) = ins, outs, sems

        def pieces(q):
            two = Move(
                x.at[:, lanes(src_tile(q, pc.t), 2)],
                g.at[pc.p, pc.r, :, lanes(dst_tile(q, pc.t), 2)],
                s1.at[q],
                r1.at[pc.p],
                pc.dev(q, pc.r, pc.t),
                g.at[q, pc.r, :, lanes(dst_tile(pc.p, pc.t), 2)],
                r1.at[q],
            )
            one = Move(
                x.at[:, lanes(src_tile(q, pc.t) + 2, 1)],
                g.at[pc.p, pc.r, :, lanes(dst_tile(q, pc.t) + 2, 1)],
                s2.at[q],
                r2.at[pc.p],
                pc.dev(q, pc.r, pc.t),
                g.at[q, pc.r, :, lanes(dst_tile(pc.p, pc.t) + 2, 1)],
                r2.at[q],
            )
            return two, one

        for q in others(pc.n_p, pc.p):
            two, one = pieces(q)
            two.start()
            pl.when(width3(q, pc.t))(one.start)
        own2 = pltpu.make_async_copy(
            x.at[:, lanes(src_tile(pc.p, pc.t), 2)],
            g.at[pc.p, pc.r, :, lanes(dst_tile(pc.p, pc.t), 2)],
            ls.at[0],
        )
        own1 = pltpu.make_async_copy(
            x.at[:, lanes(src_tile(pc.p, pc.t) + 2, 1)],
            g.at[pc.p, pc.r, :, lanes(dst_tile(pc.p, pc.t) + 2, 1)],
            ls.at[1],
        )
        own2.start()
        pl.when(width3(pc.p, pc.t))(own1.start)
        yield
        own2.wait()
        pl.when(width3(pc.p, pc.t))(own1.wait)
        for q in others(pc.n_p, pc.p):
            two, one = pieces(q)
            two.wait_recv()
            two.wait_send()
            pl.when(width3(pc.p, pc.t))(one.wait_recv)
            pl.when(width3(q, pc.t))(one.wait_send)


class HiddenGather:
    groups = ("tall", "near")
    aliases = {0: 0}

    def __init__(self, pc, x):
        self.ins = [x]
        self.outs = [jax.ShapeDtypeStruct(x.shape, x.dtype)]
        self.sems = [pc.n_t, pc.n_t, pc.n_t, pc.n_t, pc.n_r, pc.n_r]

    def run(self, pc, ins, outs, sems):
        (g,), (s1, r1, s2, r2, s3, r3) = outs, sems

        def pieces(q):
            here = dst_tile(pc.p, pc.t)
            there = dst_tile(pc.p, q)
            dev = pc.dev(pc.p, pc.r, q)
            two = Move(
                g.at[:, pc.r, :, lanes(here, 2)],
                g.at[:, pc.r, :, lanes(here, 2)],
                s1.at[q],
                r1.at[pc.t],
                dev,
                g.at[:, pc.r, :, lanes(there, 2)],
                r1.at[q],
            )
            one = Move(
                g.at[:, pc.r, :, lanes(here + 2, 1)],
                g.at[:, pc.r, :, lanes(here + 2, 1)],
                s2.at[q],
                r2.at[pc.t],
                dev,
                g.at[:, pc.r, :, lanes(there + 2, 1)],
                r2.at[q],
            )
            return two, one

        for q in others(pc.n_t, pc.t):
            two, one = pieces(q)
            two.start()
            pl.when(width3(pc.p, pc.t))(one.start)
        yield
        for q in others(pc.n_t, pc.t):
            two, one = pieces(q)
            two.wait_recv()
            pl.when(width3(pc.p, q))(one.wait_recv)
        third = [
            Move(g.at[:, pc.r], g.at[:, pc.r], s3.at[q], r3.at[pc.r], pc.dev(pc.p, q, pc.t), g.at[:, q], r3.at[q])
            for q in others(pc.n_r, pc.r)
        ]
        for m in third:
            m.start()
        yield
        for m in third:
            m.wait_recv()
            m.wait_send()
        for q in others(pc.n_t, pc.t):
            two, one = pieces(q)
            two.wait_send()
            pl.when(width3(pc.p, pc.t))(one.wait_send)


class NearScatter:
    groups = ("near",)
    aliases = {}

    def __init__(self, pc, x):
        self.ins = [x]
        self.outs = [jax.ShapeDtypeStruct((pc.n_r, x.shape[0]) + x.shape[2:], x.dtype)]
        self.sems = [pc.n_r, pc.n_r]

    def run(self, pc, ins, outs, sems):
        (x,), (y,), (ss, rs) = ins, outs, sems
        moves = [
            Move(x.at[:, q], y.at[pc.r], ss.at[q], rs.at[pc.r], pc.dev(pc.p, q, pc.t), y.at[q], rs.at[q])
            for q in others(pc.n_r, pc.r)
        ]
        for m in moves:
            m.start()
        yield
        for m in moves:
            m.wait_recv()
            m.wait_send()


class HiddenTall:
    groups = ("tall",)
    aliases = {}

    def __init__(self, pc, x):
        n_p, rows, _ = x.shape
        self.ins = [x]
        self.outs = [jax.ShapeDtypeStruct((pc.n_t, n_p, rows, 3 * LANES), x.dtype)]
        self.sems = [pc.n_t, pc.n_t, pc.n_t, pc.n_t, 2]

    def run(self, pc, ins, outs, sems):
        (x,), (y,), (s1, r1, s2, r2, ls) = ins, outs, sems

        def pieces(q):
            there = dst_tile(pc.p, q)
            dev = pc.dev(pc.p, pc.r, q)
            two = Move(
                x.at[:, :, lanes(there, 2)],
                y.at[pc.t, :, :, pl.ds(0, 2 * LANES)],
                s1.at[q],
                r1.at[pc.t],
                dev,
                y.at[q, :, :, pl.ds(0, 2 * LANES)],
                r1.at[q],
            )
            one = Move(
                x.at[:, :, lanes(there + 2, 1)],
                y.at[pc.t, :, :, pl.ds(2 * LANES, LANES)],
                s2.at[q],
                r2.at[pc.t],
                dev,
                y.at[q, :, :, pl.ds(2 * LANES, LANES)],
                r2.at[q],
            )
            return two, one

        for q in others(pc.n_t, pc.t):
            two, one = pieces(q)
            two.start()
            pl.when(width3(pc.p, q))(one.start)
        here = dst_tile(pc.p, pc.t)
        own2 = pltpu.make_async_copy(x.at[:, :, lanes(here, 2)], y.at[pc.t, :, :, pl.ds(0, 2 * LANES)], ls.at[0])
        own1 = pltpu.make_async_copy(
            x.at[:, :, lanes(here + 2, 1)], y.at[pc.t, :, :, pl.ds(2 * LANES, LANES)], ls.at[1]
        )
        own2.start()
        pl.when(width3(pc.p, pc.t))(own1.start)
        yield
        own2.wait()
        pl.when(width3(pc.p, pc.t))(own1.wait)
        for q in others(pc.n_t, pc.t):
            two, one = pieces(q)
            two.wait_recv()
            two.wait_send()
            pl.when(width3(pc.p, pc.t))(one.wait_recv)
            pl.when(width3(pc.p, q))(one.wait_send)


class HiddenPlane:
    groups = ("plane",)
    aliases = {}

    def __init__(self, pc, x, hidden):
        self.ins = [x]
        self.outs = [jax.ShapeDtypeStruct((x.shape[1], hidden), x.dtype)]
        self.sems = [pc.n_p, pc.n_p, pc.n_p, pc.n_p, 2]

    def run(self, pc, ins, outs, sems):
        (x,), (y,), (s1, r1, s2, r2, ls) = ins, outs, sems
        here = src_tile(pc.p, pc.t)

        def pieces(q):
            there = src_tile(q, pc.t)
            dev = pc.dev(q, pc.r, pc.t)
            two = Move(
                x.at[q, :, pl.ds(0, 2 * LANES)],
                y.at[:, lanes(here, 2)],
                s1.at[q],
                r1.at[pc.p],
                dev,
                y.at[:, lanes(there, 2)],
                r1.at[q],
            )
            one = Move(
                x.at[q, :, pl.ds(2 * LANES, LANES)],
                y.at[:, lanes(here + 2, 1)],
                s2.at[q],
                r2.at[pc.p],
                dev,
                y.at[:, lanes(there + 2, 1)],
                r2.at[q],
            )
            return two, one

        for q in others(pc.n_p, pc.p):
            two, one = pieces(q)
            two.start()
            pl.when(width3(pc.p, pc.t))(one.start)
        own2 = pltpu.make_async_copy(x.at[pc.p, :, pl.ds(0, 2 * LANES)], y.at[:, lanes(here, 2)], ls.at[0])
        own1 = pltpu.make_async_copy(
            x.at[pc.p, :, pl.ds(2 * LANES, LANES)], y.at[:, lanes(here + 2, 1)], ls.at[1]
        )
        own2.start()
        pl.when(width3(pc.p, pc.t))(own1.start)
        yield
        own2.wait()
        pl.when(width3(pc.p, pc.t))(own1.wait)
        for q in others(pc.n_p, pc.p):
            two, one = pieces(q)
            two.wait_recv()
            two.wait_send()
            pl.when(width3(q, pc.t))(one.wait_recv)
            pl.when(width3(pc.p, pc.t))(one.wait_send)


def greet(pc, groups):
    barrier = pltpu.get_barrier_semaphore()

    def signal(dev):
        pl.semaphore_signal(barrier, inc=1, device_id=dev, device_id_type=MESH)

    if "all" in groups:

        def step(i, carry):
            signal(pc.flat((pc.me + i) % pc.n_dev))
            return carry

        lax.fori_loop(1, pc.n_dev, step, 0)
        count = pc.n_dev - 1
    else:
        devs = []
        if "plane" in groups:
            devs += [pc.dev(q, pc.r, pc.t) for q in others(pc.n_p, pc.p)]
        if "tall" in groups:
            devs += [pc.dev(pc.p, pc.r, q) for q in others(pc.n_t, pc.t)]
        if "near" in groups:
            devs += [pc.dev(pc.p, q, pc.t) for q in others(pc.n_r, pc.r)]
        for dev in devs:
            signal(dev)
        count = len(devs)
    pl.semaphore_wait(barrier, count)


def exchange(collective_id, tasks):
    ins = [x for task in tasks for x in task.ins]
    outs = [y for task in tasks for y in task.outs]
    sems = [n for task in tasks for n in task.sems]
    aliases = {}
    at_in = at_out = 0
    for task in tasks:
        for i, o in task.aliases.items():
            aliases[at_in + i] = at_out + o
        at_in += len(task.ins)
        at_out += len(task.outs)
    groups = sorted({g for task in tasks for g in task.groups})

    def kernel(*refs):
        pc = Place()
        in_refs = list(refs[: len(ins)])
        out_refs = list(refs[len(ins) : len(ins) + len(outs)])
        sem_refs = list(refs[len(ins) + len(outs) :])
        greet(pc, groups)
        live = []
        for task in tasks:
            args = [[refs_.pop(0) for _ in range(n)] for refs_, n in (
                (in_refs, len(task.ins)),
                (out_refs, len(task.outs)),
                (sem_refs, len(task.sems)),
            )]
            live.append(task.run(pc, *args))
        while live:
            still = []
            for gen in live:
                try:
                    next(gen)
                    still.append(gen)
                except StopIteration:
                    pass
            live = still

    results = pl.pallas_call(
        kernel,
        out_shape=tuple(outs),
        in_specs=[pl.BlockSpec(memory_space=pl.ANY)] * len(ins),
        out_specs=tuple([pl.BlockSpec(memory_space=pl.ANY)] * len(outs)),
        scratch_shapes=[pltpu.SemaphoreType.DMA((n,)) for n in sems],
        input_output_aliases=aliases,
        compiler_params=pltpu.CompilerParams(collective_id=collective_id, has_side_effects=True),
    )(*ins)
    results = list(results)
    return [[results.pop(0) for _ in task.outs] for task in tasks]


def merged(slots, own, at):
    total = own.astype(F32)
    for q in range(slots.shape[0]):
        total = total + jnp.where(q == at, 0, slots[q]).astype(F32)
    return total


def pick(x, at, axis):
    return lax.dynamic_index_in_dim(x, at, axis, keepdims=False)


def rms_norm(values_in):
    return values_in * lax.rsqrt(jnp.mean(values_in * values_in, axis=-1, keepdims=True) + EPSILON)


def residual_step(hidden, branch, rate):
    return rms_norm(hidden + rate * (rms_norm(branch) - hidden))


def head_norm(query_raw, keys_raw, scale_grid):
    return (scale_grid * rms_norm(query_raw), scale_grid * rms_norm(keys_raw))


def swiglu(up_raw, gate_raw, scale_upper, scale_gating):
    return jax.nn.silu(scale_gating * gate_raw) * (scale_upper * up_raw)


def mm(a, b):
    return jnp.dot(a, b, preferred_element_type=F32)


def times_rows(operand, weight_mat):
    return lax.dot_general(operand, weight_mat, (((1,), (1,)), ((), ())), preferred_element_type=F32)


def times_cols(operand, other_mat):
    return lax.dot_general(operand, other_mat, (((0,), (0,)), ((), ())), preferred_element_type=F32)


def doc_allowed(lengths_row, tok_count):
    count = lengths_row.shape[0]
    upto = jnp.arange(count)[:, None] >= jnp.arange(count)[None, :]
    doc_ends = jnp.sum(jnp.where(upto, lengths_row[None, :], 0), axis=1)
    places = jnp.arange(tok_count, dtype=jnp.int32)
    segment = jnp.sum((places[:, None] >= doc_ends[None, :]).astype(jnp.int32), axis=1)
    return (segment[:, None] == segment[None, :]) & (places[None, :] <= places[:, None])


def body(
    tokens,
    cotangent,
    slot,
    lengths,
    w_query,
    w_key,
    w_value,
    w_out,
    w_up,
    w_gate,
    w_down,
    scale_qk,
    scale_up,
    scale_gate,
    rate_attn,
    rate_mlp,
):
    pc = Place()
    n_p, n_r, n_t, n_dev = pc.n_p, pc.n_r, pc.n_t, pc.n_dev
    rows_dev, width = tokens.shape
    part = rows_dev // MB
    tok_count = part * n_p
    all_tok = MB * tok_count
    cap = rows_dev // n_dev
    w_rows = w_query.shape[1]
    head_cols = w_query.shape[2]
    heads = head_cols // HEAD_DIM
    hid = w_up.shape[2]
    group = pc.r * n_t + pc.t
    owner = group * n_p + pc.p

    table = slot.reshape(n_dev, rows_dev)
    own_slots = lax.dynamic_index_in_dim(table, pc.me, 0, keepdims=False)
    d = own_slots // rows_dev
    to_dev = ((d % n_p) * n_r + (d // n_p) // n_t) * n_t + (d // n_p) % n_t
    places = jnp.arange(rows_dev, dtype=jnp.int32)
    before = (d[:, None] == d[None, :]) & (places[None, :] < places[:, None])
    rank = jnp.sum(before.astype(jnp.int32), axis=1)
    send_at = to_dev * cap + rank
    send_hot = (places[:, None] == send_at[None, :]).astype(BF)

    sel = table // rows_dev == owner
    tri = (places[:, None] < places[None, :]).astype(BF)
    ranks = mm(sel.astype(BF), tri).astype(jnp.int32)
    kth = sel[:, None, :] & (ranks[:, None, :] == jnp.arange(cap, dtype=jnp.int32)[None, :, None])
    owner_rows = jnp.sum(jnp.where(kth, (table - owner * rows_dev)[:, None, :], 0), axis=2).reshape(rows_dev)
    recv_hot = (places[:, None] == owner_rows[None, :]).astype(BF)

    sent = jnp.concatenate(
        [
            mm(send_hot, tokens).astype(BF).reshape(n_dev, cap, width),
            mm(send_hot, cotangent).astype(BF).reshape(n_dev, cap, width),
        ],
        axis=1,
    )
    w4 = jnp.concatenate([w_query, w_key, w_value, w_out], axis=0)
    small = jnp.concatenate([scale_qk[0], scale_up[0], scale_gate[0]])
    small_rows = -(-small.shape[0] // (8 * LANES)) * 8
    small_sent = jnp.pad(small, (0, small_rows * LANES - small.shape[0])).reshape(small_rows, LANES)
    (arrived,), (small,), (_, wh), (gu,), (gg,), (gd,) = exchange(
        0,
        [
            Deal(pc, sent),
            TallGather(pc, small_sent),
            HeadWeights(pc, w4),
            HiddenSplit(pc, w_up[0]),
            HiddenSplit(pc, w_gate[0]),
            HiddenSplit(pc, w_down[0]),
        ],
    )
    wh = wh.reshape(4, width, head_cols)
    tok_b = mm(recv_hot, arrived[:, :cap].reshape(rows_dev, width)).astype(BF)
    grad_in = mm(recv_hot, arrived[:, cap:].reshape(rows_dev, width))
    hidden = tok_b.astype(F32)

    small = small.reshape(n_t, small_rows * LANES)
    sqk = lax.dynamic_index_in_dim(small[:, :head_cols], pc.p, 0, keepdims=False).reshape(heads, HEAD_DIM)
    tiles = hid // LANES
    t_all = jnp.arange(n_t * tiles, dtype=jnp.int32) // tiles
    tile_all = jnp.arange(n_t * tiles, dtype=jnp.int32) % tiles
    first = src_tile(pc.p, t_all)
    count = 2 + width3(pc.p, t_all).astype(jnp.int32)
    mine = (tile_all >= first) & (tile_all < first + count)
    spot = jnp.where(mine, dst_tile(pc.p, t_all) + tile_all - first, -1)
    hot = spot[None, :] == jnp.arange(tiles, dtype=jnp.int32)[:, None]

    def take_tiles(x):
        return jnp.sum(jnp.where(hot[:, :, None], x.reshape(1, n_t * tiles, LANES), 0.0), axis=1).reshape(hid)

    def put_tiles(x):
        return jnp.sum(jnp.where(hot[:, :, None], x.reshape(tiles, 1, LANES), 0.0), axis=0).reshape(n_t * hid)

    sup = take_tiles(small[:, head_cols : head_cols + hid])
    sgate = take_tiles(small[:, head_cols + hid : head_cols + 2 * hid])
    rattn, rmlp = rate_attn[0], rate_mlp[0]

    (hb,), (gu,) = exchange(1, [PlaneGather(pc, tok_b.reshape(MB, part, width)), HiddenGather(pc, gu)])
    hb = hb.reshape(all_tok, width)
    wup = gu.reshape(width, hid)
    grid = (MB, tok_count, heads, HEAD_DIM)
    q_raw = mm(hb, wh[0]).reshape(grid)
    k_raw = mm(hb, wh[1]).reshape(grid)
    v_b = mm(hb, wh[2]).astype(BF).reshape(grid)
    q_hat, k_hat = head_norm(q_raw, k_raw, sqk)
    q_b, k_b = q_hat.astype(BF), k_hat.astype(BF)
    own_lengths = lax.dynamic_slice_in_dim(lengths, group * MB, MB, 0)
    allowed = jnp.stack([doc_allowed(own_lengths[m], tok_count) for m in range(MB)])

    def scores_of():
        s = jnp.einsum("mqhd,mkhd->mhqk", q_b, k_b, preferred_element_type=F32) * HEAD_DIM ** (-0.5)
        return jnp.where(allowed[:, None], s, MASKED)

    scores = scores_of()
    row_max = jnp.max(scores, axis=-1, keepdims=True)
    lse = row_max + jnp.log(jnp.sum(jnp.exp(scores - row_max), axis=-1, keepdims=True))
    probs_b = jnp.exp(scores - lse).astype(BF)
    o_b = jnp.einsum("mhqk,mkhd->mqhd", probs_b, v_b, preferred_element_type=F32).astype(BF).reshape(all_tok, head_cols)
    part_a = times_rows(o_b, wh[3]).astype(BF).reshape(MB, n_p, part, width)
    (got_a,), (gg,) = exchange(2, [PlaneScatter(pc, part_a), HiddenGather(pc, gg)])
    wgate = gg.reshape(width, hid)
    branch = merged(got_a, pick(part_a, pc.p, 1), pc.p).reshape(rows_dev, width)
    middle, pull_attn = jax.vjp(residual_step, hidden, branch, rattn)

    (hb1,), (gd,) = exchange(3, [PlaneGather(pc, middle.astype(BF).reshape(MB, part, width)), HiddenGather(pc, gd)])
    hb1 = hb1.reshape(all_tok, width)
    wdown = gd.reshape(width, hid)
    up_raw = mm(hb1, wup)
    gate_raw = mm(hb1, wgate)
    act, pull_glu = jax.vjp(swiglu, up_raw, gate_raw, sup, sgate)
    act_b = act.astype(BF)
    part_c = times_rows(act_b, wdown).astype(BF).reshape(MB, n_p, part, width)
    ((got_c,),) = exchange(4, [PlaneScatter(pc, part_c)])
    branch_mlp = merged(got_c, pick(part_c, pc.p, 1), pc.p).reshape(rows_dev, width)
    output, pull_mlp = jax.vjp(residual_step, middle, branch_mlp, rmlp)

    def to_arrival(x):
        return times_cols(recv_hot, x.astype(BF)).astype(BF).reshape(n_dev, cap, width)

    grad_middle, grad_c, grad_rmlp = pull_mlp(grad_in)
    (dcb,), (back_out,) = exchange(
        5, [PlaneGather(pc, grad_c.astype(BF).reshape(MB, part, width)), Deal(pc, to_arrival(output))]
    )
    dcb = dcb.reshape(all_tok, width)
    d_act = mm(dcb, wdown)
    d_up, d_gate, grad_sup, grad_sgate = pull_glu(d_act)
    dub, dgb = d_up.astype(BF), d_gate.astype(BF)
    part_h1 = (times_rows(dub, wup) + times_rows(dgb, wgate)).astype(BF).reshape(MB, n_p, part, width)
    split = (n_p, n_r, w_rows, hid)
    g_down = times_cols(dcb, act_b).astype(BF).reshape(split)
    g_up = times_cols(hb1, dub).astype(BF).reshape(split)
    g_gate = times_cols(hb1, dgb).astype(BF).reshape(split)

    def near_sum(x, own):
        return merged(x, pick(own, pc.r, 1), pc.r).astype(BF)

    (got_h1,), (n_down,), (n_up,), (n_gate,) = exchange(
        6,
        [PlaneScatter(pc, part_h1), NearScatter(pc, g_down), NearScatter(pc, g_up), NearScatter(pc, g_gate)],
    )
    grad_middle = grad_middle + merged(got_h1, pick(part_h1, pc.p, 1), pc.p).reshape(rows_dev, width)
    grad_hidden, grad_a, grad_rattn = pull_attn(grad_middle)
    (dab,), (t_down,) = exchange(
        7, [PlaneGather(pc, grad_a.astype(BF).reshape(MB, part, width)), HiddenTall(pc, near_sum(n_down, g_down))]
    )

    def tall_sum(x):
        valid = jnp.arange(3 * LANES) < jnp.where(width3(pc.p, pc.t), 3, 2) * LANES
        return jnp.sum(jnp.where(valid, x, 0).astype(F32), axis=0).astype(BF)

    dab = dab.reshape(all_tok, width)
    do_b = mm(dab, wh[3]).astype(BF).reshape(grid)
    probs = jnp.exp(scores_of() - lse)
    probs_b2 = probs.astype(BF)
    d_probs = jnp.einsum("mqhd,mkhd->mhqk", do_b, v_b, preferred_element_type=F32)
    dvb = jnp.einsum("mhqk,mqhd->mkhd", probs_b2, do_b, preferred_element_type=F32).astype(BF).reshape(all_tok, head_cols)
    inner = jnp.sum(probs * d_probs, axis=-1, keepdims=True)
    d_s = (probs * (d_probs - inner)).astype(BF)
    d_qhat = jnp.einsum("mhqk,mkhd->mqhd", d_s, k_b, preferred_element_type=F32) * HEAD_DIM ** (-0.5)
    d_khat = jnp.einsum("mhqk,mqhd->mkhd", d_s, q_b, preferred_element_type=F32) * HEAD_DIM ** (-0.5)
    _, pull_norm = jax.vjp(head_norm, q_raw, k_raw, sqk)
    d_q, d_k, grad_sqk = pull_norm((d_qhat, d_khat))
    dqb = d_q.astype(BF).reshape(all_tok, head_cols)
    dkb = d_k.astype(BF).reshape(all_tok, head_cols)
    part_h = (times_rows(dqb, wh[0]) + times_rows(dkb, wh[1]) + times_rows(dvb, wh[2])).astype(BF)
    part_h = part_h.reshape(MB, n_p, part, width)
    g_heads = jnp.stack([times_cols(hb, dqb), times_cols(hb, dkb), times_cols(hb, dvb), times_cols(dab, o_b)])
    g_heads = g_heads.astype(BF).reshape(4 * n_p, n_r, w_rows, head_cols)
    (got_h,), (n_heads,), (t_up,), (f_down,) = exchange(
        8,
        [
            PlaneScatter(pc, part_h),
            NearScatter(pc, g_heads),
            HiddenTall(pc, near_sum(n_up, g_up)),
            HiddenPlane(pc, tall_sum(t_down), hid),
        ],
    )
    grad_hidden = grad_hidden + merged(got_h, pick(part_h, pc.p, 1), pc.p).reshape(rows_dev, width)
    s_heads = near_sum(n_heads, g_heads).reshape(4, n_p, w_rows, head_cols)
    qk_full = lax.dynamic_update_slice(jnp.zeros((n_t * head_cols,), F32), grad_sqk.reshape(-1), (pc.p * head_cols,))
    vec = jnp.concatenate([qk_full, put_tiles(grad_sup), put_tiles(grad_sgate), grad_rattn, grad_rmlp])
    vec = jnp.pad(vec, (0, -vec.shape[0] % (n_dev * 8 * LANES))).reshape(n_dev, -1, LANES)
    (back_grad,), (vec_got,), (t_gate,), (f_up,), (p_heads,) = exchange(
        9,
        [
            Deal(pc, to_arrival(grad_hidden)),
            Deal(pc, vec),
            HiddenTall(pc, near_sum(n_gate, g_gate)),
            HiddenPlane(pc, tall_sum(t_up), hid),
            PlaneScatter(pc, s_heads),
        ],
    )
    own_slot = (jnp.arange(n_p) == pc.p)[:, None, None, None]
    p_heads = jnp.where(own_slot, pick(s_heads, pc.p, 1)[None], p_heads)
    vec_sum = jnp.sum(vec_got, axis=0)
    (z_heads,), (f_gate,), (vec,) = exchange(
        10, [TallScatter(pc, p_heads), HiddenPlane(pc, tall_sum(t_gate), hid), Spread(pc, vec_sum)]
    )
    w_out_all = merged(z_heads, pick(p_heads, pc.t, 0), pc.t)[:, None]
    vec = vec.reshape(-1)

    at = n_t * head_cols
    out_sqk = lax.dynamic_slice_in_dim(vec[:at], pc.t * head_cols, head_cols)[None]
    out_sup = lax.dynamic_slice_in_dim(vec[at : at + n_t * hid], pc.t * hid, hid)[None]
    out_sgate = lax.dynamic_slice_in_dim(vec[at + n_t * hid : at + 2 * n_t * hid], pc.t * hid, hid)[None]
    at = at + 2 * n_t * hid
    out_rattn = vec[at : at + width][None]
    out_rmlp = vec[at + width : at + 2 * width][None]

    def from_back(x):
        return times_cols(send_hot, x.reshape(rows_dev, width))

    return (
        from_back(back_out),
        from_back(back_grad),
        w_out_all[0],
        w_out_all[1],
        w_out_all[2],
        w_out_all[3],
        f_up.astype(F32)[None],
        f_gate.astype(F32)[None],
        f_down.astype(F32)[None],
        out_sqk,
        out_sup,
        out_sgate,
        out_rattn,
        out_rmlp,
    )


def solution(mesh):
    tok = P(("dp", "tensor"), None)
    mat = P(None, "dp", "tensor")
    vec = P(None, "tensor")
    in_specs = (tok, tok, P(), P()) + (mat,) * 7 + (vec,) * 3 + (P(), P())
    out_specs = (tok, tok) + (mat,) * 7 + (vec,) * 3 + (P(), P())
    return jax.shard_map(body, mesh=mesh, in_specs=in_specs, out_specs=out_specs, check_vma=False)
```

```python
import types

import jax
import jax.numpy as jnp
from jax import lax
from jax.experimental import pallas as pl
from jax.experimental.pallas import tpu as pltpu
from jax.sharding import PartitionSpec as P

HEAD_DIM = 64
MB = 2
LANES = 128
QUADS = 4 * HEAD_DIM
CHUNK = 2 * LANES
ROW_STEP = 32
PAD = 8
VMEM_LIMIT = 63 * 2**20

EPSILON = 1e-06
MASKED = -1e30
BF = jnp.bfloat16
F32 = jnp.float32
MESH = pl.DeviceIdType.MESH
VM = pltpu.VMEM
DMA = pltpu.SemaphoreType.DMA
SDS = jax.ShapeDtypeStruct


class Place:
    def __init__(self):
        self.n_t = lax.axis_size("tensor")
        self.n_dp = lax.axis_size("dp")
        self.n_p = self.n_t
        self.n_r = self.n_dp // self.n_p
        self.n_dev = self.n_dp * self.n_t
        if self.n_t != 4:
            raise ValueError("tensor size")
        dp = lax.axis_index("dp")
        self.t = lax.axis_index("tensor")
        self.p = dp // self.n_r
        self.r = dp % self.n_r
        self.me = dp * self.n_t + self.t

    def dev(self, p, r, t):
        return (p * self.n_r + r, t)

    def flat(self, j):
        return (j // self.n_t, j % self.n_t)


def width3(p, t):
    return (p + t) % 2 == 0


def src_tile(p, t):
    return 5 * (p // 2) + (p % 2) * (3 - t % 2)


def dst_tile(p, t):
    return 5 * (t // 2) + (t % 2) * (3 - p % 2)


def lanes(tile, count):
    return pl.ds(pl.multiple_of(tile * LANES, LANES), count * LANES)


TWO, ONE = pl.ds(0, 2 * LANES), pl.ds(2 * LANES, LANES)


def remote(src, dst, send, recv, dev):
    return pltpu.make_async_remote_copy(
        src_ref=src, dst_ref=dst, send_sem=send, recv_sem=recv, device_id=dev, device_id_type=MESH
    )


class Move:
    def __init__(self, src, dst, send, recv, dev, landing, landed, cond_out=None, cond_in=None):
        self.going = (src, dst, send, recv, dev)
        self.coming = (landing, landing, send, landed, dev)
        self.cond_out, self.cond_in = cond_out, cond_in

    @staticmethod
    def under(cond, act):
        if cond is None:
            act()
        else:
            pl.when(cond)(act)

    def start(self):
        self.under(self.cond_out, lambda: remote(*self.going).start())

    def wait_send(self):
        self.under(self.cond_out, lambda: remote(*self.going).wait_send())

    def wait_recv(self):
        self.under(self.cond_in, lambda: remote(*self.coming).wait_recv())


class Moves:
    def __init__(self, moves):
        self.moves = moves

    def start(self):
        for m in self.moves:
            m.start()

    def wait_recv(self):
        for m in self.moves:
            m.wait_recv()

    def wait_send(self):
        for m in self.moves:
            m.wait_send()


def others(count, own):
    order = [2, 1, 3] if count == 4 else list(range(1, count))
    return [(own + k) % count for k in order]


def pair(n):
    return [DMA((n,)), DMA((n,))]


class Deal:
    @staticmethod
    def sems(pc):
        return [DMA((pc.n_dev,)), DMA((pc.n_dev,)), DMA((1,))]

    def __init__(self, pc, x, y, sems, same=False):
        self.pc, self.x, self.y, self.sems, self.same = pc, x, y, sems, same

    def src(self, j):
        return self.x if self.same else self.x.at[j]

    def move(self, i):
        pc, (ss, rs, _) = self.pc, self.sems
        j = (pc.me + i) % pc.n_dev
        k = (pc.me + pc.n_dev - i) % pc.n_dev
        return Move(self.src(j), self.y.at[pc.me], ss.at[j], rs.at[pc.me], pc.flat(j), self.y.at[k], rs.at[k])

    def loop(self, act):
        def step(i, carry):
            act(self.move(i))
            return carry

        lax.fori_loop(1, self.pc.n_dev, step, 0)

    def own(self):
        return pltpu.make_async_copy(self.src(self.pc.me), self.y.at[self.pc.me], self.sems[2].at[0])

    def start(self):
        self.loop(lambda m: m.start())
        self.own().start()

    def wait_recv(self):
        self.own().wait()
        self.loop(lambda m: m.wait_recv())

    def wait_send(self):
        self.loop(lambda m: m.wait_send())


class Tall:
    @staticmethod
    def sems(pc, pieces):
        return [DMA((pieces, pc.n_t + 1)), DMA((pieces, pc.n_t))]

    def __init__(self, pc, shard, own, sems):
        t = pc.t
        middle = (t == 1) | (t == 2)
        far, end = jnp.where(t == 2, 0, 3), jnp.where(t == 2, 3, 0)
        send, recv = sems

        def both(a, b):
            return a if b is None else a & b

        self.first, self.passed, self.at_relay = [], [], []
        for q in others(pc.n_t, t):
            for i, ((dst, c_out), src, (here, c_in)) in enumerate(zip(shard(t), own, shard(q))):
                self.first.append(
                    Move(
                        src, dst, send.at[i, q], recv.at[i, t], pc.dev(pc.p, pc.r, q), here, recv.at[i, q],
                        both(jnp.abs(q - t) != 3, c_out), both(jnp.logical_not(middle & (q == far)), c_in),
                    )
                )
        for i, (ref, c) in enumerate(shard(far)):
            self.passed.append(
                Move(
                    ref, ref, send.at[i, pc.n_t], recv.at[i, far], pc.dev(pc.p, pc.r, end), ref, recv.at[i, far],
                    both(middle, c), both(middle, c),
                )
            )

    def start(self):
        for m in self.first:
            m.start()

    def relay(self):
        for m in self.passed:
            m.wait_recv()
            m.start()

    def wait_recv(self):
        for m in self.first:
            m.wait_recv()

    def wait_send(self):
        for m in self.first + self.passed:
            m.wait_send()


def by_shard(pc, ref):
    return ref.reshape(pc.n_p, pc.n_r, ref.shape[0] // (pc.n_p * pc.n_r), ref.shape[1])


class HeadWeights:
    @staticmethod
    def sems(pc):
        return [Tall.sems(pc, 1), pair(pc.n_p), pair(pc.n_r), DMA((2,))]

    def __init__(self, pc, x, a, w, sems):
        tall, (s2, r2), (s3, r3), ls = sems
        f = by_shard(pc, w)
        self.first = Tall(pc, lambda q: [(a.at[q], None)], [x], tall)
        self.second = Moves(
            [
                Move(a.at[q], f.at[pc.p, pc.r], s2.at[q], r2.at[pc.p], pc.dev(q, pc.r, pc.t), f.at[q, pc.r], r2.at[q])
                for q in others(pc.n_p, pc.p)
            ]
        )
        self.third = Moves(
            [
                Move(f.at[:, pc.r], f.at[:, pc.r], s3.at[q], r3.at[pc.r], pc.dev(pc.p, q, pc.t), f.at[:, q], r3.at[q])
                for q in others(pc.n_r, pc.r)
            ]
        )
        self.keep1 = pltpu.make_async_copy(x, a.at[pc.t], ls.at[0])
        self.keep2 = pltpu.make_async_copy(a.at[pc.p], f.at[pc.p, pc.r], ls.at[1])

    def start(self):
        self.first.start()
        self.keep1.start()

    def relay(self):
        self.first.relay()

    def plane(self):
        self.keep1.wait()
        self.first.wait_recv()
        self.second.start()
        self.keep2.start()

    def near(self):
        self.keep2.wait()
        self.second.wait_recv()
        self.third.start()

    def wait_recv(self):
        self.third.wait_recv()

    def wait_send(self):
        self.first.wait_send()
        self.second.wait_send()
        self.third.wait_send()


class HiddenWeights:
    @staticmethod
    def sems(pc):
        return [pair(pc.n_p), pair(pc.n_p), Tall.sems(pc, 2), pair(pc.n_r), DMA((2,))]

    def __init__(self, pc, x, w, sems):
        (s1, r1), (s2, r2), tall, (s3, r3), ls = sems
        g = by_shard(pc, w)
        p, r, t = pc.p, pc.r, pc.t

        def spot(q, row, extra):
            at = dst_tile(q, t)
            return g.at[row, r, :, lanes(at + 2, 1) if extra else lanes(at, 2)]

        def piece(q, extra):
            at = src_tile(q, t)
            return x.at[:, lanes(at + 2, 1) if extra else lanes(at, 2)]

        moves = []
        for q in others(pc.n_p, p):
            dev = pc.dev(q, r, t)
            moves.append(
                Move(piece(q, False), spot(q, p, False), s1.at[q], r1.at[p], dev, spot(p, q, False), r1.at[q])
            )
            moves.append(
                Move(
                    piece(q, True), spot(q, p, True), s2.at[q], r2.at[p], dev, spot(p, q, True), r2.at[q],
                    width3(q, t), width3(p, t),
                )
            )
        self.first = Moves(moves)
        self.own = [
            (None, pltpu.make_async_copy(piece(p, False), spot(p, p, False), ls.at[0])),
            (width3(p, t), pltpu.make_async_copy(piece(p, True), spot(p, p, True), ls.at[1])),
        ]

        def shard(q):
            at = dst_tile(p, q)
            return [(g.at[:, r, :, lanes(at, 2)], None), (g.at[:, r, :, lanes(at + 2, 1)], width3(p, q))]

        self.second = Tall(pc, shard, [ref for ref, _ in shard(t)], tall)
        self.third = Moves(
            [
                Move(g.at[:, r], g.at[:, r], s3.at[q], r3.at[r], pc.dev(p, q, t), g.at[:, q], r3.at[q])
                for q in others(pc.n_r, r)
            ]
        )

    def start(self):
        self.first.start()
        for cond, copy in self.own:
            Move.under(cond, copy.start)

    def tall(self):
        for cond, copy in self.own:
            Move.under(cond, copy.wait)
        self.first.wait_recv()
        self.second.start()

    def relay(self):
        self.second.relay()

    def near(self):
        self.second.wait_recv()
        self.third.start()

    def wait_recv(self):
        self.third.wait_recv()

    def wait_send(self):
        self.first.wait_send()
        self.second.wait_send()
        self.third.wait_send()


class PlanePass:
    @staticmethod
    def sems(pc):
        return [DMA((MB, pc.n_p)), DMA((MB, pc.n_p))]

    def __init__(self, pc, source, landing, sems):
        send, recv = sems
        self.by_m = [
            Moves(
                [
                    Move(
                        source(m, q), landing(m, pc.p), send.at[m, q], recv.at[m, pc.p], pc.dev(q, pc.r, pc.t),
                        landing(m, q), recv.at[m, q],
                    )
                    for q in others(pc.n_p, pc.p)
                ]
            )
            for m in range(MB)
        ]

    def start(self, m):
        self.by_m[m].start()

    def wait_recv(self, m):
        self.by_m[m].wait_recv()

    def wait_send(self, m):
        self.by_m[m].wait_send()


def greet(pc):
    barrier = pltpu.get_barrier_semaphore()

    def step(i, carry):
        dev = pc.flat((pc.me + i) % pc.n_dev)
        pl.semaphore_signal(barrier, inc=1, device_id=dev, device_id_type=MESH)
        return carry

    lax.fori_loop(1, pc.n_dev, step, 0)
    pl.semaphore_wait(barrier, pc.n_dev - 1)


def fused(collective_id, kernel, near_ins, far_ins, outs, scratch):
    ins_leaves, ins_tree = jax.tree.flatten((near_ins, far_ins))
    outs_leaves, outs_tree = jax.tree.flatten(outs)
    scratch_leaves, scratch_tree = jax.tree.flatten(scratch)
    a, b = len(ins_leaves), len(outs_leaves)
    near = len(jax.tree.leaves(near_ins))

    def run(*refs):
        first, second = jax.tree.unflatten(ins_tree, refs[:a])
        third = jax.tree.unflatten(outs_tree, refs[a : a + b])
        fourth = jax.tree.unflatten(scratch_tree, refs[a + b :])
        kernel(
            Place(),
            types.SimpleNamespace(**first),
            types.SimpleNamespace(**second),
            types.SimpleNamespace(**third),
            types.SimpleNamespace(**fourth),
        )

    got = pl.pallas_call(
        run,
        out_shape=tuple(outs_leaves),
        in_specs=[pl.BlockSpec(memory_space=VM if i < near else pl.ANY) for i in range(a)],
        out_specs=tuple([pl.BlockSpec(memory_space=pl.ANY)] * b),
        scratch_shapes=scratch_leaves,
        compiler_params=pltpu.CompilerParams(
            collective_id=collective_id, has_side_effects=True, vmem_limit_bytes=VMEM_LIMIT
        ),
    )(*ins_leaves)
    return types.SimpleNamespace(**jax.tree.unflatten(outs_tree, got))


def dot_nt(a, b):
    return lax.dot_general(a, b, (((1,), (1,)), ((), ())), preferred_element_type=F32)


def dot_tn(a, b):
    return lax.dot_general(a, b, (((0,), (0,)), ((), ())), preferred_element_type=F32)


def dot_nn(a, b):
    return lax.dot_general(a, b, (((1,), (0,)), ((), ())), preferred_element_type=F32)


def half_means(x):
    a = lax.broadcasted_iota(jnp.int32, (LANES, LANES), 0) // HEAD_DIM
    b = lax.broadcasted_iota(jnp.int32, (LANES, LANES), 1) // HEAD_DIM
    same = jnp.where(a == b, 1.0 / HEAD_DIM, 0.0).astype(F32)
    return lax.dot_general(x, same, (((1,), (0,)), ((), ())), precision=lax.Precision.HIGHEST, preferred_element_type=F32)


def swap_halves(x):
    return pltpu.roll(x, HEAD_DIM, 1)


def low_lanes(shape):
    return lax.broadcasted_iota(jnp.int32, shape, len(shape) - 1) < HEAD_DIM


def row_mean(x):
    return jnp.mean(x, axis=-1, keepdims=True)


def inv_rms(x):
    return lax.rsqrt(row_mean(x * x) + EPSILON)


def tile_of(j):
    return slice(j * LANES, (j + 1) * LANES)


def rows_loop(count, fn):
    def step(i, carry):
        fn(pl.ds(pl.multiple_of(i * ROW_STEP, ROW_STEP), ROW_STEP))
        return carry

    lax.fori_loop(0, count // ROW_STEP, step, 0)


def chunks(count, fn):
    def step(c, carry):
        fn(pl.ds(pl.multiple_of(c * CHUNK, CHUNK), CHUNK))
        return carry

    lax.fori_loop(0, count // CHUNK, step, 0)


def take_rows(hot, arrived, put):
    def block(at):
        x = arrived[:, :, at].astype(F32).reshape(-1, CHUNK).astype(BF)
        put(at, dot_nn(hot[...], x))

    chunks(arrived.shape[2], block)


def give_rows(hot, rows, out):
    def block(at):
        y = dot_tn(hot[...], rows(at))
        out[:, :, at] = y.reshape(out.shape[0], PAD, CHUNK).astype(BF)

    chunks(out.shape[2], block)


def fill_mask(bias, segq, segk):
    seq = bias.shape[0]
    rows = lax.broadcasted_iota(jnp.int32, (seq, seq), 0)
    cols = lax.broadcasted_iota(jnp.int32, (seq, seq), 1)
    bias[...] = jnp.where((segq == segk) & (cols <= rows), 0.0, MASKED)


def forward(pc, tok_sent, cot_sent, wqk, wvo, wup, wgate, wdown, small, hot, rattn, rmlp, segq, segk):
    n_dev, _, width = tok_sent.shape
    part = hot.shape[0] // MB
    seq = part * pc.n_p
    qk_cols, vo_cols, hid = wqk.shape[1], wvo.shape[1], wup.shape[1]
    o_cols = QUADS + LANES
    tiles = hid // LANES
    blocks = (MB, pc.n_p, part, width)
    kept = dict(
        hb=(blocks, BF),
        qk=((MB, seq, qk_cols), F32),
        qkb=((MB, seq, qk_cols), BF),
        vb=((MB, seq, o_cols), BF),
        ob=((MB, seq, o_cols), BF),
        lse=((MB, seq, LANES), F32),
        tok=((MB, part, width), BF),
        a=((MB, part, width), F32),
        h1=((MB, part, width), F32),
        c=((MB, part, width), F32),
        hb1=(blocks, BF),
        u=((MB, seq, hid), BF),
        g=((MB, seq, hid), BF),
        mb=((MB, seq, hid), BF),
        h2=((MB, part, width), BF),
    )
    whole = dict(
        wqk=((width, qk_cols), BF),
        wvo=((width, vo_cols), BF),
        wup=((width, hid), BF),
        wgate=((width, hid), BF),
        wdown=((width, hid), BF),
        sup=((1, hid), F32),
        sgate=((1, hid), F32),
        sqk=((1, qk_cols), F32),
    )
    outs = {n: SDS(*x) for n, x in (kept | whole).items()} | dict(cot=SDS(cot_sent.shape, BF))
    scratch = {n: VM(*x) for n, x in (kept | whole).items()} | dict(
        arrived=VM(tok_sent.shape, BF),
        aqk=VM((pc.n_t,) + wqk.shape, BF),
        avo=VM((pc.n_t,) + wvo.shape, BF),
        small=VM((pc.n_t,) + small.shape, F32),
        bias=VM((seq, seq), F32),
        sent=VM(blocks, BF),
        got=VM((pc.n_p, MB, part, width), BF),
        kept_sem={n: DMA((MB,)) for n in kept},
        whole_sem={n: DMA((1,)) for n in whole},
        tok_sem=Deal.sems(pc),
        cot_sem=Deal.sems(pc),
        small_sem=pair(pc.n_t) + [DMA((1,))],
        qk_sem=HeadWeights.sems(pc),
        vo_sem=HeadWeights.sems(pc),
        up_sem=HiddenWeights.sems(pc),
        gate_sem=HiddenWeights.sems(pc),
        down_sem=HiddenWeights.sems(pc),
        ag_sem=PlanePass.sems(pc),
        ra_sem=PlanePass.sems(pc),
        ag1_sem=PlanePass.sems(pc),
        rc_sem=PlanePass.sems(pc),
    )
    near_ins = dict(hot=hot, rattn=rattn, rmlp=rmlp, segq=segq, segk=segk)
    far_ins = dict(
        tok=tok_sent, cot=cot_sent, wqk=wqk, wvo=wvo, wup=wup, wgate=wgate, wdown=wdown, small=small
    )

    def kernel(pc, v, x, o, k):
        own_p = pc.p
        greet(pc)
        deal = Deal(pc, x.tok, k.arrived, k.tok_sem)
        deal_cot = Deal(pc, x.cot, o.cot, k.cot_sem)
        head_qk = HeadWeights(pc, x.wqk, k.aqk, k.wqk, k.qk_sem)
        head_vo = HeadWeights(pc, x.wvo, k.avo, k.wvo, k.vo_sem)
        up = HiddenWeights(pc, x.wup, k.wup, k.up_sem)
        gate = HiddenWeights(pc, x.wgate, k.wgate, k.gate_sem)
        down = HiddenWeights(pc, x.wdown, k.wdown, k.down_sem)
        ss, rs, ls = k.small_sem
        scales = Moves(
            [
                Move(
                    x.small, k.small.at[pc.t], ss.at[q], rs.at[pc.t], pc.dev(pc.p, pc.r, q), k.small.at[q], rs.at[q]
                )
                for q in others(pc.n_t, pc.t)
            ]
        )
        own_scales = pltpu.make_async_copy(x.small, k.small.at[pc.t], ls.at[0])

        def gather(buf, sems):
            return PlanePass(pc, lambda m, q: buf.at[m, own_p], lambda m, q: buf.at[m, q], sems)

        def scatter(sems):
            return PlanePass(pc, lambda m, q: k.sent.at[m, q], lambda m, q: k.got.at[q, m], sems)

        ag, ag1, ra, rc = gather(k.hb, k.ag_sem), gather(k.hb1, k.ag1_sem), scatter(k.ra_sem), scatter(k.rc_sem)
        names = vars(k)
        out_names = vars(o)
        copies = []

        def keep(m, *refs):
            for n in kept:
                if any(names[n] is ref for ref in refs):
                    copy = pltpu.make_async_copy(names[n].at[m], out_names[n].at[m], k.kept_sem[n].at[m])
                    copy.start()
                    copies.append(copy)

        def keep_whole(*refs):
            for n in whole:
                if any(names[n] is ref for ref in refs):
                    copy = pltpu.make_async_copy(names[n], out_names[n], k.whole_sem[n].at[0])
                    copy.start()
                    copies.append(copy)

        def attend(m):
            fill_mask(k.bias, v.segq[m], v.segk[m])
            ag.wait_recv(m)
            keep(m, k.hb)

            def project(i, carry):
                rows = k.hb[m, pl.ds(2 * i, 2)].reshape(2 * part, width)
                at = pl.ds(pl.multiple_of(i * 2 * part, 2 * part), 2 * part)
                qk = dot_nn(rows, k.wqk[...])
                k.qk[m, at, :] = qk
                for j in range(qk_cols // LANES):
                    s = qk[:, tile_of(j)]
                    n = s * lax.rsqrt(half_means(s * s) + EPSILON)
                    k.qkb[m, at, tile_of(j)] = (n * k.sqk[:, tile_of(j)]).astype(BF)
                k.vb[m, at, :QUADS] = dot_nn(rows, k.wvo[:, :QUADS]).astype(BF)
                last = dot_nn(rows, k.wvo[:, 2 * QUADS :])
                k.vb[m, at, QUADS:] = jnp.where(low_lanes(last.shape), last, 0.0).astype(BF)
                return carry

            lax.fori_loop(0, pc.n_p // 2, project, 0)
            keep(m, k.qk, k.qkb, k.vb)
            blk = seq // 2
            for i in range(2):
                nk = (i + 1) * blk
                at = slice(i * blk, nk)
                bias = k.bias[at, :nk]
                lse = jnp.zeros((blk, LANES), F32)
                lane = lax.broadcasted_iota(jnp.int32, (blk, LANES), 1)
                for slab in range(3):
                    if slab < 2:
                        qs = k.qkb[m, at, tile_of(slab)]
                        ks = k.qkb[m, :nk, tile_of(2 + slab)]
                    else:
                        qs = k.qkb[m, at, 2 * QUADS :]
                        ks = swap_halves(k.qkb[m, :nk, 2 * QUADS :].astype(F32)).astype(BF)
                    vs = k.vb[m, :nk, tile_of(slab)]
                    res = []
                    for half in range(2 if slab < 2 else 1):
                        low = low_lanes(qs.shape)
                        q1 = jnp.where(low if half == 0 else jnp.logical_not(low), qs, jnp.zeros_like(qs))
                        s = dot_nt(q1, ks) * HEAD_DIM ** (-0.5) + bias
                        top = jnp.max(s, axis=1, keepdims=True)
                        e = jnp.exp(s - top)
                        tot = jnp.sum(e, axis=1, keepdims=True)
                        lse = jnp.where(lane == 2 * slab + half, top + jnp.log(tot), lse)
                        res.append(dot_nn((e * (1.0 / tot)).astype(BF), vs))
                    if slab < 2:
                        res = jnp.where(low_lanes(res[0].shape), res[0], res[1])
                    else:
                        res = swap_halves(res[0])
                    k.ob[m, at, tile_of(slab)] = res.astype(BF)
                k.lse[m, at, :] = lse
            keep(m, k.ob, k.lse)

            def branch(i, carry):
                at = pl.ds(pl.multiple_of(i * 2 * part, 2 * part), 2 * part)
                y = dot_nt(k.ob[m, at, :], k.wvo[:, QUADS:])
                k.sent[m, pl.ds(2 * i, 2)] = y.astype(BF).reshape(2, part, width)
                return carry

            lax.fori_loop(0, pc.n_p // 2, branch, 0)
            ra.start(m)

        def summed(m, at):
            total = k.sent[m, own_p, at, :].astype(F32)
            for q in others(pc.n_p, own_p):
                total = total + k.got[q, m, at, :].astype(F32)
            return total

        def middle(m):
            ra.wait_recv(m)

            def rows(at):
                a = summed(m, at)
                h = k.tok[m, at, :].astype(F32)
                y = h + v.rattn[...] * (a * inv_rms(a) - h)
                h1 = y * inv_rms(y)
                k.a[m, at, :] = a
                k.h1[m, at, :] = h1
                k.hb1[m, own_p, at, :] = h1.astype(BF)

            rows_loop(part, rows)
            ag1.start(m)
            keep(m, k.a, k.h1)

        def feed(m):
            ag1.wait_recv(m)
            keep(m, k.hb1)

            def hidden(at):
                rows = k.hb1[m].reshape(seq, width)
                u = dot_nn(rows, k.wup[:, at])
                g = dot_nn(rows, k.wgate[:, at])
                k.u[m, :, at] = u.astype(BF)
                k.g[m, :, at] = g.astype(BF)
                z = k.sgate[:, at] * g
                k.mb[m, :, at] = (z / (1.0 + jnp.exp(-z)) * (k.sup[:, at] * u)).astype(BF)

            chunks(hid, hidden)
            keep(m, k.u, k.g, k.mb)

        def shrink(m):
            ra.wait_send(m)

            def columns(at):
                y = dot_nt(k.mb[m], k.wdown[at, :])
                k.sent[m, :, :, at] = y.astype(BF).reshape(pc.n_p, part, CHUNK)

            chunks(width, columns)
            rc.start(m)

        def finish(m):
            rc.wait_recv(m)

            def rows(at):
                c = summed(m, at)
                h1 = k.h1[m, at, :]
                z = h1 + v.rmlp[...] * (c * inv_rms(c) - h1)
                k.c[m, at, :] = c
                k.h2[m, at, :] = (z * inv_rms(z)).astype(BF)

            rows_loop(part, rows)
            keep(m, k.c, k.h2)

        deal.start()
        head_qk.start()
        head_vo.start()
        scales.start()
        own_scales.start()
        for w in (up, gate, down):
            w.start()
        head_qk.relay()
        head_vo.relay()
        deal.wait_recv()

        def put(at, y):
            for m in range(MB):
                rows = y[m * part : (m + 1) * part].astype(BF)
                k.tok[m, :, at] = rows
                k.hb[m, own_p, :, at] = rows

        take_rows(v.hot, k.arrived, put)
        for m in range(MB):
            ag.start(m)
            keep(m, k.tok)
        head_qk.plane()
        head_vo.plane()
        up.tall()
        gate.tall()
        own_scales.wait()
        scales.wait_recv()
        for t in range(pc.n_t):
            for j in range(3):

                def move(t=t, j=j):
                    at = lanes(dst_tile(pc.p, t) + j, 1)
                    k.sup[:, at] = k.small[t, pl.ds(src_tile(pc.p, t) + j, 1), :]
                    k.sgate[:, at] = k.small[t, pl.ds(tiles + src_tile(pc.p, t) + j, 1), :]

                Move.under(width3(pc.p, t) if j == 2 else None, move)
        for j in range(qk_cols // LANES):
            k.sqk[:, tile_of(j)] = k.small[own_p, 2 * tiles + j : 2 * tiles + j + 1, :]
        keep_whole(k.sup, k.sgate, k.sqk)
        head_qk.near()
        head_vo.near()
        head_qk.wait_recv()
        head_vo.wait_recv()
        keep_whole(k.wqk, k.wvo)
        attend(0)
        up.relay()
        gate.relay()
        down.tall()
        deal_cot.start()
        attend(1)
        up.near()
        gate.near()
        middle(0)
        down.relay()
        middle(1)
        up.wait_recv()
        gate.wait_recv()
        keep_whole(k.wup, k.wgate)
        feed(0)
        down.near()
        down.wait_recv()
        keep_whole(k.wdown)
        shrink(0)
        feed(1)
        shrink(1)
        for m in range(MB):
            finish(m)
        deal_cot.wait_recv()
        for w in (deal, deal_cot, head_qk, head_vo, up, gate, down, scales):
            w.wait_send()
        for m in range(MB):
            for w in (ag, ag1, rc):
                w.wait_send(m)
        for copy in copies:
            copy.wait()

    return fused(1, kernel, near_ins, far_ins, outs, scratch)


def backward(pc, f, hot, rattn, rmlp, segq, segk):
    n_dev = f.cot.shape[0]
    part, width = f.h2.shape[1], f.h2.shape[2]
    seq = part * pc.n_p
    all_tok = MB * seq
    qk_cols, hid = f.wqk.shape[1], f.wup.shape[1]
    o_cols = QUADS + LANES
    tiles = hid // LANES
    n_rows = width // (pc.n_p * pc.n_r)
    step_rows = n_rows // 5
    if n_rows % 5 or hid != width:
        raise ValueError("sizes")
    blocks = (MB, pc.n_p, part, width)
    dealt = (n_dev, PAD, width)
    vec_rows = 4 * tiles
    heads_shape = (pc.n_p, n_rows, qk_cols)
    outs = dict(
        back_out=SDS(dealt, BF),
        back_grad=SDS(dealt, BF),
        vec=SDS((n_dev, PAD, LANES), F32),
        tall=[SDS((pc.n_t, pc.n_p, n_rows, 3 * LANES), BF) for _ in range(3)],
        final=[SDS((n_rows, hid), BF) for _ in range(3)],
        head_p=[SDS(heads_shape, BF) for _ in range(2)],
        head_t=[SDS(heads_shape, BF) for _ in range(2)],
    )
    loaded = dict(
        c=f.c,
        h1=f.h1,
        wdown=f.wdown,
        u=f.u,
        g=f.g,
        sup=f.sup,
        sgate=f.sgate,
        wup=f.wup,
        wgate=f.wgate,
        mb=f.mb,
        hb1=f.hb1,
        tok=f.tok,
        wvo=f.wvo,
        vb=f.vb,
        qkb=f.qkb,
        lse=f.lse,
        qk=f.qk,
        sqk=f.sqk,
        wqk=f.wqk,
        ob=f.ob,
    )
    later = dict(a=f.a, hb=f.hb, cot=f.cot, h2=f.h2)
    sums = dict(gsup=hid, gsgate=hid, gsqk=qk_cols, grattn=width, grmlp=width)
    scratch = {n: VM(y.shape, y.dtype) for n, y in loaded.items()} | {n: VM((1, y), F32) for n, y in sums.items()}
    scratch |= dict(
        load_sem={n: DMA((1,)) for n in loaded},
        later_sem=[DMA((1,)) for _ in later],
        dcb=VM(blocks, BF),
        dab=VM(blocks, BF),
        mid=VM((MB, part, width), F32),
        bias=VM((seq, seq), F32),
        sent=VM(blocks, BF),
        got=VM((pc.n_p, MB, part, width), BF),
        tbuf=VM((pc.n_t, pc.n_p, n_rows, 3 * LANES), BF),
        dealbuf=VM(dealt, BF),
        vec=VM((n_dev * PAD, LANES), F32),
        vec_got=VM((n_dev, PAD, LANES), F32),
        vec_sum=VM((PAD, LANES), F32),
        near=[VM((pc.n_r - 1, pc.n_p, n_rows, y), BF) for y in (hid, hid, hid, qk_cols, qk_cols)],
        near_sem=[pair(pc.n_r) for _ in range(5)],
        tall_sem=[[DMA((2, pc.n_t)) for _ in range(3)] for _ in range(3)],
        plane_sem=[[DMA((2, pc.n_p)) for _ in range(2)] for _ in range(5)],
        head_sem=[pair(pc.n_t) + [DMA((1,))] for _ in range(2)],
        out_sem=Deal.sems(pc),
        grad_sem=Deal.sems(pc),
        vec_sem=Deal.sems(pc),
        spread_sem=Deal.sems(pc),
        ag_sem=PlanePass.sems(pc),
        ag1_sem=PlanePass.sems(pc),
        rh1_sem=PlanePass.sems(pc),
        rh_sem=PlanePass.sems(pc),
    )
    near_ins = dict(hot=hot, rattn=rattn, rmlp=rmlp, segq=segq, segk=segk)

    def kernel(pc, v, x, o, k):
        own_p = pc.p
        refs = vars(k)
        sources = vars(x)
        loads = {n: pltpu.make_async_copy(sources[n], refs[n], k.load_sem[n].at[0]) for n in loaded}
        for n in loaded:
            loads[n].start()
        cot_load = pltpu.make_async_copy(x.cot, k.dealbuf, k.later_sem[2].at[0])
        h2_load = pltpu.make_async_copy(x.h2, k.dab.at[:, own_p], k.later_sem[3].at[0])
        cot_load.start()
        h2_load.start()
        k_dqk, k_dv = k.u.at[:, :, pl.ds(0, qk_cols)], k.u.at[:, :, pl.ds(qk_cols, o_cols)]
        k_do = k.g.at[0, :, pl.ds(0, o_cols)]
        a_load = pltpu.make_async_copy(x.a, k.c, k.later_sem[0].at[0])
        hb_load = pltpu.make_async_copy(x.hb.reshape(MB, seq, width), k.mb, k.later_sem[1].at[0])
        waited = set()

        def ready(*wanted):
            for n in loaded:
                if n not in waited and any(refs[n] is ref for ref in wanted):
                    waited.add(n)
                    loads[n].wait()

        for n in sums:
            refs[n][...] = jnp.zeros(refs[n].shape, F32)
        k.vec[...] = jnp.zeros(k.vec.shape, F32)
        greet(pc)

        def gather(buf, sems):
            return PlanePass(pc, lambda m, q: buf.at[m, own_p], lambda m, q: buf.at[m, q], sems)

        def scatter(sems):
            return PlanePass(pc, lambda m, q: k.sent.at[m, q], lambda m, q: k.got.at[q, m], sems)

        ag, ag1, rh1, rh = gather(k.dcb, k.ag_sem), gather(k.dab, k.ag1_sem), scatter(k.rh1_sem), scatter(k.rh_sem)
        deal_out = Deal(pc, k.dealbuf, o.back_out, k.out_sem)
        deal_grad = Deal(pc, k.dealbuf, o.back_grad, k.grad_sem)

        class Chunked:
            @staticmethod
            def at_chunk(j):
                return k.vec.at[pl.ds(pl.multiple_of(j * PAD, PAD), PAD)]

        deal_vec = Deal(pc, Chunked, k.vec_got, k.vec_sem)
        deal_vec.src = Chunked.at_chunk
        spread = Deal(pc, k.vec_sum, o.vec, k.spread_sem, same=True)

        def add_rows(ref, y, at=slice(None)):
            ref[:, at] += jnp.sum(y, axis=0, keepdims=True)

        def top(m):
            def rows(at):
                c, h1, ct = k.c[m, at, :], k.h1[m, at, :], k.mid[m, at, :]
                r_c = inv_rms(c)
                n_c = c * r_c
                z = h1 + v.rmlp[...] * (n_c - h1)
                r_z = inv_rms(z)
                h2 = z * r_z
                dz = r_z * (ct - h2 * row_mean(ct * h2))
                add_rows(k.grmlp, dz * (n_c - h1))
                k.mid[m, at, :] = (1.0 - v.rmlp[...]) * dz
                dn = v.rmlp[...] * dz
                k.dcb[m, own_p, at, :] = (r_c * (dn - n_c * row_mean(dn * n_c))).astype(BF)

            rows_loop(part, rows)
            ag.start(m)

        def summed(m, at):
            total = k.sent[m, own_p, at, :].astype(F32)
            for q in others(pc.n_p, own_p):
                total = total + k.got[q, m, at, :].astype(F32)
            return total

        def feed(m):
            ag.wait_recv(m)

            def hidden(at):
                dm = dot_nn(k.dcb[m].reshape(seq, width), k.wdown[:, at])
                u, g = k.u[m, :, at].astype(F32), k.g[m, :, at].astype(F32)
                y = k.sgate[:, at] * g
                sig = 1.0 / (1.0 + jnp.exp(-y))
                du = dm * (y * sig)
                dx = dm * (k.sup[:, at] * u) * (sig * (1.0 + y * (1.0 - sig)))
                add_rows(k.gsup, du * u, at)
                add_rows(k.gsgate, dx * g, at)
                k.u[m, :, at] = (k.sup[:, at] * du).astype(BF)
                k.g[m, :, at] = (k.sgate[:, at] * dx).astype(BF)

            chunks(hid, hidden)

        def shrink(m):
            def columns(at):
                y = dot_nt(k.u[m], k.wup[at, :]) + dot_nt(k.g[m], k.wgate[at, :])
                k.sent[m, :, :, at] = y.astype(BF).reshape(pc.n_p, part, CHUNK)

            chunks(width, columns)
            rh1.start(m)

        grads = [k.wdown, k.wup, k.wgate, k.wqk, k.wvo]

        def near_slot(source, at):
            return (source - at + pc.n_r - 1) % pc.n_r

        def near_moves(i):
            send, recv = k.near_sem[i]
            return Moves(
                [
                    Move(
                        by_shard(pc, grads[i]).at[:, q], k.near[i].at[near_slot(pc.r, q)], send.at[q], recv.at[pc.r],
                        pc.dev(pc.p, q, pc.t), k.near[i].at[near_slot(q, pc.r)], recv.at[q],
                    )
                    for q in others(pc.n_r, pc.r)
                ]
            )

        near = [near_moves(i) for i in range(5)]

        def row_blocks(fn):
            def block(i, carry):
                fn(i // 5, pl.ds(pl.multiple_of((i % 5) * step_rows, step_rows), step_rows))
                return carry

            lax.fori_loop(0, pc.n_p * 5, block, 0)

        def near_sum(i):
            near[i].wait_recv()
            own = by_shard(pc, grads[i])

            def block(p, at):
                total = own[p, pc.r, at, :].astype(F32)
                for j in range(pc.n_r - 1):
                    total = total + k.near[i][j, p, at, :].astype(F32)
                k.near[i][0, p, at, :] = total.astype(BF)

            row_blocks(block)

        def tall_moves(i):
            send, recv, _ = k.tall_sem[i]
            src, y = k.near[i].at[0], o.tall[i]
            moves = []
            for q in others(pc.n_t, pc.t):
                there = dst_tile(pc.p, q)
                dev = pc.dev(pc.p, pc.r, q)
                moves.append(
                    Move(
                        src.at[:, :, lanes(there, 2)], y.at[pc.t, :, :, TWO], send.at[0, q], recv.at[0, pc.t], dev,
                        y.at[q, :, :, TWO], recv.at[0, q],
                    )
                )
                moves.append(
                    Move(
                        src.at[:, :, lanes(there + 2, 1)], y.at[pc.t, :, :, ONE], send.at[1, q], recv.at[1, pc.t], dev,
                        y.at[q, :, :, ONE], recv.at[1, q], width3(pc.p, q), width3(pc.p, pc.t),
                    )
                )
            return Moves(moves)

        tall = [tall_moves(i) for i in range(3)]
        wide = width3(pc.p, pc.t)

        def tall_sum(i):
            tall[i].wait_recv()
            local = []
            for q in others(pc.n_t, pc.t):
                for j, (w, cond) in enumerate(((TWO, None), (ONE, wide))):
                    copy = pltpu.make_async_copy(
                        o.tall[i].at[q, :, :, w], k.tbuf.at[q, :, :, w], k.tall_sem[i][2].at[j, q]
                    )
                    Move.under(cond, copy.start)
                    local.append((cond, copy))
            for cond, copy in local:
                Move.under(cond, copy.wait)
            here = dst_tile(pc.p, pc.t)

            def add(source, target):
                def block(p, at):
                    total = k.near[i][0, p, at, source].astype(F32)
                    for q in others(pc.n_t, pc.t):
                        total = total + k.tbuf[q, p, at, target].astype(F32)
                    k.tbuf[pc.t, p, at, target] = total.astype(BF)

                row_blocks(block)

            add(lanes(here, 2), TWO)
            pl.when(wide)(lambda: add(lanes(here + 2, 1), ONE))

        def plane_moves(i):
            send, recv = k.plane_sem[i]
            y, src = o.final[i], k.tbuf.at[pc.t]
            here = src_tile(pc.p, pc.t)
            moves = []
            for q in others(pc.n_p, pc.p):
                there = src_tile(q, pc.t)
                dev = pc.dev(q, pc.r, pc.t)
                moves.append(
                    Move(
                        src.at[q, :, TWO], y.at[:, lanes(here, 2)], send.at[0, q], recv.at[0, pc.p], dev,
                        y.at[:, lanes(there, 2)], recv.at[0, q],
                    )
                )
                moves.append(
                    Move(
                        src.at[q, :, ONE], y.at[:, lanes(here + 2, 1)], send.at[1, q], recv.at[1, pc.p], dev,
                        y.at[:, lanes(there + 2, 1)], recv.at[1, q], wide, width3(q, pc.t),
                    )
                )
            own = (
                (None, pltpu.make_async_copy(src.at[own_p, :, TWO], y.at[:, lanes(here, 2)], send.at[0, pc.p])),
                (wide, pltpu.make_async_copy(src.at[own_p, :, ONE], y.at[:, lanes(here + 2, 1)], send.at[1, pc.p])),
            )
            return Moves(moves), own

        plane = [plane_moves(i) for i in range(3)]

        def plane_start(i):
            moves, own = plane[i]
            moves.start()
            for cond, copy in own:
                Move.under(cond, copy.start)

        def plane_sent(i):
            moves, own = plane[i]
            moves.wait_send()
            for cond, copy in own:
                Move.under(cond, copy.wait)

        def head_planes(i):
            send, recv = k.plane_sem[3 + i]
            src, y = k.near[3 + i].at[0], o.head_p[i]
            return Moves(
                [
                    Move(
                        src.at[q], y.at[pc.p], send.at[0, q], recv.at[0, pc.p], pc.dev(q, pc.r, pc.t), y.at[q],
                        recv.at[0, q],
                    )
                    for q in others(pc.n_p, pc.p)
                ]
            )

        def head_talls(i):
            send, recv, _ = k.head_sem[i]
            src, y = o.head_p[i], o.head_t[i]
            return Moves(
                [
                    Move(
                        src.at[q], y.at[pc.t], send.at[q], recv.at[pc.t], pc.dev(pc.p, pc.r, q), y.at[q], recv.at[q]
                    )
                    for q in others(pc.n_t, pc.t)
                ]
            )

        head_plane = [head_planes(i) for i in range(2)]
        head_tall = [head_talls(i) for i in range(2)]
        head_own = [
            pltpu.make_async_copy(k.near[3 + i].at[0, own_p], o.head_p[i].at[pc.p], k.head_sem[i][2].at[0])
            for i in range(2)
        ]

        def middle(m):
            rh1.wait_recv(m)

            def rows(at):
                dh1 = k.mid[m, at, :] + summed(m, at)
                a, h = k.c[m, at, :], k.tok[m, at, :].astype(F32)
                r_a = inv_rms(a)
                n_a = a * r_a
                y = h + v.rattn[...] * (n_a - h)
                r_y = inv_rms(y)
                h1 = y * r_y
                dy = r_y * (dh1 - h1 * row_mean(dh1 * h1))
                add_rows(k.grattn, dy * (n_a - h))
                k.mid[m, at, :] = (1.0 - v.rattn[...]) * dy
                dn = v.rattn[...] * dy
                k.dab[m, own_p, at, :] = (r_a * (dn - n_a * row_mean(dn * n_a))).astype(BF)

            rows_loop(part, rows)
            ag1.start(m)

        def flat(ref, at=slice(None)):
            return ref[:, :, at].reshape(all_tok, -1)

        def columns_of(ref, at):
            return ref[:, :, :, at].reshape(all_tok, CHUNK)

        def weight_grad(target, left, right):
            def block(at):
                target[at, :] = dot_tn(columns_of(left, at), flat(right)).astype(BF)

            chunks(width, block)

        score = HEAD_DIM ** (-0.5)
        blk = seq // 2

        def attend(m):
            fill_mask(k.bias, v.segq[m], v.segk[m])
            ag1.wait_recv(m)

            def project(i, carry):
                rows = k.dab[m, pl.ds(2 * i, 2)].reshape(2 * part, width)
                at = pl.ds(pl.multiple_of(i * 2 * part, 2 * part), 2 * part)
                k_do[at, :] = dot_nn(rows, k.wvo[:, QUADS:]).astype(BF)
                return carry

            lax.fori_loop(0, pc.n_p // 2, project, 0)

            def norm_grad(tile, d):
                at = tile_of(tile)
                raw = k.qk[m, :, at]
                r = lax.rsqrt(half_means(raw * raw) + EPSILON)
                n = raw * r
                d = d * score
                add_rows(k.gsqk, d * n, at)
                dy = d * k.sqk[:, at]
                k_dqk[m, :, at] = (r * (dy - n * half_means(dy * n))).astype(BF)

            for slab in range(3):
                own = tile_of(slab)
                if slab < 2:
                    q_all = k.qkb[m, :, own]
                    k_all = k.qkb[m, :, tile_of(2 + slab)]
                    do_all = k_do[:, own]
                else:
                    q_all = k.qkb[m, :, 2 * QUADS :]
                    k_all = swap_halves(q_all.astype(F32)).astype(BF)
                    do_all = swap_halves(k_do[:, own].astype(F32)).astype(BF)
                v_all = k.vb[m, :, own]
                low = low_lanes((blk, LANES))
                dq, dk, dv = [], None, None
                for i in range(2):
                    nk = (i + 1) * blk
                    at = slice(i * blk, nk)
                    bias = k.bias[at, :nk]
                    dq_i = None
                    for half in range(2 if slab < 2 else 1):
                        here = low if half == 0 else jnp.logical_not(low)
                        zero = jnp.zeros((blk, LANES), BF)
                        q1, do1 = jnp.where(here, q_all[at], zero), jnp.where(here, do_all[at], zero)
                        lse = k.lse[m, at, 2 * slab + half : 2 * slab + half + 1]
                        prob = jnp.exp(dot_nt(q1, k_all[:nk]) * score + bias - lse)
                        dp = dot_nt(do1, v_all[:nk])
                        w = prob * dp
                        ds = (w - prob * jnp.sum(w, axis=1, keepdims=True)).astype(BF)
                        y = jnp.where(here, dot_nn(ds, k_all[:nk]), 0.0)
                        dq_i = y if dq_i is None else dq_i + y
                        dk_i, dv_i = dot_tn(ds, q1), dot_tn(prob.astype(BF), do1)
                        if i == 0:
                            dk = dk_i if dk is None else dk + dk_i
                            dv = dv_i if dv is None else dv + dv_i
                        else:
                            if half == 0:
                                dk = jnp.concatenate([dk, jnp.zeros((blk, LANES), F32)], axis=0)
                                dv = jnp.concatenate([dv, jnp.zeros((blk, LANES), F32)], axis=0)
                            dk, dv = dk + dk_i, dv + dv_i
                    dq.append(dq_i)
                dq = jnp.concatenate(dq, axis=0)
                k_dv[m, :, own] = dv.astype(BF)
                if slab < 2:
                    norm_grad(slab, dq)
                    norm_grad(2 + slab, dk)
                else:
                    norm_grad(4, dq + swap_halves(dk))
            rh1.wait_send(m)

            def columns(at):
                y = dot_nt(k_dqk[m], k.wqk[at, :])
                y = y + dot_nt(k_dv[m, :, :QUADS], k.wvo[at, :QUADS])
                y = y + dot_nt(k_dv[m, :, QUADS:], k.wvo[at, 2 * QUADS :])
                k.sent[m, :, :, at] = y.astype(BF).reshape(pc.n_p, part, CHUNK)

            chunks(width, columns)
            rh.start(m)

        def heads_grad(at):
            hb, dab = flat(k.mb, at), columns_of(k.dab, at)
            quads = slice(0, QUADS)
            rest = slice(QUADS, None)
            k.wqk[at, :] = dot_tn(hb, flat(k_dqk)).astype(BF)
            k.wvo[at, :QUADS] = dot_tn(hb, flat(k_dv, quads)).astype(BF)
            k.wvo[at, QUADS : 2 * QUADS] = dot_tn(dab, flat(k.ob, quads)).astype(BF)
            k.wvo[at, 2 * QUADS :] = (dot_tn(hb, flat(k_dv, rest)) + dot_tn(dab, flat(k.ob, rest))).astype(BF)

        def bottom(m):
            rh.wait_recv(m)

            def rows(at):
                k.mid[m, at, :] = k.mid[m, at, :] + summed(m, at)

            rows_loop(part, rows)

        def collect():
            for t in range(pc.n_t):
                for j in range(3):

                    def move(t=t, j=j):
                        here = lanes(dst_tile(pc.p, t) + j, 1)
                        row = t * tiles + src_tile(pc.p, t) + j
                        k.vec[pl.ds(row, 1), :] = k.gsup[:, here]
                        k.vec[pl.ds(vec_rows + row, 1), :] = k.gsgate[:, here]

                    Move.under(width3(pc.p, t) if j == 2 else None, move)
            at = 2 * vec_rows
            for j in range(tiles):
                k.vec[at + j : at + j + 1, :] = k.grattn[:, tile_of(j)]
                k.vec[at + tiles + j : at + tiles + j + 1, :] = k.grmlp[:, tile_of(j)]
            count = qk_cols // LANES
            for j in range(count):
                k.vec[pl.ds(at + 2 * tiles + own_p * count + j, 1), :] = k.gsqk[:, tile_of(j)]

        ready(k.c, k.h1)
        cot_load.wait()

        def put(at, y):
            for m in range(MB):
                k.mid[m, :, at] = y[m * part : (m + 1) * part]

        take_rows(v.hot, k.dealbuf, put)
        for m in range(MB):
            top(m)
        a_load.start()
        h2_load.wait()
        give_rows(v.hot, lambda at: k.dab[:, own_p, :, at].reshape(MB * part, CHUNK), k.dealbuf)
        deal_out.start()
        ready(k.wdown, k.u, k.g, k.wup, k.wgate, k.sup, k.sgate)
        for m in range(MB):
            feed(m)
            shrink(m)
        ready(k.mb, k.hb1)
        weight_grad(k.wdown, k.dcb, k.mb)
        hb_load.start()
        near[0].start()
        ready(k.tok)
        a_load.wait()
        middle(0)
        weight_grad(k.wup, k.hb1, k.u)
        near[1].start()
        near_sum(0)
        tall[0].start()
        middle(1)
        weight_grad(k.wgate, k.hb1, k.g)
        near[2].start()
        near_sum(1)
        tall[1].start()
        ready(k.wvo, k.vb, k.qkb, k.lse, k.qk, k.sqk, k.wqk, k.ob)
        attend(0)
        near_sum(2)
        tall[2].start()
        attend(1)
        hb_load.wait()
        chunks(width, heads_grad)
        for i in range(2):
            near[3 + i].start()
        tall_sum(0)
        plane_start(0)
        for i in range(2):
            near_sum(3 + i)
            head_plane[i].start()
            head_own[i].start()
        collect()
        deal_vec.start()
        for m in range(MB):
            bottom(m)
        deal_out.wait_recv()
        deal_out.wait_send()
        give_rows(v.hot, lambda at: k.mid[:, :, at].reshape(MB * part, CHUNK).astype(BF), k.dealbuf)
        deal_grad.start()
        for i in range(2):
            head_plane[i].wait_recv()
            head_own[i].wait()
            head_tall[i].start()
        plane_sent(0)
        tall_sum(1)
        plane_start(1)
        deal_vec.wait_recv()
        total = k.vec_got[0]
        for j in range(1, n_dev):
            total = total + k.vec_got[j]
        k.vec_sum[...] = total
        spread.start()
        plane_sent(1)
        tall_sum(2)
        plane_start(2)
        plane_sent(2)
        for w in tall + head_plane + head_tall + near + [deal_grad, deal_vec, spread]:
            w.wait_send()
        for i in range(3):
            plane[i][0].wait_recv()
        for w in head_tall + [deal_grad, spread]:
            w.wait_recv()
        for m in range(MB):
            ag.wait_send(m)
            ag1.wait_send(m)
            rh.wait_send(m)

    return fused(2, kernel, near_ins, loaded | later, outs, scratch)


def merged(slots, own, at):
    total = own.astype(F32)
    for q in range(slots.shape[0]):
        total = total + jnp.where(q == at, 0, slots[q]).astype(F32)
    return total


def pick(x, at, axis):
    return lax.dynamic_index_in_dim(x, at, axis, keepdims=False)


def mm(a, b):
    return jnp.dot(a, b, preferred_element_type=F32)


def segment_ids(lengths_row, tok_count):
    count = lengths_row.shape[0]
    upto = jnp.arange(count)[:, None] >= jnp.arange(count)[None, :]
    doc_ends = jnp.sum(jnp.where(upto, lengths_row[None, :], 0), axis=1)
    places = jnp.arange(tok_count, dtype=jnp.int32)
    return jnp.sum((places[:, None] >= doc_ends[None, :]).astype(jnp.int32), axis=1)


def packed(x, y):
    return jnp.concatenate([x[:, :QUADS], y[:, :QUADS], x[:, QUADS:], y[:, QUADS:]], axis=1)


def unpacked(z):
    mid = 2 * QUADS + HEAD_DIM
    return (
        jnp.concatenate([z[..., :QUADS], z[..., 2 * QUADS : mid]], axis=-1),
        jnp.concatenate([z[..., QUADS : 2 * QUADS], z[..., mid:]], axis=-1),
    )


def body(
    tokens,
    cotangent,
    slot,
    lengths,
    w_query,
    w_key,
    w_value,
    w_out,
    w_up,
    w_gate,
    w_down,
    scale_qk,
    scale_up,
    scale_gate,
    rate_attn,
    rate_mlp,
):
    pc = Place()
    n_p, n_r, n_t, n_dev = pc.n_p, pc.n_r, pc.n_t, pc.n_dev
    rows_dev, width = tokens.shape
    tok_count = rows_dev // MB * n_p
    head_cols = w_query.shape[2]
    hid = w_up.shape[2]
    tiles = hid // LANES
    group = pc.r * n_t + pc.t
    owner = group * n_p + pc.p
    if rows_dev // n_dev > PAD or head_cols != QUADS + HEAD_DIM:
        raise ValueError("sizes")

    table = slot.reshape(n_dev, rows_dev)
    own_slots = lax.dynamic_index_in_dim(table, pc.me, 0, keepdims=False)
    d = own_slots // rows_dev
    to_dev = ((d % n_p) * n_r + (d // n_p) // n_t) * n_t + (d // n_p) % n_t
    places = jnp.arange(rows_dev, dtype=jnp.int32)
    spots = jnp.arange(n_dev * PAD, dtype=jnp.int32)
    before = (d[:, None] == d[None, :]) & (places[None, :] < places[:, None])
    rank = jnp.sum(before.astype(jnp.int32), axis=1)
    send_hot = (spots[:, None] == (to_dev * PAD + rank)[None, :]).astype(BF)

    sel = table // rows_dev == owner
    tri = (places[:, None] < places[None, :]).astype(BF)
    ranks = mm(sel.astype(BF), tri).astype(jnp.int32)
    kth = sel[:, None, :] & (ranks[:, None, :] == jnp.arange(PAD, dtype=jnp.int32)[None, :, None])
    owner_rows = jnp.sum(jnp.where(kth, (table - owner * rows_dev + 1)[:, None, :], 0), axis=2).reshape(-1) - 1
    recv_hot = (places[:, None] == owner_rows[None, :]).astype(BF)

    def to_send(x):
        return mm(send_hot, x).astype(BF).reshape(n_dev, PAD, width)

    qk_scale = packed(scale_qk, scale_qk).reshape(-1, LANES)
    small = jnp.concatenate([scale_up.reshape(-1, LANES), scale_gate.reshape(-1, LANES), qk_scale])
    small = jnp.pad(small, ((0, -small.shape[0] % 8), (0, 0)))
    own_lengths = lax.dynamic_slice_in_dim(lengths, group * MB, MB, 0)
    segments = jnp.stack([segment_ids(own_lengths[m], tok_count) for m in range(MB)])
    shared = (recv_hot, rate_attn, rate_mlp, segments[:, :, None], segments[:, None, :])

    f = forward(
        pc,
        to_send(tokens),
        to_send(cotangent),
        packed(w_query[0], w_key[0]),
        packed(w_value[0], w_out[0]),
        w_up[0],
        w_gate[0],
        w_down[0],
        small,
        *shared,
    )
    b = backward(pc, f, *shared)

    vec = b.vec.reshape(-1, LANES)
    at = n_t * tiles

    def own_row(x):
        return lax.dynamic_index_in_dim(x.reshape(n_t, -1), pc.t, 0)

    qk_rows = qk_scale.shape[0]
    out_sup, out_sgate = own_row(vec[:at]), own_row(vec[at : 2 * at])
    at = 2 * at
    out_rattn, out_rmlp = vec[at : at + tiles].reshape(1, -1), vec[at + tiles : at + 2 * tiles].reshape(1, -1)
    at = at + 2 * tiles
    out_sqk = sum(unpacked(own_row(vec[at : at + n_t * qk_rows])))
    heads = [
        x[None]
        for got, sent in zip(b.head_t, b.head_p)
        for x in unpacked(merged(got, pick(sent, pc.t, 0), pc.t))
    ]

    def from_back(x):
        return lax.dot_general(
            send_hot, x.reshape(-1, width), (((0,), (0,)), ((), ())), preferred_element_type=F32
        )

    down, up, gate = (x.astype(F32)[None] for x in b.final)
    return (
        from_back(b.back_out),
        from_back(b.back_grad),
        *heads,
        up,
        gate,
        down,
        out_sqk,
        out_sup,
        out_sgate,
        out_rattn,
        out_rmlp,
    )


def solution(mesh):
    tok = P(("dp", "tensor"), None)
    mat = P(None, "dp", "tensor")
    vec = P(None, "tensor")
    in_specs = (tok, tok, P(), P()) + (mat,) * 7 + (vec,) * 3 + (P(), P())
    out_specs = (tok, tok) + (mat,) * 7 + (vec,) * 3 + (P(), P())
    return jax.shard_map(body, mesh=mesh, in_specs=in_specs, out_specs=out_specs, check_vma=False)
```

```python
import types

import jax
import jax.numpy as jnp
from jax import lax
from jax.experimental import pallas as pl
from jax.experimental.pallas import tpu as pltpu
from jax.sharding import PartitionSpec as P

HEAD_DIM = 64
MB = 2
LANES = 128
QUADS = 4 * HEAD_DIM
CHUNK = 2 * LANES
ROW_STEP = 32
PAD = 8
VMEM_LIMIT = 127 * 2**19

EPSILON = 1e-06
MASKED = -1e30
BF = jnp.bfloat16
F32 = jnp.float32
MESH = pl.DeviceIdType.MESH
VM = pltpu.VMEM
DMA = pltpu.SemaphoreType.DMA
SDS = jax.ShapeDtypeStruct


class Place:
    def __init__(self):
        self.n_t = lax.axis_size("tensor")
        self.n_dp = lax.axis_size("dp")
        self.n_p = self.n_t
        self.n_r = self.n_dp // self.n_p
        self.n_dev = self.n_dp * self.n_t
        if self.n_t != 4:
            raise ValueError("tensor size")
        dp = lax.axis_index("dp")
        self.t = lax.axis_index("tensor")
        self.p = dp // self.n_r
        self.r = dp % self.n_r
        self.me = dp * self.n_t + self.t

    def dev(self, p, r, t):
        return (p * self.n_r + r, t)

    def flat(self, j):
        return (j // self.n_t, j % self.n_t)


def width3(p, t):
    return (p + t) % 2 == 0


def src_tile(p, t):
    return 5 * (p // 2) + (p % 2) * (3 - t % 2)


def dst_tile(p, t):
    return 5 * (t // 2) + (t % 2) * (3 - p % 2)


def lanes(tile, count):
    return pl.ds(pl.multiple_of(tile * LANES, LANES), count * LANES)


TWO, ONE = pl.ds(0, 2 * LANES), pl.ds(2 * LANES, LANES)


def remote(src, dst, send, recv, dev):
    return pltpu.make_async_remote_copy(
        src_ref=src, dst_ref=dst, send_sem=send, recv_sem=recv, device_id=dev, device_id_type=MESH
    )


class Move:
    def __init__(self, src, dst, send, recv, dev, landing, landed, cond_out=None, cond_in=None):
        self.going = (src, dst, send, recv, dev)
        self.coming = (landing, landing, send, landed, dev)
        self.cond_out, self.cond_in = cond_out, cond_in

    @staticmethod
    def under(cond, act):
        if cond is None:
            act()
        else:
            pl.when(cond)(act)

    def start(self):
        self.under(self.cond_out, lambda: remote(*self.going).start())

    def wait_send(self):
        self.under(self.cond_out, lambda: remote(*self.going).wait_send())

    def wait_recv(self):
        self.under(self.cond_in, lambda: remote(*self.coming).wait_recv())


class Moves:
    def __init__(self, moves):
        self.moves = moves

    def start(self):
        for m in self.moves:
            m.start()

    def wait_recv(self):
        for m in self.moves:
            m.wait_recv()

    def wait_send(self):
        for m in self.moves:
            m.wait_send()


def others(count, own):
    order = [2, 1, 3] if count == 4 else list(range(1, count))
    return [(own + k) % count for k in order]


def pair(n):
    return [DMA((n,)), DMA((n,))]


class Deal:
    @staticmethod
    def sems(pc):
        return [DMA((1,)), DMA((1,)), DMA((1,))]

    def __init__(self, pc, x, y, sems):
        self.pc, self.x, self.y = pc, x, y
        self.send, self.recv, self.local = (sem.at[0] for sem in sems)

    def copy(self, j, src, dst):
        return remote(src, dst, self.send, self.recv, self.pc.flat(j))

    def own(self):
        return pltpu.make_async_copy(self.x.at[self.pc.me], self.y.at[self.pc.me], self.local)

    def start(self):
        pc = self.pc

        def step(i, carry):
            j = (pc.me + i) % pc.n_dev
            self.copy(j, self.x.at[j], self.y.at[pc.me]).start()
            return carry

        lax.fori_loop(1, pc.n_dev, step, 0)
        self.own().start()

    def all_but_own(self):
        part = self.y.at[pl.ds(0, self.pc.n_dev - 1)]
        return self.copy((self.pc.me + 1) % self.pc.n_dev, part, part)

    def wait_recv(self):
        self.own().wait()
        self.all_but_own().wait_recv()

    def wait_send(self):
        self.all_but_own().wait_send()


class Tall:
    @staticmethod
    def sems(pc, pieces):
        return [DMA((pieces, pc.n_t + 1)), DMA((pieces, pc.n_t))]

    def __init__(self, pc, shard, own, sems):
        t = pc.t
        middle = (t == 1) | (t == 2)
        far, end = jnp.where(t == 2, 0, 3), jnp.where(t == 2, 3, 0)
        send, recv = sems

        def both(a, b):
            return a if b is None else a & b

        self.first, self.passed, self.at_relay = [], [], []
        for q in others(pc.n_t, t):
            for i, ((dst, c_out), src, (here, c_in)) in enumerate(zip(shard(t), own, shard(q))):
                self.first.append(
                    Move(
                        src, dst, send.at[i, q], recv.at[i, t], pc.dev(pc.p, pc.r, q), here, recv.at[i, q],
                        both(jnp.abs(q - t) != 3, c_out), both(jnp.logical_not(middle & (q == far)), c_in),
                    )
                )
        for i, (ref, c) in enumerate(shard(far)):
            self.passed.append(
                Move(
                    ref, ref, send.at[i, pc.n_t], recv.at[i, far], pc.dev(pc.p, pc.r, end), ref, recv.at[i, far],
                    both(middle, c), both(middle, c),
                )
            )

    def start(self):
        for m in self.first:
            m.start()

    def relay(self):
        for m in self.passed:
            m.wait_recv()
            m.start()

    def wait_recv(self):
        for m in self.first:
            m.wait_recv()

    def wait_send(self):
        for m in self.first + self.passed:
            m.wait_send()


def by_shard(pc, ref):
    return ref.reshape(pc.n_p, pc.n_r, ref.shape[0] // (pc.n_p * pc.n_r), ref.shape[1])


class HeadWeights:
    @staticmethod
    def sems(pc):
        return [Tall.sems(pc, 1), pair(pc.n_p), pair(pc.n_r), DMA((2,))]

    def __init__(self, pc, x, a, w, sems):
        tall, (s2, r2), (s3, r3), ls = sems
        f = by_shard(pc, w)
        self.first = Tall(pc, lambda q: [(a.at[q], None)], [x], tall)
        self.second = Moves(
            [
                Move(a.at[q], f.at[pc.p, pc.r], s2.at[q], r2.at[pc.p], pc.dev(q, pc.r, pc.t), f.at[q, pc.r], r2.at[q])
                for q in others(pc.n_p, pc.p)
            ]
        )
        self.third = Moves(
            [
                Move(f.at[:, pc.r], f.at[:, pc.r], s3.at[q], r3.at[pc.r], pc.dev(pc.p, q, pc.t), f.at[:, q], r3.at[q])
                for q in others(pc.n_r, pc.r)
            ]
        )
        self.keep1 = pltpu.make_async_copy(x, a.at[pc.t], ls.at[0])
        self.keep2 = pltpu.make_async_copy(a.at[pc.p], f.at[pc.p, pc.r], ls.at[1])

    def start(self):
        self.first.start()
        self.keep1.start()

    def relay(self):
        self.first.relay()

    def plane(self):
        self.keep1.wait()
        self.first.wait_recv()
        self.second.start()
        self.keep2.start()

    def near(self):
        self.keep2.wait()
        self.second.wait_recv()
        self.third.start()

    def wait_recv(self):
        self.third.wait_recv()

    def wait_send(self):
        self.first.wait_send()
        self.second.wait_send()
        self.third.wait_send()


class HiddenWeights:
    @staticmethod
    def sems(pc):
        return [pair(pc.n_p), pair(pc.n_p), Tall.sems(pc, 2), pair(pc.n_r), DMA((2,))]

    def __init__(self, pc, x, w, sems):
        (s1, r1), (s2, r2), tall, (s3, r3), ls = sems
        g = by_shard(pc, w)
        p, r, t = pc.p, pc.r, pc.t

        def spot(q, row, extra):
            at = dst_tile(q, t)
            return g.at[row, r, :, lanes(at + 2, 1) if extra else lanes(at, 2)]

        def piece(q, extra):
            at = src_tile(q, t)
            return x.at[:, lanes(at + 2, 1) if extra else lanes(at, 2)]

        moves = []
        for q in others(pc.n_p, p):
            dev = pc.dev(q, r, t)
            moves.append(
                Move(piece(q, False), spot(q, p, False), s1.at[q], r1.at[p], dev, spot(p, q, False), r1.at[q])
            )
            moves.append(
                Move(
                    piece(q, True), spot(q, p, True), s2.at[q], r2.at[p], dev, spot(p, q, True), r2.at[q],
                    width3(q, t), width3(p, t),
                )
            )
        self.first = Moves(moves)
        self.own = [
            (None, pltpu.make_async_copy(piece(p, False), spot(p, p, False), ls.at[0])),
            (width3(p, t), pltpu.make_async_copy(piece(p, True), spot(p, p, True), ls.at[1])),
        ]

        def shard(q):
            at = dst_tile(p, q)
            return [(g.at[:, r, :, lanes(at, 2)], None), (g.at[:, r, :, lanes(at + 2, 1)], width3(p, q))]

        self.second = Tall(pc, shard, [ref for ref, _ in shard(t)], tall)
        self.third = Moves(
            [
                Move(g.at[:, r], g.at[:, r], s3.at[q], r3.at[r], pc.dev(p, q, t), g.at[:, q], r3.at[q])
                for q in others(pc.n_r, r)
            ]
        )

    def start(self):
        self.first.start()
        for cond, copy in self.own:
            Move.under(cond, copy.start)

    def tall(self):
        for cond, copy in self.own:
            Move.under(cond, copy.wait)
        self.first.wait_recv()
        self.second.start()

    def relay(self):
        self.second.relay()

    def near(self):
        self.second.wait_recv()
        self.third.start()

    def wait_recv(self):
        self.third.wait_recv()

    def wait_send(self):
        self.first.wait_send()
        self.second.wait_send()
        self.third.wait_send()


class PlanePass:
    @staticmethod
    def sems(pc):
        return [DMA((MB, pc.n_p)), DMA((MB, pc.n_p))]

    def __init__(self, pc, source, landing, sems):
        send, recv = sems
        self.by_m = [
            Moves(
                [
                    Move(
                        source(m, q), landing(m, pc.p), send.at[m, q], recv.at[m, pc.p], pc.dev(q, pc.r, pc.t),
                        landing(m, q), recv.at[m, q],
                    )
                    for q in others(pc.n_p, pc.p)
                ]
            )
            for m in range(MB)
        ]

    def start(self, m):
        self.by_m[m].start()

    def wait_recv(self, m):
        self.by_m[m].wait_recv()

    def wait_send(self, m):
        self.by_m[m].wait_send()


def greet(pc):
    barrier = pltpu.get_barrier_semaphore()

    def step(i, carry):
        dev = pc.flat((pc.me + i) % pc.n_dev)
        pl.semaphore_signal(barrier, inc=1, device_id=dev, device_id_type=MESH)
        return carry

    lax.fori_loop(1, pc.n_dev, step, 0)
    pl.semaphore_wait(barrier, pc.n_dev - 1)


def fused(collective_id, kernel, near_ins, far_ins, outs, scratch):
    ins_leaves, ins_tree = jax.tree.flatten((near_ins, far_ins))
    outs_leaves, outs_tree = jax.tree.flatten(outs)
    scratch_leaves, scratch_tree = jax.tree.flatten(scratch)
    a, b = len(ins_leaves), len(outs_leaves)
    near = len(jax.tree.leaves(near_ins))

    def run(*refs):
        first, second = jax.tree.unflatten(ins_tree, refs[:a])
        third = jax.tree.unflatten(outs_tree, refs[a : a + b])
        fourth = jax.tree.unflatten(scratch_tree, refs[a + b :])
        kernel(
            Place(),
            types.SimpleNamespace(**first),
            types.SimpleNamespace(**second),
            types.SimpleNamespace(**third),
            types.SimpleNamespace(**fourth),
        )

    got = pl.pallas_call(
        run,
        out_shape=tuple(outs_leaves),
        in_specs=[pl.BlockSpec(memory_space=VM if i < near else pl.ANY) for i in range(a)],
        out_specs=tuple([pl.BlockSpec(memory_space=pl.ANY)] * b),
        scratch_shapes=scratch_leaves,
        compiler_params=pltpu.CompilerParams(
            collective_id=collective_id, has_side_effects=True, vmem_limit_bytes=VMEM_LIMIT
        ),
    )(*ins_leaves)
    return types.SimpleNamespace(**jax.tree.unflatten(outs_tree, got))


def dot_nt(a, b):
    return lax.dot_general(a, b, (((1,), (1,)), ((), ())), preferred_element_type=F32)


def dot_tn(a, b):
    return lax.dot_general(a, b, (((0,), (0,)), ((), ())), preferred_element_type=F32)


def dot_nn(a, b):
    return lax.dot_general(a, b, (((1,), (0,)), ((), ())), preferred_element_type=F32)


def half_means(x):
    a = lax.broadcasted_iota(jnp.int32, (LANES, LANES), 0) // HEAD_DIM
    b = lax.broadcasted_iota(jnp.int32, (LANES, LANES), 1) // HEAD_DIM
    same = jnp.where(a == b, 1.0 / HEAD_DIM, 0.0).astype(F32)
    return lax.dot_general(x, same, (((1,), (0,)), ((), ())), precision=lax.Precision.HIGHEST, preferred_element_type=F32)


def swap_halves(x):
    return pltpu.roll(x, HEAD_DIM, 1)


def low_lanes(shape):
    return lax.broadcasted_iota(jnp.int32, shape, len(shape) - 1) < HEAD_DIM


def row_mean(x):
    return jnp.mean(x, axis=-1, keepdims=True)


def inv_rms(x):
    return lax.rsqrt(row_mean(x * x) + EPSILON)


def tile_of(j):
    return slice(j * LANES, (j + 1) * LANES)


def rows_loop(count, fn):
    def step(i, carry):
        fn(pl.ds(pl.multiple_of(i * ROW_STEP, ROW_STEP), ROW_STEP))
        return carry

    lax.fori_loop(0, count // ROW_STEP, step, 0)


def chunks(count, fn):
    def step(c, carry):
        fn(pl.ds(pl.multiple_of(c * CHUNK, CHUNK), CHUNK))
        return carry

    lax.fori_loop(0, count // CHUNK, step, 0)


def take_rows(hot, arrived, put):
    def block(at):
        x = arrived[:, :, at].astype(F32).reshape(-1, CHUNK).astype(BF)
        put(at, dot_nn(hot[...], x))

    chunks(arrived.shape[2], block)


def give_rows(hot, rows, out):
    def block(at):
        y = dot_tn(hot[...], rows(at))
        out[:, :, at] = y.reshape(out.shape[0], PAD, CHUNK).astype(BF)

    chunks(out.shape[2], block)


def fill_mask(bias, segq, segk):
    seq = bias.shape[0]
    rows = lax.broadcasted_iota(jnp.int32, (seq, seq), 0)
    cols = lax.broadcasted_iota(jnp.int32, (seq, seq), 1)
    bias[...] = jnp.where((segq == segk) & (cols <= rows), 0.0, MASKED)


def forward(pc, tok_sent, cot_sent, wqk, wvo, wup, wgate, wdown, small, hot, rattn, rmlp, segq, segk):
    n_dev, _, width = tok_sent.shape
    part = hot.shape[0] // MB
    seq = part * pc.n_p
    qk_cols, vo_cols, hid = wqk.shape[1], wvo.shape[1], wup.shape[1]
    o_cols = QUADS + LANES
    tiles = hid // LANES
    blocks = (MB, pc.n_p, part, width)
    kept = dict(
        hb=(blocks, BF),
        qk=((MB, seq, qk_cols), F32),
        qkb=((MB, seq, qk_cols), BF),
        vb=((MB, seq, o_cols), BF),
        ob=((MB, seq, o_cols), BF),
        lse=((MB, seq, LANES), F32),
        tok=((MB, part, width), BF),
        a=((MB, part, width), F32),
        h1=((MB, part, width), F32),
        c=((MB, part, width), F32),
        hb1=(blocks, BF),
        u=((MB, seq, hid), BF),
        g=((MB, seq, hid), BF),
        mb=((MB, seq, hid), BF),
        h2=((MB, part, width), BF),
    )
    whole = dict(
        wqk=((width, qk_cols), BF),
        wvo=((width, vo_cols), BF),
        wup=((width, hid), BF),
        wgate=((width, hid), BF),
        wdown=((width, hid), BF),
        sup=((1, hid), F32),
        sgate=((1, hid), F32),
        sqk=((1, qk_cols), F32),
    )
    outs = {n: SDS(*x) for n, x in (kept | whole).items()} | dict(cot=SDS(cot_sent.shape, BF))
    scratch = {n: VM(*x) for n, x in (kept | whole).items()} | dict(
        arrived=VM(tok_sent.shape, BF),
        aqk=VM((pc.n_t,) + wqk.shape, BF),
        avo=VM((pc.n_t,) + wvo.shape, BF),
        small=VM((pc.n_t,) + small.shape, F32),
        bias=VM((seq, seq), F32),
        sent=VM(blocks, BF),
        got=VM((pc.n_p, MB, part, width), BF),
        kept_sem={n: DMA((MB,)) for n in kept},
        whole_sem={n: DMA((1,)) for n in whole},
        tok_sem=Deal.sems(pc),
        cot_sem=Deal.sems(pc),
        small_sem=pair(pc.n_t) + [DMA((1,))],
        qk_sem=HeadWeights.sems(pc),
        vo_sem=HeadWeights.sems(pc),
        up_sem=HiddenWeights.sems(pc),
        gate_sem=HiddenWeights.sems(pc),
        down_sem=HiddenWeights.sems(pc),
        ag_sem=PlanePass.sems(pc),
        ra_sem=PlanePass.sems(pc),
        ag1_sem=PlanePass.sems(pc),
        rc_sem=PlanePass.sems(pc),
    )
    near_ins = dict(hot=hot, rattn=rattn, rmlp=rmlp, segq=segq, segk=segk)
    far_ins = dict(
        tok=tok_sent, cot=cot_sent, wqk=wqk, wvo=wvo, wup=wup, wgate=wgate, wdown=wdown, small=small
    )

    def kernel(pc, v, x, o, k):
        own_p = pc.p
        greet(pc)
        deal = Deal(pc, x.tok, k.arrived, k.tok_sem)
        deal_cot = Deal(pc, x.cot, o.cot, k.cot_sem)
        head_qk = HeadWeights(pc, x.wqk, k.aqk, k.wqk, k.qk_sem)
        head_vo = HeadWeights(pc, x.wvo, k.avo, k.wvo, k.vo_sem)
        up = HiddenWeights(pc, x.wup, k.wup, k.up_sem)
        gate = HiddenWeights(pc, x.wgate, k.wgate, k.gate_sem)
        down = HiddenWeights(pc, x.wdown, k.wdown, k.down_sem)
        ss, rs, ls = k.small_sem
        scales = Moves(
            [
                Move(
                    x.small, k.small.at[pc.t], ss.at[q], rs.at[pc.t], pc.dev(pc.p, pc.r, q), k.small.at[q], rs.at[q]
                )
                for q in others(pc.n_t, pc.t)
            ]
        )
        own_scales = pltpu.make_async_copy(x.small, k.small.at[pc.t], ls.at[0])

        def gather(buf, sems):
            return PlanePass(pc, lambda m, q: buf.at[m, own_p], lambda m, q: buf.at[m, q], sems)

        def scatter(sems):
            return PlanePass(pc, lambda m, q: k.sent.at[m, q], lambda m, q: k.got.at[q, m], sems)

        ag, ag1, ra, rc = gather(k.hb, k.ag_sem), gather(k.hb1, k.ag1_sem), scatter(k.ra_sem), scatter(k.rc_sem)
        names = vars(k)
        out_names = vars(o)
        copies = []

        def keep(m, *refs):
            for n in kept:
                if any(names[n] is ref for ref in refs):
                    copy = pltpu.make_async_copy(names[n].at[m], out_names[n].at[m], k.kept_sem[n].at[m])
                    copy.start()
                    copies.append(copy)

        def keep_whole(*refs):
            for n in whole:
                if any(names[n] is ref for ref in refs):
                    copy = pltpu.make_async_copy(names[n], out_names[n], k.whole_sem[n].at[0])
                    copy.start()
                    copies.append(copy)

        def attend(m):
            fill_mask(k.bias, v.segq[m], v.segk[m])
            ag.wait_recv(m)
            keep(m, k.hb)

            def project(i, carry):
                rows = k.hb[m, pl.ds(2 * i, 2)].reshape(2 * part, width)
                at = pl.ds(pl.multiple_of(i * 2 * part, 2 * part), 2 * part)
                qk = dot_nn(rows, k.wqk[...])
                k.qk[m, at, :] = qk
                for j in range(qk_cols // LANES):
                    s = qk[:, tile_of(j)]
                    n = s * lax.rsqrt(half_means(s * s) + EPSILON)
                    k.qkb[m, at, tile_of(j)] = (n * k.sqk[:, tile_of(j)]).astype(BF)
                k.vb[m, at, :QUADS] = dot_nn(rows, k.wvo[:, :QUADS]).astype(BF)
                last = dot_nn(rows, k.wvo[:, 2 * QUADS :])
                k.vb[m, at, QUADS:] = jnp.where(low_lanes(last.shape), last, 0.0).astype(BF)
                return carry

            lax.fori_loop(0, pc.n_p // 2, project, 0)
            keep(m, k.qk, k.qkb, k.vb)
            blk = seq // 2
            for i in range(2):
                nk = (i + 1) * blk
                at = slice(i * blk, nk)
                bias = k.bias[at, :nk]
                lse = jnp.zeros((blk, LANES), F32)
                lane = lax.broadcasted_iota(jnp.int32, (blk, LANES), 1)
                for slab in range(3):
                    if slab < 2:
                        qs = k.qkb[m, at, tile_of(slab)]
                        ks = k.qkb[m, :nk, tile_of(2 + slab)]
                    else:
                        qs = k.qkb[m, at, 2 * QUADS :]
                        ks = swap_halves(k.qkb[m, :nk, 2 * QUADS :].astype(F32)).astype(BF)
                    vs = k.vb[m, :nk, tile_of(slab)]
                    res = []
                    for half in range(2 if slab < 2 else 1):
                        low = low_lanes(qs.shape)
                        q1 = jnp.where(low if half == 0 else jnp.logical_not(low), qs, jnp.zeros_like(qs))
                        s = dot_nt(q1, ks) * HEAD_DIM ** (-0.5) + bias
                        top = jnp.max(s, axis=1, keepdims=True)
                        e = jnp.exp(s - top)
                        tot = jnp.sum(e, axis=1, keepdims=True)
                        lse = jnp.where(lane == 2 * slab + half, top + jnp.log(tot), lse)
                        res.append(dot_nn((e * (1.0 / tot)).astype(BF), vs))
                    if slab < 2:
                        res = jnp.where(low_lanes(res[0].shape), res[0], res[1])
                    else:
                        res = swap_halves(res[0])
                    k.ob[m, at, tile_of(slab)] = res.astype(BF)
                k.lse[m, at, :] = lse
            keep(m, k.ob, k.lse)

            def branch(i, carry):
                at = pl.ds(pl.multiple_of(i * 2 * part, 2 * part), 2 * part)
                y = dot_nt(k.ob[m, at, :], k.wvo[:, QUADS:])
                k.sent[m, pl.ds(2 * i, 2)] = y.astype(BF).reshape(2, part, width)
                return carry

            lax.fori_loop(0, pc.n_p // 2, branch, 0)
            ra.start(m)

        def summed(m, at):
            total = k.sent[m, own_p, at, :].astype(F32)
            for q in others(pc.n_p, own_p):
                total = total + k.got[q, m, at, :].astype(F32)
            return total

        def middle(m):
            ra.wait_recv(m)

            def rows(at):
                a = summed(m, at)
                h = k.tok[m, at, :].astype(F32)
                y = h + v.rattn[...] * (a * inv_rms(a) - h)
                h1 = y * inv_rms(y)
                k.a[m, at, :] = a
                k.h1[m, at, :] = h1
                k.hb1[m, own_p, at, :] = h1.astype(BF)

            rows_loop(part, rows)
            ag1.start(m)
            keep(m, k.a, k.h1)

        def feed(m):
            ag1.wait_recv(m)
            keep(m, k.hb1)

            def hidden(at):
                rows = k.hb1[m].reshape(seq, width)
                u = dot_nn(rows, k.wup[:, at])
                g = dot_nn(rows, k.wgate[:, at])
                k.u[m, :, at] = u.astype(BF)
                k.g[m, :, at] = g.astype(BF)
                z = k.sgate[:, at] * g
                k.mb[m, :, at] = (z / (1.0 + jnp.exp(-z)) * (k.sup[:, at] * u)).astype(BF)

            chunks(hid, hidden)
            keep(m, k.u, k.g, k.mb)

        def shrink(m):
            ra.wait_send(m)

            def columns(at):
                y = dot_nt(k.mb[m], k.wdown[at, :])
                k.sent[m, :, :, at] = y.astype(BF).reshape(pc.n_p, part, CHUNK)

            chunks(width, columns)
            rc.start(m)

        def finish(m):
            rc.wait_recv(m)

            def rows(at):
                c = summed(m, at)
                h1 = k.h1[m, at, :]
                z = h1 + v.rmlp[...] * (c * inv_rms(c) - h1)
                k.c[m, at, :] = c
                k.h2[m, at, :] = (z * inv_rms(z)).astype(BF)

            rows_loop(part, rows)
            keep(m, k.c, k.h2)

        deal.start()
        head_qk.start()
        head_vo.start()
        scales.start()
        own_scales.start()
        for w in (up, gate, down):
            w.start()
        head_qk.relay()
        head_vo.relay()
        deal.wait_recv()

        def put(at, y):
            for m in range(MB):
                rows = y[m * part : (m + 1) * part].astype(BF)
                k.tok[m, :, at] = rows
                k.hb[m, own_p, :, at] = rows

        take_rows(v.hot, k.arrived, put)
        for m in range(MB):
            ag.start(m)
            keep(m, k.tok)
        head_qk.plane()
        head_vo.plane()
        up.tall()
        gate.tall()
        own_scales.wait()
        scales.wait_recv()
        for t in range(pc.n_t):
            for j in range(3):

                def move(t=t, j=j):
                    at = lanes(dst_tile(pc.p, t) + j, 1)
                    k.sup[:, at] = k.small[t, pl.ds(src_tile(pc.p, t) + j, 1), :]
                    k.sgate[:, at] = k.small[t, pl.ds(tiles + src_tile(pc.p, t) + j, 1), :]

                Move.under(width3(pc.p, t) if j == 2 else None, move)
        for j in range(qk_cols // LANES):
            k.sqk[:, tile_of(j)] = k.small[own_p, 2 * tiles + j : 2 * tiles + j + 1, :]
        keep_whole(k.sup, k.sgate, k.sqk)
        head_qk.near()
        head_vo.near()
        head_qk.wait_recv()
        head_vo.wait_recv()
        keep_whole(k.wqk, k.wvo)
        attend(0)
        up.relay()
        gate.relay()
        down.tall()
        deal_cot.start()
        attend(1)
        up.near()
        gate.near()
        middle(0)
        down.relay()
        middle(1)
        up.wait_recv()
        gate.wait_recv()
        keep_whole(k.wup, k.wgate)
        feed(0)
        down.near()
        down.wait_recv()
        keep_whole(k.wdown)
        shrink(0)
        feed(1)
        shrink(1)
        for m in range(MB):
            finish(m)
        deal_cot.wait_recv()
        for w in (deal, deal_cot, head_qk, head_vo, up, gate, down, scales):
            w.wait_send()
        for m in range(MB):
            for w in (ag, ag1, rc):
                w.wait_send(m)
        for copy in copies:
            copy.wait()

    return fused(1, kernel, near_ins, far_ins, outs, scratch)


def backward(pc, f, hot, rattn, rmlp, segq, segk):
    n_dev = f.cot.shape[0]
    part, width = f.h2.shape[1], f.h2.shape[2]
    seq = part * pc.n_p
    all_tok = MB * seq
    qk_cols, hid = f.wqk.shape[1], f.wup.shape[1]
    o_cols = QUADS + LANES
    tiles = hid // LANES
    n_rows = width // (pc.n_p * pc.n_r)
    step_rows = n_rows // 5
    if n_rows % 5 or hid != width:
        raise ValueError("sizes")
    blocks = (MB, pc.n_p, part, width)
    dealt = (n_dev, PAD, width)
    vec_rows = 4 * tiles
    vec_total = -(-(2 * vec_rows + 2 * tiles + pc.n_p * qk_cols // LANES) // PAD) * PAD
    heads_shape = (pc.n_p, n_rows, qk_cols)
    outs = dict(
        back_out=SDS(dealt, BF),
        back_grad=SDS(dealt, BF),
        vec=SDS((vec_total, LANES), F32),
        relay=[SDS((pc.n_p, n_rows, 3 * LANES), BF) for _ in range(3)],
        head_relay=[SDS((n_rows, qk_cols), BF) for _ in range(2)],
        tall=[SDS((pc.n_t, pc.n_p, n_rows, 3 * LANES), BF) for _ in range(3)],
        final=[SDS((n_rows, hid), BF) for _ in range(3)],
        head_p=[SDS(heads_shape, BF) for _ in range(2)],
        head_t=[SDS(heads_shape, BF) for _ in range(2)],
    )
    loaded = dict(
        c=f.c,
        h1=f.h1,
        wdown=f.wdown,
        u=f.u,
        g=f.g,
        sup=f.sup,
        sgate=f.sgate,
        wup=f.wup,
        wgate=f.wgate,
        mb=f.mb,
        hb1=f.hb1,
        tok=f.tok,
        wvo=f.wvo,
        vb=f.vb,
        qkb=f.qkb,
        lse=f.lse,
        qk=f.qk,
        sqk=f.sqk,
        wqk=f.wqk,
        ob=f.ob,
    )
    later = dict(a=f.a, hb=f.hb, cot=f.cot, h2=f.h2)
    sums = dict(gsup=hid, gsgate=hid, gsqk=qk_cols, grattn=width, grmlp=width)
    scratch = {n: VM(y.shape, y.dtype) for n, y in loaded.items()} | {n: VM((1, y), F32) for n, y in sums.items()}
    scratch |= dict(
        load_sem={n: DMA((1,)) for n in loaded},
        later_sem=[DMA((1,)) for _ in later],
        dcb=VM(blocks, BF),
        dab=VM(blocks, BF),
        mid=VM((MB, part, width), F32),
        bias=VM((seq, seq), F32),
        sent=VM(blocks, BF),
        got=VM((pc.n_p, MB, part, width), BF),
        tbuf=VM((pc.n_t, pc.n_p, n_rows, 3 * LANES), BF),
        dealbuf=VM(dealt, BF),
        vec=VM((vec_total, LANES), F32),
        vec_got=[VM((y, vec_total, LANES), F32) for y in (pc.n_r, pc.n_t, pc.n_p)],
        rbuf=VM((pc.n_p, n_rows, 3 * LANES), BF),
        hbuf=[VM((2, n_rows, qk_cols), BF) for _ in range(2)],
        near=[VM((pc.n_r - 1, pc.n_p, n_rows, y), BF) for y in (hid, hid, hid, qk_cols, qk_cols)],
        near_sem=[pair(pc.n_r) for _ in range(5)],
        tall_sem=[[DMA((2, pc.n_t)) for _ in range(3)] for _ in range(3)],
        plane_sem=[[DMA((2, pc.n_p)) for _ in range(2)] for _ in range(5)],
        relay_sem=[[DMA((2,)) for _ in range(5)] for _ in range(3)],
        head_sem=[pair(pc.n_t) + [DMA((1,))] for _ in range(2)],
        head_relay_sem=[[DMA((1,)) for _ in range(5)] for _ in range(2)],
        out_sem=Deal.sems(pc),
        grad_sem=Deal.sems(pc),
        vec_sem=[pair(y) for y in (pc.n_r, pc.n_t, pc.n_p)],
        vec_out=DMA((1,)),
        ag_sem=PlanePass.sems(pc),
        ag1_sem=PlanePass.sems(pc),
        rh1_sem=PlanePass.sems(pc),
        rh_sem=PlanePass.sems(pc),
    )
    near_ins = dict(hot=hot, rattn=rattn, rmlp=rmlp, segq=segq, segk=segk)

    def kernel(pc, v, x, o, k):
        own_p = pc.p
        refs = vars(k)
        sources = vars(x)
        loads = {n: pltpu.make_async_copy(sources[n], refs[n], k.load_sem[n].at[0]) for n in loaded}
        for n in loaded:
            loads[n].start()
        cot_load = pltpu.make_async_copy(x.cot, k.dealbuf, k.later_sem[2].at[0])
        h2_load = pltpu.make_async_copy(x.h2, k.dab.at[:, own_p], k.later_sem[3].at[0])
        cot_load.start()
        h2_load.start()
        k_dqk, k_dv = k.u.at[:, :, pl.ds(0, qk_cols)], k.u.at[:, :, pl.ds(qk_cols, o_cols)]
        k_do = k.g.at[0, :, pl.ds(0, o_cols)]
        a_load = pltpu.make_async_copy(x.a, k.c, k.later_sem[0].at[0])
        hb_load = pltpu.make_async_copy(x.hb.reshape(MB, seq, width), k.mb, k.later_sem[1].at[0])
        waited = set()

        def ready(*wanted):
            for n in loaded:
                if n not in waited and any(refs[n] is ref for ref in wanted):
                    waited.add(n)
                    loads[n].wait()

        for n in sums:
            refs[n][...] = jnp.zeros(refs[n].shape, F32)
        k.vec[...] = jnp.zeros(k.vec.shape, F32)
        greet(pc)

        def gather(buf, sems):
            return PlanePass(pc, lambda m, q: buf.at[m, own_p], lambda m, q: buf.at[m, q], sems)

        def scatter(sems):
            return PlanePass(pc, lambda m, q: k.sent.at[m, q], lambda m, q: k.got.at[q, m], sems)

        ag, ag1, rh1, rh = gather(k.dcb, k.ag_sem), gather(k.dab, k.ag1_sem), scatter(k.rh1_sem), scatter(k.rh_sem)
        deal_out = Deal(pc, k.dealbuf, o.back_out, k.out_sem)
        deal_grad = Deal(pc, k.dealbuf, o.back_grad, k.grad_sem)

        def add_rows(ref, y, at=slice(None)):
            ref[:, at] += jnp.sum(y, axis=0, keepdims=True)

        def top(m):
            def rows(at):
                c, h1, ct = k.c[m, at, :], k.h1[m, at, :], k.mid[m, at, :]
                r_c = inv_rms(c)
                n_c = c * r_c
                z = h1 + v.rmlp[...] * (n_c - h1)
                r_z = inv_rms(z)
                h2 = z * r_z
                dz = r_z * (ct - h2 * row_mean(ct * h2))
                add_rows(k.grmlp, dz * (n_c - h1))
                k.mid[m, at, :] = (1.0 - v.rmlp[...]) * dz
                dn = v.rmlp[...] * dz
                k.dcb[m, own_p, at, :] = (r_c * (dn - n_c * row_mean(dn * n_c))).astype(BF)

            rows_loop(part, rows)
            ag.start(m)

        def summed(m, at):
            total = k.sent[m, own_p, at, :].astype(F32)
            for q in others(pc.n_p, own_p):
                total = total + k.got[q, m, at, :].astype(F32)
            return total

        def feed(m):
            ag.wait_recv(m)

            def hidden(at):
                dm = dot_nn(k.dcb[m].reshape(seq, width), k.wdown[:, at])
                u, g = k.u[m, :, at].astype(F32), k.g[m, :, at].astype(F32)
                y = k.sgate[:, at] * g
                sig = 1.0 / (1.0 + jnp.exp(-y))
                du = dm * (y * sig)
                dx = dm * (k.sup[:, at] * u) * (sig * (1.0 + y * (1.0 - sig)))
                add_rows(k.gsup, du * u, at)
                add_rows(k.gsgate, dx * g, at)
                k.u[m, :, at] = (k.sup[:, at] * du).astype(BF)
                k.g[m, :, at] = (k.sgate[:, at] * dx).astype(BF)

            chunks(hid, hidden)

        def shrink(m):
            def columns(at):
                y = dot_nt(k.u[m], k.wup[at, :]) + dot_nt(k.g[m], k.wgate[at, :])
                k.sent[m, :, :, at] = y.astype(BF).reshape(pc.n_p, part, CHUNK)

            chunks(width, columns)
            rh1.start(m)

        grads = [k.wdown, k.wup, k.wgate, k.wqk, k.wvo]

        def near_slot(source, at):
            return (source - at + pc.n_r - 1) % pc.n_r

        def near_moves(i):
            send, recv = k.near_sem[i]
            return Moves(
                [
                    Move(
                        by_shard(pc, grads[i]).at[:, q], k.near[i].at[near_slot(pc.r, q)], send.at[q], recv.at[pc.r],
                        pc.dev(pc.p, q, pc.t), k.near[i].at[near_slot(q, pc.r)], recv.at[q],
                    )
                    for q in others(pc.n_r, pc.r)
                ]
            )

        near = [near_moves(i) for i in range(5)]

        def row_blocks(fn):
            def block(i, carry):
                fn(i // 5, pl.ds(pl.multiple_of((i % 5) * step_rows, step_rows), step_rows))
                return carry

            lax.fori_loop(0, pc.n_p * 5, block, 0)

        def near_sum(i):
            near[i].wait_recv()
            own = by_shard(pc, grads[i])

            def block(p, at):
                total = own[p, pc.r, at, :].astype(F32)
                for j in range(pc.n_r - 1):
                    total = total + k.near[i][j, p, at, :].astype(F32)
                k.near[i][0, p, at, :] = total.astype(BF)

            row_blocks(block)

        t = pc.t
        middle_dev = (t == 1) | (t == 2)
        end_dev = jnp.logical_not(middle_dev)
        far = jnp.where((t == 2) | (t == 3), 0, 3)
        by = jnp.where(t == 0, 1, 2)
        wide = width3(pc.p, t)
        wide_far = width3(pc.p, far)

        def direct_out(q):
            return (jnp.abs(q - t) != 3) & jnp.logical_not(middle_dev & (q == far))

        def comes(q):
            return jnp.abs(q - t) != 3

        def tall_moves(i):
            send, recv, _ = k.tall_sem[i]
            src, y = k.near[i].at[0], o.tall[i]
            moves = []
            for q in others(pc.n_t, t):
                there = dst_tile(pc.p, q)
                dev = pc.dev(pc.p, pc.r, q)
                moves.append(
                    Move(
                        src.at[:, :, lanes(there, 2)], y.at[t, :, :, TWO], send.at[0, q], recv.at[0, t], dev,
                        y.at[q, :, :, TWO], recv.at[0, q], direct_out(q), comes(q),
                    )
                )
                moves.append(
                    Move(
                        src.at[:, :, lanes(there + 2, 1)], y.at[t, :, :, ONE], send.at[1, q], recv.at[1, t], dev,
                        y.at[q, :, :, ONE], recv.at[1, q], direct_out(q) & width3(pc.p, q), comes(q) & wide,
                    )
                )
            return Moves(moves)

        def far_parts(i):
            at = dst_tile(pc.p, far)
            return ((TWO, lanes(at, 2), None), (ONE, lanes(at + 2, 1), wide_far))

        def both(a, b):
            return a if b is None else a & b

        def handed_moves(i):
            s1, r1, _, _, _ = k.relay_sem[i]
            src, y = k.near[i].at[0], o.relay[i]
            return Moves(
                [
                    Move(
                        src.at[:, :, at], y.at[:, :, w], s1.at[j], r1.at[j], pc.dev(pc.p, pc.r, by), y.at[:, :, w],
                        r1.at[j], both(end_dev, cond), both(middle_dev, cond),
                    )
                    for j, (w, at, cond) in enumerate(far_parts(i))
                ]
            )

        def passed_moves(i):
            _, _, s2, _, _ = k.relay_sem[i]
            recv = k.tall_sem[i][1]
            return Moves(
                [
                    Move(
                        k.rbuf.at[:, :, w], o.tall[i].at[t, :, :, w], s2.at[j], recv.at[j, t], pc.dev(pc.p, pc.r, far),
                        None, None, both(middle_dev, cond),
                    )
                    for j, (w, at, cond) in enumerate(far_parts(i))
                ]
            )

        tall = [tall_moves(i) for i in range(3)]
        handed = [handed_moves(i) for i in range(3)]
        passed = [passed_moves(i) for i in range(3)]

        def tall_start(i):
            handed[i].start()
            tall[i].start()

        def tall_relay(i):
            handed[i].wait_recv()

            @pl.when(middle_dev)
            def _():
                copy = pltpu.make_async_copy(o.relay[i], k.rbuf, k.relay_sem[i][3].at[0])
                copy.start()
                copy.wait()

                def add(w, at):
                    def block(p, rows):
                        total = k.rbuf[p, rows, w].astype(F32) + k.near[i][0, p, rows, at].astype(F32)
                        k.rbuf[p, rows, w] = total.astype(BF)

                    row_blocks(block)

                for w, at, cond in far_parts(i):
                    Move.under(cond, lambda w=w, at=at: add(w, at))

            passed[i].start()

        def tall_sum(i):
            tall[i].wait_recv()
            local = []
            for q in others(pc.n_t, t):
                for j, (w, cond) in enumerate(((TWO, comes(q)), (ONE, comes(q) & wide))):
                    copy = pltpu.make_async_copy(
                        o.tall[i].at[q, :, :, w], k.tbuf.at[q, :, :, w], k.tall_sem[i][2].at[j, q]
                    )
                    Move.under(cond, copy.start)
                    local.append((cond, copy))
            for cond, copy in local:
                Move.under(cond, copy.wait)
            here = dst_tile(pc.p, t)

            def add(source, target):
                def block(p, at):
                    total = k.near[i][0, p, at, source].astype(F32)
                    for q in others(pc.n_t, t):
                        total = total + jnp.where(comes(q), k.tbuf[q, p, at, target].astype(F32), 0.0)
                    k.tbuf[t, p, at, target] = total.astype(BF)

                row_blocks(block)

            add(lanes(here, 2), TWO)
            pl.when(wide)(lambda: add(lanes(here + 2, 1), ONE))

        def plane_moves(i):
            send, recv = k.plane_sem[i]
            y, src = o.final[i], k.tbuf.at[pc.t]
            here = src_tile(pc.p, pc.t)
            moves = []
            for q in others(pc.n_p, pc.p):
                there = src_tile(q, pc.t)
                dev = pc.dev(q, pc.r, pc.t)
                moves.append(
                    Move(
                        src.at[q, :, TWO], y.at[:, lanes(here, 2)], send.at[0, q], recv.at[0, pc.p], dev,
                        y.at[:, lanes(there, 2)], recv.at[0, q],
                    )
                )
                moves.append(
                    Move(
                        src.at[q, :, ONE], y.at[:, lanes(here + 2, 1)], send.at[1, q], recv.at[1, pc.p], dev,
                        y.at[:, lanes(there + 2, 1)], recv.at[1, q], wide, width3(q, pc.t),
                    )
                )
            own = (
                (None, pltpu.make_async_copy(src.at[own_p, :, TWO], y.at[:, lanes(here, 2)], send.at[0, pc.p])),
                (wide, pltpu.make_async_copy(src.at[own_p, :, ONE], y.at[:, lanes(here + 2, 1)], send.at[1, pc.p])),
            )
            return Moves(moves), own

        plane = [plane_moves(i) for i in range(3)]

        def plane_start(i):
            moves, own = plane[i]
            moves.start()
            for cond, copy in own:
                Move.under(cond, copy.start)

        def plane_sent(i):
            moves, own = plane[i]
            moves.wait_send()
            for cond, copy in own:
                Move.under(cond, copy.wait)

        def head_planes(i):
            send, recv = k.plane_sem[3 + i]
            src, y = k.near[3 + i].at[0], o.head_p[i]
            return Moves(
                [
                    Move(
                        src.at[q], y.at[pc.p], send.at[0, q], recv.at[0, pc.p], pc.dev(q, pc.r, pc.t), y.at[q],
                        recv.at[0, q],
                    )
                    for q in others(pc.n_p, pc.p)
                ]
            )

        def head_talls(i):
            send, recv, _ = k.head_sem[i]
            src, y = o.head_p[i], o.head_t[i]
            return Moves(
                [
                    Move(
                        src.at[q], y.at[t], send.at[q], recv.at[t], pc.dev(pc.p, pc.r, q), y.at[q], recv.at[q],
                        direct_out(q), comes(q),
                    )
                    for q in others(pc.n_t, t)
                ]
            )

        def head_handed(i):
            s1, r1, _, _, _ = k.head_relay_sem[i]
            y = o.head_relay[i]
            return Move(
                o.head_p[i].at[far], y, s1.at[0], r1.at[0], pc.dev(pc.p, pc.r, by), y, r1.at[0], end_dev, middle_dev
            )

        def head_passed(i):
            _, _, s2, _, _ = k.head_relay_sem[i]
            recv = k.head_sem[i][1]
            return Move(
                k.hbuf[i].at[0], o.head_t[i].at[t], s2.at[0], recv.at[t], pc.dev(pc.p, pc.r, far), None, None, middle_dev
            )

        head_first = [head_handed(i) for i in range(2)]
        head_last = [head_passed(i) for i in range(2)]

        def head_start(i):
            head_first[i].start()
            head_tall[i].start()

        def head_relay(i):
            head_first[i].wait_recv()

            @pl.when(middle_dev)
            def _():
                copies = [
                    pltpu.make_async_copy(o.head_relay[i], k.hbuf[i].at[0], k.head_relay_sem[i][3].at[0]),
                    pltpu.make_async_copy(o.head_p[i].at[far], k.hbuf[i].at[1], k.head_relay_sem[i][4].at[0]),
                ]
                for copy in copies:
                    copy.start()
                for copy in copies:
                    copy.wait()
                k.hbuf[i][0] = (k.hbuf[i][0].astype(F32) + k.hbuf[i][1].astype(F32)).astype(BF)

            head_last[i].start()

        head_plane = [head_planes(i) for i in range(2)]
        head_tall = [head_talls(i) for i in range(2)]
        head_own = [
            pltpu.make_async_copy(k.near[3 + i].at[0, own_p], o.head_p[i].at[pc.p], k.head_sem[i][2].at[0])
            for i in range(2)
        ]

        def middle(m):
            rh1.wait_recv(m)

            def rows(at):
                dh1 = k.mid[m, at, :] + summed(m, at)
                a, h = k.c[m, at, :], k.tok[m, at, :].astype(F32)
                r_a = inv_rms(a)
                n_a = a * r_a
                y = h + v.rattn[...] * (n_a - h)
                r_y = inv_rms(y)
                h1 = y * r_y
                dy = r_y * (dh1 - h1 * row_mean(dh1 * h1))
                add_rows(k.grattn, dy * (n_a - h))
                k.mid[m, at, :] = (1.0 - v.rattn[...]) * dy
                dn = v.rattn[...] * dy
                k.dab[m, own_p, at, :] = (r_a * (dn - n_a * row_mean(dn * n_a))).astype(BF)

            rows_loop(part, rows)
            ag1.start(m)

        def flat(ref, at=slice(None)):
            return ref[:, :, at].reshape(all_tok, -1)

        def columns_of(ref, at):
            return ref[:, :, :, at].reshape(all_tok, CHUNK)

        def weight_grad(target, left, right):
            def block(at):
                target[at, :] = dot_tn(columns_of(left, at), flat(right)).astype(BF)

            chunks(width, block)

        score = HEAD_DIM ** (-0.5)
        blk = seq // 2

        def attend(m):
            fill_mask(k.bias, v.segq[m], v.segk[m])
            ag1.wait_recv(m)

            def project(i, carry):
                rows = k.dab[m, pl.ds(2 * i, 2)].reshape(2 * part, width)
                at = pl.ds(pl.multiple_of(i * 2 * part, 2 * part), 2 * part)
                k_do[at, :] = dot_nn(rows, k.wvo[:, QUADS:]).astype(BF)
                return carry

            lax.fori_loop(0, pc.n_p // 2, project, 0)

            def norm_grad(tile, d):
                at = tile_of(tile)
                raw = k.qk[m, :, at]
                r = lax.rsqrt(half_means(raw * raw) + EPSILON)
                n = raw * r
                d = d * score
                add_rows(k.gsqk, d * n, at)
                dy = d * k.sqk[:, at]
                k_dqk[m, :, at] = (r * (dy - n * half_means(dy * n))).astype(BF)

            for slab in range(3):
                own = tile_of(slab)
                if slab < 2:
                    q_all = k.qkb[m, :, own]
                    k_all = k.qkb[m, :, tile_of(2 + slab)]
                    do_all = k_do[:, own]
                else:
                    q_all = k.qkb[m, :, 2 * QUADS :]
                    k_all = swap_halves(q_all.astype(F32)).astype(BF)
                    do_all = swap_halves(k_do[:, own].astype(F32)).astype(BF)
                v_all = k.vb[m, :, own]
                low = low_lanes((blk, LANES))
                dq, dk, dv = [], None, None
                for i in range(2):
                    nk = (i + 1) * blk
                    at = slice(i * blk, nk)
                    bias = k.bias[at, :nk]
                    dq_i = None
                    for half in range(2 if slab < 2 else 1):
                        here = low if half == 0 else jnp.logical_not(low)
                        zero = jnp.zeros((blk, LANES), BF)
                        q1, do1 = jnp.where(here, q_all[at], zero), jnp.where(here, do_all[at], zero)
                        lse = k.lse[m, at, 2 * slab + half : 2 * slab + half + 1]
                        prob = jnp.exp(dot_nt(q1, k_all[:nk]) * score + bias - lse)
                        dp = dot_nt(do1, v_all[:nk])
                        w = prob * dp
                        ds = (w - prob * jnp.sum(w, axis=1, keepdims=True)).astype(BF)
                        y = jnp.where(here, dot_nn(ds, k_all[:nk]), 0.0)
                        dq_i = y if dq_i is None else dq_i + y
                        dk_i, dv_i = dot_tn(ds, q1), dot_tn(prob.astype(BF), do1)
                        if i == 0:
                            dk = dk_i if dk is None else dk + dk_i
                            dv = dv_i if dv is None else dv + dv_i
                        else:
                            if half == 0:
                                dk = jnp.concatenate([dk, jnp.zeros((blk, LANES), F32)], axis=0)
                                dv = jnp.concatenate([dv, jnp.zeros((blk, LANES), F32)], axis=0)
                            dk, dv = dk + dk_i, dv + dv_i
                    dq.append(dq_i)
                dq = jnp.concatenate(dq, axis=0)
                k_dv[m, :, own] = dv.astype(BF)
                if slab < 2:
                    norm_grad(slab, dq)
                    norm_grad(2 + slab, dk)
                else:
                    norm_grad(4, dq + swap_halves(dk))
            rh1.wait_send(m)

            def columns(at):
                y = dot_nt(k_dqk[m], k.wqk[at, :])
                y = y + dot_nt(k_dv[m, :, :QUADS], k.wvo[at, :QUADS])
                y = y + dot_nt(k_dv[m, :, QUADS:], k.wvo[at, 2 * QUADS :])
                k.sent[m, :, :, at] = y.astype(BF).reshape(pc.n_p, part, CHUNK)

            chunks(width, columns)
            rh.start(m)

        def heads_grad(at):
            hb, dab = flat(k.mb, at), columns_of(k.dab, at)
            quads = slice(0, QUADS)
            rest = slice(QUADS, None)
            k.wqk[at, :] = dot_tn(hb, flat(k_dqk)).astype(BF)
            k.wvo[at, :QUADS] = dot_tn(hb, flat(k_dv, quads)).astype(BF)
            k.wvo[at, QUADS : 2 * QUADS] = dot_tn(dab, flat(k.ob, quads)).astype(BF)
            k.wvo[at, 2 * QUADS :] = (dot_tn(hb, flat(k_dv, rest)) + dot_tn(dab, flat(k.ob, rest))).astype(BF)

        def bottom(m):
            rh.wait_recv(m)

            def rows(at):
                k.mid[m, at, :] = k.mid[m, at, :] + summed(m, at)

            rows_loop(part, rows)

        def collect():
            for t in range(pc.n_t):
                for j in range(3):

                    def move(t=t, j=j):
                        here = lanes(dst_tile(pc.p, t) + j, 1)
                        row = t * tiles + src_tile(pc.p, t) + j
                        k.vec[pl.ds(row, 1), :] = k.gsup[:, here]
                        k.vec[pl.ds(vec_rows + row, 1), :] = k.gsgate[:, here]

                    Move.under(width3(pc.p, t) if j == 2 else None, move)
            at = 2 * vec_rows
            for j in range(tiles):
                k.vec[at + j : at + j + 1, :] = k.grattn[:, tile_of(j)]
                k.vec[at + tiles + j : at + tiles + j + 1, :] = k.grmlp[:, tile_of(j)]
            count = qk_cols // LANES
            for j in range(count):
                k.vec[pl.ds(at + 2 * tiles + own_p * count + j, 1), :] = k.gsqk[:, tile_of(j)]

        def vec_stage(n, count, own, dev_of):
            send, recv = k.vec_sem[n]
            buf = k.vec_got[n]
            moves = Moves(
                [
                    Move(buf.at[own], buf.at[own], send.at[q], recv.at[own], dev_of(q), buf.at[q], recv.at[q])
                    for q in others(count, own)
                ]
            )

            def start():
                buf[own] = k.vec[...]
                moves.start()

            def finish():
                moves.wait_recv()
                total = buf[0]
                for q in range(1, count):
                    total = total + buf[q]
                k.vec[...] = total

            return start, finish, moves

        vec_stages = [
            vec_stage(0, pc.n_r, pc.r, lambda q: pc.dev(pc.p, q, pc.t)),
            vec_stage(1, pc.n_t, pc.t, lambda q: pc.dev(pc.p, pc.r, q)),
            vec_stage(2, pc.n_p, pc.p, lambda q: pc.dev(q, pc.r, pc.t)),
        ]
        vec_keep = pltpu.make_async_copy(k.vec, o.vec, k.vec_out.at[0])

        ready(k.c, k.h1)
        cot_load.wait()

        def put(at, y):
            for m in range(MB):
                k.mid[m, :, at] = y[m * part : (m + 1) * part]

        take_rows(v.hot, k.dealbuf, put)
        for m in range(MB):
            top(m)
        a_load.start()
        h2_load.wait()
        give_rows(v.hot, lambda at: k.dab[:, own_p, :, at].reshape(MB * part, CHUNK), k.dealbuf)
        deal_out.start()
        ready(k.wdown, k.u, k.g, k.wup, k.wgate, k.sup, k.sgate)
        feed(0)
        shrink(0)
        feed(1)
        ready(k.mb, k.hb1)
        weight_grad(k.wdown, k.dcb, k.mb)
        near[0].start()
        hb_load.start()
        shrink(1)
        near_sum(0)
        tall_start(0)
        weight_grad(k.wup, k.hb1, k.u)
        near[1].start()
        ready(k.tok)
        a_load.wait()
        middle(0)
        near_sum(1)
        tall_relay(0)
        tall_start(1)
        weight_grad(k.wgate, k.hb1, k.g)
        near[2].start()
        middle(1)
        near_sum(2)
        tall_start(2)
        ready(k.wvo, k.vb, k.qkb, k.lse, k.qk, k.sqk, k.wqk, k.ob)
        attend(0)
        passed[0].wait_send()
        tall_relay(1)
        attend(1)
        hb_load.wait()
        chunks(width, heads_grad)
        for i in range(2):
            near[3 + i].start()
        collect()
        vec_stages[0][0]()
        for i in range(2):
            near_sum(3 + i)
            head_plane[i].start()
            head_own[i].start()
        passed[1].wait_send()
        tall_relay(2)
        tall_sum(0)
        plane_start(0)
        vec_stages[0][1]()
        vec_stages[1][0]()
        for m in range(MB):
            bottom(m)
        deal_out.wait_recv()
        deal_out.wait_send()
        give_rows(v.hot, lambda at: k.mid[:, :, at].reshape(MB * part, CHUNK).astype(BF), k.dealbuf)
        deal_grad.start()
        for i in range(2):
            head_plane[i].wait_recv()
            head_own[i].wait()
            head_start(i)
        plane_sent(0)
        tall_sum(1)
        plane_start(1)
        vec_stages[1][1]()
        vec_stages[2][0]()
        for i in range(2):
            head_relay(i)
        plane_sent(1)
        tall_sum(2)
        plane_start(2)
        vec_stages[2][1]()
        vec_keep.start()
        plane_sent(2)
        passed[2].wait_send()
        for w in tall + handed + head_first + head_last + head_plane + head_tall + near + [deal_grad]:
            w.wait_send()
        for stage in vec_stages:
            stage[2].wait_send()
        for i in range(3):
            plane[i][0].wait_recv()
        for w in head_tall + [deal_grad]:
            w.wait_recv()
        vec_keep.wait()
        for m in range(MB):
            ag.wait_send(m)
            ag1.wait_send(m)
            rh.wait_send(m)

    return fused(2, kernel, near_ins, loaded | later, outs, scratch)


def merged(slots, own, at):
    total = own.astype(F32)
    for q in range(slots.shape[0]):
        total = total + jnp.where((q == at) | (jnp.abs(q - at) == 3), 0, slots[q]).astype(F32)
    return total


def pick(x, at, axis):
    return lax.dynamic_index_in_dim(x, at, axis, keepdims=False)


def mm(a, b):
    return jnp.dot(a, b, preferred_element_type=F32)


def segment_ids(lengths_row, tok_count):
    count = lengths_row.shape[0]
    upto = jnp.arange(count)[:, None] >= jnp.arange(count)[None, :]
    doc_ends = jnp.sum(jnp.where(upto, lengths_row[None, :], 0), axis=1)
    places = jnp.arange(tok_count, dtype=jnp.int32)
    return jnp.sum((places[:, None] >= doc_ends[None, :]).astype(jnp.int32), axis=1)


def packed(x, y):
    return jnp.concatenate([x[:, :QUADS], y[:, :QUADS], x[:, QUADS:], y[:, QUADS:]], axis=1)


def unpacked(z):
    mid = 2 * QUADS + HEAD_DIM
    return (
        jnp.concatenate([z[..., :QUADS], z[..., 2 * QUADS : mid]], axis=-1),
        jnp.concatenate([z[..., QUADS : 2 * QUADS], z[..., mid:]], axis=-1),
    )


def body(
    tokens,
    cotangent,
    slot,
    lengths,
    w_query,
    w_key,
    w_value,
    w_out,
    w_up,
    w_gate,
    w_down,
    scale_qk,
    scale_up,
    scale_gate,
    rate_attn,
    rate_mlp,
):
    pc = Place()
    n_p, n_r, n_t, n_dev = pc.n_p, pc.n_r, pc.n_t, pc.n_dev
    rows_dev, width = tokens.shape
    tok_count = rows_dev // MB * n_p
    head_cols = w_query.shape[2]
    hid = w_up.shape[2]
    tiles = hid // LANES
    group = pc.r * n_t + pc.t
    owner = group * n_p + pc.p
    if rows_dev // n_dev > PAD or head_cols != QUADS + HEAD_DIM:
        raise ValueError("sizes")

    table = slot.reshape(n_dev, rows_dev)
    own_slots = lax.dynamic_index_in_dim(table, pc.me, 0, keepdims=False)
    d = own_slots // rows_dev
    to_dev = ((d % n_p) * n_r + (d // n_p) // n_t) * n_t + (d // n_p) % n_t
    places = jnp.arange(rows_dev, dtype=jnp.int32)
    spots = jnp.arange(n_dev * PAD, dtype=jnp.int32)
    before = (d[:, None] == d[None, :]) & (places[None, :] < places[:, None])
    rank = jnp.sum(before.astype(jnp.int32), axis=1)
    send_hot = (spots[:, None] == (to_dev * PAD + rank)[None, :]).astype(BF)

    sel = table // rows_dev == owner
    tri = (places[:, None] < places[None, :]).astype(BF)
    ranks = mm(sel.astype(BF), tri).astype(jnp.int32)
    kth = sel[:, None, :] & (ranks[:, None, :] == jnp.arange(PAD, dtype=jnp.int32)[None, :, None])
    owner_rows = jnp.sum(jnp.where(kth, (table - owner * rows_dev + 1)[:, None, :], 0), axis=2).reshape(-1) - 1
    recv_hot = (places[:, None] == owner_rows[None, :]).astype(BF)

    def to_send(x):
        return mm(send_hot, x).astype(BF).reshape(n_dev, PAD, width)

    qk_scale = packed(scale_qk, scale_qk).reshape(-1, LANES)
    small = jnp.concatenate([scale_up.reshape(-1, LANES), scale_gate.reshape(-1, LANES), qk_scale])
    small = jnp.pad(small, ((0, -small.shape[0] % 8), (0, 0)))
    own_lengths = lax.dynamic_slice_in_dim(lengths, group * MB, MB, 0)
    segments = jnp.stack([segment_ids(own_lengths[m], tok_count) for m in range(MB)])
    shared = (recv_hot, rate_attn, rate_mlp, segments[:, :, None], segments[:, None, :])

    f = forward(
        pc,
        to_send(tokens),
        to_send(cotangent),
        packed(w_query[0], w_key[0]),
        packed(w_value[0], w_out[0]),
        w_up[0],
        w_gate[0],
        w_down[0],
        small,
        *shared,
    )
    b = backward(pc, f, *shared)

    vec = b.vec
    at = n_t * tiles

    def own_row(x):
        return lax.dynamic_index_in_dim(x.reshape(n_t, -1), pc.t, 0)

    qk_rows = qk_scale.shape[0]
    out_sup, out_sgate = own_row(vec[:at]), own_row(vec[at : 2 * at])
    at = 2 * at
    out_rattn, out_rmlp = vec[at : at + tiles].reshape(1, -1), vec[at + tiles : at + 2 * tiles].reshape(1, -1)
    at = at + 2 * tiles
    out_sqk = sum(unpacked(own_row(vec[at : at + n_t * qk_rows])))
    heads = [
        x[None]
        for got, sent in zip(b.head_t, b.head_p)
        for x in unpacked(merged(got, pick(sent, pc.t, 0), pc.t))
    ]

    def from_back(x):
        return lax.dot_general(
            send_hot, x.reshape(-1, width), (((0,), (0,)), ((), ())), preferred_element_type=F32
        )

    down, up, gate = (x.astype(F32)[None] for x in b.final)
    return (
        from_back(b.back_out),
        from_back(b.back_grad),
        *heads,
        up,
        gate,
        down,
        out_sqk,
        out_sup,
        out_sgate,
        out_rattn,
        out_rmlp,
    )


def solution(mesh):
    tok = P(("dp", "tensor"), None)
    mat = P(None, "dp", "tensor")
    vec = P(None, "tensor")
    in_specs = (tok, tok, P(), P()) + (mat,) * 7 + (vec,) * 3 + (P(), P())
    out_specs = (tok, tok) + (mat,) * 7 + (vec,) * 3 + (P(), P())
    return jax.shard_map(body, mesh=mesh, in_specs=in_specs, out_specs=out_specs, check_vma=False)
```

```python
import types

import jax
import jax.numpy as jnp
from jax import lax
from jax.experimental import pallas as pl
from jax.experimental.pallas import tpu as pltpu
from jax.sharding import PartitionSpec as P

HEAD_DIM = 64
MB = 2
LANES = 128
QUADS = 4 * HEAD_DIM
CHUNK = 2 * LANES
ROW_STEP = 32
PAD = 8
VMEM_LIMIT = 127 * 2**19

EPSILON = 1e-06
MASKED = -1e30
BF = jnp.bfloat16
F32 = jnp.float32
MESH = pl.DeviceIdType.MESH
VM = pltpu.VMEM
DMA = pltpu.SemaphoreType.DMA
SDS = jax.ShapeDtypeStruct


class Place:
    def __init__(self):
        self.n_t = lax.axis_size("tensor")
        self.n_dp = lax.axis_size("dp")
        self.n_p = self.n_t
        self.n_r = self.n_dp // self.n_p
        self.n_dev = self.n_dp * self.n_t
        if self.n_t != 4:
            raise ValueError("tensor size")
        dp = lax.axis_index("dp")
        self.t = lax.axis_index("tensor")
        self.p = dp // self.n_r
        self.r = dp % self.n_r
        self.me = dp * self.n_t + self.t

    def dev(self, p, r, t):
        return (p * self.n_r + r, t)

    def flat(self, j):
        return (j // self.n_t, j % self.n_t)


def width3(p, t):
    return (p + t) % 2 == 0


def src_tile(p, t):
    return 5 * (p // 2) + (p % 2) * (3 - t % 2)


def dst_tile(p, t):
    return 5 * (t // 2) + (t % 2) * (3 - p % 2)


def lanes(tile, count):
    return pl.ds(pl.multiple_of(tile * LANES, LANES), count * LANES)


TWO, ONE = pl.ds(0, 2 * LANES), pl.ds(2 * LANES, LANES)


def remote(src, dst, send, recv, dev):
    return pltpu.make_async_remote_copy(
        src_ref=src, dst_ref=dst, send_sem=send, recv_sem=recv, device_id=dev, device_id_type=MESH
    )


class Move:
    def __init__(self, src, dst, send, recv, dev, landing, landed, cond_out=None, cond_in=None):
        self.going = (src, dst, send, recv, dev)
        self.coming = (landing, landing, send, landed, dev)
        self.cond_out, self.cond_in = cond_out, cond_in

    @staticmethod
    def under(cond, act):
        if cond is None:
            act()
        else:
            pl.when(cond)(act)

    def start(self):
        self.under(self.cond_out, lambda: remote(*self.going).start())

    def wait_send(self):
        self.under(self.cond_out, lambda: remote(*self.going).wait_send())

    def wait_recv(self):
        self.under(self.cond_in, lambda: remote(*self.coming).wait_recv())


class Moves:
    def __init__(self, moves):
        self.moves = moves

    def start(self):
        for m in self.moves:
            m.start()

    def wait_recv(self):
        for m in self.moves:
            m.wait_recv()

    def wait_send(self):
        for m in self.moves:
            m.wait_send()


def others(count, own):
    order = [2, 1, 3] if count == 4 else list(range(1, count))
    return [(own + k) % count for k in order]


def pair(n):
    return [DMA((n,)), DMA((n,))]


class Deal:
    @staticmethod
    def sems(pc):
        return [DMA((1,)), DMA((1,)), DMA((1,))]

    def __init__(self, pc, x, y, sems):
        self.pc, self.x, self.y = pc, x, y
        self.send, self.recv, self.local = (sem.at[0] for sem in sems)

    def copy(self, j, src, dst):
        return remote(src, dst, self.send, self.recv, self.pc.flat(j))

    def own(self):
        return pltpu.make_async_copy(self.x.at[self.pc.me], self.y.at[self.pc.me], self.local)

    def start(self):
        pc = self.pc

        def step(i, carry):
            j = (pc.me + i) % pc.n_dev
            self.copy(j, self.x.at[j], self.y.at[pc.me]).start()
            return carry

        lax.fori_loop(1, pc.n_dev, step, 0)
        self.own().start()

    def all_but_own(self):
        part = self.y.at[pl.ds(0, self.pc.n_dev - 1)]
        return self.copy((self.pc.me + 1) % self.pc.n_dev, part, part)

    def wait_recv(self):
        self.own().wait()
        self.all_but_own().wait_recv()

    def wait_send(self):
        self.all_but_own().wait_send()


class Tall:
    @staticmethod
    def sems(pc, pieces):
        return [DMA((pieces, pc.n_t + 1)), DMA((pieces, pc.n_t))]

    def __init__(self, pc, shard, own, sems):
        t = pc.t
        middle = (t == 1) | (t == 2)
        far, end = jnp.where(t == 2, 0, 3), jnp.where(t == 2, 3, 0)
        send, recv = sems

        def both(a, b):
            return a if b is None else a & b

        self.first, self.passed = [], []
        for q in others(pc.n_t, t):
            for i, ((dst, c_out), src, (here, c_in)) in enumerate(zip(shard(t), own, shard(q))):
                args = (src, dst, send.at[i, q], recv.at[i, t], pc.dev(pc.p, pc.r, q), here, recv.at[i, q])
                c_in = both(jnp.logical_not(middle & (q == far)), c_in)
                self.first.append(Move(*args, both(jnp.abs(q - t) != 3, c_out), c_in))
        for i, (ref, c) in enumerate(shard(far)):
            self.passed.append(
                Move(
                    ref, ref, send.at[i, pc.n_t], recv.at[i, far], pc.dev(pc.p, pc.r, end), ref, recv.at[i, far],
                    both(middle, c), both(middle, c),
                )
            )

    def start(self):
        for m in self.first:
            m.start()

    def relay(self):
        for m in self.passed:
            m.wait_recv()
            m.start()

    def wait_recv(self):
        for m in self.first:
            m.wait_recv()

    def wait_send(self):
        for m in self.first + self.passed:
            m.wait_send()


def by_shard(pc, ref):
    return ref.reshape(pc.n_p, pc.n_r, ref.shape[0] // (pc.n_p * pc.n_r), ref.shape[1])


class HeadWeights:
    @staticmethod
    def sems(pc):
        return [Tall.sems(pc, 1), pair(pc.n_p), pair(pc.n_r), DMA((2,))]

    def __init__(self, pc, x, a, w, sems):
        tall, (s2, r2), (s3, r3), ls = sems
        f = by_shard(pc, w)
        self.first = Tall(pc, lambda q: [(a.at[q], None)], [x], tall)
        self.second = Moves(
            [
                Move(a.at[q], f.at[pc.p, pc.r], s2.at[q], r2.at[pc.p], pc.dev(q, pc.r, pc.t), f.at[q, pc.r], r2.at[q])
                for q in others(pc.n_p, pc.p)
            ]
        )
        self.third = Moves(
            [
                Move(f.at[:, pc.r], f.at[:, pc.r], s3.at[q], r3.at[pc.r], pc.dev(pc.p, q, pc.t), f.at[:, q], r3.at[q])
                for q in others(pc.n_r, pc.r)
            ]
        )
        self.keep1 = pltpu.make_async_copy(x, a.at[pc.t], ls.at[0])
        self.keep2 = pltpu.make_async_copy(a.at[pc.p], f.at[pc.p, pc.r], ls.at[1])

    def start(self):
        self.first.start()
        self.keep1.start()

    def relay(self):
        self.first.relay()

    def plane(self):
        self.keep1.wait()
        self.first.wait_recv()
        self.second.start()
        self.keep2.start()

    def near(self):
        self.keep2.wait()
        self.second.wait_recv()
        self.third.start()

    def wait_recv(self):
        self.third.wait_recv()

    def wait_send(self):
        self.first.wait_send()
        self.second.wait_send()
        self.third.wait_send()


class HiddenWeights:
    @staticmethod
    def sems(pc):
        return [pair(pc.n_p), pair(pc.n_p), Tall.sems(pc, 2), pair(pc.n_r), DMA((2,))]

    def __init__(self, pc, x, w, sems):
        (s1, r1), (s2, r2), tall, (s3, r3), ls = sems
        g = by_shard(pc, w)
        p, r, t = pc.p, pc.r, pc.t

        def spot(q, row, extra):
            at = dst_tile(q, t)
            return g.at[row, r, :, lanes(at + 2, 1) if extra else lanes(at, 2)]

        def piece(q, extra):
            at = src_tile(q, t)
            return x.at[:, lanes(at + 2, 1) if extra else lanes(at, 2)]

        moves = []
        for q in others(pc.n_p, p):
            dev = pc.dev(q, r, t)
            moves.append(
                Move(piece(q, False), spot(q, p, False), s1.at[q], r1.at[p], dev, spot(p, q, False), r1.at[q])
            )
            moves.append(
                Move(
                    piece(q, True), spot(q, p, True), s2.at[q], r2.at[p], dev, spot(p, q, True), r2.at[q],
                    width3(q, t), width3(p, t),
                )
            )
        self.first = Moves(moves)
        self.own = [
            (None, pltpu.make_async_copy(piece(p, False), spot(p, p, False), ls.at[0])),
            (width3(p, t), pltpu.make_async_copy(piece(p, True), spot(p, p, True), ls.at[1])),
        ]

        def shard(q):
            at = dst_tile(p, q)
            return [(g.at[:, r, :, lanes(at, 2)], None), (g.at[:, r, :, lanes(at + 2, 1)], width3(p, q))]

        self.second = Tall(pc, shard, [ref for ref, _ in shard(t)], tall)
        self.third = Moves(
            [
                Move(g.at[:, r], g.at[:, r], s3.at[q], r3.at[r], pc.dev(p, q, t), g.at[:, q], r3.at[q])
                for q in others(pc.n_r, r)
            ]
        )

    def start(self):
        self.first.start()
        for cond, copy in self.own:
            Move.under(cond, copy.start)

    def tall(self):
        for cond, copy in self.own:
            Move.under(cond, copy.wait)
        self.first.wait_recv()
        self.second.start()

    def relay(self):
        self.second.relay()

    def near(self):
        self.second.wait_recv()
        self.third.start()

    def wait_recv(self):
        self.third.wait_recv()

    def wait_send(self):
        self.first.wait_send()
        self.second.wait_send()
        self.third.wait_send()


def add_into(target, term, rows):
    step = rows // 2

    def block(i, carry):
        at = pl.ds(pl.multiple_of(i * step, step), step)
        target[at, :] = (target[at, :].astype(F32) + term[at, :].astype(F32)).astype(BF)
        return carry

    lax.fori_loop(0, 2, block, 0)


class Plane:
    def __init__(self, pc):
        self.x, self.y, self.d = pc.p + 1 - 2 * (pc.p % 2), (pc.p + 2) % 4, 3 - pc.p
        self.to_x, self.to_y = pc.dev(self.x, pc.r, pc.t), pc.dev(self.y, pc.r, pc.t)

    def halves(self, ref):
        half = ref.shape[0] // 2
        return ref.at[pl.ds(0, half)], ref.at[pl.ds(half, half)]

    def wait_send(self, m):
        for move in self.first[m] + self.second[m]:
            move.wait_send()


class PlaneGather(Plane):
    @staticmethod
    def sems(pc):
        return [DMA((MB, 4)), DMA((MB, 4))]

    def __init__(self, pc, spot, sems):
        super().__init__(pc)
        send, recv = sems
        self.first, self.second = [], []
        for m in range(MB):
            own, from_x, from_y = spot(m, pc.p), spot(m, self.x), spot(m, self.y)
            (a, _), (_, b), (here_a, here_b) = self.halves(from_x), self.halves(from_y), self.halves(spot(m, self.d))
            self.first.append(
                [
                    Move(own, own, send.at[m, 0], recv.at[m, 0], self.to_x, from_x, recv.at[m, 0]),
                    Move(own, own, send.at[m, 1], recv.at[m, 1], self.to_y, from_y, recv.at[m, 1]),
                ]
            )
            self.second.append(
                [
                    Move(a, a, send.at[m, 2], recv.at[m, 2], self.to_y, here_a, recv.at[m, 2]),
                    Move(b, b, send.at[m, 3], recv.at[m, 3], self.to_x, here_b, recv.at[m, 3]),
                ]
            )

    def start(self, m):
        for move in self.first[m]:
            move.start()

    def relay(self, m):
        for arrived, move in zip(self.first[m], self.second[m]):
            arrived.wait_recv()
            move.start()

    def wait_recv(self, m):
        for move in self.second[m]:
            move.wait_recv()


class PlaneScatter(Plane):
    @staticmethod
    def sems(pc):
        return [DMA((MB, 6)), DMA((MB, 6))]

    def __init__(self, pc, sent, got, sems):
        super().__init__(pc)
        send, recv = sems
        self.first, self.second, self.adds = [], [], []
        for m in range(MB):

            def move(i, src, dst, dev, landing):
                return Move(src, dst, send.at[m, i], recv.at[m, i], dev, landing, recv.at[m, i])

            for_x, for_y, for_d = (self.halves(sent.at[m, q]) for q in (self.x, self.y, self.d))
            hop = self.halves(got.at[pc.p, m])
            hop_x, hop_y = self.halves(got.at[self.x, m]), self.halves(got.at[self.y, m])
            mine = hop
            self.first.append(
                [
                    move(0, for_d[0], hop_x[0], self.to_x, hop[0]),
                    move(1, for_d[1], hop_y[1], self.to_y, hop[1]),
                    move(2, for_x[0], mine[0], self.to_x, hop_x[0]),
                    move(3, for_y[1], mine[1], self.to_y, hop_y[1]),
                ]
            )
            self.second.append(
                [
                    move(5, for_y[0], mine[0], self.to_y, hop_y[0]),
                    move(4, for_x[1], mine[1], self.to_x, hop_x[1]),
                ]
            )
            self.adds.append([(for_y[0], hop[0]), (for_x[1], hop[1])])

    def start(self, m):
        for move in self.first[m]:
            move.start()

    def relay(self, m):
        for arrived, (target, term), move in zip(self.first[m], self.adds[m], self.second[m]):
            arrived.wait_recv()
            add_into(target, term, target.shape[0])
            move.start()

    def wait_recv(self, m):
        for move in self.first[m][2:] + self.second[m]:
            move.wait_recv()


def plane_sum(pc, sent, got, m, at):
    total = sent[m, pc.p, at, :].astype(F32)
    for q in (pc.p + 1 - 2 * (pc.p % 2), (pc.p + 2) % 4):
        total = total + got[q, m, at, :].astype(F32)
    return total


def greet(pc):
    barrier = pltpu.get_barrier_semaphore()

    def step(i, carry):
        dev = pc.flat((pc.me + i) % pc.n_dev)
        pl.semaphore_signal(barrier, inc=1, device_id=dev, device_id_type=MESH)
        return carry

    lax.fori_loop(1, pc.n_dev, step, 0)
    pl.semaphore_wait(barrier, pc.n_dev - 1)


def fused(collective_id, kernel, near_ins, far_ins, outs, scratch):
    ins_leaves, ins_tree = jax.tree.flatten((near_ins, far_ins))
    outs_leaves, outs_tree = jax.tree.flatten(outs)
    scratch_leaves, scratch_tree = jax.tree.flatten(scratch)
    a, b = len(ins_leaves), len(outs_leaves)
    near = len(jax.tree.leaves(near_ins))

    def run(*refs):
        first, second = jax.tree.unflatten(ins_tree, refs[:a])
        third = jax.tree.unflatten(outs_tree, refs[a : a + b])
        fourth = jax.tree.unflatten(scratch_tree, refs[a + b :])
        kernel(
            Place(),
            types.SimpleNamespace(**first),
            types.SimpleNamespace(**second),
            types.SimpleNamespace(**third),
            types.SimpleNamespace(**fourth),
        )

    got = pl.pallas_call(
        run,
        out_shape=tuple(outs_leaves),
        in_specs=[pl.BlockSpec(memory_space=VM if i < near else pl.ANY) for i in range(a)],
        out_specs=tuple([pl.BlockSpec(memory_space=pl.ANY)] * b),
        scratch_shapes=scratch_leaves,
        compiler_params=pltpu.CompilerParams(
            collective_id=collective_id, has_side_effects=True, vmem_limit_bytes=VMEM_LIMIT
        ),
    )(*ins_leaves)
    return types.SimpleNamespace(**jax.tree.unflatten(outs_tree, got))


def dot_nt(a, b):
    return lax.dot_general(a, b, (((1,), (1,)), ((), ())), preferred_element_type=F32)


def dot_tn(a, b):
    return lax.dot_general(a, b, (((0,), (0,)), ((), ())), preferred_element_type=F32)


def dot_nn(a, b):
    return lax.dot_general(a, b, (((1,), (0,)), ((), ())), preferred_element_type=F32)


def half_means(x):
    a = lax.broadcasted_iota(jnp.int32, (LANES, LANES), 0) // HEAD_DIM
    b = lax.broadcasted_iota(jnp.int32, (LANES, LANES), 1) // HEAD_DIM
    same = jnp.where(a == b, 1.0 / HEAD_DIM, 0.0).astype(F32)
    return lax.dot_general(x, same, (((1,), (0,)), ((), ())), precision=lax.Precision.HIGHEST, preferred_element_type=F32)


def swap_halves(x):
    return pltpu.roll(x, HEAD_DIM, 1)


def low_lanes(shape):
    return lax.broadcasted_iota(jnp.int32, shape, len(shape) - 1) < HEAD_DIM


def row_mean(x):
    return jnp.mean(x, axis=-1, keepdims=True)


def inv_rms(x):
    return lax.rsqrt(row_mean(x * x) + EPSILON)


def tile_of(j):
    return slice(j * LANES, (j + 1) * LANES)


def rows_loop(count, fn):
    def step(i, carry):
        fn(pl.ds(pl.multiple_of(i * ROW_STEP, ROW_STEP), ROW_STEP))
        return carry

    lax.fori_loop(0, count // ROW_STEP, step, 0)


def chunks(count, fn):
    def step(c, carry):
        fn(pl.ds(pl.multiple_of(c * CHUNK, CHUNK), CHUNK))
        return carry

    lax.fori_loop(0, count // CHUNK, step, 0)


def take_rows(hot, arrived, put):
    def block(at):
        x = arrived[:, :, at].astype(F32).reshape(-1, CHUNK).astype(BF)
        put(at, dot_nn(hot[...], x))

    chunks(arrived.shape[2], block)


def give_rows(hot, rows, out):
    def block(at):
        y = dot_tn(hot[...], rows(at))
        out[:, :, at] = y.reshape(out.shape[0], PAD, CHUNK).astype(BF)

    chunks(out.shape[2], block)


def fill_mask(bias, segq, segk):
    seq = bias.shape[0]
    rows = lax.broadcasted_iota(jnp.int32, (seq, seq), 0)
    cols = lax.broadcasted_iota(jnp.int32, (seq, seq), 1)
    bias[...] = jnp.where((segq == segk) & (cols <= rows), 0.0, MASKED)


def forward(pc, tok_sent, cot_sent, wqk, wvo, wup, wgate, wdown, small, hot, rattn, rmlp, segq, segk):
    n_dev, _, width = tok_sent.shape
    part = hot.shape[0] // MB
    seq = part * pc.n_p
    qk_cols, vo_cols, hid = wqk.shape[1], wvo.shape[1], wup.shape[1]
    o_cols = QUADS + LANES
    tiles = hid // LANES
    blocks = (MB, pc.n_p, part, width)
    kept = dict(
        hb=(blocks, BF),
        qk=((MB, seq, qk_cols), F32),
        qkb=((MB, seq, qk_cols), BF),
        vb=((MB, seq, o_cols), BF),
        ob=((MB, seq, o_cols), BF),
        lse=((MB, seq, LANES), F32),
        tok=((MB, part, width), BF),
        a=((MB, part, width), F32),
        h1=((MB, part, width), F32),
        c=((MB, part, width), F32),
        hb1=(blocks, BF),
        u=((MB, seq, hid), BF),
        g=((MB, seq, hid), BF),
        mb=((MB, seq, hid), BF),
        h2=((MB, part, width), BF),
    )
    whole = dict(
        wqk=((width, qk_cols), BF),
        wvo=((width, vo_cols), BF),
        wup=((width, hid), BF),
        wgate=((width, hid), BF),
        wdown=((width, hid), BF),
        sup=((1, hid), F32),
        sgate=((1, hid), F32),
        sqk=((1, qk_cols), F32),
    )
    outs = {n: SDS(*x) for n, x in (kept | whole).items()} | dict(cot=SDS(cot_sent.shape, BF))
    scratch = {n: VM(*x) for n, x in (kept | whole).items()} | dict(
        arrived=VM(tok_sent.shape, BF),
        aqk=VM((pc.n_t,) + wqk.shape, BF),
        avo=VM((pc.n_t,) + wvo.shape, BF),
        small=VM((pc.n_t,) + small.shape, F32),
        bias=VM((seq, seq), F32),
        sent=VM(blocks, BF),
        got=VM((pc.n_p, MB, part, width), BF),
        kept_sem={n: DMA((MB,)) for n in kept},
        whole_sem={n: DMA((1,)) for n in whole},
        tok_sem=Deal.sems(pc),
        cot_sem=Deal.sems(pc),
        small_sem=pair(pc.n_t) + [DMA((1,))],
        qk_sem=HeadWeights.sems(pc),
        vo_sem=HeadWeights.sems(pc),
        up_sem=HiddenWeights.sems(pc),
        gate_sem=HiddenWeights.sems(pc),
        down_sem=HiddenWeights.sems(pc),
        ag_sem=PlaneGather.sems(pc),
        ra_sem=PlaneScatter.sems(pc),
        ag1_sem=PlaneGather.sems(pc),
        rc_sem=PlaneScatter.sems(pc),
    )
    near_ins = dict(hot=hot, rattn=rattn, rmlp=rmlp, segq=segq, segk=segk)
    far_ins = dict(
        tok=tok_sent, cot=cot_sent, wqk=wqk, wvo=wvo, wup=wup, wgate=wgate, wdown=wdown, small=small
    )

    def kernel(pc, v, x, o, k):
        own_p = pc.p
        greet(pc)
        deal = Deal(pc, x.tok, k.arrived, k.tok_sem)
        deal_cot = Deal(pc, x.cot, o.cot, k.cot_sem)
        head_qk = HeadWeights(pc, x.wqk, k.aqk, k.wqk, k.qk_sem)
        head_vo = HeadWeights(pc, x.wvo, k.avo, k.wvo, k.vo_sem)
        up = HiddenWeights(pc, x.wup, k.wup, k.up_sem)
        gate = HiddenWeights(pc, x.wgate, k.wgate, k.gate_sem)
        down = HiddenWeights(pc, x.wdown, k.wdown, k.down_sem)
        ss, rs, ls = k.small_sem
        scales = Moves(
            [
                Move(
                    x.small, k.small.at[pc.t], ss.at[q], rs.at[pc.t], pc.dev(pc.p, pc.r, q), k.small.at[q], rs.at[q]
                )
                for q in others(pc.n_t, pc.t)
            ]
        )
        own_scales = pltpu.make_async_copy(x.small, k.small.at[pc.t], ls.at[0])

        def gather(buf, sems):
            return PlaneGather(pc, lambda m, q: buf.at[m, q], sems)

        ag, ag1 = gather(k.hb, k.ag_sem), gather(k.hb1, k.ag1_sem)
        ra, rc = (PlaneScatter(pc, k.sent, k.got, sems) for sems in (k.ra_sem, k.rc_sem))
        names = vars(k)
        out_names = vars(o)
        copies = []

        def keep(m, *refs):
            for n in kept:
                if any(names[n] is ref for ref in refs):
                    copy = pltpu.make_async_copy(names[n].at[m], out_names[n].at[m], k.kept_sem[n].at[m])
                    copy.start()
                    copies.append(copy)

        def keep_whole(*refs):
            for n in whole:
                if any(names[n] is ref for ref in refs):
                    copy = pltpu.make_async_copy(names[n], out_names[n], k.whole_sem[n].at[0])
                    copy.start()
                    copies.append(copy)

        def attend(m):
            fill_mask(k.bias, v.segq[m], v.segk[m])
            ag.wait_recv(m)
            keep(m, k.hb)

            def project(i, carry):
                rows = k.hb[m, pl.ds(2 * i, 2)].reshape(2 * part, width)
                at = pl.ds(pl.multiple_of(i * 2 * part, 2 * part), 2 * part)
                qk = dot_nn(rows, k.wqk[...])
                k.qk[m, at, :] = qk
                for j in range(qk_cols // LANES):
                    s = qk[:, tile_of(j)]
                    n = s * lax.rsqrt(half_means(s * s) + EPSILON)
                    k.qkb[m, at, tile_of(j)] = (n * k.sqk[:, tile_of(j)]).astype(BF)
                k.vb[m, at, :QUADS] = dot_nn(rows, k.wvo[:, :QUADS]).astype(BF)
                last = dot_nn(rows, k.wvo[:, 2 * QUADS :])
                k.vb[m, at, QUADS:] = jnp.where(low_lanes(last.shape), last, 0.0).astype(BF)
                return carry

            lax.fori_loop(0, pc.n_p // 2, project, 0)
            keep(m, k.qk, k.qkb, k.vb)
            if m == 1:
                ra.relay(0)
            blk = seq // 2
            for i in range(2):
                nk = (i + 1) * blk
                at = slice(i * blk, nk)
                bias = k.bias[at, :nk]
                lse = jnp.zeros((blk, LANES), F32)
                lane = lax.broadcasted_iota(jnp.int32, (blk, LANES), 1)
                for slab in range(3):
                    if slab < 2:
                        qs = k.qkb[m, at, tile_of(slab)]
                        ks = k.qkb[m, :nk, tile_of(2 + slab)]
                    else:
                        qs = k.qkb[m, at, 2 * QUADS :]
                        ks = swap_halves(k.qkb[m, :nk, 2 * QUADS :].astype(F32)).astype(BF)
                    vs = k.vb[m, :nk, tile_of(slab)]
                    res = []
                    for half in range(2 if slab < 2 else 1):
                        low = low_lanes(qs.shape)
                        q1 = jnp.where(low if half == 0 else jnp.logical_not(low), qs, jnp.zeros_like(qs))
                        s = dot_nt(q1, ks) * HEAD_DIM ** (-0.5) + bias
                        top = jnp.max(s, axis=1, keepdims=True)
                        e = jnp.exp(s - top)
                        tot = jnp.sum(e, axis=1, keepdims=True)
                        lse = jnp.where(lane == 2 * slab + half, top + jnp.log(tot), lse)
                        res.append(dot_nn((e * (1.0 / tot)).astype(BF), vs))
                    if slab < 2:
                        res = jnp.where(low_lanes(res[0].shape), res[0], res[1])
                    else:
                        res = swap_halves(res[0])
                    k.ob[m, at, tile_of(slab)] = res.astype(BF)
                k.lse[m, at, :] = lse
            keep(m, k.ob, k.lse)
            if m == 0:
                ag.relay(1)

            def branch(i, carry):
                at = pl.ds(pl.multiple_of(i * 2 * part, 2 * part), 2 * part)
                y = dot_nt(k.ob[m, at, :], k.wvo[:, QUADS:])
                k.sent[m, pl.ds(2 * i, 2)] = y.astype(BF).reshape(2, part, width)
                return carry

            lax.fori_loop(0, pc.n_p // 2, branch, 0)
            ra.start(m)

        def summed(m, at):
            return plane_sum(pc, k.sent, k.got, m, at)

        def middle(m):
            ra.wait_recv(m)

            def rows(at):
                a = summed(m, at)
                h = k.tok[m, at, :].astype(F32)
                y = h + v.rattn[...] * (a * inv_rms(a) - h)
                h1 = y * inv_rms(y)
                k.a[m, at, :] = a
                k.h1[m, at, :] = h1
                k.hb1[m, own_p, at, :] = h1.astype(BF)

            rows_loop(part, rows)
            ag1.start(m)
            keep(m, k.a, k.h1)

        def feed(m):
            ag1.wait_recv(m)
            keep(m, k.hb1)

            def hidden(at):
                rows = k.hb1[m].reshape(seq, width)
                u = dot_nn(rows, k.wup[:, at])
                g = dot_nn(rows, k.wgate[:, at])
                k.u[m, :, at] = u.astype(BF)
                k.g[m, :, at] = g.astype(BF)
                z = k.sgate[:, at] * g
                k.mb[m, :, at] = (z / (1.0 + jnp.exp(-z)) * (k.sup[:, at] * u)).astype(BF)

            chunks(hid, hidden)
            keep(m, k.u, k.g, k.mb)

        def shrink(m):
            ra.wait_send(m)

            def columns(at):
                y = dot_nt(k.mb[m], k.wdown[at, :])
                k.sent[m, :, :, at] = y.astype(BF).reshape(pc.n_p, part, CHUNK)

            chunks(width, columns)
            rc.start(m)

        def finish(m):
            rc.wait_recv(m)

            def rows(at):
                c = summed(m, at)
                h1 = k.h1[m, at, :]
                z = h1 + v.rmlp[...] * (c * inv_rms(c) - h1)
                k.c[m, at, :] = c
                k.h2[m, at, :] = (z * inv_rms(z)).astype(BF)

            rows_loop(part, rows)
            keep(m, k.c, k.h2)

        deal.start()
        head_qk.start()
        head_vo.start()
        scales.start()
        own_scales.start()
        for w in (up, gate, down):
            w.start()
        head_qk.relay()
        head_vo.relay()
        deal.wait_recv()

        def put(at, y):
            for m in range(MB):
                rows = y[m * part : (m + 1) * part].astype(BF)
                k.tok[m, :, at] = rows
                k.hb[m, own_p, :, at] = rows

        take_rows(v.hot, k.arrived, put)
        for m in range(MB):
            ag.start(m)
            keep(m, k.tok)
        head_qk.plane()
        head_vo.plane()
        up.tall()
        gate.tall()
        own_scales.wait()
        scales.wait_recv()
        for t in range(pc.n_t):
            for j in range(3):

                def move(t=t, j=j):
                    at = lanes(dst_tile(pc.p, t) + j, 1)
                    k.sup[:, at] = k.small[t, pl.ds(src_tile(pc.p, t) + j, 1), :]
                    k.sgate[:, at] = k.small[t, pl.ds(tiles + src_tile(pc.p, t) + j, 1), :]

                Move.under(width3(pc.p, t) if j == 2 else None, move)
        for j in range(qk_cols // LANES):
            k.sqk[:, tile_of(j)] = k.small[own_p, 2 * tiles + j : 2 * tiles + j + 1, :]
        keep_whole(k.sup, k.sgate, k.sqk)
        head_qk.near()
        head_vo.near()
        head_qk.wait_recv()
        head_vo.wait_recv()
        keep_whole(k.wqk, k.wvo)
        ag.relay(0)
        attend(0)
        down.tall()
        attend(1)
        up.relay()
        gate.relay()
        middle(0)
        ra.relay(1)
        middle(1)
        ag1.relay(0)
        up.near()
        gate.near()
        ag1.relay(1)
        up.wait_recv()
        gate.wait_recv()
        down.relay()
        feed(0)
        keep_whole(k.wup, k.wgate)
        feed(1)
        down.near()
        down.wait_recv()
        deal_cot.start()
        shrink(0)
        rc.relay(0)
        keep_whole(k.wdown)
        shrink(1)
        rc.relay(1)
        for m in range(MB):
            finish(m)
        deal_cot.wait_recv()
        for w in (deal, deal_cot, head_qk, head_vo, up, gate, down, scales):
            w.wait_send()
        for m in range(MB):
            for w in (ag, ag1, rc):
                w.wait_send(m)
        for copy in copies:
            copy.wait()

    return fused(1, kernel, near_ins, far_ins, outs, scratch)


def backward(pc, f, hot, rattn, rmlp, segq, segk):
    n_dev = f.cot.shape[0]
    part, width = f.h2.shape[1], f.h2.shape[2]
    seq = part * pc.n_p
    all_tok = MB * seq
    qk_cols, hid = f.wqk.shape[1], f.wup.shape[1]
    o_cols = QUADS + LANES
    tiles = hid // LANES
    n_rows = width // (pc.n_p * pc.n_r)
    step_rows = n_rows // 5
    if n_rows % 5 or hid != width:
        raise ValueError("sizes")
    blocks = (MB, pc.n_p, part, width)
    dealt = (n_dev, PAD, width)
    vec_rows = 4 * tiles
    vec_total = -(-(2 * vec_rows + 2 * tiles + pc.n_p * qk_cols // LANES) // PAD) * PAD
    heads_shape = (pc.n_p, n_rows, qk_cols)
    outs = dict(
        back_out=SDS(dealt, BF),
        back_grad=SDS(dealt, BF),
        vec=SDS((vec_total, LANES), F32),
        relay=[SDS((pc.n_p, n_rows, 3 * LANES), BF) for _ in range(3)],
        head_relay=[SDS((n_rows, qk_cols), BF) for _ in range(2)],
        tall=[SDS((pc.n_t, pc.n_p, n_rows, 3 * LANES), BF) for _ in range(3)],
        final=[SDS((n_rows, hid), BF) for _ in range(3)],
        head_p=[SDS(heads_shape, BF) for _ in range(2)],
        head_t=[SDS(heads_shape, BF) for _ in range(2)],
    )
    loaded = dict(
        c=f.c,
        h1=f.h1,
        wdown=f.wdown,
        u=f.u,
        g=f.g,
        sup=f.sup,
        sgate=f.sgate,
        wup=f.wup,
        wgate=f.wgate,
        mb=f.mb,
        hb1=f.hb1,
        tok=f.tok,
        wvo=f.wvo,
        vb=f.vb,
        qkb=f.qkb,
        lse=f.lse,
        qk=f.qk,
        sqk=f.sqk,
        wqk=f.wqk,
        ob=f.ob,
    )
    later = dict(a=f.a, hb=f.hb, cot=f.cot, h2=f.h2)
    sums = dict(gsup=hid, gsgate=hid, gsqk=qk_cols, grattn=width, grmlp=width)
    scratch = {n: VM(y.shape, y.dtype) for n, y in loaded.items()} | {n: VM((1, y), F32) for n, y in sums.items()}
    scratch |= dict(
        load_sem={n: DMA((1,)) for n in loaded},
        later_sem=[DMA((1,)) for _ in later],
        dcb=VM(blocks, BF),
        dab=VM(blocks, BF),
        mid=VM((MB, part, width), F32),
        bias=VM((seq, seq), F32),
        sent=VM(blocks, BF),
        got=VM((pc.n_p, MB, part, width), BF),
        tbuf=VM((pc.n_t, pc.n_p, n_rows, 3 * LANES), BF),
        dealbuf=VM(dealt, BF),
        vec=VM((vec_total, LANES), F32),
        vec_got=[VM((y, vec_total, LANES), F32) for y in (pc.n_r, pc.n_t, pc.n_p)],
        rbuf=VM((pc.n_p, n_rows, 3 * LANES), BF),
        hbuf=[VM((2, n_rows, qk_cols), BF) for _ in range(2)],
        near=[VM((pc.n_r - 1, pc.n_p, n_rows, y), BF) for y in (hid, hid, hid, qk_cols, qk_cols)],
        near_sem=[pair(pc.n_r) for _ in range(5)],
        tall_sem=[[DMA((2, pc.n_t)) for _ in range(3)] for _ in range(3)],
        plane_sem=[[DMA((2, pc.n_p)) for _ in range(2)] for _ in range(5)],
        relay_sem=[[DMA((2,)) for _ in range(5)] for _ in range(3)],
        head_sem=[pair(pc.n_t) + [DMA((1,))] for _ in range(2)],
        head_relay_sem=[[DMA((1,)) for _ in range(5)] for _ in range(2)],
        out_sem=Deal.sems(pc),
        grad_sem=Deal.sems(pc),
        vec_sem=[pair(y) for y in (pc.n_r, pc.n_t, pc.n_p)],
        vec_out=DMA((1,)),
        ag_sem=PlaneGather.sems(pc),
        ag1_sem=PlaneGather.sems(pc),
        rh1_sem=PlaneScatter.sems(pc),
        rh_sem=PlaneScatter.sems(pc),
    )
    near_ins = dict(hot=hot, rattn=rattn, rmlp=rmlp, segq=segq, segk=segk)

    def kernel(pc, v, x, o, k):
        own_p = pc.p
        refs = vars(k)
        sources = vars(x)
        loads = {n: pltpu.make_async_copy(sources[n], refs[n], k.load_sem[n].at[0]) for n in loaded}
        for n in loaded:
            loads[n].start()
        cot_load = pltpu.make_async_copy(x.cot, k.dealbuf, k.later_sem[2].at[0])
        h2_load = pltpu.make_async_copy(x.h2, k.dab.at[:, own_p], k.later_sem[3].at[0])
        cot_load.start()
        h2_load.start()
        k_dqk, k_dv = k.u.at[:, :, pl.ds(0, qk_cols)], k.u.at[:, :, pl.ds(qk_cols, o_cols)]
        k_do = k.g.at[0, :, pl.ds(0, o_cols)]
        a_load = pltpu.make_async_copy(x.a, k.c, k.later_sem[0].at[0])
        hb_load = pltpu.make_async_copy(x.hb.reshape(MB, seq, width), k.mb, k.later_sem[1].at[0])
        waited = set()

        def ready(*wanted):
            for n in loaded:
                if n not in waited and any(refs[n] is ref for ref in wanted):
                    waited.add(n)
                    loads[n].wait()

        for n in sums:
            refs[n][...] = jnp.zeros(refs[n].shape, F32)
        k.vec[...] = jnp.zeros(k.vec.shape, F32)
        greet(pc)

        ag, ag1 = (
            PlaneGather(pc, lambda m, q, buf=buf: buf.at[m, q], sems)
            for buf, sems in ((k.dcb, k.ag_sem), (k.dab, k.ag1_sem))
        )
        rh1, rh = (PlaneScatter(pc, k.sent, k.got, sems) for sems in (k.rh1_sem, k.rh_sem))
        deal_out = Deal(pc, k.dealbuf, o.back_out, k.out_sem)
        deal_grad = Deal(pc, k.dealbuf, o.back_grad, k.grad_sem)

        def add_rows(ref, y, at=slice(None)):
            ref[:, at] += jnp.sum(y, axis=0, keepdims=True)

        def top(m):
            def rows(at):
                c, h1, ct = k.c[m, at, :], k.h1[m, at, :], k.mid[m, at, :]
                r_c = inv_rms(c)
                n_c = c * r_c
                z = h1 + v.rmlp[...] * (n_c - h1)
                r_z = inv_rms(z)
                h2 = z * r_z
                dz = r_z * (ct - h2 * row_mean(ct * h2))
                add_rows(k.grmlp, dz * (n_c - h1))
                k.mid[m, at, :] = (1.0 - v.rmlp[...]) * dz
                dn = v.rmlp[...] * dz
                k.dcb[m, own_p, at, :] = (r_c * (dn - n_c * row_mean(dn * n_c))).astype(BF)

            rows_loop(part, rows)
            ag.start(m)

        def summed(m, at):
            return plane_sum(pc, k.sent, k.got, m, at)

        def feed(m):
            ag.wait_recv(m)

            def hidden(at):
                dm = dot_nn(k.dcb[m].reshape(seq, width), k.wdown[:, at])
                u, g = k.u[m, :, at].astype(F32), k.g[m, :, at].astype(F32)
                y = k.sgate[:, at] * g
                sig = 1.0 / (1.0 + jnp.exp(-y))
                du = dm * (y * sig)
                dx = dm * (k.sup[:, at] * u) * (sig * (1.0 + y * (1.0 - sig)))
                add_rows(k.gsup, du * u, at)
                add_rows(k.gsgate, dx * g, at)
                k.u[m, :, at] = (k.sup[:, at] * du).astype(BF)
                k.g[m, :, at] = (k.sgate[:, at] * dx).astype(BF)

            chunks(hid, hidden)

        def shrink(m):
            def columns(at):
                y = dot_nt(k.u[m], k.wup[at, :]) + dot_nt(k.g[m], k.wgate[at, :])
                k.sent[m, :, :, at] = y.astype(BF).reshape(pc.n_p, part, CHUNK)

            chunks(width, columns)
            rh1.start(m)

        grads = [k.wdown, k.wup, k.wgate, k.wqk, k.wvo]

        def near_slot(source, at):
            return (source - at + pc.n_r - 1) % pc.n_r

        def near_moves(i):
            send, recv = k.near_sem[i]
            return Moves(
                [
                    Move(
                        by_shard(pc, grads[i]).at[:, q], k.near[i].at[near_slot(pc.r, q)], send.at[q], recv.at[pc.r],
                        pc.dev(pc.p, q, pc.t), k.near[i].at[near_slot(q, pc.r)], recv.at[q],
                    )
                    for q in others(pc.n_r, pc.r)
                ]
            )

        near = [near_moves(i) for i in range(5)]

        def row_blocks(fn):
            def block(i, carry):
                fn(i // 5, pl.ds(pl.multiple_of((i % 5) * step_rows, step_rows), step_rows))
                return carry

            lax.fori_loop(0, pc.n_p * 5, block, 0)

        def near_sum(i):
            near[i].wait_recv()
            own = by_shard(pc, grads[i])

            def block(p, at):
                total = own[p, pc.r, at, :].astype(F32)
                for j in range(pc.n_r - 1):
                    total = total + k.near[i][j, p, at, :].astype(F32)
                k.near[i][0, p, at, :] = total.astype(BF)

            row_blocks(block)

        t = pc.t
        middle_dev = (t == 1) | (t == 2)
        end_dev = jnp.logical_not(middle_dev)
        far = jnp.where((t == 2) | (t == 3), 0, 3)
        by = jnp.where(t == 0, 1, 2)
        wide = width3(pc.p, t)
        wide_far = width3(pc.p, far)

        def direct_out(q):
            return (jnp.abs(q - t) != 3) & jnp.logical_not(middle_dev & (q == far))

        def comes(q):
            return jnp.abs(q - t) != 3

        def tall_moves(i):
            send, recv, _ = k.tall_sem[i]
            src, y = k.near[i].at[0], o.tall[i]
            moves = []
            for q in others(pc.n_t, t):
                there = dst_tile(pc.p, q)
                dev = pc.dev(pc.p, pc.r, q)
                moves.append(
                    Move(
                        src.at[:, :, lanes(there, 2)], y.at[t, :, :, TWO], send.at[0, q], recv.at[0, t], dev,
                        y.at[q, :, :, TWO], recv.at[0, q], direct_out(q), comes(q),
                    )
                )
                moves.append(
                    Move(
                        src.at[:, :, lanes(there + 2, 1)], y.at[t, :, :, ONE], send.at[1, q], recv.at[1, t], dev,
                        y.at[q, :, :, ONE], recv.at[1, q], direct_out(q) & width3(pc.p, q), comes(q) & wide,
                    )
                )
            return Moves(moves)

        def far_parts(i):
            at = dst_tile(pc.p, far)
            return ((TWO, lanes(at, 2), None), (ONE, lanes(at + 2, 1), wide_far))

        def both(a, b):
            return a if b is None else a & b

        def handed_moves(i):
            s1, r1, _, _, _ = k.relay_sem[i]
            src, y = k.near[i].at[0], o.relay[i]
            return Moves(
                [
                    Move(
                        src.at[:, :, at], y.at[:, :, w], s1.at[j], r1.at[j], pc.dev(pc.p, pc.r, by), y.at[:, :, w],
                        r1.at[j], both(end_dev, cond), both(middle_dev, cond),
                    )
                    for j, (w, at, cond) in enumerate(far_parts(i))
                ]
            )

        def passed_moves(i):
            _, _, s2, _, _ = k.relay_sem[i]
            recv = k.tall_sem[i][1]
            return Moves(
                [
                    Move(
                        k.rbuf.at[:, :, w], o.tall[i].at[t, :, :, w], s2.at[j], recv.at[j, t], pc.dev(pc.p, pc.r, far),
                        None, None, both(middle_dev, cond),
                    )
                    for j, (w, at, cond) in enumerate(far_parts(i))
                ]
            )

        tall = [tall_moves(i) for i in range(3)]
        handed = [handed_moves(i) for i in range(3)]
        passed = [passed_moves(i) for i in range(3)]

        def tall_start(i):
            handed[i].start()
            tall[i].start()

        def tall_relay(i):
            handed[i].wait_recv()

            @pl.when(middle_dev)
            def _():
                copy = pltpu.make_async_copy(o.relay[i], k.rbuf, k.relay_sem[i][3].at[0])
                copy.start()
                copy.wait()

                def add(w, at):
                    def block(p, rows):
                        total = k.rbuf[p, rows, w].astype(F32) + k.near[i][0, p, rows, at].astype(F32)
                        k.rbuf[p, rows, w] = total.astype(BF)

                    row_blocks(block)

                for w, at, cond in far_parts(i):
                    Move.under(cond, lambda w=w, at=at: add(w, at))

            passed[i].start()

        def tall_sum(i):
            tall[i].wait_recv()
            local = []
            for q in others(pc.n_t, t):
                for j, (w, cond) in enumerate(((TWO, comes(q)), (ONE, comes(q) & wide))):
                    copy = pltpu.make_async_copy(
                        o.tall[i].at[q, :, :, w], k.tbuf.at[q, :, :, w], k.tall_sem[i][2].at[j, q]
                    )
                    Move.under(cond, copy.start)
                    local.append((cond, copy))
            for cond, copy in local:
                Move.under(cond, copy.wait)
            here = dst_tile(pc.p, t)

            def add(source, target):
                def block(p, at):
                    total = k.near[i][0, p, at, source].astype(F32)
                    for q in others(pc.n_t, t):
                        total = total + jnp.where(comes(q), k.tbuf[q, p, at, target].astype(F32), 0.0)
                    k.tbuf[t, p, at, target] = total.astype(BF)

                row_blocks(block)

            add(lanes(here, 2), TWO)
            pl.when(wide)(lambda: add(lanes(here + 2, 1), ONE))

        def plane_moves(i):
            send, recv = k.plane_sem[i]
            y, src = o.final[i], k.tbuf.at[pc.t]
            here = src_tile(pc.p, pc.t)
            moves = []
            for q in others(pc.n_p, pc.p):
                there = src_tile(q, pc.t)
                dev = pc.dev(q, pc.r, pc.t)
                moves.append(
                    Move(
                        src.at[q, :, TWO], y.at[:, lanes(here, 2)], send.at[0, q], recv.at[0, pc.p], dev,
                        y.at[:, lanes(there, 2)], recv.at[0, q],
                    )
                )
                moves.append(
                    Move(
                        src.at[q, :, ONE], y.at[:, lanes(here + 2, 1)], send.at[1, q], recv.at[1, pc.p], dev,
                        y.at[:, lanes(there + 2, 1)], recv.at[1, q], wide, width3(q, pc.t),
                    )
                )
            own = (
                (None, pltpu.make_async_copy(src.at[own_p, :, TWO], y.at[:, lanes(here, 2)], send.at[0, pc.p])),
                (wide, pltpu.make_async_copy(src.at[own_p, :, ONE], y.at[:, lanes(here + 2, 1)], send.at[1, pc.p])),
            )
            return Moves(moves), own

        plane = [plane_moves(i) for i in range(3)]

        def plane_start(i):
            moves, own = plane[i]
            moves.start()
            for cond, copy in own:
                Move.under(cond, copy.start)

        def plane_sent(i):
            moves, own = plane[i]
            moves.wait_send()
            for cond, copy in own:
                Move.under(cond, copy.wait)

        def head_planes(i):
            send, recv = k.plane_sem[3 + i]
            src, y = k.near[3 + i].at[0], o.head_p[i]
            return Moves(
                [
                    Move(
                        src.at[q], y.at[pc.p], send.at[0, q], recv.at[0, pc.p], pc.dev(q, pc.r, pc.t), y.at[q],
                        recv.at[0, q],
                    )
                    for q in others(pc.n_p, pc.p)
                ]
            )

        def head_talls(i):
            send, recv, _ = k.head_sem[i]
            src, y = o.head_p[i], o.head_t[i]
            return Moves(
                [
                    Move(
                        src.at[q], y.at[t], send.at[q], recv.at[t], pc.dev(pc.p, pc.r, q), y.at[q], recv.at[q],
                        direct_out(q), comes(q),
                    )
                    for q in others(pc.n_t, t)
                ]
            )

        def head_handed(i):
            s1, r1, _, _, _ = k.head_relay_sem[i]
            y = o.head_relay[i]
            return Move(
                o.head_p[i].at[far], y, s1.at[0], r1.at[0], pc.dev(pc.p, pc.r, by), y, r1.at[0], end_dev, middle_dev
            )

        def head_passed(i):
            _, _, s2, _, _ = k.head_relay_sem[i]
            recv = k.head_sem[i][1]
            return Move(
                k.hbuf[i].at[0], o.head_t[i].at[t], s2.at[0], recv.at[t], pc.dev(pc.p, pc.r, far), None, None, middle_dev
            )

        head_first = [head_handed(i) for i in range(2)]
        head_last = [head_passed(i) for i in range(2)]

        def head_start(i):
            head_first[i].start()
            head_tall[i].start()

        def head_relay(i):
            head_first[i].wait_recv()

            @pl.when(middle_dev)
            def _():
                copies = [
                    pltpu.make_async_copy(o.head_relay[i], k.hbuf[i].at[0], k.head_relay_sem[i][3].at[0]),
                    pltpu.make_async_copy(o.head_p[i].at[far], k.hbuf[i].at[1], k.head_relay_sem[i][4].at[0]),
                ]
                for copy in copies:
                    copy.start()
                for copy in copies:
                    copy.wait()
                k.hbuf[i][0] = (k.hbuf[i][0].astype(F32) + k.hbuf[i][1].astype(F32)).astype(BF)

            head_last[i].start()

        head_plane = [head_planes(i) for i in range(2)]
        head_tall = [head_talls(i) for i in range(2)]
        head_own = [
            pltpu.make_async_copy(k.near[3 + i].at[0, own_p], o.head_p[i].at[pc.p], k.head_sem[i][2].at[0])
            for i in range(2)
        ]

        def middle(m):
            rh1.wait_recv(m)

            def rows(at):
                dh1 = k.mid[m, at, :] + summed(m, at)
                a, h = k.c[m, at, :], k.tok[m, at, :].astype(F32)
                r_a = inv_rms(a)
                n_a = a * r_a
                y = h + v.rattn[...] * (n_a - h)
                r_y = inv_rms(y)
                h1 = y * r_y
                dy = r_y * (dh1 - h1 * row_mean(dh1 * h1))
                add_rows(k.grattn, dy * (n_a - h))
                k.mid[m, at, :] = (1.0 - v.rattn[...]) * dy
                dn = v.rattn[...] * dy
                k.dab[m, own_p, at, :] = (r_a * (dn - n_a * row_mean(dn * n_a))).astype(BF)

            rows_loop(part, rows)
            ag1.start(m)

        def flat(ref, at=slice(None)):
            return ref[:, :, at].reshape(all_tok, -1)

        def columns_of(ref, at):
            return ref[:, :, :, at].reshape(all_tok, CHUNK)

        def weight_grad(target, left, right):
            def block(at):
                target[at, :] = dot_tn(columns_of(left, at), flat(right)).astype(BF)

            chunks(width, block)

        score = HEAD_DIM ** (-0.5)
        blk = seq // 2

        def attend(m):
            fill_mask(k.bias, v.segq[m], v.segk[m])
            ag1.wait_recv(m)

            def project(i, carry):
                rows = k.dab[m, pl.ds(2 * i, 2)].reshape(2 * part, width)
                at = pl.ds(pl.multiple_of(i * 2 * part, 2 * part), 2 * part)
                k_do[at, :] = dot_nn(rows, k.wvo[:, QUADS:]).astype(BF)
                return carry

            lax.fori_loop(0, pc.n_p // 2, project, 0)

            def norm_grad(tile, d):
                at = tile_of(tile)
                raw = k.qk[m, :, at]
                r = lax.rsqrt(half_means(raw * raw) + EPSILON)
                n = raw * r
                d = d * score
                add_rows(k.gsqk, d * n, at)
                dy = d * k.sqk[:, at]
                k_dqk[m, :, at] = (r * (dy - n * half_means(dy * n))).astype(BF)

            for slab in range(3):
                own = tile_of(slab)
                if slab < 2:
                    q_all = k.qkb[m, :, own]
                    k_all = k.qkb[m, :, tile_of(2 + slab)]
                    do_all = k_do[:, own]
                else:
                    q_all = k.qkb[m, :, 2 * QUADS :]
                    k_all = swap_halves(q_all.astype(F32)).astype(BF)
                    do_all = swap_halves(k_do[:, own].astype(F32)).astype(BF)
                v_all = k.vb[m, :, own]
                low = low_lanes((blk, LANES))
                dq, dk, dv = [], None, None
                for i in range(2):
                    nk = (i + 1) * blk
                    at = slice(i * blk, nk)
                    bias = k.bias[at, :nk]
                    dq_i = None
                    for half in range(2 if slab < 2 else 1):
                        here = low if half == 0 else jnp.logical_not(low)
                        zero = jnp.zeros((blk, LANES), BF)
                        q1, do1 = jnp.where(here, q_all[at], zero), jnp.where(here, do_all[at], zero)
                        lse = k.lse[m, at, 2 * slab + half : 2 * slab + half + 1]
                        prob = jnp.exp(dot_nt(q1, k_all[:nk]) * score + bias - lse)
                        dp = dot_nt(do1, v_all[:nk])
                        w = prob * dp
                        ds = (w - prob * jnp.sum(w, axis=1, keepdims=True)).astype(BF)
                        y = jnp.where(here, dot_nn(ds, k_all[:nk]), 0.0)
                        dq_i = y if dq_i is None else dq_i + y
                        dk_i, dv_i = dot_tn(ds, q1), dot_tn(prob.astype(BF), do1)
                        if i == 0:
                            dk = dk_i if dk is None else dk + dk_i
                            dv = dv_i if dv is None else dv + dv_i
                        else:
                            if half == 0:
                                dk = jnp.concatenate([dk, jnp.zeros((blk, LANES), F32)], axis=0)
                                dv = jnp.concatenate([dv, jnp.zeros((blk, LANES), F32)], axis=0)
                            dk, dv = dk + dk_i, dv + dv_i
                    dq.append(dq_i)
                dq = jnp.concatenate(dq, axis=0)
                k_dv[m, :, own] = dv.astype(BF)
                if slab < 2:
                    norm_grad(slab, dq)
                    norm_grad(2 + slab, dk)
                else:
                    norm_grad(4, dq + swap_halves(dk))
            if m == 0:
                ag1.relay(1)
            else:
                rh.relay(0)
            rh1.wait_send(m)

            def columns(at):
                y = dot_nt(k_dqk[m], k.wqk[at, :])
                y = y + dot_nt(k_dv[m, :, :QUADS], k.wvo[at, :QUADS])
                y = y + dot_nt(k_dv[m, :, QUADS:], k.wvo[at, 2 * QUADS :])
                k.sent[m, :, :, at] = y.astype(BF).reshape(pc.n_p, part, CHUNK)

            chunks(width, columns)
            rh.start(m)

        def heads_grad(at):
            hb, dab = flat(k.mb, at), columns_of(k.dab, at)
            quads = slice(0, QUADS)
            rest = slice(QUADS, None)
            k.wqk[at, :] = dot_tn(hb, flat(k_dqk)).astype(BF)
            k.wvo[at, :QUADS] = dot_tn(hb, flat(k_dv, quads)).astype(BF)
            k.wvo[at, QUADS : 2 * QUADS] = dot_tn(dab, flat(k.ob, quads)).astype(BF)
            k.wvo[at, 2 * QUADS :] = (dot_tn(hb, flat(k_dv, rest)) + dot_tn(dab, flat(k.ob, rest))).astype(BF)

        def bottom(m):
            rh.wait_recv(m)

            def rows(at):
                k.mid[m, at, :] = k.mid[m, at, :] + summed(m, at)

            rows_loop(part, rows)

        def collect():
            for t in range(pc.n_t):
                for j in range(3):

                    def move(t=t, j=j):
                        here = lanes(dst_tile(pc.p, t) + j, 1)
                        row = t * tiles + src_tile(pc.p, t) + j
                        k.vec[pl.ds(row, 1), :] = k.gsup[:, here]
                        k.vec[pl.ds(vec_rows + row, 1), :] = k.gsgate[:, here]

                    Move.under(width3(pc.p, t) if j == 2 else None, move)
            at = 2 * vec_rows
            for j in range(tiles):
                k.vec[at + j : at + j + 1, :] = k.grattn[:, tile_of(j)]
                k.vec[at + tiles + j : at + tiles + j + 1, :] = k.grmlp[:, tile_of(j)]
            count = qk_cols // LANES
            for j in range(count):
                k.vec[pl.ds(at + 2 * tiles + own_p * count + j, 1), :] = k.gsqk[:, tile_of(j)]

        def vec_stage(n, count, own, dev_of):
            send, recv = k.vec_sem[n]
            buf = k.vec_got[n]
            moves = Moves(
                [
                    Move(buf.at[own], buf.at[own], send.at[q], recv.at[own], dev_of(q), buf.at[q], recv.at[q])
                    for q in others(count, own)
                ]
            )

            def start():
                buf[own] = k.vec[...]
                moves.start()

            def finish():
                moves.wait_recv()
                total = buf[0]
                for q in range(1, count):
                    total = total + buf[q]
                k.vec[...] = total

            return start, finish, moves

        vec_stages = [
            vec_stage(0, pc.n_r, pc.r, lambda q: pc.dev(pc.p, q, pc.t)),
            vec_stage(1, pc.n_t, pc.t, lambda q: pc.dev(pc.p, pc.r, q)),
            vec_stage(2, pc.n_p, pc.p, lambda q: pc.dev(q, pc.r, pc.t)),
        ]
        vec_keep = pltpu.make_async_copy(k.vec, o.vec, k.vec_out.at[0])

        ready(k.c, k.h1)
        cot_load.wait()

        def put(at, y):
            for m in range(MB):
                k.mid[m, :, at] = y[m * part : (m + 1) * part]

        take_rows(v.hot, k.dealbuf, put)
        for m in range(MB):
            top(m)
        a_load.start()
        ag.relay(0)
        h2_load.wait()
        give_rows(v.hot, lambda at: k.dab[:, own_p, :, at].reshape(MB * part, CHUNK), k.dealbuf)
        deal_out.start()
        ready(k.wdown, k.u, k.g, k.wup, k.wgate, k.sup, k.sgate)
        feed(0)
        ag.relay(1)
        shrink(0)
        feed(1)
        rh1.relay(0)
        ready(k.mb, k.hb1)
        weight_grad(k.wdown, k.dcb, k.mb)
        near[0].start()
        hb_load.start()
        shrink(1)
        near_sum(0)
        tall_start(0)
        rh1.relay(1)
        weight_grad(k.wup, k.hb1, k.u)
        near[1].start()
        ready(k.tok)
        a_load.wait()
        middle(0)
        near_sum(1)
        tall_relay(0)
        tall_start(1)
        weight_grad(k.wgate, k.hb1, k.g)
        near[2].start()
        middle(1)
        ag1.relay(0)
        near_sum(2)
        tall_start(2)
        ready(k.wvo, k.vb, k.qkb, k.lse, k.qk, k.sqk, k.wqk, k.ob)
        attend(0)
        passed[0].wait_send()
        tall_relay(1)
        attend(1)
        hb_load.wait()
        rh.relay(1)
        chunks(width, heads_grad)
        for i in range(2):
            near[3 + i].start()
        collect()
        vec_stages[0][0]()
        for i in range(2):
            near_sum(3 + i)
            head_plane[i].start()
            head_own[i].start()
        passed[1].wait_send()
        tall_relay(2)
        tall_sum(0)
        plane_start(0)
        vec_stages[0][1]()
        vec_stages[1][0]()
        for m in range(MB):
            bottom(m)
        deal_out.wait_recv()
        deal_out.wait_send()
        give_rows(v.hot, lambda at: k.mid[:, :, at].reshape(MB * part, CHUNK).astype(BF), k.dealbuf)
        deal_grad.start()
        for i in range(2):
            head_plane[i].wait_recv()
            head_own[i].wait()
            head_start(i)
        plane_sent(0)
        tall_sum(1)
        plane_start(1)
        vec_stages[1][1]()
        vec_stages[2][0]()
        for i in range(2):
            head_relay(i)
        plane_sent(1)
        tall_sum(2)
        plane_start(2)
        vec_stages[2][1]()
        vec_keep.start()
        plane_sent(2)
        passed[2].wait_send()
        for w in tall + handed + head_first + head_last + head_plane + head_tall + near + [deal_grad]:
            w.wait_send()
        for stage in vec_stages:
            stage[2].wait_send()
        for i in range(3):
            plane[i][0].wait_recv()
        for w in head_tall + [deal_grad]:
            w.wait_recv()
        vec_keep.wait()
        for m in range(MB):
            ag.wait_send(m)
            ag1.wait_send(m)
            rh.wait_send(m)

    return fused(2, kernel, near_ins, loaded | later, outs, scratch)


def merged(slots, own, at):
    total = own.astype(F32)
    for q in range(slots.shape[0]):
        total = total + jnp.where((q == at) | (jnp.abs(q - at) == 3), 0, slots[q]).astype(F32)
    return total


def pick(x, at, axis):
    return lax.dynamic_index_in_dim(x, at, axis, keepdims=False)


def mm(a, b):
    return jnp.dot(a, b, preferred_element_type=F32)


def segment_ids(lengths_row, tok_count):
    count = lengths_row.shape[0]
    upto = jnp.arange(count)[:, None] >= jnp.arange(count)[None, :]
    doc_ends = jnp.sum(jnp.where(upto, lengths_row[None, :], 0), axis=1)
    places = jnp.arange(tok_count, dtype=jnp.int32)
    return jnp.sum((places[:, None] >= doc_ends[None, :]).astype(jnp.int32), axis=1)


def packed(x, y):
    return jnp.concatenate([x[:, :QUADS], y[:, :QUADS], x[:, QUADS:], y[:, QUADS:]], axis=1)


def unpacked(z):
    mid = 2 * QUADS + HEAD_DIM
    return (
        jnp.concatenate([z[..., :QUADS], z[..., 2 * QUADS : mid]], axis=-1),
        jnp.concatenate([z[..., QUADS : 2 * QUADS], z[..., mid:]], axis=-1),
    )


def body(
    tokens,
    cotangent,
    slot,
    lengths,
    w_query,
    w_key,
    w_value,
    w_out,
    w_up,
    w_gate,
    w_down,
    scale_qk,
    scale_up,
    scale_gate,
    rate_attn,
    rate_mlp,
):
    pc = Place()
    n_p, n_r, n_t, n_dev = pc.n_p, pc.n_r, pc.n_t, pc.n_dev
    rows_dev, width = tokens.shape
    tok_count = rows_dev // MB * n_p
    head_cols = w_query.shape[2]
    hid = w_up.shape[2]
    tiles = hid // LANES
    group = pc.r * n_t + pc.t
    owner = group * n_p + pc.p
    if rows_dev // n_dev > PAD or head_cols != QUADS + HEAD_DIM:
        raise ValueError("sizes")

    table = slot.reshape(n_dev, rows_dev)
    own_slots = lax.dynamic_index_in_dim(table, pc.me, 0, keepdims=False)
    d = own_slots // rows_dev
    to_dev = ((d % n_p) * n_r + (d // n_p) // n_t) * n_t + (d // n_p) % n_t
    places = jnp.arange(rows_dev, dtype=jnp.int32)
    spots = jnp.arange(n_dev * PAD, dtype=jnp.int32)
    before = (d[:, None] == d[None, :]) & (places[None, :] < places[:, None])
    rank = jnp.sum(before.astype(jnp.int32), axis=1)
    send_hot = (spots[:, None] == (to_dev * PAD + rank)[None, :]).astype(BF)

    sel = table // rows_dev == owner
    tri = (places[:, None] < places[None, :]).astype(BF)
    ranks = mm(sel.astype(BF), tri).astype(jnp.int32)
    kth = sel[:, None, :] & (ranks[:, None, :] == jnp.arange(PAD, dtype=jnp.int32)[None, :, None])
    owner_rows = jnp.sum(jnp.where(kth, (table - owner * rows_dev + 1)[:, None, :], 0), axis=2).reshape(-1) - 1
    recv_hot = (places[:, None] == owner_rows[None, :]).astype(BF)

    def to_send(x):
        return mm(send_hot, x).astype(BF).reshape(n_dev, PAD, width)

    qk_scale = packed(scale_qk, scale_qk).reshape(-1, LANES)
    small = jnp.concatenate([scale_up.reshape(-1, LANES), scale_gate.reshape(-1, LANES), qk_scale])
    small = jnp.pad(small, ((0, -small.shape[0] % 8), (0, 0)))
    own_lengths = lax.dynamic_slice_in_dim(lengths, group * MB, MB, 0)
    segments = jnp.stack([segment_ids(own_lengths[m], tok_count) for m in range(MB)])
    shared = (recv_hot, rate_attn, rate_mlp, segments[:, :, None], segments[:, None, :])

    f = forward(
        pc,
        to_send(tokens),
        to_send(cotangent),
        packed(w_query[0], w_key[0]),
        packed(w_value[0], w_out[0]),
        w_up[0],
        w_gate[0],
        w_down[0],
        small,
        *shared,
    )
    b = backward(pc, f, *shared)

    vec = b.vec
    at = n_t * tiles

    def own_row(x):
        return lax.dynamic_index_in_dim(x.reshape(n_t, -1), pc.t, 0)

    qk_rows = qk_scale.shape[0]
    out_sup, out_sgate = own_row(vec[:at]), own_row(vec[at : 2 * at])
    at = 2 * at
    out_rattn, out_rmlp = vec[at : at + tiles].reshape(1, -1), vec[at + tiles : at + 2 * tiles].reshape(1, -1)
    at = at + 2 * tiles
    out_sqk = sum(unpacked(own_row(vec[at : at + n_t * qk_rows])))
    heads = [
        x[None]
        for got, sent in zip(b.head_t, b.head_p)
        for x in unpacked(merged(got, pick(sent, pc.t, 0), pc.t))
    ]

    def from_back(x):
        return lax.dot_general(
            send_hot, x.reshape(-1, width), (((0,), (0,)), ((), ())), preferred_element_type=F32
        )

    down, up, gate = (x.astype(F32)[None] for x in b.final)
    return (
        from_back(b.back_out),
        from_back(b.back_grad),
        *heads,
        up,
        gate,
        down,
        out_sqk,
        out_sup,
        out_sgate,
        out_rattn,
        out_rmlp,
    )


def solution(mesh):
    tok = P(("dp", "tensor"), None)
    mat = P(None, "dp", "tensor")
    vec = P(None, "tensor")
    in_specs = (tok, tok, P(), P()) + (mat,) * 7 + (vec,) * 3 + (P(), P())
    out_specs = (tok, tok) + (mat,) * 7 + (vec,) * 3 + (P(), P())
    return jax.shard_map(body, mesh=mesh, in_specs=in_specs, out_specs=out_specs, check_vma=False)
```

```python
import types

import jax
import jax.numpy as jnp
from jax import lax
from jax.experimental import pallas as pl
from jax.experimental.pallas import tpu as pltpu
from jax.sharding import PartitionSpec as P

HEAD_DIM = 64
MB = 2
LANES = 128
QUADS = 4 * HEAD_DIM
CHUNK = 2 * LANES
ROW_STEP = 32
PAD = 8
VMEM_LIMIT = 127 * 2**19

EPSILON = 1e-06
MASKED = -1e30
BF = jnp.bfloat16
F32 = jnp.float32
MESH = pl.DeviceIdType.MESH
VM = pltpu.VMEM
DMA = pltpu.SemaphoreType.DMA
SDS = jax.ShapeDtypeStruct


class Place:
    def __init__(self):
        self.n_t = lax.axis_size("tensor")
        self.n_dp = lax.axis_size("dp")
        self.n_p = self.n_t
        self.n_r = self.n_dp // self.n_p
        self.n_dev = self.n_dp * self.n_t
        if self.n_t != 4:
            raise ValueError("tensor size")
        dp = lax.axis_index("dp")
        self.t = lax.axis_index("tensor")
        self.p = dp // self.n_r
        self.r = dp % self.n_r
        self.me = dp * self.n_t + self.t

    def dev(self, p, r, t):
        return (p * self.n_r + r, t)

    def flat(self, j):
        return (j // self.n_t, j % self.n_t)


def width3(p, t):
    return (p + t) % 2 == 0


def src_tile(p, t):
    return 5 * (p // 2) + (p % 2) * (3 - t % 2)


def dst_tile(p, t):
    return 5 * (t // 2) + (t % 2) * (3 - p % 2)


def lanes(tile, count):
    return pl.ds(pl.multiple_of(tile * LANES, LANES), count * LANES)


TWO, ONE = pl.ds(0, 2 * LANES), pl.ds(2 * LANES, LANES)


def remote(src, dst, send, recv, dev):
    return pltpu.make_async_remote_copy(
        src_ref=src, dst_ref=dst, send_sem=send, recv_sem=recv, device_id=dev, device_id_type=MESH
    )


class Move:
    def __init__(self, src, dst, send, recv, dev, landing, landed, cond_out=None, cond_in=None):
        self.going = (src, dst, send, recv, dev)
        self.coming = (landing, landing, send, landed, dev)
        self.cond_out, self.cond_in = cond_out, cond_in

    @staticmethod
    def under(cond, act):
        if cond is None:
            act()
        else:
            pl.when(cond)(act)

    def start(self):
        self.under(self.cond_out, lambda: remote(*self.going).start())

    def wait_send(self):
        self.under(self.cond_out, lambda: remote(*self.going).wait_send())

    def wait_recv(self):
        self.under(self.cond_in, lambda: remote(*self.coming).wait_recv())


class Moves:
    def __init__(self, moves):
        self.moves = moves

    def start(self):
        for m in self.moves:
            m.start()

    def wait_recv(self):
        for m in self.moves:
            m.wait_recv()

    def wait_send(self):
        for m in self.moves:
            m.wait_send()


def others(count, own):
    order = [2, 1, 3] if count == 4 else list(range(1, count))
    return [(own + k) % count for k in order]


def pair(n):
    return [DMA((n,)), DMA((n,))]


class Deal:
    @staticmethod
    def sems(pc):
        return [DMA((1,)), DMA((1,)), DMA((1,))]

    def __init__(self, pc, x, y, sems):
        self.pc, self.x, self.y = pc, x, y
        self.send, self.recv, self.local = (sem.at[0] for sem in sems)

    def copy(self, j, src, dst):
        return remote(src, dst, self.send, self.recv, self.pc.flat(j))

    def own(self):
        return pltpu.make_async_copy(self.x.at[self.pc.me], self.y.at[self.pc.me], self.local)

    def start(self):
        pc = self.pc

        def step(i, carry):
            j = (pc.me + i) % pc.n_dev
            self.copy(j, self.x.at[j], self.y.at[pc.me]).start()
            return carry

        lax.fori_loop(1, pc.n_dev, step, 0)
        self.own().start()

    def all_but_own(self):
        part = self.y.at[pl.ds(0, self.pc.n_dev - 1)]
        return self.copy((self.pc.me + 1) % self.pc.n_dev, part, part)

    def wait_recv(self):
        self.own().wait()
        self.all_but_own().wait_recv()

    def wait_send(self):
        self.all_but_own().wait_send()


class Tall:
    @staticmethod
    def sems(pc, pieces):
        return [DMA((pieces, pc.n_t + 1)), DMA((pieces, pc.n_t))]

    def __init__(self, pc, shard, own, sems):
        t = pc.t
        middle = (t == 1) | (t == 2)
        far, end = jnp.where(t == 2, 0, 3), jnp.where(t == 2, 3, 0)
        send, recv = sems

        def both(a, b):
            return a if b is None else a & b

        self.first, self.passed = [], []
        for q in others(pc.n_t, t):
            for i, ((dst, c_out), src, (here, c_in)) in enumerate(zip(shard(t), own, shard(q))):
                args = (src, dst, send.at[i, q], recv.at[i, t], pc.dev(pc.p, pc.r, q), here, recv.at[i, q])
                c_in = both(jnp.logical_not(middle & (q == far)), c_in)
                self.first.append(Move(*args, both(jnp.abs(q - t) != 3, c_out), c_in))
        for i, (ref, c) in enumerate(shard(far)):
            self.passed.append(
                Move(
                    ref, ref, send.at[i, pc.n_t], recv.at[i, far], pc.dev(pc.p, pc.r, end), ref, recv.at[i, far],
                    both(middle, c), both(middle, c),
                )
            )

    def start(self):
        for m in self.first:
            m.start()

    def relay(self):
        for m in self.passed:
            m.wait_recv()
            m.start()

    def wait_recv(self):
        for m in self.first:
            m.wait_recv()

    def wait_send(self):
        for m in self.first + self.passed:
            m.wait_send()


def by_shard(pc, ref):
    return ref.reshape(pc.n_p, pc.n_r, ref.shape[0] // (pc.n_p * pc.n_r), ref.shape[1])


class HeadWeights:
    @staticmethod
    def sems(pc):
        return [Tall.sems(pc, 1), pair(pc.n_p), pair(pc.n_r), DMA((2,))]

    def __init__(self, pc, x, a, w, sems):
        tall, (s2, r2), (s3, r3), ls = sems
        f = by_shard(pc, w)
        self.first = Tall(pc, lambda q: [(a.at[q], None)], [x], tall)
        self.second = Moves(
            [
                Move(a.at[q], f.at[pc.p, pc.r], s2.at[q], r2.at[pc.p], pc.dev(q, pc.r, pc.t), f.at[q, pc.r], r2.at[q])
                for q in others(pc.n_p, pc.p)
            ]
        )
        self.third = Moves(
            [
                Move(f.at[:, pc.r], f.at[:, pc.r], s3.at[q], r3.at[pc.r], pc.dev(pc.p, q, pc.t), f.at[:, q], r3.at[q])
                for q in others(pc.n_r, pc.r)
            ]
        )
        self.keep1 = pltpu.make_async_copy(x, a.at[pc.t], ls.at[0])
        self.keep2 = pltpu.make_async_copy(a.at[pc.p], f.at[pc.p, pc.r], ls.at[1])

    def start(self):
        self.first.start()
        self.keep1.start()

    def relay(self):
        self.first.relay()

    def plane(self):
        self.keep1.wait()
        self.first.wait_recv()
        self.second.start()
        self.keep2.start()

    def near(self):
        self.keep2.wait()
        self.second.wait_recv()
        self.third.start()

    def wait_recv(self):
        self.third.wait_recv()

    def wait_send(self):
        self.first.wait_send()
        self.second.wait_send()
        self.third.wait_send()


class HiddenWeights:
    @staticmethod
    def sems(pc):
        return [pair(pc.n_p), pair(pc.n_p), Tall.sems(pc, 2), pair(pc.n_r), DMA((2,))]

    def __init__(self, pc, x, w, sems):
        (s1, r1), (s2, r2), tall, (s3, r3), ls = sems
        g = by_shard(pc, w)
        p, r, t = pc.p, pc.r, pc.t

        def spot(q, row, extra):
            at = dst_tile(q, t)
            return g.at[row, r, :, lanes(at + 2, 1) if extra else lanes(at, 2)]

        def piece(q, extra):
            at = src_tile(q, t)
            return x.at[:, lanes(at + 2, 1) if extra else lanes(at, 2)]

        moves = []
        for q in others(pc.n_p, p):
            dev = pc.dev(q, r, t)
            moves.append(
                Move(piece(q, False), spot(q, p, False), s1.at[q], r1.at[p], dev, spot(p, q, False), r1.at[q])
            )
            moves.append(
                Move(
                    piece(q, True), spot(q, p, True), s2.at[q], r2.at[p], dev, spot(p, q, True), r2.at[q],
                    width3(q, t), width3(p, t),
                )
            )
        self.first = Moves(moves)
        self.own = [
            (None, pltpu.make_async_copy(piece(p, False), spot(p, p, False), ls.at[0])),
            (width3(p, t), pltpu.make_async_copy(piece(p, True), spot(p, p, True), ls.at[1])),
        ]

        def shard(q):
            at = dst_tile(p, q)
            return [(g.at[:, r, :, lanes(at, 2)], None), (g.at[:, r, :, lanes(at + 2, 1)], width3(p, q))]

        self.second = Tall(pc, shard, [ref for ref, _ in shard(t)], tall)
        self.third = Moves(
            [
                Move(g.at[:, r], g.at[:, r], s3.at[q], r3.at[r], pc.dev(p, q, t), g.at[:, q], r3.at[q])
                for q in others(pc.n_r, r)
            ]
        )

    def start(self):
        self.first.start()
        for cond, copy in self.own:
            Move.under(cond, copy.start)

    def tall(self):
        for cond, copy in self.own:
            Move.under(cond, copy.wait)
        self.first.wait_recv()
        self.second.start()

    def relay(self):
        self.second.relay()

    def near(self):
        self.second.wait_recv()
        self.third.start()

    def wait_recv(self):
        self.third.wait_recv()

    def wait_send(self):
        self.first.wait_send()
        self.second.wait_send()
        self.third.wait_send()


def add_into(target, term, rows):
    step = rows // 2

    def block(i, carry):
        at = pl.ds(pl.multiple_of(i * step, step), step)
        target[at, :] = (target[at, :].astype(F32) + term[at, :].astype(F32)).astype(BF)
        return carry

    lax.fori_loop(0, 2, block, 0)


class Plane:
    def __init__(self, pc):
        self.x, self.y, self.d = pc.p + 1 - 2 * (pc.p % 2), (pc.p + 2) % 4, 3 - pc.p
        self.to_x, self.to_y = pc.dev(self.x, pc.r, pc.t), pc.dev(self.y, pc.r, pc.t)

    def halves(self, ref):
        half = ref.shape[0] // 2
        return ref.at[pl.ds(0, half)], ref.at[pl.ds(half, half)]

    def wait_send(self, m):
        for move in self.first[m] + self.second[m]:
            move.wait_send()


class PlaneGather(Plane):
    @staticmethod
    def sems(pc):
        return [DMA((MB, 4)), DMA((MB, 4))]

    def __init__(self, pc, spot, sems):
        super().__init__(pc)
        send, recv = sems
        self.first, self.second = [], []
        for m in range(MB):
            own, from_x, from_y = spot(m, pc.p), spot(m, self.x), spot(m, self.y)
            (a, _), (_, b), (here_a, here_b) = self.halves(from_x), self.halves(from_y), self.halves(spot(m, self.d))
            self.first.append(
                [
                    Move(own, own, send.at[m, 0], recv.at[m, 0], self.to_x, from_x, recv.at[m, 0]),
                    Move(own, own, send.at[m, 1], recv.at[m, 1], self.to_y, from_y, recv.at[m, 1]),
                ]
            )
            self.second.append(
                [
                    Move(a, a, send.at[m, 2], recv.at[m, 2], self.to_y, here_a, recv.at[m, 2]),
                    Move(b, b, send.at[m, 3], recv.at[m, 3], self.to_x, here_b, recv.at[m, 3]),
                ]
            )

    def start(self, m):
        for move in self.first[m]:
            move.start()

    def relay(self, m):
        for arrived, move in zip(self.first[m], self.second[m]):
            arrived.wait_recv()
            move.start()

    def wait_recv(self, m):
        for move in self.second[m]:
            move.wait_recv()


class PlaneScatter(Plane):
    @staticmethod
    def sems(pc):
        return [DMA((MB, 6)), DMA((MB, 6))]

    def __init__(self, pc, sent, got, sems):
        super().__init__(pc)
        send, recv = sems
        self.first, self.second, self.adds = [], [], []
        for m in range(MB):

            def move(i, src, dst, dev, landing):
                return Move(src, dst, send.at[m, i], recv.at[m, i], dev, landing, recv.at[m, i])

            for_x, for_y, for_d = (self.halves(sent.at[m, q]) for q in (self.x, self.y, self.d))
            hop = self.halves(got.at[pc.p, m])
            hop_x, hop_y = self.halves(got.at[self.x, m]), self.halves(got.at[self.y, m])
            mine = hop
            self.first.append(
                [
                    move(0, for_d[0], hop_x[0], self.to_x, hop[0]),
                    move(1, for_d[1], hop_y[1], self.to_y, hop[1]),
                    move(2, for_x[0], mine[0], self.to_x, hop_x[0]),
                    move(3, for_y[1], mine[1], self.to_y, hop_y[1]),
                ]
            )
            self.second.append(
                [
                    move(5, for_y[0], mine[0], self.to_y, hop_y[0]),
                    move(4, for_x[1], mine[1], self.to_x, hop_x[1]),
                ]
            )
            self.adds.append([(for_y[0], hop[0]), (for_x[1], hop[1])])

    def start(self, m):
        for move in self.first[m]:
            move.start()

    def relay(self, m):
        for arrived, (target, term), move in zip(self.first[m], self.adds[m], self.second[m]):
            arrived.wait_recv()
            add_into(target, term, target.shape[0])
            move.start()

    def wait_recv(self, m):
        for move in self.first[m][2:] + self.second[m]:
            move.wait_recv()


def plane_sum(pc, sent, got, m, at):
    total = sent[m, pc.p, at, :].astype(F32)
    for q in (pc.p + 1 - 2 * (pc.p % 2), (pc.p + 2) % 4):
        total = total + got[q, m, at, :].astype(F32)
    return total


def greet(pc):
    barrier = pltpu.get_barrier_semaphore()

    def step(i, carry):
        dev = pc.flat((pc.me + i) % pc.n_dev)
        pl.semaphore_signal(barrier, inc=1, device_id=dev, device_id_type=MESH)
        return carry

    lax.fori_loop(1, pc.n_dev, step, 0)
    pl.semaphore_wait(barrier, pc.n_dev - 1)


def fused(collective_id, kernel, near_ins, far_ins, outs, scratch):
    ins_leaves, ins_tree = jax.tree.flatten((near_ins, far_ins))
    outs_leaves, outs_tree = jax.tree.flatten(outs)
    scratch_leaves, scratch_tree = jax.tree.flatten(scratch)
    a, b = len(ins_leaves), len(outs_leaves)
    near = len(jax.tree.leaves(near_ins))

    def run(*refs):
        first, second = jax.tree.unflatten(ins_tree, refs[:a])
        third = jax.tree.unflatten(outs_tree, refs[a : a + b])
        fourth = jax.tree.unflatten(scratch_tree, refs[a + b :])
        kernel(
            Place(),
            types.SimpleNamespace(**first),
            types.SimpleNamespace(**second),
            types.SimpleNamespace(**third),
            types.SimpleNamespace(**fourth),
        )

    got = pl.pallas_call(
        run,
        out_shape=tuple(outs_leaves),
        in_specs=[pl.BlockSpec(memory_space=VM if i < near else pl.ANY) for i in range(a)],
        out_specs=tuple([pl.BlockSpec(memory_space=pl.ANY)] * b),
        scratch_shapes=scratch_leaves,
        compiler_params=pltpu.CompilerParams(
            collective_id=collective_id, has_side_effects=True, vmem_limit_bytes=VMEM_LIMIT
        ),
    )(*ins_leaves)
    return types.SimpleNamespace(**jax.tree.unflatten(outs_tree, got))


def dot_nt(a, b):
    return lax.dot_general(a, b, (((1,), (1,)), ((), ())), preferred_element_type=F32)


def dot_tn(a, b):
    return lax.dot_general(a, b, (((0,), (0,)), ((), ())), preferred_element_type=F32)


def dot_nn(a, b):
    return lax.dot_general(a, b, (((1,), (0,)), ((), ())), preferred_element_type=F32)


def half_means(x):
    a = lax.broadcasted_iota(jnp.int32, (LANES, LANES), 0) // HEAD_DIM
    b = lax.broadcasted_iota(jnp.int32, (LANES, LANES), 1) // HEAD_DIM
    same = jnp.where(a == b, 1.0 / HEAD_DIM, 0.0).astype(F32)
    return lax.dot_general(x, same, (((1,), (0,)), ((), ())), precision=lax.Precision.HIGHEST, preferred_element_type=F32)


def swap_halves(x):
    return pltpu.roll(x, HEAD_DIM, 1)


def low_lanes(shape):
    return lax.broadcasted_iota(jnp.int32, shape, len(shape) - 1) < HEAD_DIM


def row_mean(x):
    return jnp.mean(x, axis=-1, keepdims=True)


def inv_rms(x):
    return lax.rsqrt(row_mean(x * x) + EPSILON)


def tile_of(j):
    return slice(j * LANES, (j + 1) * LANES)


def rows_loop(count, fn):
    def step(i, carry):
        fn(pl.ds(pl.multiple_of(i * ROW_STEP, ROW_STEP), ROW_STEP))
        return carry

    lax.fori_loop(0, count // ROW_STEP, step, 0)


def chunks(count, fn):
    def step(c, carry):
        fn(pl.ds(pl.multiple_of(c * CHUNK, CHUNK), CHUNK))
        return carry

    lax.fori_loop(0, count // CHUNK, step, 0)


def take_rows(hot, arrived, put):
    def block(at):
        x = arrived[:, :, at].astype(F32).reshape(-1, CHUNK).astype(BF)
        put(at, dot_nn(hot[...], x))

    chunks(arrived.shape[2], block)


def give_rows(hot, rows, out):
    def block(at):
        y = dot_tn(hot[...], rows(at))
        out[:, :, at] = y.reshape(out.shape[0], PAD, CHUNK).astype(BF)

    chunks(out.shape[2], block)


def fill_mask(bias, segq, segk):
    seq = bias.shape[0]
    rows = lax.broadcasted_iota(jnp.int32, (seq, seq), 0)
    cols = lax.broadcasted_iota(jnp.int32, (seq, seq), 1)
    bias[...] = jnp.where((segq == segk) & (cols <= rows), 0.0, MASKED)


def forward(pc, tok_sent, cot_sent, wqk, wvo, wup, wgate, wdown, small, hot, rattn, rmlp, segq, segk):
    n_dev, _, width = tok_sent.shape
    part = hot.shape[0] // MB
    seq = part * pc.n_p
    qk_cols, vo_cols, hid = wqk.shape[1], wvo.shape[1], wup.shape[1]
    o_cols = QUADS + LANES
    tiles = hid // LANES
    blocks = (MB, pc.n_p, part, width)
    kept = dict(
        hb=(blocks, BF),
        qk=((MB, seq, qk_cols), F32),
        qkb=((MB, seq, qk_cols), BF),
        vb=((MB, seq, o_cols), BF),
        ob=((MB, seq, o_cols), BF),
        lse=((MB, seq, LANES), F32),
        tok=((MB, part, width), BF),
        a=((MB, part, width), F32),
        h1=((MB, part, width), F32),
        c=((MB, part, width), F32),
        hb1=(blocks, BF),
        u=((MB, seq, hid), BF),
        g=((MB, seq, hid), BF),
        mb=((MB, seq, hid), BF),
        h2=((MB, part, width), BF),
    )
    whole = dict(
        wqk=((width, qk_cols), BF),
        wvo=((width, vo_cols), BF),
        wup=((width, hid), BF),
        wgate=((width, hid), BF),
        wdown=((width, hid), BF),
        sup=((1, hid), F32),
        sgate=((1, hid), F32),
        sqk=((1, qk_cols), F32),
    )
    outs = {n: SDS(*x) for n, x in (kept | whole).items()} | dict(cot=SDS(cot_sent.shape, BF))
    scratch = {n: VM(*x) for n, x in (kept | whole).items()} | dict(
        arrived=VM(tok_sent.shape, BF),
        aqk=VM((pc.n_t,) + wqk.shape, BF),
        avo=VM((pc.n_t,) + wvo.shape, BF),
        small=VM((pc.n_t,) + small.shape, F32),
        bias=VM((seq, seq), F32),
        sent=VM(blocks, BF),
        got=VM((pc.n_p, MB, part, width), BF),
        kept_sem={n: DMA((MB,)) for n in kept},
        whole_sem={n: DMA((1,)) for n in whole},
        tok_sem=Deal.sems(pc),
        cot_sem=Deal.sems(pc),
        small_sem=pair(pc.n_t) + [DMA((1,))],
        qk_sem=HeadWeights.sems(pc),
        vo_sem=HeadWeights.sems(pc),
        up_sem=HiddenWeights.sems(pc),
        gate_sem=HiddenWeights.sems(pc),
        down_sem=HiddenWeights.sems(pc),
        ag_sem=PlaneGather.sems(pc),
        ra_sem=PlaneScatter.sems(pc),
        ag1_sem=PlaneGather.sems(pc),
        rc_sem=PlaneScatter.sems(pc),
    )
    near_ins = dict(hot=hot, rattn=rattn, rmlp=rmlp, segq=segq, segk=segk)
    far_ins = dict(
        tok=tok_sent, cot=cot_sent, wqk=wqk, wvo=wvo, wup=wup, wgate=wgate, wdown=wdown, small=small
    )

    def kernel(pc, v, x, o, k):
        own_p = pc.p
        greet(pc)
        deal = Deal(pc, x.tok, k.arrived, k.tok_sem)
        deal_cot = Deal(pc, x.cot, o.cot, k.cot_sem)
        head_qk = HeadWeights(pc, x.wqk, k.aqk, k.wqk, k.qk_sem)
        head_vo = HeadWeights(pc, x.wvo, k.avo, k.wvo, k.vo_sem)
        up = HiddenWeights(pc, x.wup, k.wup, k.up_sem)
        gate = HiddenWeights(pc, x.wgate, k.wgate, k.gate_sem)
        down = HiddenWeights(pc, x.wdown, k.wdown, k.down_sem)
        ss, rs, ls = k.small_sem
        scales = Moves(
            [
                Move(
                    x.small, k.small.at[pc.t], ss.at[q], rs.at[pc.t], pc.dev(pc.p, pc.r, q), k.small.at[q], rs.at[q]
                )
                for q in others(pc.n_t, pc.t)
            ]
        )
        own_scales = pltpu.make_async_copy(x.small, k.small.at[pc.t], ls.at[0])

        def gather(buf, sems):
            return PlaneGather(pc, lambda m, q: buf.at[m, q], sems)

        ag, ag1 = gather(k.hb, k.ag_sem), gather(k.hb1, k.ag1_sem)
        ra, rc = (PlaneScatter(pc, k.sent, k.got, sems) for sems in (k.ra_sem, k.rc_sem))
        names = vars(k)
        out_names = vars(o)
        copies = []

        def keep(m, *refs):
            for n in kept:
                if any(names[n] is ref for ref in refs):
                    copy = pltpu.make_async_copy(names[n].at[m], out_names[n].at[m], k.kept_sem[n].at[m])
                    copy.start()
                    copies.append(copy)

        def keep_whole(*refs):
            for n in whole:
                if any(names[n] is ref for ref in refs):
                    copy = pltpu.make_async_copy(names[n], out_names[n], k.whole_sem[n].at[0])
                    copy.start()
                    copies.append(copy)

        def attend(m):
            fill_mask(k.bias, v.segq[m], v.segk[m])
            ag.wait_recv(m)
            keep(m, k.hb)

            def project(i, carry):
                rows = k.hb[m, pl.ds(2 * i, 2)].reshape(2 * part, width)
                at = pl.ds(pl.multiple_of(i * 2 * part, 2 * part), 2 * part)
                qk = dot_nn(rows, k.wqk[...])
                k.qk[m, at, :] = qk
                for j in range(qk_cols // LANES):
                    s = qk[:, tile_of(j)]
                    n = s * lax.rsqrt(half_means(s * s) + EPSILON)
                    k.qkb[m, at, tile_of(j)] = (n * k.sqk[:, tile_of(j)]).astype(BF)
                k.vb[m, at, :QUADS] = dot_nn(rows, k.wvo[:, :QUADS]).astype(BF)
                last = dot_nn(rows, k.wvo[:, 2 * QUADS :])
                k.vb[m, at, QUADS:] = jnp.where(low_lanes(last.shape), last, 0.0).astype(BF)
                return carry

            lax.fori_loop(0, pc.n_p // 2, project, 0)
            keep(m, k.qk, k.qkb, k.vb)
            if m == 1:
                ra.relay(0)
            blk = seq // 2
            for i in range(2):
                nk = (i + 1) * blk
                at = slice(i * blk, nk)
                bias = k.bias[at, :nk]
                lse = jnp.zeros((blk, LANES), F32)
                lane = lax.broadcasted_iota(jnp.int32, (blk, LANES), 1)
                for slab in range(3):
                    if slab < 2:
                        qs = k.qkb[m, at, tile_of(slab)]
                        ks = k.qkb[m, :nk, tile_of(2 + slab)]
                    else:
                        qs = k.qkb[m, at, 2 * QUADS :]
                        ks = swap_halves(k.qkb[m, :nk, 2 * QUADS :].astype(F32)).astype(BF)
                    vs = k.vb[m, :nk, tile_of(slab)]
                    res = []
                    for half in range(2 if slab < 2 else 1):
                        low = low_lanes(qs.shape)
                        q1 = jnp.where(low if half == 0 else jnp.logical_not(low), qs, jnp.zeros_like(qs))
                        s = dot_nt(q1, ks) * HEAD_DIM ** (-0.5) + bias
                        top = jnp.max(s, axis=1, keepdims=True)
                        e = jnp.exp(s - top)
                        tot = jnp.sum(e, axis=1, keepdims=True)
                        lse = jnp.where(lane == 2 * slab + half, top + jnp.log(tot), lse)
                        res.append(dot_nn((e * (1.0 / tot)).astype(BF), vs))
                    if slab < 2:
                        res = jnp.where(low_lanes(res[0].shape), res[0], res[1])
                    else:
                        res = swap_halves(res[0])
                    k.ob[m, at, tile_of(slab)] = res.astype(BF)
                k.lse[m, at, :] = lse
            keep(m, k.ob, k.lse)
            if m == 0:
                ag.relay(1)

            def branch(i, carry):
                at = pl.ds(pl.multiple_of(i * 2 * part, 2 * part), 2 * part)
                y = dot_nt(k.ob[m, at, :], k.wvo[:, QUADS:])
                k.sent[m, pl.ds(2 * i, 2)] = y.astype(BF).reshape(2, part, width)
                return carry

            lax.fori_loop(0, pc.n_p // 2, branch, 0)
            ra.start(m)

        def summed(m, at):
            return plane_sum(pc, k.sent, k.got, m, at)

        def middle(m):
            ra.wait_recv(m)

            def rows(at):
                a = summed(m, at)
                h = k.tok[m, at, :].astype(F32)
                y = h + v.rattn[...] * (a * inv_rms(a) - h)
                h1 = y * inv_rms(y)
                k.a[m, at, :] = a
                k.h1[m, at, :] = h1
                k.hb1[m, own_p, at, :] = h1.astype(BF)

            rows_loop(part, rows)
            ag1.start(m)
            keep(m, k.a, k.h1)

        def feed(m):
            ag1.wait_recv(m)
            keep(m, k.hb1)

            def hidden(at):
                rows = k.hb1[m].reshape(seq, width)
                u = dot_nn(rows, k.wup[:, at])
                g = dot_nn(rows, k.wgate[:, at])
                k.u[m, :, at] = u.astype(BF)
                k.g[m, :, at] = g.astype(BF)
                z = k.sgate[:, at] * g
                k.mb[m, :, at] = (z / (1.0 + jnp.exp(-z)) * (k.sup[:, at] * u)).astype(BF)

            chunks(hid, hidden)
            keep(m, k.u, k.g, k.mb)

        def shrink(m):
            ra.wait_send(m)

            def columns(at):
                y = dot_nt(k.mb[m], k.wdown[at, :])
                k.sent[m, :, :, at] = y.astype(BF).reshape(pc.n_p, part, CHUNK)

            chunks(width, columns)
            rc.start(m)

        def finish(m):
            rc.wait_recv(m)

            def rows(at):
                c = summed(m, at)
                h1 = k.h1[m, at, :]
                z = h1 + v.rmlp[...] * (c * inv_rms(c) - h1)
                k.c[m, at, :] = c
                k.h2[m, at, :] = (z * inv_rms(z)).astype(BF)

            rows_loop(part, rows)
            keep(m, k.c, k.h2)

        deal.start()
        head_qk.start()
        head_vo.start()
        scales.start()
        own_scales.start()
        for w in (up, gate, down):
            w.start()
        head_qk.relay()
        head_vo.relay()
        deal.wait_recv()

        def put(at, y):
            for m in range(MB):
                rows = y[m * part : (m + 1) * part].astype(BF)
                k.tok[m, :, at] = rows
                k.hb[m, own_p, :, at] = rows

        take_rows(v.hot, k.arrived, put)
        for m in range(MB):
            ag.start(m)
            keep(m, k.tok)
        head_qk.plane()
        head_vo.plane()
        up.tall()
        gate.tall()
        own_scales.wait()
        scales.wait_recv()
        for t in range(pc.n_t):
            for j in range(3):

                def move(t=t, j=j):
                    at = lanes(dst_tile(pc.p, t) + j, 1)
                    k.sup[:, at] = k.small[t, pl.ds(src_tile(pc.p, t) + j, 1), :]
                    k.sgate[:, at] = k.small[t, pl.ds(tiles + src_tile(pc.p, t) + j, 1), :]

                Move.under(width3(pc.p, t) if j == 2 else None, move)
        for j in range(qk_cols // LANES):
            k.sqk[:, tile_of(j)] = k.small[own_p, 2 * tiles + j : 2 * tiles + j + 1, :]
        keep_whole(k.sup, k.sgate, k.sqk)
        head_qk.near()
        head_vo.near()
        head_qk.wait_recv()
        head_vo.wait_recv()
        keep_whole(k.wqk, k.wvo)
        ag.relay(0)
        attend(0)
        down.tall()
        attend(1)
        up.relay()
        gate.relay()
        middle(0)
        ra.relay(1)
        middle(1)
        ag1.relay(0)
        up.near()
        gate.near()
        ag1.relay(1)
        up.wait_recv()
        gate.wait_recv()
        down.relay()
        feed(0)
        keep_whole(k.wup, k.wgate)
        feed(1)
        down.near()
        down.wait_recv()
        deal_cot.start()
        shrink(0)
        rc.relay(0)
        keep_whole(k.wdown)
        shrink(1)
        rc.relay(1)
        for m in range(MB):
            finish(m)
        deal_cot.wait_recv()
        for w in (deal, deal_cot, head_qk, head_vo, up, gate, down, scales):
            w.wait_send()
        for m in range(MB):
            for w in (ag, ag1, rc):
                w.wait_send(m)
        for copy in copies:
            copy.wait()

    return fused(1, kernel, near_ins, far_ins, outs, scratch)


def backward(pc, f, hot, rattn, rmlp, segq, segk):
    n_dev = f.cot.shape[0]
    part, width = f.h2.shape[1], f.h2.shape[2]
    seq = part * pc.n_p
    all_tok = MB * seq
    qk_cols, hid = f.wqk.shape[1], f.wup.shape[1]
    o_cols = QUADS + LANES
    tiles = hid // LANES
    n_rows = width // (pc.n_p * pc.n_r)
    step_rows = n_rows // 5
    if n_rows % 5 or hid != width:
        raise ValueError("sizes")
    blocks = (MB, pc.n_p, part, width)
    dealt = (n_dev, PAD, width)
    vec_rows = 4 * tiles
    vec_total = -(-(2 * vec_rows + 2 * tiles + pc.n_p * qk_cols // LANES) // PAD) * PAD
    heads_shape = (pc.n_p, n_rows, qk_cols)
    outs = dict(
        back_out=SDS(dealt, BF),
        back_grad=SDS(dealt, BF),
        vec=SDS((vec_total, LANES), F32),
        relay=[SDS((pc.n_p, n_rows, 3 * LANES), BF) for _ in range(3)],
        head_relay=[SDS((n_rows, qk_cols), BF) for _ in range(2)],
        tall=[SDS((pc.n_t, pc.n_p, n_rows, 3 * LANES), BF) for _ in range(3)],
        final=[SDS((n_rows, hid), BF) for _ in range(3)],
        head_p=[SDS(heads_shape, BF) for _ in range(2)],
        head_t=[SDS(heads_shape, BF) for _ in range(2)],
    )
    loaded = dict(
        c=f.c,
        h1=f.h1,
        wdown=f.wdown,
        u=f.u,
        g=f.g,
        sup=f.sup,
        sgate=f.sgate,
        wup=f.wup,
        wgate=f.wgate,
        mb=f.mb,
        hb1=f.hb1,
        tok=f.tok,
        wvo=f.wvo,
        vb=f.vb,
        qkb=f.qkb,
        lse=f.lse,
        qk=f.qk,
        sqk=f.sqk,
        wqk=f.wqk,
        ob=f.ob,
    )
    later = dict(a=f.a, hb=f.hb, cot=f.cot, h2=f.h2)
    sums = dict(gsup=hid, gsgate=hid, gsqk=qk_cols, grattn=width, grmlp=width)
    scratch = {n: VM(y.shape, y.dtype) for n, y in loaded.items()} | {n: VM((1, y), F32) for n, y in sums.items()}
    scratch |= dict(
        load_sem={n: DMA((1,)) for n in loaded},
        later_sem=[DMA((1,)) for _ in later],
        dcb=VM(blocks, BF),
        dab=VM(blocks, BF),
        mid=VM((MB, part, width), F32),
        bias=VM((seq, seq), F32),
        sent=VM(blocks, BF),
        got=VM((pc.n_p, MB, part, width), BF),
        tbuf=VM((pc.n_t, pc.n_p, n_rows, 3 * LANES), BF),
        dealbuf=VM(dealt, BF),
        vec=VM((vec_total, LANES), F32),
        vec_got=[VM((y, vec_total, LANES), F32) for y in (pc.n_r, pc.n_t, pc.n_p)],
        rbuf=VM((pc.n_p, n_rows, 3 * LANES), BF),
        hbuf=[VM((2, n_rows, qk_cols), BF) for _ in range(2)],
        near=[VM((pc.n_r - 1, pc.n_p, n_rows, y), BF) for y in (hid, hid, hid, qk_cols, qk_cols)],
        near_sem=[pair(pc.n_r) for _ in range(5)],
        tall_sem=[[DMA((2, pc.n_t)) for _ in range(3)] for _ in range(3)],
        plane_sem=[[DMA((2, pc.n_p)) for _ in range(2)] for _ in range(5)],
        relay_sem=[[DMA((2,)) for _ in range(5)] for _ in range(3)],
        head_sem=[pair(pc.n_t) + [DMA((1,))] for _ in range(2)],
        head_relay_sem=[[DMA((1,)) for _ in range(5)] for _ in range(2)],
        out_sem=Deal.sems(pc),
        grad_sem=Deal.sems(pc),
        vec_sem=[pair(y) for y in (pc.n_r, pc.n_t, pc.n_p)],
        vec_out=DMA((1,)),
        ag_sem=PlaneGather.sems(pc),
        ag1_sem=PlaneGather.sems(pc),
        rh1_sem=PlaneScatter.sems(pc),
        rh_sem=PlaneScatter.sems(pc),
    )
    near_ins = dict(hot=hot, rattn=rattn, rmlp=rmlp, segq=segq, segk=segk)

    def kernel(pc, v, x, o, k):
        own_p = pc.p
        refs = vars(k)
        sources = vars(x)
        loads = {n: pltpu.make_async_copy(sources[n], refs[n], k.load_sem[n].at[0]) for n in loaded}
        for n in loaded:
            loads[n].start()
        cot_load = pltpu.make_async_copy(x.cot, k.dealbuf, k.later_sem[2].at[0])
        h2_load = pltpu.make_async_copy(x.h2, k.dab.at[:, own_p], k.later_sem[3].at[0])
        cot_load.start()
        h2_load.start()
        k_dqk, k_dv = k.u.at[:, :, pl.ds(0, qk_cols)], k.u.at[:, :, pl.ds(qk_cols, o_cols)]
        k_do = k.g.at[0, :, pl.ds(0, o_cols)]
        a_load = pltpu.make_async_copy(x.a, k.c, k.later_sem[0].at[0])
        hb_load = pltpu.make_async_copy(x.hb.reshape(MB, seq, width), k.mb, k.later_sem[1].at[0])
        waited = set()

        def ready(*wanted):
            for n in loaded:
                if n not in waited and any(refs[n] is ref for ref in wanted):
                    waited.add(n)
                    loads[n].wait()

        for n in sums:
            refs[n][...] = jnp.zeros(refs[n].shape, F32)
        k.vec[...] = jnp.zeros(k.vec.shape, F32)
        greet(pc)

        ag, ag1 = (
            PlaneGather(pc, lambda m, q, buf=buf: buf.at[m, q], sems)
            for buf, sems in ((k.dcb, k.ag_sem), (k.dab, k.ag1_sem))
        )
        rh1, rh = (PlaneScatter(pc, k.sent, k.got, sems) for sems in (k.rh1_sem, k.rh_sem))
        deal_out = Deal(pc, k.dealbuf, o.back_out, k.out_sem)
        deal_grad = Deal(pc, k.dealbuf, o.back_grad, k.grad_sem)

        def add_rows(ref, y, at=slice(None)):
            ref[:, at] += jnp.sum(y, axis=0, keepdims=True)

        def top(m):
            def rows(at):
                c, h1, ct = k.c[m, at, :], k.h1[m, at, :], k.mid[m, at, :]
                r_c = inv_rms(c)
                n_c = c * r_c
                z = h1 + v.rmlp[...] * (n_c - h1)
                r_z = inv_rms(z)
                h2 = z * r_z
                dz = r_z * (ct - h2 * row_mean(ct * h2))
                add_rows(k.grmlp, dz * (n_c - h1))
                k.mid[m, at, :] = (1.0 - v.rmlp[...]) * dz
                dn = v.rmlp[...] * dz
                k.dcb[m, own_p, at, :] = (r_c * (dn - n_c * row_mean(dn * n_c))).astype(BF)

            rows_loop(part, rows)
            ag.start(m)

        def summed(m, at):
            return plane_sum(pc, k.sent, k.got, m, at)

        def feed(m):
            ag.wait_recv(m)

            def hidden(at):
                dm = dot_nn(k.dcb[m].reshape(seq, width), k.wdown[:, at])
                u, g = k.u[m, :, at].astype(F32), k.g[m, :, at].astype(F32)
                y = k.sgate[:, at] * g
                sig = 1.0 / (1.0 + jnp.exp(-y))
                du = dm * (y * sig)
                dx = dm * (k.sup[:, at] * u) * (sig * (1.0 + y * (1.0 - sig)))
                add_rows(k.gsup, du * u, at)
                add_rows(k.gsgate, dx * g, at)
                k.u[m, :, at] = (k.sup[:, at] * du).astype(BF)
                k.g[m, :, at] = (k.sgate[:, at] * dx).astype(BF)

            chunks(hid, hidden)

        def shrink(m):
            def columns(at):
                y = dot_nt(k.u[m], k.wup[at, :]) + dot_nt(k.g[m], k.wgate[at, :])
                k.sent[m, :, :, at] = y.astype(BF).reshape(pc.n_p, part, CHUNK)

            chunks(width, columns)
            rh1.start(m)

        grads = [k.wdown, k.wup, k.wgate, k.wqk, k.wvo]

        def near_slot(source, at):
            return (source - at + pc.n_r - 1) % pc.n_r

        def near_moves(i):
            send, recv = k.near_sem[i]
            return Moves(
                [
                    Move(
                        by_shard(pc, grads[i]).at[:, q], k.near[i].at[near_slot(pc.r, q)], send.at[q], recv.at[pc.r],
                        pc.dev(pc.p, q, pc.t), k.near[i].at[near_slot(q, pc.r)], recv.at[q],
                    )
                    for q in others(pc.n_r, pc.r)
                ]
            )

        near = [near_moves(i) for i in range(5)]

        def row_blocks(fn):
            def block(i, carry):
                fn(i // 5, pl.ds(pl.multiple_of((i % 5) * step_rows, step_rows), step_rows))
                return carry

            lax.fori_loop(0, pc.n_p * 5, block, 0)

        def near_sum(i):
            near[i].wait_recv()
            own = by_shard(pc, grads[i])

            def block(p, at):
                total = own[p, pc.r, at, :].astype(F32)
                for j in range(pc.n_r - 1):
                    total = total + k.near[i][j, p, at, :].astype(F32)
                k.near[i][0, p, at, :] = total.astype(BF)

            row_blocks(block)

        t = pc.t
        middle_dev = (t == 1) | (t == 2)
        end_dev = jnp.logical_not(middle_dev)
        far = jnp.where((t == 2) | (t == 3), 0, 3)
        by = jnp.where(t == 0, 1, 2)
        wide = width3(pc.p, t)
        wide_far = width3(pc.p, far)

        def direct_out(q):
            return (jnp.abs(q - t) != 3) & jnp.logical_not(middle_dev & (q == far))

        def comes(q):
            return jnp.abs(q - t) != 3

        def tall_moves(i):
            send, recv, _ = k.tall_sem[i]
            src, y = k.near[i].at[0], o.tall[i]
            moves = []
            for q in others(pc.n_t, t):
                there = dst_tile(pc.p, q)
                dev = pc.dev(pc.p, pc.r, q)
                moves.append(
                    Move(
                        src.at[:, :, lanes(there, 2)], y.at[t, :, :, TWO], send.at[0, q], recv.at[0, t], dev,
                        y.at[q, :, :, TWO], recv.at[0, q], direct_out(q), comes(q),
                    )
                )
                moves.append(
                    Move(
                        src.at[:, :, lanes(there + 2, 1)], y.at[t, :, :, ONE], send.at[1, q], recv.at[1, t], dev,
                        y.at[q, :, :, ONE], recv.at[1, q], direct_out(q) & width3(pc.p, q), comes(q) & wide,
                    )
                )
            return Moves(moves)

        def far_parts(i):
            at = dst_tile(pc.p, far)
            return ((TWO, lanes(at, 2), None), (ONE, lanes(at + 2, 1), wide_far))

        def both(a, b):
            return a if b is None else a & b

        def handed_moves(i):
            s1, r1, _, _, _ = k.relay_sem[i]
            src, y = k.near[i].at[0], o.relay[i]
            return Moves(
                [
                    Move(
                        src.at[:, :, at], y.at[:, :, w], s1.at[j], r1.at[j], pc.dev(pc.p, pc.r, by), y.at[:, :, w],
                        r1.at[j], both(end_dev, cond), both(middle_dev, cond),
                    )
                    for j, (w, at, cond) in enumerate(far_parts(i))
                ]
            )

        def passed_moves(i):
            _, _, s2, _, _ = k.relay_sem[i]
            recv = k.tall_sem[i][1]
            return Moves(
                [
                    Move(
                        k.rbuf.at[:, :, w], o.tall[i].at[t, :, :, w], s2.at[j], recv.at[j, t], pc.dev(pc.p, pc.r, far),
                        None, None, both(middle_dev, cond),
                    )
                    for j, (w, at, cond) in enumerate(far_parts(i))
                ]
            )

        tall = [tall_moves(i) for i in range(3)]
        handed = [handed_moves(i) for i in range(3)]
        passed = [passed_moves(i) for i in range(3)]

        def tall_start(i):
            handed[i].start()
            tall[i].start()

        def tall_relay(i):
            handed[i].wait_recv()

            @pl.when(middle_dev)
            def _():
                copy = pltpu.make_async_copy(o.relay[i], k.rbuf, k.relay_sem[i][3].at[0])
                copy.start()
                copy.wait()

                def add(w, at):
                    def block(p, rows):
                        total = k.rbuf[p, rows, w].astype(F32) + k.near[i][0, p, rows, at].astype(F32)
                        k.rbuf[p, rows, w] = total.astype(BF)

                    row_blocks(block)

                for w, at, cond in far_parts(i):
                    Move.under(cond, lambda w=w, at=at: add(w, at))

            passed[i].start()

        def tall_sum(i):
            tall[i].wait_recv()
            local = []
            for q in others(pc.n_t, t):
                for j, (w, cond) in enumerate(((TWO, comes(q)), (ONE, comes(q) & wide))):
                    copy = pltpu.make_async_copy(
                        o.tall[i].at[q, :, :, w], k.tbuf.at[q, :, :, w], k.tall_sem[i][2].at[j, q]
                    )
                    Move.under(cond, copy.start)
                    local.append((cond, copy))
            for cond, copy in local:
                Move.under(cond, copy.wait)
            here = dst_tile(pc.p, t)

            def add(source, target):
                def block(p, at):
                    total = k.near[i][0, p, at, source].astype(F32)
                    for q in others(pc.n_t, t):
                        total = total + jnp.where(comes(q), k.tbuf[q, p, at, target].astype(F32), 0.0)
                    k.tbuf[t, p, at, target] = total.astype(BF)

                row_blocks(block)

            add(lanes(here, 2), TWO)
            pl.when(wide)(lambda: add(lanes(here + 2, 1), ONE))

        def plane_moves(i):
            send, recv = k.plane_sem[i]
            y, src = o.final[i], k.tbuf.at[pc.t]
            here = src_tile(pc.p, pc.t)
            moves = []
            for q in others(pc.n_p, pc.p):
                there = src_tile(q, pc.t)
                dev = pc.dev(q, pc.r, pc.t)
                moves.append(
                    Move(
                        src.at[q, :, TWO], y.at[:, lanes(here, 2)], send.at[0, q], recv.at[0, pc.p], dev,
                        y.at[:, lanes(there, 2)], recv.at[0, q],
                    )
                )
                moves.append(
                    Move(
                        src.at[q, :, ONE], y.at[:, lanes(here + 2, 1)], send.at[1, q], recv.at[1, pc.p], dev,
                        y.at[:, lanes(there + 2, 1)], recv.at[1, q], wide, width3(q, pc.t),
                    )
                )
            own = (
                (None, pltpu.make_async_copy(src.at[own_p, :, TWO], y.at[:, lanes(here, 2)], send.at[0, pc.p])),
                (wide, pltpu.make_async_copy(src.at[own_p, :, ONE], y.at[:, lanes(here + 2, 1)], send.at[1, pc.p])),
            )
            return Moves(moves), own

        plane = [plane_moves(i) for i in range(3)]

        def plane_start(i):
            moves, own = plane[i]
            moves.start()
            for cond, copy in own:
                Move.under(cond, copy.start)

        def plane_sent(i):
            moves, own = plane[i]
            moves.wait_send()
            for cond, copy in own:
                Move.under(cond, copy.wait)

        def head_planes(i):
            send, recv = k.plane_sem[3 + i]
            src, y = k.near[3 + i].at[0], o.head_p[i]
            return Moves(
                [
                    Move(
                        src.at[q], y.at[pc.p], send.at[0, q], recv.at[0, pc.p], pc.dev(q, pc.r, pc.t), y.at[q],
                        recv.at[0, q],
                    )
                    for q in others(pc.n_p, pc.p)
                ]
            )

        def head_talls(i):
            send, recv, _ = k.head_sem[i]
            src, y = o.head_p[i], o.head_t[i]
            return Moves(
                [
                    Move(
                        src.at[q], y.at[t], send.at[q], recv.at[t], pc.dev(pc.p, pc.r, q), y.at[q], recv.at[q],
                        direct_out(q), comes(q),
                    )
                    for q in others(pc.n_t, t)
                ]
            )

        def head_handed(i):
            s1, r1, _, _, _ = k.head_relay_sem[i]
            y = o.head_relay[i]
            return Move(
                o.head_p[i].at[far], y, s1.at[0], r1.at[0], pc.dev(pc.p, pc.r, by), y, r1.at[0], end_dev, middle_dev
            )

        def head_passed(i):
            _, _, s2, _, _ = k.head_relay_sem[i]
            recv = k.head_sem[i][1]
            return Move(
                k.hbuf[i].at[0], o.head_t[i].at[t], s2.at[0], recv.at[t], pc.dev(pc.p, pc.r, far), None, None, middle_dev
            )

        head_first = [head_handed(i) for i in range(2)]
        head_last = [head_passed(i) for i in range(2)]

        def head_start(i):
            head_first[i].start()
            head_tall[i].start()

        def head_relay(i):
            head_first[i].wait_recv()

            @pl.when(middle_dev)
            def _():
                copies = [
                    pltpu.make_async_copy(o.head_relay[i], k.hbuf[i].at[0], k.head_relay_sem[i][3].at[0]),
                    pltpu.make_async_copy(o.head_p[i].at[far], k.hbuf[i].at[1], k.head_relay_sem[i][4].at[0]),
                ]
                for copy in copies:
                    copy.start()
                for copy in copies:
                    copy.wait()
                k.hbuf[i][0] = (k.hbuf[i][0].astype(F32) + k.hbuf[i][1].astype(F32)).astype(BF)

            head_last[i].start()

        head_plane = [head_planes(i) for i in range(2)]
        head_tall = [head_talls(i) for i in range(2)]
        head_own = [
            pltpu.make_async_copy(k.near[3 + i].at[0, own_p], o.head_p[i].at[pc.p], k.head_sem[i][2].at[0])
            for i in range(2)
        ]

        def middle(m):
            rh1.wait_recv(m)

            def rows(at):
                dh1 = k.mid[m, at, :] + summed(m, at)
                a, h = k.c[m, at, :], k.tok[m, at, :].astype(F32)
                r_a = inv_rms(a)
                n_a = a * r_a
                y = h + v.rattn[...] * (n_a - h)
                r_y = inv_rms(y)
                h1 = y * r_y
                dy = r_y * (dh1 - h1 * row_mean(dh1 * h1))
                add_rows(k.grattn, dy * (n_a - h))
                k.mid[m, at, :] = (1.0 - v.rattn[...]) * dy
                dn = v.rattn[...] * dy
                k.dab[m, own_p, at, :] = (r_a * (dn - n_a * row_mean(dn * n_a))).astype(BF)

            rows_loop(part, rows)
            ag1.start(m)

        def flat(ref, at=slice(None)):
            return ref[:, :, at].reshape(all_tok, -1)

        def columns_of(ref, at):
            return ref[:, :, :, at].reshape(all_tok, CHUNK)

        def weight_grad(target, left, right):
            def block(at):
                target[at, :] = dot_tn(columns_of(left, at), flat(right)).astype(BF)

            chunks(width, block)

        score = HEAD_DIM ** (-0.5)
        blk = seq // 2

        def attend(m):
            fill_mask(k.bias, v.segq[m], v.segk[m])
            ag1.wait_recv(m)

            def project(i, carry):
                rows = k.dab[m, pl.ds(2 * i, 2)].reshape(2 * part, width)
                at = pl.ds(pl.multiple_of(i * 2 * part, 2 * part), 2 * part)
                k_do[at, :] = dot_nn(rows, k.wvo[:, QUADS:]).astype(BF)
                return carry

            lax.fori_loop(0, pc.n_p // 2, project, 0)

            def norm_grad(tile, d):
                at = tile_of(tile)
                raw = k.qk[m, :, at]
                r = lax.rsqrt(half_means(raw * raw) + EPSILON)
                n = raw * r
                d = d * score
                add_rows(k.gsqk, d * n, at)
                dy = d * k.sqk[:, at]
                k_dqk[m, :, at] = (r * (dy - n * half_means(dy * n))).astype(BF)

            for slab in range(3):
                own = tile_of(slab)
                if slab < 2:
                    q_all = k.qkb[m, :, own]
                    k_all = k.qkb[m, :, tile_of(2 + slab)]
                    do_all = k_do[:, own]
                else:
                    q_all = k.qkb[m, :, 2 * QUADS :]
                    k_all = swap_halves(q_all.astype(F32)).astype(BF)
                    do_all = swap_halves(k_do[:, own].astype(F32)).astype(BF)
                v_all = k.vb[m, :, own]
                low = low_lanes((blk, LANES))
                dq, dk, dv = [], None, None
                for i in range(2):
                    nk = (i + 1) * blk
                    at = slice(i * blk, nk)
                    bias = k.bias[at, :nk]
                    dq_i = None
                    for half in range(2 if slab < 2 else 1):
                        here = low if half == 0 else jnp.logical_not(low)
                        zero = jnp.zeros((blk, LANES), BF)
                        q1, do1 = jnp.where(here, q_all[at], zero), jnp.where(here, do_all[at], zero)
                        lse = k.lse[m, at, 2 * slab + half : 2 * slab + half + 1]
                        prob = jnp.exp(dot_nt(q1, k_all[:nk]) * score + bias - lse)
                        dp = dot_nt(do1, v_all[:nk])
                        w = prob * dp
                        ds = (w - prob * jnp.sum(w, axis=1, keepdims=True)).astype(BF)
                        y = jnp.where(here, dot_nn(ds, k_all[:nk]), 0.0)
                        dq_i = y if dq_i is None else dq_i + y
                        dk_i, dv_i = dot_tn(ds, q1), dot_tn(prob.astype(BF), do1)
                        if i == 0:
                            dk = dk_i if dk is None else dk + dk_i
                            dv = dv_i if dv is None else dv + dv_i
                        else:
                            if half == 0:
                                dk = jnp.concatenate([dk, jnp.zeros((blk, LANES), F32)], axis=0)
                                dv = jnp.concatenate([dv, jnp.zeros((blk, LANES), F32)], axis=0)
                            dk, dv = dk + dk_i, dv + dv_i
                    dq.append(dq_i)
                dq = jnp.concatenate(dq, axis=0)
                k_dv[m, :, own] = dv.astype(BF)
                if slab < 2:
                    norm_grad(slab, dq)
                    norm_grad(2 + slab, dk)
                else:
                    norm_grad(4, dq + swap_halves(dk))
            if m == 0:
                ag1.relay(1)
            else:
                rh.relay(0)
            rh1.wait_send(m)

            def columns(at):
                y = dot_nt(k_dqk[m], k.wqk[at, :])
                y = y + dot_nt(k_dv[m, :, :QUADS], k.wvo[at, :QUADS])
                y = y + dot_nt(k_dv[m, :, QUADS:], k.wvo[at, 2 * QUADS :])
                k.sent[m, :, :, at] = y.astype(BF).reshape(pc.n_p, part, CHUNK)

            chunks(width, columns)
            rh.start(m)

        def heads_grad(at):
            hb, dab = flat(k.mb, at), columns_of(k.dab, at)
            quads = slice(0, QUADS)
            rest = slice(QUADS, None)
            k.wqk[at, :] = dot_tn(hb, flat(k_dqk)).astype(BF)
            k.wvo[at, :QUADS] = dot_tn(hb, flat(k_dv, quads)).astype(BF)
            k.wvo[at, QUADS : 2 * QUADS] = dot_tn(dab, flat(k.ob, quads)).astype(BF)
            k.wvo[at, 2 * QUADS :] = (dot_tn(hb, flat(k_dv, rest)) + dot_tn(dab, flat(k.ob, rest))).astype(BF)

        def bottom(m):
            rh.wait_recv(m)

            def rows(at):
                k.mid[m, at, :] = k.mid[m, at, :] + summed(m, at)

            rows_loop(part, rows)

        def collect():
            for t in range(pc.n_t):
                for j in range(3):

                    def move(t=t, j=j):
                        here = lanes(dst_tile(pc.p, t) + j, 1)
                        row = t * tiles + src_tile(pc.p, t) + j
                        k.vec[pl.ds(row, 1), :] = k.gsup[:, here]
                        k.vec[pl.ds(vec_rows + row, 1), :] = k.gsgate[:, here]

                    Move.under(width3(pc.p, t) if j == 2 else None, move)
            at = 2 * vec_rows
            for j in range(tiles):
                k.vec[at + j : at + j + 1, :] = k.grattn[:, tile_of(j)]
                k.vec[at + tiles + j : at + tiles + j + 1, :] = k.grmlp[:, tile_of(j)]
            count = qk_cols // LANES
            for j in range(count):
                k.vec[pl.ds(at + 2 * tiles + own_p * count + j, 1), :] = k.gsqk[:, tile_of(j)]

        def vec_stage(n, count, own, dev_of):
            send, recv = k.vec_sem[n]
            buf = k.vec_got[n]
            moves = Moves(
                [
                    Move(buf.at[own], buf.at[own], send.at[q], recv.at[own], dev_of(q), buf.at[q], recv.at[q])
                    for q in others(count, own)
                ]
            )

            def start():
                buf[own] = k.vec[...]
                moves.start()

            def finish():
                moves.wait_recv()
                total = buf[0]
                for q in range(1, count):
                    total = total + buf[q]
                k.vec[...] = total

            return start, finish, moves

        vec_stages = [
            vec_stage(0, pc.n_r, pc.r, lambda q: pc.dev(pc.p, q, pc.t)),
            vec_stage(1, pc.n_t, pc.t, lambda q: pc.dev(pc.p, pc.r, q)),
            vec_stage(2, pc.n_p, pc.p, lambda q: pc.dev(q, pc.r, pc.t)),
        ]
        vec_keep = pltpu.make_async_copy(k.vec, o.vec, k.vec_out.at[0])

        ready(k.c, k.h1)
        cot_load.wait()

        def put(at, y):
            for m in range(MB):
                k.mid[m, :, at] = y[m * part : (m + 1) * part]

        take_rows(v.hot, k.dealbuf, put)
        for m in range(MB):
            top(m)
        a_load.start()
        ag.relay(0)
        h2_load.wait()
        give_rows(v.hot, lambda at: k.dab[:, own_p, :, at].reshape(MB * part, CHUNK), k.dealbuf)
        deal_out.start()
        ready(k.wdown, k.u, k.g, k.wup, k.wgate, k.sup, k.sgate)
        feed(0)
        ag.relay(1)
        feed(1)
        ready(k.mb, k.hb1)
        weight_grad(k.wdown, k.dcb, k.mb)
        near[0].start()
        hb_load.start()
        shrink(0)
        near_sum(0)
        tall_start(0)
        shrink(1)
        rh1.relay(0)
        rh1.relay(1)
        weight_grad(k.wup, k.hb1, k.u)
        near[1].start()
        ready(k.tok)
        a_load.wait()
        middle(0)
        near_sum(1)
        tall_start(1)
        weight_grad(k.wgate, k.hb1, k.g)
        near[2].start()
        middle(1)
        ag1.relay(0)
        near_sum(2)
        tall_relay(0)
        tall_start(2)
        ready(k.wvo, k.vb, k.qkb, k.lse, k.qk, k.sqk, k.wqk, k.ob)
        attend(0)
        passed[0].wait_send()
        tall_relay(1)
        attend(1)
        hb_load.wait()
        chunks(width, heads_grad)
        for i in range(2):
            near[3 + i].start()
        rh.relay(1)
        collect()
        vec_stages[0][0]()
        for i in range(2):
            near_sum(3 + i)
            head_plane[i].start()
            head_own[i].start()
        vec_stages[0][1]()
        vec_stages[1][0]()
        for m in range(MB):
            bottom(m)
        passed[1].wait_send()
        tall_relay(2)
        deal_out.wait_recv()
        deal_out.wait_send()
        give_rows(v.hot, lambda at: k.mid[:, :, at].reshape(MB * part, CHUNK).astype(BF), k.dealbuf)
        deal_grad.start()
        for i in range(2):
            head_plane[i].wait_recv()
            head_own[i].wait()
            head_start(i)
        tall_sum(0)
        plane_start(0)
        plane_sent(0)
        tall_sum(1)
        plane_start(1)
        vec_stages[1][1]()
        vec_stages[2][0]()
        for i in range(2):
            head_relay(i)
        plane_sent(1)
        tall_sum(2)
        plane_start(2)
        vec_stages[2][1]()
        vec_keep.start()
        plane_sent(2)
        passed[2].wait_send()
        for w in tall + handed + head_first + head_last + head_plane + head_tall + near + [deal_grad]:
            w.wait_send()
        for stage in vec_stages:
            stage[2].wait_send()
        for i in range(3):
            plane[i][0].wait_recv()
        for w in head_tall + [deal_grad]:
            w.wait_recv()
        vec_keep.wait()
        for m in range(MB):
            ag.wait_send(m)
            ag1.wait_send(m)
            rh.wait_send(m)

    return fused(2, kernel, near_ins, loaded | later, outs, scratch)


def merged(slots, own, at):
    total = own.astype(F32)
    for q in range(slots.shape[0]):
        total = total + jnp.where((q == at) | (jnp.abs(q - at) == 3), 0, slots[q]).astype(F32)
    return total


def pick(x, at, axis):
    return lax.dynamic_index_in_dim(x, at, axis, keepdims=False)


def mm(a, b):
    return jnp.dot(a, b, preferred_element_type=F32)


def segment_ids(lengths_row, tok_count):
    count = lengths_row.shape[0]
    upto = jnp.arange(count)[:, None] >= jnp.arange(count)[None, :]
    doc_ends = jnp.sum(jnp.where(upto, lengths_row[None, :], 0), axis=1)
    places = jnp.arange(tok_count, dtype=jnp.int32)
    return jnp.sum((places[:, None] >= doc_ends[None, :]).astype(jnp.int32), axis=1)


def packed(x, y):
    return jnp.concatenate([x[:, :QUADS], y[:, :QUADS], x[:, QUADS:], y[:, QUADS:]], axis=1)


def unpacked(z):
    mid = 2 * QUADS + HEAD_DIM
    return (
        jnp.concatenate([z[..., :QUADS], z[..., 2 * QUADS : mid]], axis=-1),
        jnp.concatenate([z[..., QUADS : 2 * QUADS], z[..., mid:]], axis=-1),
    )


def body(
    tokens,
    cotangent,
    slot,
    lengths,
    w_query,
    w_key,
    w_value,
    w_out,
    w_up,
    w_gate,
    w_down,
    scale_qk,
    scale_up,
    scale_gate,
    rate_attn,
    rate_mlp,
):
    pc = Place()
    n_p, n_r, n_t, n_dev = pc.n_p, pc.n_r, pc.n_t, pc.n_dev
    rows_dev, width = tokens.shape
    tok_count = rows_dev // MB * n_p
    head_cols = w_query.shape[2]
    hid = w_up.shape[2]
    tiles = hid // LANES
    group = pc.r * n_t + pc.t
    owner = group * n_p + pc.p
    if rows_dev // n_dev > PAD or head_cols != QUADS + HEAD_DIM:
        raise ValueError("sizes")

    table = slot.reshape(n_dev, rows_dev)
    own_slots = lax.dynamic_index_in_dim(table, pc.me, 0, keepdims=False)
    d = own_slots // rows_dev
    to_dev = ((d % n_p) * n_r + (d // n_p) // n_t) * n_t + (d // n_p) % n_t
    places = jnp.arange(rows_dev, dtype=jnp.int32)
    spots = jnp.arange(n_dev * PAD, dtype=jnp.int32)
    before = (d[:, None] == d[None, :]) & (places[None, :] < places[:, None])
    rank = jnp.sum(before.astype(jnp.int32), axis=1)
    send_hot = (spots[:, None] == (to_dev * PAD + rank)[None, :]).astype(BF)

    sel = table // rows_dev == owner
    tri = (places[:, None] < places[None, :]).astype(BF)
    ranks = mm(sel.astype(BF), tri).astype(jnp.int32)
    kth = sel[:, None, :] & (ranks[:, None, :] == jnp.arange(PAD, dtype=jnp.int32)[None, :, None])
    owner_rows = jnp.sum(jnp.where(kth, (table - owner * rows_dev + 1)[:, None, :], 0), axis=2).reshape(-1) - 1
    recv_hot = (places[:, None] == owner_rows[None, :]).astype(BF)

    def to_send(x):
        return mm(send_hot, x).astype(BF).reshape(n_dev, PAD, width)

    qk_scale = packed(scale_qk, scale_qk).reshape(-1, LANES)
    small = jnp.concatenate([scale_up.reshape(-1, LANES), scale_gate.reshape(-1, LANES), qk_scale])
    small = jnp.pad(small, ((0, -small.shape[0] % 8), (0, 0)))
    own_lengths = lax.dynamic_slice_in_dim(lengths, group * MB, MB, 0)
    segments = jnp.stack([segment_ids(own_lengths[m], tok_count) for m in range(MB)])
    shared = (recv_hot, rate_attn, rate_mlp, segments[:, :, None], segments[:, None, :])

    f = forward(
        pc,
        to_send(tokens),
        to_send(cotangent),
        packed(w_query[0], w_key[0]),
        packed(w_value[0], w_out[0]),
        w_up[0],
        w_gate[0],
        w_down[0],
        small,
        *shared,
    )
    b = backward(pc, f, *shared)

    vec = b.vec
    at = n_t * tiles

    def own_row(x):
        return lax.dynamic_index_in_dim(x.reshape(n_t, -1), pc.t, 0)

    qk_rows = qk_scale.shape[0]
    out_sup, out_sgate = own_row(vec[:at]), own_row(vec[at : 2 * at])
    at = 2 * at
    out_rattn, out_rmlp = vec[at : at + tiles].reshape(1, -1), vec[at + tiles : at + 2 * tiles].reshape(1, -1)
    at = at + 2 * tiles
    out_sqk = sum(unpacked(own_row(vec[at : at + n_t * qk_rows])))
    heads = [
        x[None]
        for got, sent in zip(b.head_t, b.head_p)
        for x in unpacked(merged(got, pick(sent, pc.t, 0), pc.t))
    ]

    def from_back(x):
        return lax.dot_general(
            send_hot, x.reshape(-1, width), (((0,), (0,)), ((), ())), preferred_element_type=F32
        )

    down, up, gate = (x.astype(F32)[None] for x in b.final)
    return (
        from_back(b.back_out),
        from_back(b.back_grad),
        *heads,
        up,
        gate,
        down,
        out_sqk,
        out_sup,
        out_sgate,
        out_rattn,
        out_rmlp,
    )


def solution(mesh):
    tok = P(("dp", "tensor"), None)
    mat = P(None, "dp", "tensor")
    vec = P(None, "tensor")
    in_specs = (tok, tok, P(), P()) + (mat,) * 7 + (vec,) * 3 + (P(), P())
    out_specs = (tok, tok) + (mat,) * 7 + (vec,) * 3 + (P(), P())
    return jax.shard_map(body, mesh=mesh, in_specs=in_specs, out_specs=out_specs, check_vma=False)
```

```python
import types

import jax
import jax.numpy as jnp
from jax import lax
from jax.experimental import pallas as pl
from jax.experimental.pallas import tpu as pltpu
from jax.sharding import PartitionSpec as P

HEAD_DIM = 64
MB = 2
LANES = 128
QUADS = 4 * HEAD_DIM
CHUNK = 2 * LANES
ROW_STEP = 32
PAD = 8
VMEM_LIMIT = 127 * 2**19

EPSILON = 1e-06
MASKED = -1e30
BF = jnp.bfloat16
F32 = jnp.float32
MESH = pl.DeviceIdType.MESH
VM = pltpu.VMEM
DMA = pltpu.SemaphoreType.DMA
SDS = jax.ShapeDtypeStruct


class Place:
    def __init__(self):
        self.n_t = lax.axis_size("tensor")
        self.n_dp = lax.axis_size("dp")
        self.n_p = self.n_t
        self.n_r = self.n_dp // self.n_p
        self.n_dev = self.n_dp * self.n_t
        if self.n_t != 4:
            raise ValueError("tensor size")
        dp = lax.axis_index("dp")
        self.t = lax.axis_index("tensor")
        self.p = dp // self.n_r
        self.r = dp % self.n_r
        self.me = dp * self.n_t + self.t

    def dev(self, p, r, t):
        return (p * self.n_r + r, t)

    def flat(self, j):
        return (j // self.n_t, j % self.n_t)


def width3(p, t):
    return (p + t) % 2 == 0


def src_tile(p, t):
    return 5 * (p // 2) + (p % 2) * (3 - t % 2)


def dst_tile(p, t):
    return 5 * (t // 2) + (t % 2) * (3 - p % 2)


def lanes(tile, count):
    return pl.ds(pl.multiple_of(tile * LANES, LANES), count * LANES)


TWO, ONE = pl.ds(0, 2 * LANES), pl.ds(2 * LANES, LANES)


def remote(src, dst, send, recv, dev):
    return pltpu.make_async_remote_copy(
        src_ref=src, dst_ref=dst, send_sem=send, recv_sem=recv, device_id=dev, device_id_type=MESH
    )


class Move:
    def __init__(self, src, dst, send, recv, dev, landing, landed, cond_out=None, cond_in=None):
        self.going = (src, dst, send, recv, dev)
        self.coming = (landing, landing, send, landed, dev)
        self.cond_out, self.cond_in = cond_out, cond_in

    @staticmethod
    def under(cond, act):
        if cond is None:
            act()
        else:
            pl.when(cond)(act)

    def start(self):
        self.under(self.cond_out, lambda: remote(*self.going).start())

    def wait_send(self):
        self.under(self.cond_out, lambda: remote(*self.going).wait_send())

    def wait_recv(self):
        self.under(self.cond_in, lambda: remote(*self.coming).wait_recv())


class Moves:
    def __init__(self, moves):
        self.moves = moves

    def start(self):
        for m in self.moves:
            m.start()

    def wait_recv(self):
        for m in self.moves:
            m.wait_recv()

    def wait_send(self):
        for m in self.moves:
            m.wait_send()


def others(count, own):
    order = [2, 1, 3] if count == 4 else list(range(1, count))
    return [(own + k) % count for k in order]


def pair(n):
    return [DMA((n,)), DMA((n,))]


class Deal:
    @staticmethod
    def sems(pc):
        return [DMA((1,)), DMA((1,)), DMA((1,))]

    def __init__(self, pc, x, y, sems):
        self.pc, self.x, self.y = pc, x, y
        self.send, self.recv, self.local = (sem.at[0] for sem in sems)

    def copy(self, j, src, dst):
        return remote(src, dst, self.send, self.recv, self.pc.flat(j))

    def own(self):
        return pltpu.make_async_copy(self.x.at[self.pc.me], self.y.at[self.pc.me], self.local)

    def start(self):
        pc = self.pc

        def step(i, carry):
            j = (pc.me + i) % pc.n_dev
            self.copy(j, self.x.at[j], self.y.at[pc.me]).start()
            return carry

        lax.fori_loop(1, pc.n_dev, step, 0)
        self.own().start()

    def all_but_own(self):
        part = self.y.at[pl.ds(0, self.pc.n_dev - 1)]
        return self.copy((self.pc.me + 1) % self.pc.n_dev, part, part)

    def wait_recv(self):
        self.own().wait()
        self.all_but_own().wait_recv()

    def wait_send(self):
        self.all_but_own().wait_send()


class Tall:
    @staticmethod
    def sems(pc, pieces):
        return [DMA((pieces, pc.n_t + 1)), DMA((pieces, pc.n_t))]

    def __init__(self, pc, shard, own, sems):
        t = pc.t
        middle = (t == 1) | (t == 2)
        far, end = jnp.where(t == 2, 0, 3), jnp.where(t == 2, 3, 0)
        send, recv = sems

        def both(a, b):
            return a if b is None else a & b

        self.first, self.passed = [], []
        for q in others(pc.n_t, t):
            for i, ((dst, c_out), src, (here, c_in)) in enumerate(zip(shard(t), own, shard(q))):
                args = (src, dst, send.at[i, q], recv.at[i, t], pc.dev(pc.p, pc.r, q), here, recv.at[i, q])
                c_in = both(jnp.logical_not(middle & (q == far)), c_in)
                self.first.append(Move(*args, both(jnp.abs(q - t) != 3, c_out), c_in))
        for i, (ref, c) in enumerate(shard(far)):
            self.passed.append(
                Move(
                    ref, ref, send.at[i, pc.n_t], recv.at[i, far], pc.dev(pc.p, pc.r, end), ref, recv.at[i, far],
                    both(middle, c), both(middle, c),
                )
            )

    def start(self):
        for m in self.first:
            m.start()

    def relay(self):
        for m in self.passed:
            m.wait_recv()
            m.start()

    def wait_recv(self):
        for m in self.first:
            m.wait_recv()

    def wait_send(self):
        for m in self.first + self.passed:
            m.wait_send()


def by_shard(pc, ref):
    return ref.reshape(pc.n_p, pc.n_r, ref.shape[0] // (pc.n_p * pc.n_r), ref.shape[1])


class HeadWeights:
    @staticmethod
    def sems(pc):
        return [Tall.sems(pc, 1), pair(pc.n_p), pair(pc.n_r), DMA((2,))]

    def __init__(self, pc, x, a, w, sems):
        tall, (s2, r2), (s3, r3), ls = sems
        f = by_shard(pc, w)
        self.first = Tall(pc, lambda q: [(a.at[q], None)], [x], tall)
        self.second = Moves(
            [
                Move(a.at[q], f.at[pc.p, pc.r], s2.at[q], r2.at[pc.p], pc.dev(q, pc.r, pc.t), f.at[q, pc.r], r2.at[q])
                for q in others(pc.n_p, pc.p)
            ]
        )
        self.third = Moves(
            [
                Move(f.at[:, pc.r], f.at[:, pc.r], s3.at[q], r3.at[pc.r], pc.dev(pc.p, q, pc.t), f.at[:, q], r3.at[q])
                for q in others(pc.n_r, pc.r)
            ]
        )
        self.keep1 = pltpu.make_async_copy(x, a.at[pc.t], ls.at[0])
        self.keep2 = pltpu.make_async_copy(a.at[pc.p], f.at[pc.p, pc.r], ls.at[1])

    def start(self):
        self.first.start()
        self.keep1.start()

    def relay(self):
        self.first.relay()

    def plane(self):
        self.keep1.wait()
        self.first.wait_recv()
        self.second.start()
        self.keep2.start()

    def near(self):
        self.keep2.wait()
        self.second.wait_recv()
        self.third.start()

    def wait_recv(self):
        self.third.wait_recv()

    def wait_send(self):
        self.first.wait_send()
        self.second.wait_send()
        self.third.wait_send()


class HiddenWeights:
    @staticmethod
    def sems(pc):
        return [pair(pc.n_p), pair(pc.n_p), Tall.sems(pc, 2), pair(pc.n_r), DMA((2,))]

    def __init__(self, pc, x, w, sems):
        (s1, r1), (s2, r2), tall, (s3, r3), ls = sems
        g = by_shard(pc, w)
        p, r, t = pc.p, pc.r, pc.t

        def spot(q, row, extra):
            at = dst_tile(q, t)
            return g.at[row, r, :, lanes(at + 2, 1) if extra else lanes(at, 2)]

        def piece(q, extra):
            at = src_tile(q, t)
            return x.at[:, lanes(at + 2, 1) if extra else lanes(at, 2)]

        moves = []
        for q in others(pc.n_p, p):
            dev = pc.dev(q, r, t)
            moves.append(
                Move(piece(q, False), spot(q, p, False), s1.at[q], r1.at[p], dev, spot(p, q, False), r1.at[q])
            )
            moves.append(
                Move(
                    piece(q, True), spot(q, p, True), s2.at[q], r2.at[p], dev, spot(p, q, True), r2.at[q],
                    width3(q, t), width3(p, t),
                )
            )
        self.first = Moves(moves)
        self.own = [
            (None, pltpu.make_async_copy(piece(p, False), spot(p, p, False), ls.at[0])),
            (width3(p, t), pltpu.make_async_copy(piece(p, True), spot(p, p, True), ls.at[1])),
        ]

        def shard(q):
            at = dst_tile(p, q)
            return [(g.at[:, r, :, lanes(at, 2)], None), (g.at[:, r, :, lanes(at + 2, 1)], width3(p, q))]

        self.second = Tall(pc, shard, [ref for ref, _ in shard(t)], tall)
        self.third = Moves(
            [
                Move(g.at[:, r], g.at[:, r], s3.at[q], r3.at[r], pc.dev(p, q, t), g.at[:, q], r3.at[q])
                for q in others(pc.n_r, r)
            ]
        )

    def start(self):
        self.first.start()
        for cond, copy in self.own:
            Move.under(cond, copy.start)

    def tall(self):
        for cond, copy in self.own:
            Move.under(cond, copy.wait)
        self.first.wait_recv()
        self.second.start()

    def relay(self):
        self.second.relay()

    def near(self):
        self.second.wait_recv()
        self.third.start()

    def wait_recv(self):
        self.third.wait_recv()

    def wait_send(self):
        self.first.wait_send()
        self.second.wait_send()
        self.third.wait_send()


def add_into(target, term, rows):
    step = rows // 2

    def block(i, carry):
        at = pl.ds(pl.multiple_of(i * step, step), step)
        target[at, :] = (target[at, :].astype(F32) + term[at, :].astype(F32)).astype(BF)
        return carry

    lax.fori_loop(0, 2, block, 0)


class Plane:
    def __init__(self, pc):
        self.x, self.y, self.d = pc.p + 1 - 2 * (pc.p % 2), (pc.p + 2) % 4, 3 - pc.p
        self.to_x, self.to_y = pc.dev(self.x, pc.r, pc.t), pc.dev(self.y, pc.r, pc.t)

    def halves(self, ref):
        half = ref.shape[0] // 2
        return ref.at[pl.ds(0, half)], ref.at[pl.ds(half, half)]

    def wait_send(self, m):
        for move in self.first[m] + self.second[m]:
            move.wait_send()


class PlaneGather(Plane):
    @staticmethod
    def sems(pc):
        return [DMA((MB, 4)), DMA((MB, 4))]

    def __init__(self, pc, spot, sems):
        super().__init__(pc)
        send, recv = sems
        self.first, self.second = [], []
        for m in range(MB):
            own, from_x, from_y = spot(m, pc.p), spot(m, self.x), spot(m, self.y)
            (a, _), (_, b), (here_a, here_b) = self.halves(from_x), self.halves(from_y), self.halves(spot(m, self.d))
            self.first.append(
                [
                    Move(own, own, send.at[m, 0], recv.at[m, 0], self.to_x, from_x, recv.at[m, 0]),
                    Move(own, own, send.at[m, 1], recv.at[m, 1], self.to_y, from_y, recv.at[m, 1]),
                ]
            )
            self.second.append(
                [
                    Move(a, a, send.at[m, 2], recv.at[m, 2], self.to_y, here_a, recv.at[m, 2]),
                    Move(b, b, send.at[m, 3], recv.at[m, 3], self.to_x, here_b, recv.at[m, 3]),
                ]
            )

    def start(self, m):
        for move in self.first[m]:
            move.start()

    def relay(self, m):
        for arrived, move in zip(self.first[m], self.second[m]):
            arrived.wait_recv()
            move.start()

    def wait_recv(self, m):
        for move in self.second[m]:
            move.wait_recv()


class PlaneScatter(Plane):
    @staticmethod
    def sems(pc):
        return [DMA((MB, 6)), DMA((MB, 6))]

    def __init__(self, pc, sent, got, sems):
        super().__init__(pc)
        send, recv = sems
        self.first, self.second, self.adds = [], [], []
        for m in range(MB):

            def move(i, src, dst, dev, landing):
                return Move(src, dst, send.at[m, i], recv.at[m, i], dev, landing, recv.at[m, i])

            for_x, for_y, for_d = (self.halves(sent.at[m, q]) for q in (self.x, self.y, self.d))
            hop = self.halves(got.at[pc.p, m])
            hop_x, hop_y = self.halves(got.at[self.x, m]), self.halves(got.at[self.y, m])
            mine = hop
            self.first.append(
                [
                    move(0, for_d[0], hop_x[0], self.to_x, hop[0]),
                    move(1, for_d[1], hop_y[1], self.to_y, hop[1]),
                    move(2, for_x[0], mine[0], self.to_x, hop_x[0]),
                    move(3, for_y[1], mine[1], self.to_y, hop_y[1]),
                ]
            )
            self.second.append(
                [
                    move(5, for_y[0], mine[0], self.to_y, hop_y[0]),
                    move(4, for_x[1], mine[1], self.to_x, hop_x[1]),
                ]
            )
            self.adds.append([(for_y[0], hop[0]), (for_x[1], hop[1])])

    def start(self, m):
        for move in self.first[m]:
            move.start()

    def relay(self, m):
        for arrived, (target, term), move in zip(self.first[m], self.adds[m], self.second[m]):
            arrived.wait_recv()
            add_into(target, term, target.shape[0])
            move.start()

    def wait_recv(self, m):
        for move in self.first[m][2:] + self.second[m]:
            move.wait_recv()


def plane_sum(pc, sent, got, m, at):
    total = sent[m, pc.p, at, :].astype(F32)
    for q in (pc.p + 1 - 2 * (pc.p % 2), (pc.p + 2) % 4):
        total = total + got[q, m, at, :].astype(F32)
    return total


def greet(pc):
    barrier = pltpu.get_barrier_semaphore()

    def step(i, carry):
        dev = pc.flat((pc.me + i) % pc.n_dev)
        pl.semaphore_signal(barrier, inc=1, device_id=dev, device_id_type=MESH)
        return carry

    lax.fori_loop(1, pc.n_dev, step, 0)
    pl.semaphore_wait(barrier, pc.n_dev - 1)


def fused(collective_id, kernel, near_ins, far_ins, outs, scratch):
    ins_leaves, ins_tree = jax.tree.flatten((near_ins, far_ins))
    outs_leaves, outs_tree = jax.tree.flatten(outs)
    scratch_leaves, scratch_tree = jax.tree.flatten(scratch)
    a, b = len(ins_leaves), len(outs_leaves)
    near = len(jax.tree.leaves(near_ins))

    def run(*refs):
        first, second = jax.tree.unflatten(ins_tree, refs[:a])
        third = jax.tree.unflatten(outs_tree, refs[a : a + b])
        fourth = jax.tree.unflatten(scratch_tree, refs[a + b :])
        kernel(
            Place(),
            types.SimpleNamespace(**first),
            types.SimpleNamespace(**second),
            types.SimpleNamespace(**third),
            types.SimpleNamespace(**fourth),
        )

    got = pl.pallas_call(
        run,
        out_shape=tuple(outs_leaves),
        in_specs=[pl.BlockSpec(memory_space=VM if i < near else pl.ANY) for i in range(a)],
        out_specs=tuple([pl.BlockSpec(memory_space=pl.ANY)] * b),
        scratch_shapes=scratch_leaves,
        compiler_params=pltpu.CompilerParams(
            collective_id=collective_id, has_side_effects=True, vmem_limit_bytes=VMEM_LIMIT
        ),
    )(*ins_leaves)
    return types.SimpleNamespace(**jax.tree.unflatten(outs_tree, got))


def dot_nt(a, b):
    return lax.dot_general(a, b, (((1,), (1,)), ((), ())), preferred_element_type=F32)


def dot_tn(a, b):
    return lax.dot_general(a, b, (((0,), (0,)), ((), ())), preferred_element_type=F32)


def dot_nn(a, b):
    return lax.dot_general(a, b, (((1,), (0,)), ((), ())), preferred_element_type=F32)


def half_means(x):
    a = lax.broadcasted_iota(jnp.int32, (LANES, LANES), 0) // HEAD_DIM
    b = lax.broadcasted_iota(jnp.int32, (LANES, LANES), 1) // HEAD_DIM
    same = jnp.where(a == b, 1.0 / HEAD_DIM, 0.0).astype(F32)
    return lax.dot_general(x, same, (((1,), (0,)), ((), ())), precision=lax.Precision.HIGHEST, preferred_element_type=F32)


def swap_halves(x):
    return pltpu.roll(x, HEAD_DIM, 1)


def low_lanes(shape):
    return lax.broadcasted_iota(jnp.int32, shape, len(shape) - 1) < HEAD_DIM


def row_mean(x):
    return jnp.mean(x, axis=-1, keepdims=True)


def inv_rms(x):
    return lax.rsqrt(row_mean(x * x) + EPSILON)


def tile_of(j):
    return slice(j * LANES, (j + 1) * LANES)


def rows_loop(count, fn):
    def step(i, carry):
        fn(pl.ds(pl.multiple_of(i * ROW_STEP, ROW_STEP), ROW_STEP))
        return carry

    lax.fori_loop(0, count // ROW_STEP, step, 0)


def chunks(count, fn):
    def step(c, carry):
        fn(pl.ds(pl.multiple_of(c * CHUNK, CHUNK), CHUNK))
        return carry

    lax.fori_loop(0, count // CHUNK, step, 0)


def take_rows(hot, arrived, put):
    def block(at):
        x = arrived[:, :, at].astype(F32).reshape(-1, CHUNK).astype(BF)
        put(at, dot_nn(hot[...], x))

    chunks(arrived.shape[2], block)


def give_rows(hot, rows, out):
    def block(at):
        y = dot_tn(hot[...], rows(at))
        out[:, :, at] = y.reshape(out.shape[0], PAD, CHUNK).astype(BF)

    chunks(out.shape[2], block)


def fill_mask(bias, segq, segk):
    seq = bias.shape[0]
    rows = lax.broadcasted_iota(jnp.int32, (seq, seq), 0)
    cols = lax.broadcasted_iota(jnp.int32, (seq, seq), 1)
    bias[...] = jnp.where((segq == segk) & (cols <= rows), 0.0, MASKED)


def forward(pc, tok_sent, cot_sent, wqk, wvo, wup, wgate, wdown, small, hot, rattn, rmlp, segq, segk):
    n_dev, _, width = tok_sent.shape
    part = hot.shape[0] // MB
    seq = part * pc.n_p
    qk_cols, vo_cols, hid = wqk.shape[1], wvo.shape[1], wup.shape[1]
    o_cols = QUADS + LANES
    tiles = hid // LANES
    blocks = (MB, pc.n_p, part, width)
    kept = dict(
        hb=(blocks, BF),
        qk=((MB, seq, qk_cols), F32),
        qkb=((MB, seq, qk_cols), BF),
        vb=((MB, seq, o_cols), BF),
        ob=((MB, seq, o_cols), BF),
        lse=((MB, seq, LANES), F32),
        tok=((MB, part, width), BF),
        a=((MB, part, width), F32),
        h1=((MB, part, width), F32),
        c=((MB, part, width), F32),
        hb1=(blocks, BF),
        u=((MB, seq, hid), BF),
        g=((MB, seq, hid), BF),
        mb=((MB, seq, hid), BF),
        h2=((MB, part, width), BF),
    )
    whole = dict(
        wqk=((width, qk_cols), BF),
        wvo=((width, vo_cols), BF),
        wup=((width, hid), BF),
        wgate=((width, hid), BF),
        wdown=((width, hid), BF),
        sup=((1, hid), F32),
        sgate=((1, hid), F32),
        sqk=((1, qk_cols), F32),
    )
    outs = {n: SDS(*x) for n, x in (kept | whole).items()} | dict(cot=SDS(cot_sent.shape, BF))
    scratch = {n: VM(*x) for n, x in (kept | whole).items()} | dict(
        arrived=VM(tok_sent.shape, BF),
        aqk=VM((pc.n_t,) + wqk.shape, BF),
        avo=VM((pc.n_t,) + wvo.shape, BF),
        small=VM((pc.n_t,) + small.shape, F32),
        bias=VM((seq, seq), F32),
        sent=VM(blocks, BF),
        got=VM((pc.n_p, MB, part, width), BF),
        kept_sem={n: DMA((MB,)) for n in kept},
        whole_sem={n: DMA((1,)) for n in whole},
        tok_sem=Deal.sems(pc),
        cot_sem=Deal.sems(pc),
        small_sem=pair(pc.n_t) + [DMA((1,))],
        qk_sem=HeadWeights.sems(pc),
        vo_sem=HeadWeights.sems(pc),
        up_sem=HiddenWeights.sems(pc),
        gate_sem=HiddenWeights.sems(pc),
        down_sem=HiddenWeights.sems(pc),
        ag_sem=PlaneGather.sems(pc),
        ra_sem=PlaneScatter.sems(pc),
        ag1_sem=PlaneGather.sems(pc),
        rc_sem=PlaneScatter.sems(pc),
    )
    near_ins = dict(hot=hot, rattn=rattn, rmlp=rmlp, segq=segq, segk=segk)
    far_ins = dict(
        tok=tok_sent, cot=cot_sent, wqk=wqk, wvo=wvo, wup=wup, wgate=wgate, wdown=wdown, small=small
    )

    def kernel(pc, v, x, o, k):
        own_p = pc.p
        greet(pc)
        deal = Deal(pc, x.tok, k.arrived, k.tok_sem)
        deal_cot = Deal(pc, x.cot, o.cot, k.cot_sem)
        head_qk = HeadWeights(pc, x.wqk, k.aqk, k.wqk, k.qk_sem)
        head_vo = HeadWeights(pc, x.wvo, k.avo, k.wvo, k.vo_sem)
        up = HiddenWeights(pc, x.wup, k.wup, k.up_sem)
        gate = HiddenWeights(pc, x.wgate, k.wgate, k.gate_sem)
        down = HiddenWeights(pc, x.wdown, k.wdown, k.down_sem)
        ss, rs, ls = k.small_sem
        scales = Moves(
            [
                Move(
                    x.small, k.small.at[pc.t], ss.at[q], rs.at[pc.t], pc.dev(pc.p, pc.r, q), k.small.at[q], rs.at[q]
                )
                for q in others(pc.n_t, pc.t)
            ]
        )
        own_scales = pltpu.make_async_copy(x.small, k.small.at[pc.t], ls.at[0])

        def gather(buf, sems):
            return PlaneGather(pc, lambda m, q: buf.at[m, q], sems)

        ag, ag1 = gather(k.hb, k.ag_sem), gather(k.hb1, k.ag1_sem)
        ra, rc = (PlaneScatter(pc, k.sent, k.got, sems) for sems in (k.ra_sem, k.rc_sem))
        names = vars(k)
        out_names = vars(o)
        copies = []

        def keep(m, *refs):
            for n in kept:
                if any(names[n] is ref for ref in refs):
                    copy = pltpu.make_async_copy(names[n].at[m], out_names[n].at[m], k.kept_sem[n].at[m])
                    copy.start()
                    copies.append(copy)

        def keep_whole(*refs):
            for n in whole:
                if any(names[n] is ref for ref in refs):
                    copy = pltpu.make_async_copy(names[n], out_names[n], k.whole_sem[n].at[0])
                    copy.start()
                    copies.append(copy)

        def attend(m):
            fill_mask(k.bias, v.segq[m], v.segk[m])
            ag.wait_recv(m)
            keep(m, k.hb)

            def project(i, carry):
                rows = k.hb[m, pl.ds(2 * i, 2)].reshape(2 * part, width)
                at = pl.ds(pl.multiple_of(i * 2 * part, 2 * part), 2 * part)
                qk = dot_nn(rows, k.wqk[...])
                k.qk[m, at, :] = qk
                for j in range(qk_cols // LANES):
                    s = qk[:, tile_of(j)]
                    n = s * lax.rsqrt(half_means(s * s) + EPSILON)
                    k.qkb[m, at, tile_of(j)] = (n * k.sqk[:, tile_of(j)]).astype(BF)
                k.vb[m, at, :QUADS] = dot_nn(rows, k.wvo[:, :QUADS]).astype(BF)
                last = dot_nn(rows, k.wvo[:, 2 * QUADS :])
                k.vb[m, at, QUADS:] = jnp.where(low_lanes(last.shape), last, 0.0).astype(BF)
                return carry

            lax.fori_loop(0, pc.n_p // 2, project, 0)
            keep(m, k.qk, k.qkb, k.vb)
            if m == 1:
                ra.relay(0)
            else:
                ag.relay(1)
            blk = seq // 2
            for i in range(2):
                nk = (i + 1) * blk
                at = slice(i * blk, nk)
                bias = k.bias[at, :nk]
                lse = jnp.zeros((blk, LANES), F32)
                lane = lax.broadcasted_iota(jnp.int32, (blk, LANES), 1)
                for slab in range(3):
                    if slab < 2:
                        qs = k.qkb[m, at, tile_of(slab)]
                        ks = k.qkb[m, :nk, tile_of(2 + slab)]
                    else:
                        qs = k.qkb[m, at, 2 * QUADS :]
                        ks = swap_halves(k.qkb[m, :nk, 2 * QUADS :].astype(F32)).astype(BF)
                    vs = k.vb[m, :nk, tile_of(slab)]
                    res = []
                    for half in range(2 if slab < 2 else 1):
                        low = low_lanes(qs.shape)
                        q1 = jnp.where(low if half == 0 else jnp.logical_not(low), qs, jnp.zeros_like(qs))
                        s = dot_nt(q1, ks) * HEAD_DIM ** (-0.5) + bias
                        top = jnp.max(s, axis=1, keepdims=True)
                        e = jnp.exp(s - top)
                        tot = jnp.sum(e, axis=1, keepdims=True)
                        lse = jnp.where(lane == 2 * slab + half, top + jnp.log(tot), lse)
                        res.append(dot_nn((e * (1.0 / tot)).astype(BF), vs))
                    if slab < 2:
                        res = jnp.where(low_lanes(res[0].shape), res[0], res[1])
                    else:
                        res = swap_halves(res[0])
                    k.ob[m, at, tile_of(slab)] = res.astype(BF)
                k.lse[m, at, :] = lse
            keep(m, k.ob, k.lse)

            def branch(i, carry):
                at = pl.ds(pl.multiple_of(i * 2 * part, 2 * part), 2 * part)
                y = dot_nt(k.ob[m, at, :], k.wvo[:, QUADS:])
                k.sent[m, pl.ds(2 * i, 2)] = y.astype(BF).reshape(2, part, width)
                return carry

            lax.fori_loop(0, pc.n_p // 2, branch, 0)
            ra.start(m)

        def summed(m, at):
            return plane_sum(pc, k.sent, k.got, m, at)

        def middle(m):
            ra.wait_recv(m)

            def rows(at):
                a = summed(m, at)
                h = k.tok[m, at, :].astype(F32)
                y = h + v.rattn[...] * (a * inv_rms(a) - h)
                h1 = y * inv_rms(y)
                k.a[m, at, :] = a
                k.h1[m, at, :] = h1
                k.hb1[m, own_p, at, :] = h1.astype(BF)

            rows_loop(part, rows)
            ag1.start(m)
            keep(m, k.a, k.h1)

        def feed(m):
            ag1.wait_recv(m)
            keep(m, k.hb1)

            def hidden(at):
                rows = k.hb1[m].reshape(seq, width)
                u = dot_nn(rows, k.wup[:, at])
                g = dot_nn(rows, k.wgate[:, at])
                k.u[m, :, at] = u.astype(BF)
                k.g[m, :, at] = g.astype(BF)
                z = k.sgate[:, at] * g
                k.mb[m, :, at] = (z / (1.0 + jnp.exp(-z)) * (k.sup[:, at] * u)).astype(BF)

            chunks(hid, hidden)
            keep(m, k.u, k.g, k.mb)

        def shrink(m):
            ra.wait_send(m)

            def columns(at):
                y = dot_nt(k.mb[m], k.wdown[at, :])
                k.sent[m, :, :, at] = y.astype(BF).reshape(pc.n_p, part, CHUNK)

            chunks(width, columns)
            rc.start(m)

        def finish(m):
            rc.wait_recv(m)

            def rows(at):
                c = summed(m, at)
                h1 = k.h1[m, at, :]
                z = h1 + v.rmlp[...] * (c * inv_rms(c) - h1)
                k.c[m, at, :] = c
                k.h2[m, at, :] = (z * inv_rms(z)).astype(BF)

            rows_loop(part, rows)
            keep(m, k.c, k.h2)

        deal.start()
        head_qk.start()
        head_vo.start()
        scales.start()
        own_scales.start()
        for w in (up, gate, down):
            w.start()
        head_qk.relay()
        head_vo.relay()
        deal.wait_recv()

        def put(at, y):
            for m in range(MB):
                rows = y[m * part : (m + 1) * part].astype(BF)
                k.tok[m, :, at] = rows
                k.hb[m, own_p, :, at] = rows

        take_rows(v.hot, k.arrived, put)
        for m in range(MB):
            ag.start(m)
            keep(m, k.tok)
        head_qk.plane()
        head_vo.plane()
        up.tall()
        gate.tall()
        own_scales.wait()
        scales.wait_recv()
        for t in range(pc.n_t):
            for j in range(3):

                def move(t=t, j=j):
                    at = lanes(dst_tile(pc.p, t) + j, 1)
                    k.sup[:, at] = k.small[t, pl.ds(src_tile(pc.p, t) + j, 1), :]
                    k.sgate[:, at] = k.small[t, pl.ds(tiles + src_tile(pc.p, t) + j, 1), :]

                Move.under(width3(pc.p, t) if j == 2 else None, move)
        for j in range(qk_cols // LANES):
            k.sqk[:, tile_of(j)] = k.small[own_p, 2 * tiles + j : 2 * tiles + j + 1, :]
        keep_whole(k.sup, k.sgate, k.sqk)
        head_qk.near()
        head_vo.near()
        head_qk.wait_recv()
        head_vo.wait_recv()
        keep_whole(k.wqk, k.wvo)
        ag.relay(0)
        attend(0)
        down.tall()
        attend(1)
        up.relay()
        gate.relay()
        middle(0)
        ra.relay(1)
        middle(1)
        ag1.relay(0)
        up.near()
        gate.near()
        ag1.relay(1)
        up.wait_recv()
        gate.wait_recv()
        down.relay()
        feed(0)
        keep_whole(k.wup, k.wgate)
        feed(1)
        down.near()
        down.wait_recv()
        deal_cot.start()
        shrink(0)
        rc.relay(0)
        keep_whole(k.wdown)
        shrink(1)
        rc.relay(1)
        for m in range(MB):
            finish(m)
        deal_cot.wait_recv()
        for w in (deal, deal_cot, head_qk, head_vo, up, gate, down, scales):
            w.wait_send()
        for m in range(MB):
            for w in (ag, ag1, rc):
                w.wait_send(m)
        for copy in copies:
            copy.wait()

    return fused(1, kernel, near_ins, far_ins, outs, scratch)


def backward(pc, f, hot, rattn, rmlp, segq, segk):
    n_dev = f.cot.shape[0]
    part, width = f.h2.shape[1], f.h2.shape[2]
    seq = part * pc.n_p
    all_tok = MB * seq
    qk_cols, hid = f.wqk.shape[1], f.wup.shape[1]
    o_cols = QUADS + LANES
    tiles = hid // LANES
    n_rows = width // (pc.n_p * pc.n_r)
    step_rows = n_rows // 5
    if n_rows % 5 or hid != width:
        raise ValueError("sizes")
    blocks = (MB, pc.n_p, part, width)
    dealt = (n_dev, PAD, width)
    vec_rows = 4 * tiles
    vec_total = -(-(2 * vec_rows + 2 * tiles + pc.n_p * qk_cols // LANES) // PAD) * PAD
    heads_shape = (pc.n_p, n_rows, qk_cols)
    outs = dict(
        back_out=SDS(dealt, BF),
        back_grad=SDS(dealt, BF),
        vec=SDS((vec_total, LANES), F32),
        relay=[SDS((pc.n_p, n_rows, 3 * LANES), BF) for _ in range(3)],
        head_relay=[SDS((n_rows, qk_cols), BF) for _ in range(2)],
        tall=[SDS((pc.n_t, pc.n_p, n_rows, 3 * LANES), BF) for _ in range(3)],
        final=[SDS((n_rows, hid), BF) for _ in range(3)],
        head_p=[SDS(heads_shape, BF) for _ in range(2)],
        head_t=[SDS(heads_shape, BF) for _ in range(2)],
    )
    loaded = dict(
        c=f.c,
        h1=f.h1,
        wdown=f.wdown,
        u=f.u,
        g=f.g,
        sup=f.sup,
        sgate=f.sgate,
        wup=f.wup,
        wgate=f.wgate,
        mb=f.mb,
        hb1=f.hb1,
        tok=f.tok,
        wvo=f.wvo,
        vb=f.vb,
        qkb=f.qkb,
        lse=f.lse,
        qk=f.qk,
        sqk=f.sqk,
        wqk=f.wqk,
        ob=f.ob,
    )
    later = dict(a=f.a, hb=f.hb, cot=f.cot, h2=f.h2)
    sums = dict(gsup=hid, gsgate=hid, gsqk=qk_cols, grattn=width, grmlp=width)
    scratch = {n: VM(y.shape, y.dtype) for n, y in loaded.items()} | {n: VM((1, y), F32) for n, y in sums.items()}
    scratch |= dict(
        load_sem={n: DMA((1,)) for n in loaded},
        later_sem=[DMA((1,)) for _ in later],
        dcb=VM(blocks, BF),
        dab=VM(blocks, BF),
        mid=VM((MB, part, width), F32),
        bias=VM((seq, seq), F32),
        sent=VM(blocks, BF),
        got=VM((pc.n_p, MB, part, width), BF),
        tbuf=VM((pc.n_t, pc.n_p, n_rows, 3 * LANES), BF),
        dealbuf=VM(dealt, BF),
        vec=VM((vec_total, LANES), F32),
        vec_got=[VM((y, vec_total, LANES), F32) for y in (pc.n_r, pc.n_t, pc.n_p)],
        rbuf=VM((pc.n_p, n_rows, 3 * LANES), BF),
        hbuf=[VM((2, n_rows, qk_cols), BF) for _ in range(2)],
        near=[VM((pc.n_r - 1, pc.n_p, n_rows, y), BF) for y in (hid, hid, hid, qk_cols, qk_cols)],
        near_sem=[pair(pc.n_r) for _ in range(5)],
        tall_sem=[[DMA((2, pc.n_t)) for _ in range(3)] for _ in range(3)],
        plane_sem=[[DMA((2, pc.n_p)) for _ in range(2)] for _ in range(5)],
        relay_sem=[[DMA((2,)) for _ in range(5)] for _ in range(3)],
        head_sem=[pair(pc.n_t) + [DMA((1,))] for _ in range(2)],
        head_relay_sem=[[DMA((1,)) for _ in range(5)] for _ in range(2)],
        out_sem=Deal.sems(pc),
        grad_sem=Deal.sems(pc),
        vec_sem=[pair(y) for y in (pc.n_r, pc.n_t, pc.n_p)],
        vec_out=DMA((1,)),
        ag_sem=PlaneGather.sems(pc),
        ag1_sem=PlaneGather.sems(pc),
        rh1_sem=PlaneScatter.sems(pc),
        rh_sem=PlaneScatter.sems(pc),
    )
    near_ins = dict(hot=hot, rattn=rattn, rmlp=rmlp, segq=segq, segk=segk)

    def kernel(pc, v, x, o, k):
        own_p = pc.p
        refs = vars(k)
        sources = vars(x)
        loads = {n: pltpu.make_async_copy(sources[n], refs[n], k.load_sem[n].at[0]) for n in loaded}
        for n in loaded:
            loads[n].start()
        cot_load = pltpu.make_async_copy(x.cot, k.dealbuf, k.later_sem[2].at[0])
        h2_load = pltpu.make_async_copy(x.h2, k.dab.at[:, own_p], k.later_sem[3].at[0])
        cot_load.start()
        h2_load.start()
        k_dqk, k_dv = k.u.at[:, :, pl.ds(0, qk_cols)], k.u.at[:, :, pl.ds(qk_cols, o_cols)]
        k_do = k.g.at[0, :, pl.ds(0, o_cols)]
        a_load = pltpu.make_async_copy(x.a, k.c, k.later_sem[0].at[0])
        hb_load = pltpu.make_async_copy(x.hb.reshape(MB, seq, width), k.mb, k.later_sem[1].at[0])
        waited = set()

        def ready(*wanted):
            for n in loaded:
                if n not in waited and any(refs[n] is ref for ref in wanted):
                    waited.add(n)
                    loads[n].wait()

        for n in sums:
            refs[n][...] = jnp.zeros(refs[n].shape, F32)
        k.vec[...] = jnp.zeros(k.vec.shape, F32)
        greet(pc)

        ag, ag1 = (
            PlaneGather(pc, lambda m, q, buf=buf: buf.at[m, q], sems)
            for buf, sems in ((k.dcb, k.ag_sem), (k.dab, k.ag1_sem))
        )
        rh1, rh = (PlaneScatter(pc, k.sent, k.got, sems) for sems in (k.rh1_sem, k.rh_sem))
        deal_out = Deal(pc, k.dealbuf, o.back_out, k.out_sem)
        deal_grad = Deal(pc, k.dealbuf, o.back_grad, k.grad_sem)

        def add_rows(ref, y, at=slice(None)):
            ref[:, at] += jnp.sum(y, axis=0, keepdims=True)

        def top(m):
            def rows(at):
                c, h1, ct = k.c[m, at, :], k.h1[m, at, :], k.mid[m, at, :]
                r_c = inv_rms(c)
                n_c = c * r_c
                z = h1 + v.rmlp[...] * (n_c - h1)
                r_z = inv_rms(z)
                h2 = z * r_z
                dz = r_z * (ct - h2 * row_mean(ct * h2))
                add_rows(k.grmlp, dz * (n_c - h1))
                k.mid[m, at, :] = (1.0 - v.rmlp[...]) * dz
                dn = v.rmlp[...] * dz
                k.dcb[m, own_p, at, :] = (r_c * (dn - n_c * row_mean(dn * n_c))).astype(BF)

            rows_loop(part, rows)
            ag.start(m)

        def summed(m, at):
            return plane_sum(pc, k.sent, k.got, m, at)

        def feed(m):
            ag.wait_recv(m)

            def hidden(at):
                dm = dot_nn(k.dcb[m].reshape(seq, width), k.wdown[:, at])
                u, g = k.u[m, :, at].astype(F32), k.g[m, :, at].astype(F32)
                y = k.sgate[:, at] * g
                sig = 1.0 / (1.0 + jnp.exp(-y))
                du = dm * (y * sig)
                dx = dm * (k.sup[:, at] * u) * (sig * (1.0 + y * (1.0 - sig)))
                add_rows(k.gsup, du * u, at)
                add_rows(k.gsgate, dx * g, at)
                k.u[m, :, at] = (k.sup[:, at] * du).astype(BF)
                k.g[m, :, at] = (k.sgate[:, at] * dx).astype(BF)

            chunks(hid, hidden)

        def shrink(m):
            def columns(at):
                y = dot_nt(k.u[m], k.wup[at, :]) + dot_nt(k.g[m], k.wgate[at, :])
                k.sent[m, :, :, at] = y.astype(BF).reshape(pc.n_p, part, CHUNK)

            chunks(width, columns)
            rh1.start(m)

        grads = [k.wdown, k.wup, k.wgate, k.wqk, k.wvo]

        def near_slot(source, at):
            return (source - at + pc.n_r - 1) % pc.n_r

        def near_moves(i):
            send, recv = k.near_sem[i]
            return Moves(
                [
                    Move(
                        by_shard(pc, grads[i]).at[:, q], k.near[i].at[near_slot(pc.r, q)], send.at[q], recv.at[pc.r],
                        pc.dev(pc.p, q, pc.t), k.near[i].at[near_slot(q, pc.r)], recv.at[q],
                    )
                    for q in others(pc.n_r, pc.r)
                ]
            )

        near = [near_moves(i) for i in range(5)]

        def row_blocks(fn):
            def block(i, carry):
                fn(i // 5, pl.ds(pl.multiple_of((i % 5) * step_rows, step_rows), step_rows))
                return carry

            lax.fori_loop(0, pc.n_p * 5, block, 0)

        def near_sum(i):
            near[i].wait_recv()
            own = by_shard(pc, grads[i])

            def block(p, at):
                total = own[p, pc.r, at, :].astype(F32)
                for j in range(pc.n_r - 1):
                    total = total + k.near[i][j, p, at, :].astype(F32)
                k.near[i][0, p, at, :] = total.astype(BF)

            row_blocks(block)

        t = pc.t
        middle_dev = (t == 1) | (t == 2)
        end_dev = jnp.logical_not(middle_dev)
        far = jnp.where((t == 2) | (t == 3), 0, 3)
        by = jnp.where(t == 0, 1, 2)
        wide = width3(pc.p, t)
        wide_far = width3(pc.p, far)

        def direct_out(q):
            return (jnp.abs(q - t) != 3) & jnp.logical_not(middle_dev & (q == far))

        def comes(q):
            return jnp.abs(q - t) != 3

        def tall_moves(i):
            send, recv, _ = k.tall_sem[i]
            src, y = k.near[i].at[0], o.tall[i]
            moves = []
            for q in others(pc.n_t, t):
                there = dst_tile(pc.p, q)
                dev = pc.dev(pc.p, pc.r, q)
                moves.append(
                    Move(
                        src.at[:, :, lanes(there, 2)], y.at[t, :, :, TWO], send.at[0, q], recv.at[0, t], dev,
                        y.at[q, :, :, TWO], recv.at[0, q], direct_out(q), comes(q),
                    )
                )
                moves.append(
                    Move(
                        src.at[:, :, lanes(there + 2, 1)], y.at[t, :, :, ONE], send.at[1, q], recv.at[1, t], dev,
                        y.at[q, :, :, ONE], recv.at[1, q], direct_out(q) & width3(pc.p, q), comes(q) & wide,
                    )
                )
            return Moves(moves)

        def far_parts(i):
            at = dst_tile(pc.p, far)
            return ((TWO, lanes(at, 2), None), (ONE, lanes(at + 2, 1), wide_far))

        def both(a, b):
            return a if b is None else a & b

        def handed_moves(i):
            s1, r1, _, _, _ = k.relay_sem[i]
            src, y = k.near[i].at[0], o.relay[i]
            return Moves(
                [
                    Move(
                        src.at[:, :, at], y.at[:, :, w], s1.at[j], r1.at[j], pc.dev(pc.p, pc.r, by), y.at[:, :, w],
                        r1.at[j], both(end_dev, cond), both(middle_dev, cond),
                    )
                    for j, (w, at, cond) in enumerate(far_parts(i))
                ]
            )

        def passed_moves(i):
            _, _, s2, _, _ = k.relay_sem[i]
            recv = k.tall_sem[i][1]
            return Moves(
                [
                    Move(
                        k.rbuf.at[:, :, w], o.tall[i].at[t, :, :, w], s2.at[j], recv.at[j, t], pc.dev(pc.p, pc.r, far),
                        None, None, both(middle_dev, cond),
                    )
                    for j, (w, at, cond) in enumerate(far_parts(i))
                ]
            )

        tall = [tall_moves(i) for i in range(3)]
        handed = [handed_moves(i) for i in range(3)]
        passed = [passed_moves(i) for i in range(3)]

        def tall_start(i):
            handed[i].start()
            tall[i].start()

        def tall_relay(i):
            handed[i].wait_recv()

            @pl.when(middle_dev)
            def _():
                copy = pltpu.make_async_copy(o.relay[i], k.rbuf, k.relay_sem[i][3].at[0])
                copy.start()
                copy.wait()

                def add(w, at):
                    def block(p, rows):
                        total = k.rbuf[p, rows, w].astype(F32) + k.near[i][0, p, rows, at].astype(F32)
                        k.rbuf[p, rows, w] = total.astype(BF)

                    row_blocks(block)

                for w, at, cond in far_parts(i):
                    Move.under(cond, lambda w=w, at=at: add(w, at))

            passed[i].start()

        def tall_sum(i):
            tall[i].wait_recv()
            local = []
            for q in others(pc.n_t, t):
                for j, (w, cond) in enumerate(((TWO, comes(q)), (ONE, comes(q) & wide))):
                    copy = pltpu.make_async_copy(
                        o.tall[i].at[q, :, :, w], k.tbuf.at[q, :, :, w], k.tall_sem[i][2].at[j, q]
                    )
                    Move.under(cond, copy.start)
                    local.append((cond, copy))
            for cond, copy in local:
                Move.under(cond, copy.wait)
            here = dst_tile(pc.p, t)

            def add(source, target):
                def block(p, at):
                    total = k.near[i][0, p, at, source].astype(F32)
                    for q in others(pc.n_t, t):
                        total = total + jnp.where(comes(q), k.tbuf[q, p, at, target].astype(F32), 0.0)
                    k.tbuf[t, p, at, target] = total.astype(BF)

                row_blocks(block)

            add(lanes(here, 2), TWO)
            pl.when(wide)(lambda: add(lanes(here + 2, 1), ONE))

        def plane_moves(i):
            send, recv = k.plane_sem[i]
            y, src = o.final[i], k.tbuf.at[pc.t]
            here = src_tile(pc.p, pc.t)
            moves = []
            for q in others(pc.n_p, pc.p):
                there = src_tile(q, pc.t)
                dev = pc.dev(q, pc.r, pc.t)
                moves.append(
                    Move(
                        src.at[q, :, TWO], y.at[:, lanes(here, 2)], send.at[0, q], recv.at[0, pc.p], dev,
                        y.at[:, lanes(there, 2)], recv.at[0, q],
                    )
                )
                moves.append(
                    Move(
                        src.at[q, :, ONE], y.at[:, lanes(here + 2, 1)], send.at[1, q], recv.at[1, pc.p], dev,
                        y.at[:, lanes(there + 2, 1)], recv.at[1, q], wide, width3(q, pc.t),
                    )
                )
            own = (
                (None, pltpu.make_async_copy(src.at[own_p, :, TWO], y.at[:, lanes(here, 2)], send.at[0, pc.p])),
                (wide, pltpu.make_async_copy(src.at[own_p, :, ONE], y.at[:, lanes(here + 2, 1)], send.at[1, pc.p])),
            )
            return Moves(moves), own

        plane = [plane_moves(i) for i in range(3)]

        def plane_start(i):
            moves, own = plane[i]
            moves.start()
            for cond, copy in own:
                Move.under(cond, copy.start)

        def plane_sent(i):
            moves, own = plane[i]
            moves.wait_send()
            for cond, copy in own:
                Move.under(cond, copy.wait)

        def head_planes(i):
            send, recv = k.plane_sem[3 + i]
            src, y = k.near[3 + i].at[0], o.head_p[i]
            return Moves(
                [
                    Move(
                        src.at[q], y.at[pc.p], send.at[0, q], recv.at[0, pc.p], pc.dev(q, pc.r, pc.t), y.at[q],
                        recv.at[0, q],
                    )
                    for q in others(pc.n_p, pc.p)
                ]
            )

        def head_talls(i):
            send, recv, _ = k.head_sem[i]
            src, y = o.head_p[i], o.head_t[i]
            return Moves(
                [
                    Move(
                        src.at[q], y.at[t], send.at[q], recv.at[t], pc.dev(pc.p, pc.r, q), y.at[q], recv.at[q],
                        direct_out(q), comes(q),
                    )
                    for q in others(pc.n_t, t)
                ]
            )

        def head_handed(i):
            s1, r1, _, _, _ = k.head_relay_sem[i]
            y = o.head_relay[i]
            return Move(
                o.head_p[i].at[far], y, s1.at[0], r1.at[0], pc.dev(pc.p, pc.r, by), y, r1.at[0], end_dev, middle_dev
            )

        def head_passed(i):
            _, _, s2, _, _ = k.head_relay_sem[i]
            recv = k.head_sem[i][1]
            return Move(
                k.hbuf[i].at[0], o.head_t[i].at[t], s2.at[0], recv.at[t], pc.dev(pc.p, pc.r, far), None, None, middle_dev
            )

        head_first = [head_handed(i) for i in range(2)]
        head_last = [head_passed(i) for i in range(2)]

        def head_start(i):
            head_first[i].start()
            head_tall[i].start()

        def head_relay(i):
            head_first[i].wait_recv()

            @pl.when(middle_dev)
            def _():
                copies = [
                    pltpu.make_async_copy(o.head_relay[i], k.hbuf[i].at[0], k.head_relay_sem[i][3].at[0]),
                    pltpu.make_async_copy(o.head_p[i].at[far], k.hbuf[i].at[1], k.head_relay_sem[i][4].at[0]),
                ]
                for copy in copies:
                    copy.start()
                for copy in copies:
                    copy.wait()
                k.hbuf[i][0] = (k.hbuf[i][0].astype(F32) + k.hbuf[i][1].astype(F32)).astype(BF)

            head_last[i].start()

        head_plane = [head_planes(i) for i in range(2)]
        head_tall = [head_talls(i) for i in range(2)]
        head_own = [
            pltpu.make_async_copy(k.near[3 + i].at[0, own_p], o.head_p[i].at[pc.p], k.head_sem[i][2].at[0])
            for i in range(2)
        ]

        def middle(m):
            rh1.wait_recv(m)

            def rows(at):
                dh1 = k.mid[m, at, :] + summed(m, at)
                a, h = k.c[m, at, :], k.tok[m, at, :].astype(F32)
                r_a = inv_rms(a)
                n_a = a * r_a
                y = h + v.rattn[...] * (n_a - h)
                r_y = inv_rms(y)
                h1 = y * r_y
                dy = r_y * (dh1 - h1 * row_mean(dh1 * h1))
                add_rows(k.grattn, dy * (n_a - h))
                k.mid[m, at, :] = (1.0 - v.rattn[...]) * dy
                dn = v.rattn[...] * dy
                k.dab[m, own_p, at, :] = (r_a * (dn - n_a * row_mean(dn * n_a))).astype(BF)

            rows_loop(part, rows)
            ag1.start(m)

        def flat(ref, at=slice(None)):
            return ref[:, :, at].reshape(all_tok, -1)

        def columns_of(ref, at):
            return ref[:, :, :, at].reshape(all_tok, CHUNK)

        def weight_grad(target, left, right):
            def block(at):
                target[at, :] = dot_tn(columns_of(left, at), flat(right)).astype(BF)

            chunks(width, block)

        score = HEAD_DIM ** (-0.5)
        blk = seq // 2

        def attend(m):
            fill_mask(k.bias, v.segq[m], v.segk[m])
            ag1.wait_recv(m)

            def project(i, carry):
                rows = k.dab[m, pl.ds(2 * i, 2)].reshape(2 * part, width)
                at = pl.ds(pl.multiple_of(i * 2 * part, 2 * part), 2 * part)
                k_do[at, :] = dot_nn(rows, k.wvo[:, QUADS:]).astype(BF)
                return carry

            lax.fori_loop(0, pc.n_p // 2, project, 0)
            if m == 0:
                ag1.relay(1)
            else:
                rh.relay(0)

            def norm_grad(tile, d):
                at = tile_of(tile)
                raw = k.qk[m, :, at]
                r = lax.rsqrt(half_means(raw * raw) + EPSILON)
                n = raw * r
                d = d * score
                add_rows(k.gsqk, d * n, at)
                dy = d * k.sqk[:, at]
                k_dqk[m, :, at] = (r * (dy - n * half_means(dy * n))).astype(BF)

            for slab in range(3):
                own = tile_of(slab)
                if slab < 2:
                    q_all = k.qkb[m, :, own]
                    k_all = k.qkb[m, :, tile_of(2 + slab)]
                    do_all = k_do[:, own]
                else:
                    q_all = k.qkb[m, :, 2 * QUADS :]
                    k_all = swap_halves(q_all.astype(F32)).astype(BF)
                    do_all = swap_halves(k_do[:, own].astype(F32)).astype(BF)
                v_all = k.vb[m, :, own]
                low = low_lanes((blk, LANES))
                dq, dk, dv = [], None, None
                for i in range(2):
                    nk = (i + 1) * blk
                    at = slice(i * blk, nk)
                    bias = k.bias[at, :nk]
                    dq_i = None
                    for half in range(2 if slab < 2 else 1):
                        here = low if half == 0 else jnp.logical_not(low)
                        zero = jnp.zeros((blk, LANES), BF)
                        q1, do1 = jnp.where(here, q_all[at], zero), jnp.where(here, do_all[at], zero)
                        lse = k.lse[m, at, 2 * slab + half : 2 * slab + half + 1]
                        prob = jnp.exp(dot_nt(q1, k_all[:nk]) * score + bias - lse)
                        dp = dot_nt(do1, v_all[:nk])
                        w = prob * dp
                        ds = (w - prob * jnp.sum(w, axis=1, keepdims=True)).astype(BF)
                        y = jnp.where(here, dot_nn(ds, k_all[:nk]), 0.0)
                        dq_i = y if dq_i is None else dq_i + y
                        dk_i, dv_i = dot_tn(ds, q1), dot_tn(prob.astype(BF), do1)
                        if i == 0:
                            dk = dk_i if dk is None else dk + dk_i
                            dv = dv_i if dv is None else dv + dv_i
                        else:
                            if half == 0:
                                dk = jnp.concatenate([dk, jnp.zeros((blk, LANES), F32)], axis=0)
                                dv = jnp.concatenate([dv, jnp.zeros((blk, LANES), F32)], axis=0)
                            dk, dv = dk + dk_i, dv + dv_i
                    dq.append(dq_i)
                dq = jnp.concatenate(dq, axis=0)
                k_dv[m, :, own] = dv.astype(BF)
                if slab < 2:
                    norm_grad(slab, dq)
                    norm_grad(2 + slab, dk)
                else:
                    norm_grad(4, dq + swap_halves(dk))
            rh1.wait_send(m)

            def columns(at):
                y = dot_nt(k_dqk[m], k.wqk[at, :])
                y = y + dot_nt(k_dv[m, :, :QUADS], k.wvo[at, :QUADS])
                y = y + dot_nt(k_dv[m, :, QUADS:], k.wvo[at, 2 * QUADS :])
                k.sent[m, :, :, at] = y.astype(BF).reshape(pc.n_p, part, CHUNK)

            chunks(width, columns)
            rh.start(m)

        def heads_grad(at):
            hb, dab = flat(k.mb, at), columns_of(k.dab, at)
            quads = slice(0, QUADS)
            rest = slice(QUADS, None)
            k.wqk[at, :] = dot_tn(hb, flat(k_dqk)).astype(BF)
            k.wvo[at, :QUADS] = dot_tn(hb, flat(k_dv, quads)).astype(BF)
            k.wvo[at, QUADS : 2 * QUADS] = dot_tn(dab, flat(k.ob, quads)).astype(BF)
            k.wvo[at, 2 * QUADS :] = (dot_tn(hb, flat(k_dv, rest)) + dot_tn(dab, flat(k.ob, rest))).astype(BF)

        def bottom(m):
            rh.wait_recv(m)

            def rows(at):
                k.mid[m, at, :] = k.mid[m, at, :] + summed(m, at)

            rows_loop(part, rows)

        def collect():
            for t in range(pc.n_t):
                for j in range(3):

                    def move(t=t, j=j):
                        here = lanes(dst_tile(pc.p, t) + j, 1)
                        row = t * tiles + src_tile(pc.p, t) + j
                        k.vec[pl.ds(row, 1), :] = k.gsup[:, here]
                        k.vec[pl.ds(vec_rows + row, 1), :] = k.gsgate[:, here]

                    Move.under(width3(pc.p, t) if j == 2 else None, move)
            at = 2 * vec_rows
            for j in range(tiles):
                k.vec[at + j : at + j + 1, :] = k.grattn[:, tile_of(j)]
                k.vec[at + tiles + j : at + tiles + j + 1, :] = k.grmlp[:, tile_of(j)]
            count = qk_cols // LANES
            for j in range(count):
                k.vec[pl.ds(at + 2 * tiles + own_p * count + j, 1), :] = k.gsqk[:, tile_of(j)]

        def vec_stage(n, count, own, dev_of):
            send, recv = k.vec_sem[n]
            buf = k.vec_got[n]
            moves = Moves(
                [
                    Move(buf.at[own], buf.at[own], send.at[q], recv.at[own], dev_of(q), buf.at[q], recv.at[q])
                    for q in others(count, own)
                ]
            )

            def start():
                buf[own] = k.vec[...]
                moves.start()

            def finish():
                moves.wait_recv()
                total = buf[0]
                for q in range(1, count):
                    total = total + buf[q]
                k.vec[...] = total

            return start, finish, moves

        vec_stages = [
            vec_stage(0, pc.n_r, pc.r, lambda q: pc.dev(pc.p, q, pc.t)),
            vec_stage(1, pc.n_t, pc.t, lambda q: pc.dev(pc.p, pc.r, q)),
            vec_stage(2, pc.n_p, pc.p, lambda q: pc.dev(q, pc.r, pc.t)),
        ]
        vec_keep = pltpu.make_async_copy(k.vec, o.vec, k.vec_out.at[0])

        ready(k.c, k.h1)
        cot_load.wait()

        def put(at, y):
            for m in range(MB):
                k.mid[m, :, at] = y[m * part : (m + 1) * part]

        take_rows(v.hot, k.dealbuf, put)
        for m in range(MB):
            top(m)
        a_load.start()
        ag.relay(0)
        h2_load.wait()
        give_rows(v.hot, lambda at: k.dab[:, own_p, :, at].reshape(MB * part, CHUNK), k.dealbuf)
        deal_out.start()
        ready(k.wdown, k.u, k.g, k.wup, k.wgate, k.sup, k.sgate)
        feed(0)
        ag.relay(1)
        feed(1)
        ready(k.mb, k.hb1)
        weight_grad(k.wdown, k.dcb, k.mb)
        near[0].start()
        hb_load.start()
        shrink(0)
        near_sum(0)
        tall_start(0)
        shrink(1)
        rh1.relay(0)
        rh1.relay(1)
        weight_grad(k.wup, k.hb1, k.u)
        near[1].start()
        ready(k.tok)
        a_load.wait()
        middle(0)
        near_sum(1)
        tall_start(1)
        weight_grad(k.wgate, k.hb1, k.g)
        near[2].start()
        middle(1)
        ag1.relay(0)
        near_sum(2)
        tall_relay(0)
        tall_start(2)
        ready(k.wvo, k.vb, k.qkb, k.lse, k.qk, k.sqk, k.wqk, k.ob)
        attend(0)
        passed[0].wait_send()
        tall_relay(1)
        attend(1)
        hb_load.wait()
        chunks(width, heads_grad)
        for i in range(2):
            near[3 + i].start()
        rh.relay(1)
        collect()
        vec_stages[0][0]()
        for i in range(2):
            near_sum(3 + i)
            head_plane[i].start()
            head_own[i].start()
        vec_stages[0][1]()
        vec_stages[1][0]()
        for m in range(MB):
            bottom(m)
        passed[1].wait_send()
        tall_relay(2)
        deal_out.wait_recv()
        deal_out.wait_send()
        give_rows(v.hot, lambda at: k.mid[:, :, at].reshape(MB * part, CHUNK).astype(BF), k.dealbuf)
        deal_grad.start()
        for i in range(2):
            head_plane[i].wait_recv()
            head_own[i].wait()
            head_start(i)
        tall_sum(0)
        plane_start(0)
        plane_sent(0)
        tall_sum(1)
        plane_start(1)
        vec_stages[1][1]()
        vec_stages[2][0]()
        for i in range(2):
            head_relay(i)
        plane_sent(1)
        tall_sum(2)
        plane_start(2)
        vec_stages[2][1]()
        vec_keep.start()
        plane_sent(2)
        passed[2].wait_send()
        for w in tall + handed + head_first + head_last + head_plane + head_tall + near + [deal_grad]:
            w.wait_send()
        for stage in vec_stages:
            stage[2].wait_send()
        for i in range(3):
            plane[i][0].wait_recv()
        for w in head_tall + [deal_grad]:
            w.wait_recv()
        vec_keep.wait()
        for m in range(MB):
            ag.wait_send(m)
            ag1.wait_send(m)
            rh.wait_send(m)

    return fused(2, kernel, near_ins, loaded | later, outs, scratch)


def merged(slots, own, at):
    total = own.astype(F32)
    for q in range(slots.shape[0]):
        total = total + jnp.where((q == at) | (jnp.abs(q - at) == 3), 0, slots[q]).astype(F32)
    return total


def pick(x, at, axis):
    return lax.dynamic_index_in_dim(x, at, axis, keepdims=False)


def mm(a, b):
    return jnp.dot(a, b, preferred_element_type=F32)


def segment_ids(lengths_row, tok_count):
    count = lengths_row.shape[0]
    upto = jnp.arange(count)[:, None] >= jnp.arange(count)[None, :]
    doc_ends = jnp.sum(jnp.where(upto, lengths_row[None, :], 0), axis=1)
    places = jnp.arange(tok_count, dtype=jnp.int32)
    return jnp.sum((places[:, None] >= doc_ends[None, :]).astype(jnp.int32), axis=1)


def packed(x, y):
    return jnp.concatenate([x[:, :QUADS], y[:, :QUADS], x[:, QUADS:], y[:, QUADS:]], axis=1)


def unpacked(z):
    mid = 2 * QUADS + HEAD_DIM
    return (
        jnp.concatenate([z[..., :QUADS], z[..., 2 * QUADS : mid]], axis=-1),
        jnp.concatenate([z[..., QUADS : 2 * QUADS], z[..., mid:]], axis=-1),
    )


def body(
    tokens,
    cotangent,
    slot,
    lengths,
    w_query,
    w_key,
    w_value,
    w_out,
    w_up,
    w_gate,
    w_down,
    scale_qk,
    scale_up,
    scale_gate,
    rate_attn,
    rate_mlp,
):
    pc = Place()
    n_p, n_r, n_t, n_dev = pc.n_p, pc.n_r, pc.n_t, pc.n_dev
    rows_dev, width = tokens.shape
    tok_count = rows_dev // MB * n_p
    head_cols = w_query.shape[2]
    hid = w_up.shape[2]
    tiles = hid // LANES
    group = pc.r * n_t + pc.t
    owner = group * n_p + pc.p
    if rows_dev // n_dev > PAD or head_cols != QUADS + HEAD_DIM:
        raise ValueError("sizes")

    table = slot.reshape(n_dev, rows_dev)
    own_slots = lax.dynamic_index_in_dim(table, pc.me, 0, keepdims=False)
    d = own_slots // rows_dev
    to_dev = ((d % n_p) * n_r + (d // n_p) // n_t) * n_t + (d // n_p) % n_t
    places = jnp.arange(rows_dev, dtype=jnp.int32)
    spots = jnp.arange(n_dev * PAD, dtype=jnp.int32)
    before = (d[:, None] == d[None, :]) & (places[None, :] < places[:, None])
    rank = jnp.sum(before.astype(jnp.int32), axis=1)
    send_hot = (spots[:, None] == (to_dev * PAD + rank)[None, :]).astype(BF)

    sel = table // rows_dev == owner
    tri = (places[:, None] < places[None, :]).astype(BF)
    ranks = mm(sel.astype(BF), tri).astype(jnp.int32)
    kth = sel[:, None, :] & (ranks[:, None, :] == jnp.arange(PAD, dtype=jnp.int32)[None, :, None])
    owner_rows = jnp.sum(jnp.where(kth, (table - owner * rows_dev + 1)[:, None, :], 0), axis=2).reshape(-1) - 1
    recv_hot = (places[:, None] == owner_rows[None, :]).astype(BF)

    def to_send(x):
        return mm(send_hot, x).astype(BF).reshape(n_dev, PAD, width)

    qk_scale = packed(scale_qk, scale_qk).reshape(-1, LANES)
    small = jnp.concatenate([scale_up.reshape(-1, LANES), scale_gate.reshape(-1, LANES), qk_scale])
    small = jnp.pad(small, ((0, -small.shape[0] % 8), (0, 0)))
    own_lengths = lax.dynamic_slice_in_dim(lengths, group * MB, MB, 0)
    segments = jnp.stack([segment_ids(own_lengths[m], tok_count) for m in range(MB)])
    shared = (recv_hot, rate_attn, rate_mlp, segments[:, :, None], segments[:, None, :])

    f = forward(
        pc,
        to_send(tokens),
        to_send(cotangent),
        packed(w_query[0], w_key[0]),
        packed(w_value[0], w_out[0]),
        w_up[0],
        w_gate[0],
        w_down[0],
        small,
        *shared,
    )
    b = backward(pc, f, *shared)

    vec = b.vec
    at = n_t * tiles

    def own_row(x):
        return lax.dynamic_index_in_dim(x.reshape(n_t, -1), pc.t, 0)

    qk_rows = qk_scale.shape[0]
    out_sup, out_sgate = own_row(vec[:at]), own_row(vec[at : 2 * at])
    at = 2 * at
    out_rattn, out_rmlp = vec[at : at + tiles].reshape(1, -1), vec[at + tiles : at + 2 * tiles].reshape(1, -1)
    at = at + 2 * tiles
    out_sqk = sum(unpacked(own_row(vec[at : at + n_t * qk_rows])))
    heads = [
        x[None]
        for got, sent in zip(b.head_t, b.head_p)
        for x in unpacked(merged(got, pick(sent, pc.t, 0), pc.t))
    ]

    def from_back(x):
        return lax.dot_general(
            send_hot, x.reshape(-1, width), (((0,), (0,)), ((), ())), preferred_element_type=F32
        )

    down, up, gate = (x.astype(F32)[None] for x in b.final)
    return (
        from_back(b.back_out),
        from_back(b.back_grad),
        *heads,
        up,
        gate,
        down,
        out_sqk,
        out_sup,
        out_sgate,
        out_rattn,
        out_rmlp,
    )


def solution(mesh):
    tok = P(("dp", "tensor"), None)
    mat = P(None, "dp", "tensor")
    vec = P(None, "tensor")
    in_specs = (tok, tok, P(), P()) + (mat,) * 7 + (vec,) * 3 + (P(), P())
    out_specs = (tok, tok) + (mat,) * 7 + (vec,) * 3 + (P(), P())
    return jax.shard_map(body, mesh=mesh, in_specs=in_specs, out_specs=out_specs, check_vma=False)
```

```python
import types

import jax
import jax.numpy as jnp
from jax import lax
from jax.experimental import pallas as pl
from jax.experimental.pallas import tpu as pltpu
from jax.sharding import PartitionSpec as P

HEAD_DIM = 64
MB = 2
LANES = 128
QUADS = 4 * HEAD_DIM
CHUNK = 2 * LANES
ROW_STEP = 32
PAD = 8
VMEM_LIMIT = 127 * 2**19

EPSILON = 1e-06
MASKED = -1e30
BF = jnp.bfloat16
F32 = jnp.float32
MESH = pl.DeviceIdType.MESH
VM = pltpu.VMEM
DMA = pltpu.SemaphoreType.DMA
SDS = jax.ShapeDtypeStruct


class Place:
    def __init__(self):
        self.n_t = lax.axis_size("tensor")
        self.n_dp = lax.axis_size("dp")
        self.n_p = self.n_t
        self.n_r = self.n_dp // self.n_p
        self.n_dev = self.n_dp * self.n_t
        if self.n_t != 4:
            raise ValueError("tensor size")
        dp = lax.axis_index("dp")
        self.t = lax.axis_index("tensor")
        self.p = dp // self.n_r
        self.r = dp % self.n_r
        self.me = dp * self.n_t + self.t

    def dev(self, p, r, t):
        return (p * self.n_r + r, t)

    def flat(self, j):
        return (j // self.n_t, j % self.n_t)


def width3(p, t):
    return (p + t) % 2 == 0


def src_tile(p, t):
    return 5 * (p // 2) + (p % 2) * (3 - t % 2)


def dst_tile(p, t):
    return 5 * (t // 2) + (t % 2) * (3 - p % 2)


def lanes(tile, count):
    return pl.ds(pl.multiple_of(tile * LANES, LANES), count * LANES)


TWO, ONE = pl.ds(0, 2 * LANES), pl.ds(2 * LANES, LANES)


def remote(src, dst, send, recv, dev):
    return pltpu.make_async_remote_copy(
        src_ref=src, dst_ref=dst, send_sem=send, recv_sem=recv, device_id=dev, device_id_type=MESH
    )


class Move:
    def __init__(self, src, dst, send, recv, dev, landing, landed, cond_out=None, cond_in=None):
        self.going = (src, dst, send, recv, dev)
        self.coming = (landing, landing, send, landed, dev)
        self.cond_out, self.cond_in = cond_out, cond_in

    @staticmethod
    def under(cond, act):
        if cond is None:
            act()
        else:
            pl.when(cond)(act)

    def start(self):
        self.under(self.cond_out, lambda: remote(*self.going).start())

    def wait_send(self):
        self.under(self.cond_out, lambda: remote(*self.going).wait_send())

    def wait_recv(self):
        self.under(self.cond_in, lambda: remote(*self.coming).wait_recv())


class Moves:
    def __init__(self, moves):
        self.moves = moves

    def start(self):
        for m in self.moves:
            m.start()

    def wait_recv(self):
        for m in self.moves:
            m.wait_recv()

    def wait_send(self):
        for m in self.moves:
            m.wait_send()


def others(count, own):
    order = [2, 1, 3] if count == 4 else list(range(1, count))
    return [(own + k) % count for k in order]


def pair(n):
    return [DMA((n,)), DMA((n,))]


class Deal:
    @staticmethod
    def sems(pc):
        return [DMA((1,)), DMA((1,)), DMA((1,))]

    def __init__(self, pc, x, y, sems):
        self.pc, self.x, self.y = pc, x, y
        self.send, self.recv, self.local = (sem.at[0] for sem in sems)

    def copy(self, j, src, dst):
        return remote(src, dst, self.send, self.recv, self.pc.flat(j))

    def own(self):
        return pltpu.make_async_copy(self.x.at[self.pc.me], self.y.at[self.pc.me], self.local)

    def start(self):
        pc = self.pc

        def step(i, carry):
            j = (pc.me + i) % pc.n_dev
            self.copy(j, self.x.at[j], self.y.at[pc.me]).start()
            return carry

        lax.fori_loop(1, pc.n_dev, step, 0)
        self.own().start()

    def all_but_own(self):
        part = self.y.at[pl.ds(0, self.pc.n_dev - 1)]
        return self.copy((self.pc.me + 1) % self.pc.n_dev, part, part)

    def wait_recv(self):
        self.own().wait()
        self.all_but_own().wait_recv()

    def wait_send(self):
        self.all_but_own().wait_send()


class Tall:
    @staticmethod
    def sems(pc, pieces):
        return [DMA((pieces, pc.n_t + 1)), DMA((pieces, pc.n_t))]

    def __init__(self, pc, shard, own, sems):
        t = pc.t
        middle = (t == 1) | (t == 2)
        far, end = jnp.where(t == 2, 0, 3), jnp.where(t == 2, 3, 0)
        send, recv = sems

        def both(a, b):
            return a if b is None else a & b

        self.first, self.passed = [], []
        for q in others(pc.n_t, t):
            for i, ((dst, c_out), src, (here, c_in)) in enumerate(zip(shard(t), own, shard(q))):
                args = (src, dst, send.at[i, q], recv.at[i, t], pc.dev(pc.p, pc.r, q), here, recv.at[i, q])
                c_in = both(jnp.logical_not(middle & (q == far)), c_in)
                self.first.append(Move(*args, both(jnp.abs(q - t) != 3, c_out), c_in))
        for i, (ref, c) in enumerate(shard(far)):
            self.passed.append(
                Move(
                    ref, ref, send.at[i, pc.n_t], recv.at[i, far], pc.dev(pc.p, pc.r, end), ref, recv.at[i, far],
                    both(middle, c), both(middle, c),
                )
            )

    def start(self):
        for m in self.first:
            m.start()

    def relay(self):
        for m in self.passed:
            m.wait_recv()
            m.start()

    def wait_recv(self):
        for m in self.first:
            m.wait_recv()

    def wait_send(self):
        for m in self.first + self.passed:
            m.wait_send()


def by_shard(pc, ref):
    return ref.reshape(pc.n_p, pc.n_r, ref.shape[0] // (pc.n_p * pc.n_r), ref.shape[1])


class HeadWeights:
    @staticmethod
    def sems(pc):
        return [Tall.sems(pc, 1), pair(pc.n_p), pair(pc.n_r), DMA((2,))]

    def __init__(self, pc, x, a, w, sems):
        tall, (s2, r2), (s3, r3), ls = sems
        f = by_shard(pc, w)
        self.first = Tall(pc, lambda q: [(a.at[q], None)], [x], tall)
        self.second = Moves(
            [
                Move(a.at[q], f.at[pc.p, pc.r], s2.at[q], r2.at[pc.p], pc.dev(q, pc.r, pc.t), f.at[q, pc.r], r2.at[q])
                for q in others(pc.n_p, pc.p)
            ]
        )
        self.third = Moves(
            [
                Move(f.at[:, pc.r], f.at[:, pc.r], s3.at[q], r3.at[pc.r], pc.dev(pc.p, q, pc.t), f.at[:, q], r3.at[q])
                for q in others(pc.n_r, pc.r)
            ]
        )
        self.keep1 = pltpu.make_async_copy(x, a.at[pc.t], ls.at[0])
        self.keep2 = pltpu.make_async_copy(a.at[pc.p], f.at[pc.p, pc.r], ls.at[1])

    def start(self):
        self.first.start()
        self.keep1.start()

    def relay(self):
        self.first.relay()

    def plane(self):
        self.keep1.wait()
        self.first.wait_recv()
        self.second.start()
        self.keep2.start()

    def near(self):
        self.keep2.wait()
        self.second.wait_recv()
        self.third.start()

    def wait_recv(self):
        self.third.wait_recv()

    def wait_send(self):
        self.first.wait_send()
        self.second.wait_send()
        self.third.wait_send()


class HiddenWeights:
    @staticmethod
    def sems(pc):
        return [pair(pc.n_p), pair(pc.n_p), Tall.sems(pc, 2), pair(pc.n_r), DMA((2,))]

    def __init__(self, pc, x, w, sems):
        (s1, r1), (s2, r2), tall, (s3, r3), ls = sems
        g = by_shard(pc, w)
        p, r, t = pc.p, pc.r, pc.t

        def spot(q, row, extra):
            at = dst_tile(q, t)
            return g.at[row, r, :, lanes(at + 2, 1) if extra else lanes(at, 2)]

        def piece(q, extra):
            at = src_tile(q, t)
            return x.at[:, lanes(at + 2, 1) if extra else lanes(at, 2)]

        moves = []
        for q in others(pc.n_p, p):
            dev = pc.dev(q, r, t)
            moves.append(
                Move(piece(q, False), spot(q, p, False), s1.at[q], r1.at[p], dev, spot(p, q, False), r1.at[q])
            )
            moves.append(
                Move(
                    piece(q, True), spot(q, p, True), s2.at[q], r2.at[p], dev, spot(p, q, True), r2.at[q],
                    width3(q, t), width3(p, t),
                )
            )
        self.first = Moves(moves)
        self.own = [
            (None, pltpu.make_async_copy(piece(p, False), spot(p, p, False), ls.at[0])),
            (width3(p, t), pltpu.make_async_copy(piece(p, True), spot(p, p, True), ls.at[1])),
        ]

        def shard(q):
            at = dst_tile(p, q)
            return [(g.at[:, r, :, lanes(at, 2)], None), (g.at[:, r, :, lanes(at + 2, 1)], width3(p, q))]

        self.second = Tall(pc, shard, [ref for ref, _ in shard(t)], tall)
        self.third = Moves(
            [
                Move(g.at[:, r], g.at[:, r], s3.at[q], r3.at[r], pc.dev(p, q, t), g.at[:, q], r3.at[q])
                for q in others(pc.n_r, r)
            ]
        )

    def start(self):
        self.first.start()
        for cond, copy in self.own:
            Move.under(cond, copy.start)

    def tall(self):
        for cond, copy in self.own:
            Move.under(cond, copy.wait)
        self.first.wait_recv()
        self.second.start()

    def relay(self):
        self.second.relay()

    def near(self):
        self.second.wait_recv()
        self.third.start()

    def wait_recv(self):
        self.third.wait_recv()

    def wait_send(self):
        self.first.wait_send()
        self.second.wait_send()
        self.third.wait_send()


def add_into(target, term, rows):
    step = rows // 2

    def block(i, carry):
        at = pl.ds(pl.multiple_of(i * step, step), step)
        target[at, :] = (target[at, :].astype(F32) + term[at, :].astype(F32)).astype(BF)
        return carry

    lax.fori_loop(0, 2, block, 0)


class Plane:
    def __init__(self, pc):
        self.x, self.y, self.d = pc.p + 1 - 2 * (pc.p % 2), (pc.p + 2) % 4, 3 - pc.p
        self.to_x, self.to_y = pc.dev(self.x, pc.r, pc.t), pc.dev(self.y, pc.r, pc.t)

    def halves(self, ref):
        half = ref.shape[0] // 2
        return ref.at[pl.ds(0, half)], ref.at[pl.ds(half, half)]

    def wait_send(self, m):
        for move in self.first[m] + self.second[m]:
            move.wait_send()


class PlaneGather(Plane):
    @staticmethod
    def sems(pc):
        return [DMA((MB, 4)), DMA((MB, 4))]

    def __init__(self, pc, spot, sems):
        super().__init__(pc)
        send, recv = sems
        self.first, self.second = [], []
        for m in range(MB):
            own, from_x, from_y = spot(m, pc.p), spot(m, self.x), spot(m, self.y)
            (a, _), (_, b), (here_a, here_b) = self.halves(from_x), self.halves(from_y), self.halves(spot(m, self.d))
            self.first.append(
                [
                    Move(own, own, send.at[m, 0], recv.at[m, 0], self.to_x, from_x, recv.at[m, 0]),
                    Move(own, own, send.at[m, 1], recv.at[m, 1], self.to_y, from_y, recv.at[m, 1]),
                ]
            )
            self.second.append(
                [
                    Move(a, a, send.at[m, 2], recv.at[m, 2], self.to_y, here_a, recv.at[m, 2]),
                    Move(b, b, send.at[m, 3], recv.at[m, 3], self.to_x, here_b, recv.at[m, 3]),
                ]
            )

    def start(self, m):
        for move in self.first[m]:
            move.start()

    def relay(self, m):
        for arrived, move in zip(self.first[m], self.second[m]):
            arrived.wait_recv()
            move.start()

    def wait_recv(self, m):
        for move in self.second[m]:
            move.wait_recv()


class PlaneScatter(Plane):
    @staticmethod
    def sems(pc):
        return [DMA((MB, 6)), DMA((MB, 6))]

    def __init__(self, pc, sent, got, sems):
        super().__init__(pc)
        send, recv = sems
        self.first, self.second, self.adds = [], [], []
        for m in range(MB):

            def move(i, src, dst, dev, landing):
                return Move(src, dst, send.at[m, i], recv.at[m, i], dev, landing, recv.at[m, i])

            for_x, for_y, for_d = (self.halves(sent.at[m, q]) for q in (self.x, self.y, self.d))
            hop = self.halves(got.at[pc.p, m])
            hop_x, hop_y = self.halves(got.at[self.x, m]), self.halves(got.at[self.y, m])
            mine = hop
            self.first.append(
                [
                    move(0, for_d[0], hop_x[0], self.to_x, hop[0]),
                    move(1, for_d[1], hop_y[1], self.to_y, hop[1]),
                    move(2, for_x[0], mine[0], self.to_x, hop_x[0]),
                    move(3, for_y[1], mine[1], self.to_y, hop_y[1]),
                ]
            )
            self.second.append(
                [
                    move(5, for_y[0], mine[0], self.to_y, hop_y[0]),
                    move(4, for_x[1], mine[1], self.to_x, hop_x[1]),
                ]
            )
            self.adds.append([(for_y[0], hop[0]), (for_x[1], hop[1])])

    def start(self, m):
        for move in self.first[m]:
            move.start()

    def relay(self, m):
        for arrived, (target, term), move in zip(self.first[m], self.adds[m], self.second[m]):
            arrived.wait_recv()
            add_into(target, term, target.shape[0])
            move.start()

    def wait_recv(self, m):
        for move in self.first[m][2:] + self.second[m]:
            move.wait_recv()


def plane_sum(pc, sent, got, m, at):
    total = sent[m, pc.p, at, :].astype(F32)
    for q in (pc.p + 1 - 2 * (pc.p % 2), (pc.p + 2) % 4):
        total = total + got[q, m, at, :].astype(F32)
    return total


def greet(pc):
    barrier = pltpu.get_barrier_semaphore()

    def step(i, carry):
        dev = pc.flat((pc.me + i) % pc.n_dev)
        pl.semaphore_signal(barrier, inc=1, device_id=dev, device_id_type=MESH)
        return carry

    lax.fori_loop(1, pc.n_dev, step, 0)
    pl.semaphore_wait(barrier, pc.n_dev - 1)


def fused(collective_id, kernel, near_ins, far_ins, outs, scratch):
    ins_leaves, ins_tree = jax.tree.flatten((near_ins, far_ins))
    outs_leaves, outs_tree = jax.tree.flatten(outs)
    scratch_leaves, scratch_tree = jax.tree.flatten(scratch)
    a, b = len(ins_leaves), len(outs_leaves)
    near = len(jax.tree.leaves(near_ins))

    def run(*refs):
        first, second = jax.tree.unflatten(ins_tree, refs[:a])
        third = jax.tree.unflatten(outs_tree, refs[a : a + b])
        fourth = jax.tree.unflatten(scratch_tree, refs[a + b :])
        kernel(
            Place(),
            types.SimpleNamespace(**first),
            types.SimpleNamespace(**second),
            types.SimpleNamespace(**third),
            types.SimpleNamespace(**fourth),
        )

    got = pl.pallas_call(
        run,
        out_shape=tuple(outs_leaves),
        in_specs=[pl.BlockSpec(memory_space=VM if i < near else pl.ANY) for i in range(a)],
        out_specs=tuple([pl.BlockSpec(memory_space=pl.ANY)] * b),
        scratch_shapes=scratch_leaves,
        compiler_params=pltpu.CompilerParams(
            collective_id=collective_id, has_side_effects=True, vmem_limit_bytes=VMEM_LIMIT
        ),
    )(*ins_leaves)
    return types.SimpleNamespace(**jax.tree.unflatten(outs_tree, got))


def dot_nt(a, b):
    return lax.dot_general(a, b, (((1,), (1,)), ((), ())), preferred_element_type=F32)


def dot_tn(a, b):
    return lax.dot_general(a, b, (((0,), (0,)), ((), ())), preferred_element_type=F32)


def dot_nn(a, b):
    return lax.dot_general(a, b, (((1,), (0,)), ((), ())), preferred_element_type=F32)


def half_means(x):
    a = lax.broadcasted_iota(jnp.int32, (LANES, LANES), 0) // HEAD_DIM
    b = lax.broadcasted_iota(jnp.int32, (LANES, LANES), 1) // HEAD_DIM
    same = jnp.where(a == b, 1.0 / HEAD_DIM, 0.0).astype(BF)
    high = x.astype(BF)
    rest = (x - high.astype(F32)).astype(BF)
    return dot_nn(high, same) + dot_nn(rest, same)


def swap_halves(x):
    return pltpu.roll(x, HEAD_DIM, 1)


def low_lanes(shape):
    return lax.broadcasted_iota(jnp.int32, shape, len(shape) - 1) < HEAD_DIM


def row_mean(x):
    return jnp.mean(x, axis=-1, keepdims=True)


def inv_rms(x):
    return lax.rsqrt(row_mean(x * x) + EPSILON)


def tile_of(j):
    return slice(j * LANES, (j + 1) * LANES)


def rows_loop(count, fn):
    def step(i, carry):
        fn(pl.ds(pl.multiple_of(i * ROW_STEP, ROW_STEP), ROW_STEP))
        return carry

    lax.fori_loop(0, count // ROW_STEP, step, 0)


def chunks(count, fn):
    def step(c, carry):
        fn(pl.ds(pl.multiple_of(c * CHUNK, CHUNK), CHUNK))
        return carry

    lax.fori_loop(0, count // CHUNK, step, 0)


def take_rows(hot, arrived, put):
    def block(at):
        x = arrived[:, :, at].astype(F32).reshape(-1, CHUNK).astype(BF)
        put(at, dot_nn(hot[...], x))

    chunks(arrived.shape[2], block)


def give_rows(hot, rows, out):
    def block(at):
        y = dot_tn(hot[...], rows(at))
        out[:, :, at] = y.reshape(out.shape[0], PAD, CHUNK).astype(BF)

    chunks(out.shape[2], block)


def fill_mask(bias, segq, segk):
    seq = bias.shape[0]
    rows = lax.broadcasted_iota(jnp.int32, (seq, seq), 0)
    cols = lax.broadcasted_iota(jnp.int32, (seq, seq), 1)
    bias[...] = jnp.where((segq == segk) & (cols <= rows), 0.0, MASKED)


def forward(pc, tok_sent, cot_sent, wqk, wvo, wup, wgate, wdown, small, hot, rattn, rmlp, segq, segk):
    n_dev, _, width = tok_sent.shape
    part = hot.shape[0] // MB
    seq = part * pc.n_p
    qk_cols, vo_cols, hid = wqk.shape[1], wvo.shape[1], wup.shape[1]
    o_cols = QUADS + LANES
    tiles = hid // LANES
    blocks = (MB, pc.n_p, part, width)
    kept = dict(
        hb=(blocks, BF),
        qk=((MB, seq, qk_cols), F32),
        qkb=((MB, seq, qk_cols), BF),
        vb=((MB, seq, o_cols), BF),
        ob=((MB, seq, o_cols), BF),
        lse=((MB, seq, LANES), F32),
        tok=((MB, part, width), BF),
        a=((MB, part, width), F32),
        h1=((MB, part, width), F32),
        c=((MB, part, width), F32),
        hb1=(blocks, BF),
        u=((MB, seq, hid), BF),
        g=((MB, seq, hid), BF),
        mb=((MB, seq, hid), BF),
        h2=((MB, part, width), BF),
    )
    whole = dict(
        wqk=((width, qk_cols), BF),
        wvo=((width, vo_cols), BF),
        wup=((width, hid), BF),
        wgate=((width, hid), BF),
        wdown=((width, hid), BF),
        sup=((1, hid), F32),
        sgate=((1, hid), F32),
        sqk=((1, qk_cols), F32),
    )
    outs = {n: SDS(*x) for n, x in (kept | whole).items()} | dict(cot=SDS(cot_sent.shape, BF))
    scratch = {n: VM(*x) for n, x in (kept | whole).items()} | dict(
        arrived=VM(tok_sent.shape, BF),
        aqk=VM((pc.n_t,) + wqk.shape, BF),
        avo=VM((pc.n_t,) + wvo.shape, BF),
        small=VM((pc.n_t,) + small.shape, F32),
        bias=VM((seq, seq), F32),
        sent=VM(blocks, BF),
        got=VM((pc.n_p, MB, part, width), BF),
        kept_sem={n: DMA((MB,)) for n in kept},
        whole_sem={n: DMA((1,)) for n in whole},
        tok_sem=Deal.sems(pc),
        cot_sem=Deal.sems(pc),
        small_sem=pair(pc.n_t) + [DMA((1,))],
        qk_sem=HeadWeights.sems(pc),
        vo_sem=HeadWeights.sems(pc),
        up_sem=HiddenWeights.sems(pc),
        gate_sem=HiddenWeights.sems(pc),
        down_sem=HiddenWeights.sems(pc),
        ag_sem=PlaneGather.sems(pc),
        ra_sem=PlaneScatter.sems(pc),
        ag1_sem=PlaneGather.sems(pc),
        rc_sem=PlaneScatter.sems(pc),
    )
    near_ins = dict(hot=hot, rattn=rattn, rmlp=rmlp, segq=segq, segk=segk)
    far_ins = dict(
        tok=tok_sent, cot=cot_sent, wqk=wqk, wvo=wvo, wup=wup, wgate=wgate, wdown=wdown, small=small
    )

    def kernel(pc, v, x, o, k):
        own_p = pc.p
        greet(pc)
        deal = Deal(pc, x.tok, k.arrived, k.tok_sem)
        deal_cot = Deal(pc, x.cot, o.cot, k.cot_sem)
        head_qk = HeadWeights(pc, x.wqk, k.aqk, k.wqk, k.qk_sem)
        head_vo = HeadWeights(pc, x.wvo, k.avo, k.wvo, k.vo_sem)
        up = HiddenWeights(pc, x.wup, k.wup, k.up_sem)
        gate = HiddenWeights(pc, x.wgate, k.wgate, k.gate_sem)
        down = HiddenWeights(pc, x.wdown, k.wdown, k.down_sem)
        ss, rs, ls = k.small_sem
        scales = Moves(
            [
                Move(
                    x.small, k.small.at[pc.t], ss.at[q], rs.at[pc.t], pc.dev(pc.p, pc.r, q), k.small.at[q], rs.at[q]
                )
                for q in others(pc.n_t, pc.t)
            ]
        )
        own_scales = pltpu.make_async_copy(x.small, k.small.at[pc.t], ls.at[0])

        def gather(buf, sems):
            return PlaneGather(pc, lambda m, q: buf.at[m, q], sems)

        ag, ag1 = gather(k.hb, k.ag_sem), gather(k.hb1, k.ag1_sem)
        ra, rc = (PlaneScatter(pc, k.sent, k.got, sems) for sems in (k.ra_sem, k.rc_sem))
        names = vars(k)
        out_names = vars(o)
        copies = []

        def keep(m, *refs):
            for n in kept:
                if any(names[n] is ref for ref in refs):
                    copy = pltpu.make_async_copy(names[n].at[m], out_names[n].at[m], k.kept_sem[n].at[m])
                    copy.start()
                    copies.append(copy)

        def keep_whole(*refs):
            for n in whole:
                if any(names[n] is ref for ref in refs):
                    copy = pltpu.make_async_copy(names[n], out_names[n], k.whole_sem[n].at[0])
                    copy.start()
                    copies.append(copy)

        def attend(m):
            fill_mask(k.bias, v.segq[m], v.segk[m])
            ag.wait_recv(m)
            keep(m, k.hb)

            def project(i, carry):
                rows = k.hb[m, pl.ds(2 * i, 2)].reshape(2 * part, width)
                at = pl.ds(pl.multiple_of(i * 2 * part, 2 * part), 2 * part)
                qk = dot_nn(rows, k.wqk[...])
                k.qk[m, at, :] = qk
                for j in range(qk_cols // LANES):
                    s = qk[:, tile_of(j)]
                    n = s * lax.rsqrt(half_means(s * s) + EPSILON)
                    k.qkb[m, at, tile_of(j)] = (n * k.sqk[:, tile_of(j)]).astype(BF)
                k.vb[m, at, :QUADS] = dot_nn(rows, k.wvo[:, :QUADS]).astype(BF)
                last = dot_nn(rows, k.wvo[:, 2 * QUADS :])
                k.vb[m, at, QUADS:] = jnp.where(low_lanes(last.shape), last, 0.0).astype(BF)
                return carry

            lax.fori_loop(0, pc.n_p // 2, project, 0)
            keep(m, k.qk, k.qkb, k.vb)
            if m == 1:
                ra.relay(0)
            blk = seq // 2
            for i in range(2):
                nk = (i + 1) * blk
                at = slice(i * blk, nk)
                bias = k.bias[at, :nk]
                lse = jnp.zeros((blk, LANES), F32)
                lane = lax.broadcasted_iota(jnp.int32, (blk, LANES), 1)
                for slab in range(3):
                    if slab < 2:
                        qs = k.qkb[m, at, tile_of(slab)]
                        ks = k.qkb[m, :nk, tile_of(2 + slab)]
                    else:
                        qs = k.qkb[m, at, 2 * QUADS :]
                        ks = swap_halves(k.qkb[m, :nk, 2 * QUADS :].astype(F32)).astype(BF)
                    vs = k.vb[m, :nk, tile_of(slab)]
                    res = []
                    for half in range(2 if slab < 2 else 1):
                        low = low_lanes(qs.shape)
                        q1 = jnp.where(low if half == 0 else jnp.logical_not(low), qs, jnp.zeros_like(qs))
                        s = dot_nt(q1, ks) * HEAD_DIM ** (-0.5) + bias
                        top = jnp.max(s, axis=1, keepdims=True)
                        e = jnp.exp(s - top)
                        tot = jnp.sum(e, axis=1, keepdims=True)
                        lse = jnp.where(lane == 2 * slab + half, top + jnp.log(tot), lse)
                        res.append(dot_nn((e * (1.0 / tot)).astype(BF), vs))
                    if slab < 2:
                        res = jnp.where(low_lanes(res[0].shape), res[0], res[1])
                    else:
                        res = swap_halves(res[0])
                    k.ob[m, at, tile_of(slab)] = res.astype(BF)
                k.lse[m, at, :] = lse
            keep(m, k.ob, k.lse)
            if m == 0:
                ag.relay(1)

            def branch(i, carry):
                at = pl.ds(pl.multiple_of(i * 2 * part, 2 * part), 2 * part)
                y = dot_nt(k.ob[m, at, :], k.wvo[:, QUADS:])
                k.sent[m, pl.ds(2 * i, 2)] = y.astype(BF).reshape(2, part, width)
                return carry

            lax.fori_loop(0, pc.n_p // 2, branch, 0)
            ra.start(m)

        def summed(m, at):
            return plane_sum(pc, k.sent, k.got, m, at)

        def middle(m):
            ra.wait_recv(m)

            def rows(at):
                a = summed(m, at)
                h = k.tok[m, at, :].astype(F32)
                y = h + v.rattn[...] * (a * inv_rms(a) - h)
                h1 = y * inv_rms(y)
                k.a[m, at, :] = a
                k.h1[m, at, :] = h1
                k.hb1[m, own_p, at, :] = h1.astype(BF)

            rows_loop(part, rows)
            ag1.start(m)
            keep(m, k.a, k.h1)

        def feed(m):
            ag1.wait_recv(m)
            keep(m, k.hb1)

            def hidden(at):
                rows = k.hb1[m].reshape(seq, width)
                u = dot_nn(rows, k.wup[:, at])
                g = dot_nn(rows, k.wgate[:, at])
                k.u[m, :, at] = u.astype(BF)
                k.g[m, :, at] = g.astype(BF)
                z = k.sgate[:, at] * g
                k.mb[m, :, at] = (z / (1.0 + jnp.exp(-z)) * (k.sup[:, at] * u)).astype(BF)

            chunks(hid, hidden)
            keep(m, k.u, k.g, k.mb)

        def shrink(m):
            ra.wait_send(m)

            def columns(at):
                y = dot_nt(k.mb[m], k.wdown[at, :])
                k.sent[m, :, :, at] = y.astype(BF).reshape(pc.n_p, part, CHUNK)

            chunks(width, columns)
            rc.start(m)

        def finish(m):
            rc.wait_recv(m)

            def rows(at):
                c = summed(m, at)
                h1 = k.h1[m, at, :]
                z = h1 + v.rmlp[...] * (c * inv_rms(c) - h1)
                k.c[m, at, :] = c
                k.h2[m, at, :] = (z * inv_rms(z)).astype(BF)

            rows_loop(part, rows)
            keep(m, k.c, k.h2)

        deal.start()
        head_qk.start()
        head_vo.start()
        scales.start()
        own_scales.start()
        for w in (up, gate, down):
            w.start()
        head_qk.relay()
        head_vo.relay()
        deal.wait_recv()

        def put(at, y):
            for m in range(MB):
                rows = y[m * part : (m + 1) * part].astype(BF)
                k.tok[m, :, at] = rows
                k.hb[m, own_p, :, at] = rows

        take_rows(v.hot, k.arrived, put)
        for m in range(MB):
            ag.start(m)
            keep(m, k.tok)
        head_qk.plane()
        head_vo.plane()
        up.tall()
        gate.tall()
        own_scales.wait()
        scales.wait_recv()
        for t in range(pc.n_t):
            for j in range(3):

                def move(t=t, j=j):
                    at = lanes(dst_tile(pc.p, t) + j, 1)
                    k.sup[:, at] = k.small[t, pl.ds(src_tile(pc.p, t) + j, 1), :]
                    k.sgate[:, at] = k.small[t, pl.ds(tiles + src_tile(pc.p, t) + j, 1), :]

                Move.under(width3(pc.p, t) if j == 2 else None, move)
        for j in range(qk_cols // LANES):
            k.sqk[:, tile_of(j)] = k.small[own_p, 2 * tiles + j : 2 * tiles + j + 1, :]
        keep_whole(k.sup, k.sgate, k.sqk)
        head_qk.near()
        head_vo.near()
        head_qk.wait_recv()
        head_vo.wait_recv()
        keep_whole(k.wqk, k.wvo)
        ag.relay(0)
        attend(0)
        down.tall()
        attend(1)
        up.relay()
        gate.relay()
        middle(0)
        ra.relay(1)
        middle(1)
        ag1.relay(0)
        up.near()
        gate.near()
        ag1.relay(1)
        up.wait_recv()
        gate.wait_recv()
        down.relay()
        feed(0)
        keep_whole(k.wup, k.wgate)
        feed(1)
        down.near()
        down.wait_recv()
        deal_cot.start()
        shrink(0)
        rc.relay(0)
        keep_whole(k.wdown)
        shrink(1)
        rc.relay(1)
        for m in range(MB):
            finish(m)
        deal_cot.wait_recv()
        for w in (deal, deal_cot, head_qk, head_vo, up, gate, down, scales):
            w.wait_send()
        for m in range(MB):
            for w in (ag, ag1, rc):
                w.wait_send(m)
        for copy in copies:
            copy.wait()

    return fused(1, kernel, near_ins, far_ins, outs, scratch)


def backward(pc, f, hot, rattn, rmlp, segq, segk):
    n_dev = f.cot.shape[0]
    part, width = f.h2.shape[1], f.h2.shape[2]
    seq = part * pc.n_p
    all_tok = MB * seq
    qk_cols, hid = f.wqk.shape[1], f.wup.shape[1]
    o_cols = QUADS + LANES
    tiles = hid // LANES
    n_rows = width // (pc.n_p * pc.n_r)
    step_rows = n_rows // 5
    if n_rows % 5 or hid != width:
        raise ValueError("sizes")
    blocks = (MB, pc.n_p, part, width)
    dealt = (n_dev, PAD, width)
    vec_rows = 4 * tiles
    vec_total = -(-(2 * vec_rows + 2 * tiles + pc.n_p * qk_cols // LANES) // PAD) * PAD
    heads_shape = (pc.n_p, n_rows, qk_cols)
    outs = dict(
        back_out=SDS(dealt, BF),
        back_grad=SDS(dealt, BF),
        vec=SDS((vec_total, LANES), F32),
        relay=[SDS((pc.n_p, n_rows, 3 * LANES), BF) for _ in range(3)],
        head_relay=[SDS((n_rows, qk_cols), BF) for _ in range(2)],
        tall=[SDS((pc.n_t, pc.n_p, n_rows, 3 * LANES), BF) for _ in range(3)],
        final=[SDS((n_rows, hid), BF) for _ in range(3)],
        head_p=[SDS(heads_shape, BF) for _ in range(2)],
        head_t=[SDS(heads_shape, BF) for _ in range(2)],
    )
    loaded = dict(
        c=f.c,
        h1=f.h1,
        wdown=f.wdown,
        u=f.u,
        g=f.g,
        sup=f.sup,
        sgate=f.sgate,
        wup=f.wup,
        wgate=f.wgate,
        mb=f.mb,
        hb1=f.hb1,
        tok=f.tok,
        wvo=f.wvo,
        vb=f.vb,
        qkb=f.qkb,
        lse=f.lse,
        qk=f.qk,
        sqk=f.sqk,
        wqk=f.wqk,
        ob=f.ob,
    )
    later = dict(a=f.a, hb=f.hb, cot=f.cot, h2=f.h2)
    sums = dict(gsup=hid, gsgate=hid, gsqk=qk_cols, grattn=width, grmlp=width)
    scratch = {n: VM(y.shape, y.dtype) for n, y in loaded.items()} | {n: VM((1, y), F32) for n, y in sums.items()}
    scratch |= dict(
        load_sem={n: DMA((1,)) for n in loaded},
        later_sem=[DMA((1,)) for _ in later],
        dcb=VM(blocks, BF),
        dab=VM(blocks, BF),
        mid=VM((MB, part, width), F32),
        bias=VM((seq, seq), F32),
        sent=VM(blocks, BF),
        got=VM((pc.n_p, MB, part, width), BF),
        tbuf=VM((pc.n_t, pc.n_p, n_rows, 3 * LANES), BF),
        dealbuf=VM(dealt, BF),
        vec=VM((vec_total, LANES), F32),
        vec_got=[VM((y, vec_total, LANES), F32) for y in (pc.n_r, pc.n_t, pc.n_p)],
        rbuf=VM((pc.n_p, n_rows, 3 * LANES), BF),
        hbuf=[VM((2, n_rows, qk_cols), BF) for _ in range(2)],
        near=[VM((pc.n_r - 1, pc.n_p, n_rows, y), BF) for y in (hid, hid, hid, qk_cols, qk_cols)],
        near_sem=[pair(pc.n_r) for _ in range(5)],
        tall_sem=[[DMA((2, pc.n_t)) for _ in range(3)] for _ in range(3)],
        plane_sem=[[DMA((2, pc.n_p)) for _ in range(2)] for _ in range(5)],
        relay_sem=[[DMA((2,)) for _ in range(5)] for _ in range(3)],
        head_sem=[pair(pc.n_t) + [DMA((1,))] for _ in range(2)],
        head_relay_sem=[[DMA((1,)) for _ in range(5)] for _ in range(2)],
        out_sem=Deal.sems(pc),
        grad_sem=Deal.sems(pc),
        vec_sem=[pair(y) for y in (pc.n_r, pc.n_t, pc.n_p)],
        vec_out=DMA((1,)),
        ag_sem=PlaneGather.sems(pc),
        ag1_sem=PlaneGather.sems(pc),
        rh1_sem=PlaneScatter.sems(pc),
        rh_sem=PlaneScatter.sems(pc),
    )
    near_ins = dict(hot=hot, rattn=rattn, rmlp=rmlp, segq=segq, segk=segk)

    def kernel(pc, v, x, o, k):
        own_p = pc.p
        refs = vars(k)
        sources = vars(x)
        loads = {n: pltpu.make_async_copy(sources[n], refs[n], k.load_sem[n].at[0]) for n in loaded}
        for n in loaded:
            loads[n].start()
        cot_load = pltpu.make_async_copy(x.cot, k.dealbuf, k.later_sem[2].at[0])
        h2_load = pltpu.make_async_copy(x.h2, k.dab.at[:, own_p], k.later_sem[3].at[0])
        cot_load.start()
        h2_load.start()
        k_dqk, k_dv = k.u.at[:, :, pl.ds(0, qk_cols)], k.u.at[:, :, pl.ds(qk_cols, o_cols)]
        k_do = k.g.at[0, :, pl.ds(0, o_cols)]
        a_load = pltpu.make_async_copy(x.a, k.c, k.later_sem[0].at[0])
        hb_load = pltpu.make_async_copy(x.hb.reshape(MB, seq, width), k.mb, k.later_sem[1].at[0])
        waited = set()

        def ready(*wanted):
            for n in loaded:
                if n not in waited and any(refs[n] is ref for ref in wanted):
                    waited.add(n)
                    loads[n].wait()

        for n in sums:
            refs[n][...] = jnp.zeros(refs[n].shape, F32)
        k.vec[...] = jnp.zeros(k.vec.shape, F32)
        greet(pc)

        ag, ag1 = (
            PlaneGather(pc, lambda m, q, buf=buf: buf.at[m, q], sems)
            for buf, sems in ((k.dcb, k.ag_sem), (k.dab, k.ag1_sem))
        )
        rh1, rh = (PlaneScatter(pc, k.sent, k.got, sems) for sems in (k.rh1_sem, k.rh_sem))
        deal_out = Deal(pc, k.dealbuf, o.back_out, k.out_sem)
        deal_grad = Deal(pc, k.dealbuf, o.back_grad, k.grad_sem)

        def add_rows(ref, y, at=slice(None)):
            ref[:, at] += jnp.sum(y, axis=0, keepdims=True)

        def top(m):
            def rows(at):
                c, h1, ct = k.c[m, at, :], k.h1[m, at, :], k.mid[m, at, :]
                r_c = inv_rms(c)
                n_c = c * r_c
                z = h1 + v.rmlp[...] * (n_c - h1)
                r_z = inv_rms(z)
                h2 = z * r_z
                dz = r_z * (ct - h2 * row_mean(ct * h2))
                add_rows(k.grmlp, dz * (n_c - h1))
                k.mid[m, at, :] = (1.0 - v.rmlp[...]) * dz
                dn = v.rmlp[...] * dz
                k.dcb[m, own_p, at, :] = (r_c * (dn - n_c * row_mean(dn * n_c))).astype(BF)

            rows_loop(part, rows)
            ag.start(m)

        def summed(m, at):
            return plane_sum(pc, k.sent, k.got, m, at)

        def feed(m):
            ag.wait_recv(m)

            def hidden(at):
                dm = dot_nn(k.dcb[m].reshape(seq, width), k.wdown[:, at])
                u, g = k.u[m, :, at].astype(F32), k.g[m, :, at].astype(F32)
                y = k.sgate[:, at] * g
                sig = 1.0 / (1.0 + jnp.exp(-y))
                du = dm * (y * sig)
                dx = dm * (k.sup[:, at] * u) * (sig * (1.0 + y * (1.0 - sig)))
                add_rows(k.gsup, du * u, at)
                add_rows(k.gsgate, dx * g, at)
                k.u[m, :, at] = (k.sup[:, at] * du).astype(BF)
                k.g[m, :, at] = (k.sgate[:, at] * dx).astype(BF)

            chunks(hid, hidden)

        def shrink(m):
            def columns(at):
                y = dot_nt(k.u[m], k.wup[at, :]) + dot_nt(k.g[m], k.wgate[at, :])
                k.sent[m, :, :, at] = y.astype(BF).reshape(pc.n_p, part, CHUNK)

            chunks(width, columns)
            rh1.start(m)

        grads = [k.wdown, k.wup, k.wgate, k.wqk, k.wvo]

        def near_slot(source, at):
            return (source - at + pc.n_r - 1) % pc.n_r

        def near_moves(i):
            send, recv = k.near_sem[i]
            return Moves(
                [
                    Move(
                        by_shard(pc, grads[i]).at[:, q], k.near[i].at[near_slot(pc.r, q)], send.at[q], recv.at[pc.r],
                        pc.dev(pc.p, q, pc.t), k.near[i].at[near_slot(q, pc.r)], recv.at[q],
                    )
                    for q in others(pc.n_r, pc.r)
                ]
            )

        near = [near_moves(i) for i in range(5)]

        def row_blocks(fn):
            def block(i, carry):
                fn(i // 5, pl.ds(pl.multiple_of((i % 5) * step_rows, step_rows), step_rows))
                return carry

            lax.fori_loop(0, pc.n_p * 5, block, 0)

        def near_sum(i):
            near[i].wait_recv()
            own = by_shard(pc, grads[i])

            def block(p, at):
                total = own[p, pc.r, at, :].astype(F32)
                for j in range(pc.n_r - 1):
                    total = total + k.near[i][j, p, at, :].astype(F32)
                k.near[i][0, p, at, :] = total.astype(BF)

            row_blocks(block)

        t = pc.t
        middle_dev = (t == 1) | (t == 2)
        end_dev = jnp.logical_not(middle_dev)
        far = jnp.where((t == 2) | (t == 3), 0, 3)
        by = jnp.where(t == 0, 1, 2)
        wide = width3(pc.p, t)
        wide_far = width3(pc.p, far)

        def direct_out(q):
            return (jnp.abs(q - t) != 3) & jnp.logical_not(middle_dev & (q == far))

        def comes(q):
            return jnp.abs(q - t) != 3

        def tall_moves(i):
            send, recv, _ = k.tall_sem[i]
            src, y = k.near[i].at[0], o.tall[i]
            moves = []
            for q in others(pc.n_t, t):
                there = dst_tile(pc.p, q)
                dev = pc.dev(pc.p, pc.r, q)
                moves.append(
                    Move(
                        src.at[:, :, lanes(there, 2)], y.at[t, :, :, TWO], send.at[0, q], recv.at[0, t], dev,
                        y.at[q, :, :, TWO], recv.at[0, q], direct_out(q), comes(q),
                    )
                )
                moves.append(
                    Move(
                        src.at[:, :, lanes(there + 2, 1)], y.at[t, :, :, ONE], send.at[1, q], recv.at[1, t], dev,
                        y.at[q, :, :, ONE], recv.at[1, q], direct_out(q) & width3(pc.p, q), comes(q) & wide,
                    )
                )
            return Moves(moves)

        def far_parts(i):
            at = dst_tile(pc.p, far)
            return ((TWO, lanes(at, 2), None), (ONE, lanes(at + 2, 1), wide_far))

        def both(a, b):
            return a if b is None else a & b

        def handed_moves(i):
            s1, r1, _, _, _ = k.relay_sem[i]
            src, y = k.near[i].at[0], o.relay[i]
            return Moves(
                [
                    Move(
                        src.at[:, :, at], y.at[:, :, w], s1.at[j], r1.at[j], pc.dev(pc.p, pc.r, by), y.at[:, :, w],
                        r1.at[j], both(end_dev, cond), both(middle_dev, cond),
                    )
                    for j, (w, at, cond) in enumerate(far_parts(i))
                ]
            )

        def passed_moves(i):
            _, _, s2, _, _ = k.relay_sem[i]
            recv = k.tall_sem[i][1]
            return Moves(
                [
                    Move(
                        k.rbuf.at[:, :, w], o.tall[i].at[t, :, :, w], s2.at[j], recv.at[j, t], pc.dev(pc.p, pc.r, far),
                        None, None, both(middle_dev, cond),
                    )
                    for j, (w, at, cond) in enumerate(far_parts(i))
                ]
            )

        tall = [tall_moves(i) for i in range(3)]
        handed = [handed_moves(i) for i in range(3)]
        passed = [passed_moves(i) for i in range(3)]

        def tall_start(i):
            handed[i].start()
            tall[i].start()

        def tall_relay(i):
            handed[i].wait_recv()

            @pl.when(middle_dev)
            def _():
                copy = pltpu.make_async_copy(o.relay[i], k.rbuf, k.relay_sem[i][3].at[0])
                copy.start()
                copy.wait()

                def add(w, at):
                    def block(p, rows):
                        total = k.rbuf[p, rows, w].astype(F32) + k.near[i][0, p, rows, at].astype(F32)
                        k.rbuf[p, rows, w] = total.astype(BF)

                    row_blocks(block)

                for w, at, cond in far_parts(i):
                    Move.under(cond, lambda w=w, at=at: add(w, at))

            passed[i].start()

        def tall_sum(i):
            tall[i].wait_recv()
            local = []
            for q in others(pc.n_t, t):
                for j, (w, cond) in enumerate(((TWO, comes(q)), (ONE, comes(q) & wide))):
                    copy = pltpu.make_async_copy(
                        o.tall[i].at[q, :, :, w], k.tbuf.at[q, :, :, w], k.tall_sem[i][2].at[j, q]
                    )
                    Move.under(cond, copy.start)
                    local.append((cond, copy))
            for cond, copy in local:
                Move.under(cond, copy.wait)
            here = dst_tile(pc.p, t)

            def add(source, target):
                def block(p, at):
                    total = k.near[i][0, p, at, source].astype(F32)
                    for q in others(pc.n_t, t):
                        total = total + jnp.where(comes(q), k.tbuf[q, p, at, target].astype(F32), 0.0)
                    k.tbuf[t, p, at, target] = total.astype(BF)

                row_blocks(block)

            add(lanes(here, 2), TWO)
            pl.when(wide)(lambda: add(lanes(here + 2, 1), ONE))

        def plane_moves(i):
            send, recv = k.plane_sem[i]
            y, src = o.final[i], k.tbuf.at[pc.t]
            here = src_tile(pc.p, pc.t)
            moves = []
            for q in others(pc.n_p, pc.p):
                there = src_tile(q, pc.t)
                dev = pc.dev(q, pc.r, pc.t)
                moves.append(
                    Move(
                        src.at[q, :, TWO], y.at[:, lanes(here, 2)], send.at[0, q], recv.at[0, pc.p], dev,
                        y.at[:, lanes(there, 2)], recv.at[0, q],
                    )
                )
                moves.append(
                    Move(
                        src.at[q, :, ONE], y.at[:, lanes(here + 2, 1)], send.at[1, q], recv.at[1, pc.p], dev,
                        y.at[:, lanes(there + 2, 1)], recv.at[1, q], wide, width3(q, pc.t),
                    )
                )
            own = (
                (None, pltpu.make_async_copy(src.at[own_p, :, TWO], y.at[:, lanes(here, 2)], send.at[0, pc.p])),
                (wide, pltpu.make_async_copy(src.at[own_p, :, ONE], y.at[:, lanes(here + 2, 1)], send.at[1, pc.p])),
            )
            return Moves(moves), own

        plane = [plane_moves(i) for i in range(3)]

        def plane_start(i):
            moves, own = plane[i]
            moves.start()
            for cond, copy in own:
                Move.under(cond, copy.start)

        def plane_sent(i):
            moves, own = plane[i]
            moves.wait_send()
            for cond, copy in own:
                Move.under(cond, copy.wait)

        def head_planes(i):
            send, recv = k.plane_sem[3 + i]
            src, y = k.near[3 + i].at[0], o.head_p[i]
            return Moves(
                [
                    Move(
                        src.at[q], y.at[pc.p], send.at[0, q], recv.at[0, pc.p], pc.dev(q, pc.r, pc.t), y.at[q],
                        recv.at[0, q],
                    )
                    for q in others(pc.n_p, pc.p)
                ]
            )

        def head_talls(i):
            send, recv, _ = k.head_sem[i]
            src, y = o.head_p[i], o.head_t[i]
            return Moves(
                [
                    Move(
                        src.at[q], y.at[t], send.at[q], recv.at[t], pc.dev(pc.p, pc.r, q), y.at[q], recv.at[q],
                        direct_out(q), comes(q),
                    )
                    for q in others(pc.n_t, t)
                ]
            )

        def head_handed(i):
            s1, r1, _, _, _ = k.head_relay_sem[i]
            y = o.head_relay[i]
            return Move(
                o.head_p[i].at[far], y, s1.at[0], r1.at[0], pc.dev(pc.p, pc.r, by), y, r1.at[0], end_dev, middle_dev
            )

        def head_passed(i):
            _, _, s2, _, _ = k.head_relay_sem[i]
            recv = k.head_sem[i][1]
            return Move(
                k.hbuf[i].at[0], o.head_t[i].at[t], s2.at[0], recv.at[t], pc.dev(pc.p, pc.r, far), None, None, middle_dev
            )

        head_first = [head_handed(i) for i in range(2)]
        head_last = [head_passed(i) for i in range(2)]

        def head_start(i):
            head_first[i].start()
            head_tall[i].start()

        def head_relay(i):
            head_first[i].wait_recv()

            @pl.when(middle_dev)
            def _():
                copies = [
                    pltpu.make_async_copy(o.head_relay[i], k.hbuf[i].at[0], k.head_relay_sem[i][3].at[0]),
                    pltpu.make_async_copy(o.head_p[i].at[far], k.hbuf[i].at[1], k.head_relay_sem[i][4].at[0]),
                ]
                for copy in copies:
                    copy.start()
                for copy in copies:
                    copy.wait()
                k.hbuf[i][0] = (k.hbuf[i][0].astype(F32) + k.hbuf[i][1].astype(F32)).astype(BF)

            head_last[i].start()

        head_plane = [head_planes(i) for i in range(2)]
        head_tall = [head_talls(i) for i in range(2)]
        head_own = [
            pltpu.make_async_copy(k.near[3 + i].at[0, own_p], o.head_p[i].at[pc.p], k.head_sem[i][2].at[0])
            for i in range(2)
        ]

        def middle(m):
            rh1.wait_recv(m)

            def rows(at):
                dh1 = k.mid[m, at, :] + summed(m, at)
                a, h = k.c[m, at, :], k.tok[m, at, :].astype(F32)
                r_a = inv_rms(a)
                n_a = a * r_a
                y = h + v.rattn[...] * (n_a - h)
                r_y = inv_rms(y)
                h1 = y * r_y
                dy = r_y * (dh1 - h1 * row_mean(dh1 * h1))
                add_rows(k.grattn, dy * (n_a - h))
                k.mid[m, at, :] = (1.0 - v.rattn[...]) * dy
                dn = v.rattn[...] * dy
                k.dab[m, own_p, at, :] = (r_a * (dn - n_a * row_mean(dn * n_a))).astype(BF)

            rows_loop(part, rows)
            ag1.start(m)

        def flat(ref, at=slice(None)):
            return ref[:, :, at].reshape(all_tok, -1)

        def columns_of(ref, at):
            return ref[:, :, :, at].reshape(all_tok, CHUNK)

        def weight_grad(target, left, right):
            def block(at):
                target[at, :] = dot_tn(columns_of(left, at), flat(right)).astype(BF)

            chunks(width, block)

        score = HEAD_DIM ** (-0.5)
        blk = seq // 2

        def attend(m):
            fill_mask(k.bias, v.segq[m], v.segk[m])
            ag1.wait_recv(m)

            def project(i, carry):
                rows = k.dab[m, pl.ds(2 * i, 2)].reshape(2 * part, width)
                at = pl.ds(pl.multiple_of(i * 2 * part, 2 * part), 2 * part)
                k_do[at, :] = dot_nn(rows, k.wvo[:, QUADS:]).astype(BF)
                return carry

            lax.fori_loop(0, pc.n_p // 2, project, 0)

            def norm_grad(tile, d):
                at = tile_of(tile)
                raw = k.qk[m, :, at]
                r = lax.rsqrt(half_means(raw * raw) + EPSILON)
                n = raw * r
                d = d * score
                add_rows(k.gsqk, d * n, at)
                dy = d * k.sqk[:, at]
                k_dqk[m, :, at] = (r * (dy - n * half_means(dy * n))).astype(BF)

            for slab in range(3):
                own = tile_of(slab)
                if slab < 2:
                    q_all = k.qkb[m, :, own]
                    k_all = k.qkb[m, :, tile_of(2 + slab)]
                    do_all = k_do[:, own]
                else:
                    q_all = k.qkb[m, :, 2 * QUADS :]
                    k_all = swap_halves(q_all.astype(F32)).astype(BF)
                    do_all = swap_halves(k_do[:, own].astype(F32)).astype(BF)
                v_all = k.vb[m, :, own]
                low = low_lanes((blk, LANES))
                dq, dk, dv = [], None, None
                for i in range(2):
                    nk = (i + 1) * blk
                    at = slice(i * blk, nk)
                    bias = k.bias[at, :nk]
                    dq_i = None
                    for half in range(2 if slab < 2 else 1):
                        here = low if half == 0 else jnp.logical_not(low)
                        zero = jnp.zeros((blk, LANES), BF)
                        q1, do1 = jnp.where(here, q_all[at], zero), jnp.where(here, do_all[at], zero)
                        lse = k.lse[m, at, 2 * slab + half : 2 * slab + half + 1]
                        prob = jnp.exp(dot_nt(q1, k_all[:nk]) * score + bias - lse)
                        dp = dot_nt(do1, v_all[:nk])
                        w = prob * dp
                        ds = (w - prob * jnp.sum(w, axis=1, keepdims=True)).astype(BF)
                        y = jnp.where(here, dot_nn(ds, k_all[:nk]), 0.0)
                        dq_i = y if dq_i is None else dq_i + y
                        dk_i, dv_i = dot_tn(ds, q1), dot_tn(prob.astype(BF), do1)
                        if i == 0:
                            dk = dk_i if dk is None else dk + dk_i
                            dv = dv_i if dv is None else dv + dv_i
                        else:
                            if half == 0:
                                dk = jnp.concatenate([dk, jnp.zeros((blk, LANES), F32)], axis=0)
                                dv = jnp.concatenate([dv, jnp.zeros((blk, LANES), F32)], axis=0)
                            dk, dv = dk + dk_i, dv + dv_i
                    dq.append(dq_i)
                dq = jnp.concatenate(dq, axis=0)
                k_dv[m, :, own] = dv.astype(BF)
                if slab < 2:
                    norm_grad(slab, dq)
                    norm_grad(2 + slab, dk)
                else:
                    norm_grad(4, dq + swap_halves(dk))
            if m == 0:
                ag1.relay(1)
            else:
                rh.relay(0)
            rh1.wait_send(m)

            def columns(at):
                y = dot_nt(k_dqk[m], k.wqk[at, :])
                y = y + dot_nt(k_dv[m, :, :QUADS], k.wvo[at, :QUADS])
                y = y + dot_nt(k_dv[m, :, QUADS:], k.wvo[at, 2 * QUADS :])
                k.sent[m, :, :, at] = y.astype(BF).reshape(pc.n_p, part, CHUNK)

            chunks(width, columns)
            rh.start(m)

        def heads_grad(at):
            hb, dab = flat(k.mb, at), columns_of(k.dab, at)
            quads = slice(0, QUADS)
            rest = slice(QUADS, None)
            k.wqk[at, :] = dot_tn(hb, flat(k_dqk)).astype(BF)
            k.wvo[at, :QUADS] = dot_tn(hb, flat(k_dv, quads)).astype(BF)
            k.wvo[at, QUADS : 2 * QUADS] = dot_tn(dab, flat(k.ob, quads)).astype(BF)
            k.wvo[at, 2 * QUADS :] = (dot_tn(hb, flat(k_dv, rest)) + dot_tn(dab, flat(k.ob, rest))).astype(BF)

        def bottom(m):
            rh.wait_recv(m)

            def rows(at):
                k.mid[m, at, :] = k.mid[m, at, :] + summed(m, at)

            rows_loop(part, rows)

        def collect():
            for t in range(pc.n_t):
                for j in range(3):

                    def move(t=t, j=j):
                        here = lanes(dst_tile(pc.p, t) + j, 1)
                        row = t * tiles + src_tile(pc.p, t) + j
                        k.vec[pl.ds(row, 1), :] = k.gsup[:, here]
                        k.vec[pl.ds(vec_rows + row, 1), :] = k.gsgate[:, here]

                    Move.under(width3(pc.p, t) if j == 2 else None, move)
            at = 2 * vec_rows
            for j in range(tiles):
                k.vec[at + j : at + j + 1, :] = k.grattn[:, tile_of(j)]
                k.vec[at + tiles + j : at + tiles + j + 1, :] = k.grmlp[:, tile_of(j)]
            count = qk_cols // LANES
            for j in range(count):
                k.vec[pl.ds(at + 2 * tiles + own_p * count + j, 1), :] = k.gsqk[:, tile_of(j)]

        def vec_stage(n, count, own, dev_of):
            send, recv = k.vec_sem[n]
            buf = k.vec_got[n]
            moves = Moves(
                [
                    Move(buf.at[own], buf.at[own], send.at[q], recv.at[own], dev_of(q), buf.at[q], recv.at[q])
                    for q in others(count, own)
                ]
            )

            def start():
                buf[own] = k.vec[...]
                moves.start()

            def finish():
                moves.wait_recv()
                total = buf[0]
                for q in range(1, count):
                    total = total + buf[q]
                k.vec[...] = total

            return start, finish, moves

        vec_stages = [
            vec_stage(0, pc.n_r, pc.r, lambda q: pc.dev(pc.p, q, pc.t)),
            vec_stage(1, pc.n_t, pc.t, lambda q: pc.dev(pc.p, pc.r, q)),
            vec_stage(2, pc.n_p, pc.p, lambda q: pc.dev(q, pc.r, pc.t)),
        ]
        vec_keep = pltpu.make_async_copy(k.vec, o.vec, k.vec_out.at[0])

        ready(k.c, k.h1)
        cot_load.wait()

        def put(at, y):
            for m in range(MB):
                k.mid[m, :, at] = y[m * part : (m + 1) * part]

        take_rows(v.hot, k.dealbuf, put)
        for m in range(MB):
            top(m)
        a_load.start()
        ag.relay(0)
        h2_load.wait()
        give_rows(v.hot, lambda at: k.dab[:, own_p, :, at].reshape(MB * part, CHUNK), k.dealbuf)
        deal_out.start()
        ready(k.wdown, k.u, k.g, k.wup, k.wgate, k.sup, k.sgate)
        feed(0)
        ag.relay(1)
        feed(1)
        ready(k.mb, k.hb1)
        weight_grad(k.wdown, k.dcb, k.mb)
        near[0].start()
        hb_load.start()
        shrink(0)
        near_sum(0)
        tall_start(0)
        shrink(1)
        rh1.relay(0)
        rh1.relay(1)
        weight_grad(k.wup, k.hb1, k.u)
        near[1].start()
        ready(k.tok)
        a_load.wait()
        middle(0)
        near_sum(1)
        tall_start(1)
        weight_grad(k.wgate, k.hb1, k.g)
        near[2].start()
        middle(1)
        ag1.relay(0)
        near_sum(2)
        tall_relay(0)
        tall_start(2)
        ready(k.wvo, k.vb, k.qkb, k.lse, k.qk, k.sqk, k.wqk, k.ob)
        attend(0)
        passed[0].wait_send()
        tall_relay(1)
        attend(1)
        hb_load.wait()
        chunks(width, heads_grad)
        for i in range(2):
            near[3 + i].start()
        rh.relay(1)
        collect()
        vec_stages[0][0]()
        for i in range(2):
            near_sum(3 + i)
            head_plane[i].start()
            head_own[i].start()
        vec_stages[0][1]()
        vec_stages[1][0]()
        for m in range(MB):
            bottom(m)
        passed[1].wait_send()
        tall_relay(2)
        deal_out.wait_recv()
        deal_out.wait_send()
        give_rows(v.hot, lambda at: k.mid[:, :, at].reshape(MB * part, CHUNK).astype(BF), k.dealbuf)
        deal_grad.start()
        for i in range(2):
            head_plane[i].wait_recv()
            head_own[i].wait()
            head_start(i)
        tall_sum(0)
        plane_start(0)
        plane_sent(0)
        tall_sum(1)
        plane_start(1)
        vec_stages[1][1]()
        vec_stages[2][0]()
        for i in range(2):
            head_relay(i)
        plane_sent(1)
        tall_sum(2)
        plane_start(2)
        vec_stages[2][1]()
        vec_keep.start()
        plane_sent(2)
        passed[2].wait_send()
        for w in tall + handed + head_first + head_last + head_plane + head_tall + near + [deal_grad]:
            w.wait_send()
        for stage in vec_stages:
            stage[2].wait_send()
        for i in range(3):
            plane[i][0].wait_recv()
        for w in head_tall + [deal_grad]:
            w.wait_recv()
        vec_keep.wait()
        for m in range(MB):
            ag.wait_send(m)
            ag1.wait_send(m)
            rh.wait_send(m)

    return fused(2, kernel, near_ins, loaded | later, outs, scratch)


def merged(slots, own, at):
    total = own.astype(F32)
    for q in range(slots.shape[0]):
        total = total + jnp.where((q == at) | (jnp.abs(q - at) == 3), 0, slots[q]).astype(F32)
    return total


def pick(x, at, axis):
    return lax.dynamic_index_in_dim(x, at, axis, keepdims=False)


def mm(a, b):
    return jnp.dot(a, b, preferred_element_type=F32)


def segment_ids(lengths_row, tok_count):
    count = lengths_row.shape[0]
    upto = jnp.arange(count)[:, None] >= jnp.arange(count)[None, :]
    doc_ends = jnp.sum(jnp.where(upto, lengths_row[None, :], 0), axis=1)
    places = jnp.arange(tok_count, dtype=jnp.int32)
    return jnp.sum((places[:, None] >= doc_ends[None, :]).astype(jnp.int32), axis=1)


def packed(x, y):
    return jnp.concatenate([x[:, :QUADS], y[:, :QUADS], x[:, QUADS:], y[:, QUADS:]], axis=1)


def unpacked(z):
    mid = 2 * QUADS + HEAD_DIM
    return (
        jnp.concatenate([z[..., :QUADS], z[..., 2 * QUADS : mid]], axis=-1),
        jnp.concatenate([z[..., QUADS : 2 * QUADS], z[..., mid:]], axis=-1),
    )


def body(
    tokens,
    cotangent,
    slot,
    lengths,
    w_query,
    w_key,
    w_value,
    w_out,
    w_up,
    w_gate,
    w_down,
    scale_qk,
    scale_up,
    scale_gate,
    rate_attn,
    rate_mlp,
):
    pc = Place()
    n_p, n_r, n_t, n_dev = pc.n_p, pc.n_r, pc.n_t, pc.n_dev
    rows_dev, width = tokens.shape
    tok_count = rows_dev // MB * n_p
    head_cols = w_query.shape[2]
    hid = w_up.shape[2]
    tiles = hid // LANES
    group = pc.r * n_t + pc.t
    owner = group * n_p + pc.p
    if rows_dev // n_dev > PAD or head_cols != QUADS + HEAD_DIM:
        raise ValueError("sizes")

    table = slot.reshape(n_dev, rows_dev)
    own_slots = lax.dynamic_index_in_dim(table, pc.me, 0, keepdims=False)
    d = own_slots // rows_dev
    to_dev = ((d % n_p) * n_r + (d // n_p) // n_t) * n_t + (d // n_p) % n_t
    places = jnp.arange(rows_dev, dtype=jnp.int32)
    spots = jnp.arange(n_dev * PAD, dtype=jnp.int32)
    before = (d[:, None] == d[None, :]) & (places[None, :] < places[:, None])
    rank = jnp.sum(before.astype(jnp.int32), axis=1)
    send_hot = (spots[:, None] == (to_dev * PAD + rank)[None, :]).astype(BF)

    sel = table // rows_dev == owner
    tri = (places[:, None] < places[None, :]).astype(BF)
    ranks = mm(sel.astype(BF), tri).astype(jnp.int32)
    kth = sel[:, None, :] & (ranks[:, None, :] == jnp.arange(PAD, dtype=jnp.int32)[None, :, None])
    owner_rows = jnp.sum(jnp.where(kth, (table - owner * rows_dev + 1)[:, None, :], 0), axis=2).reshape(-1) - 1
    recv_hot = (places[:, None] == owner_rows[None, :]).astype(BF)

    def to_send(x):
        return mm(send_hot, x).astype(BF).reshape(n_dev, PAD, width)

    qk_scale = packed(scale_qk, scale_qk).reshape(-1, LANES)
    small = jnp.concatenate([scale_up.reshape(-1, LANES), scale_gate.reshape(-1, LANES), qk_scale])
    small = jnp.pad(small, ((0, -small.shape[0] % 8), (0, 0)))
    own_lengths = lax.dynamic_slice_in_dim(lengths, group * MB, MB, 0)
    segments = jnp.stack([segment_ids(own_lengths[m], tok_count) for m in range(MB)])
    shared = (recv_hot, rate_attn, rate_mlp, segments[:, :, None], segments[:, None, :])

    f = forward(
        pc,
        to_send(tokens),
        to_send(cotangent),
        packed(w_query[0], w_key[0]),
        packed(w_value[0], w_out[0]),
        w_up[0],
        w_gate[0],
        w_down[0],
        small,
        *shared,
    )
    b = backward(pc, f, *shared)

    vec = b.vec
    at = n_t * tiles

    def own_row(x):
        return lax.dynamic_index_in_dim(x.reshape(n_t, -1), pc.t, 0)

    qk_rows = qk_scale.shape[0]
    out_sup, out_sgate = own_row(vec[:at]), own_row(vec[at : 2 * at])
    at = 2 * at
    out_rattn, out_rmlp = vec[at : at + tiles].reshape(1, -1), vec[at + tiles : at + 2 * tiles].reshape(1, -1)
    at = at + 2 * tiles
    out_sqk = sum(unpacked(own_row(vec[at : at + n_t * qk_rows])))
    heads = [
        x[None]
        for got, sent in zip(b.head_t, b.head_p)
        for x in unpacked(merged(got, pick(sent, pc.t, 0), pc.t))
    ]

    def from_back(x):
        return lax.dot_general(
            send_hot, x.reshape(-1, width), (((0,), (0,)), ((), ())), preferred_element_type=F32
        )

    down, up, gate = (x.astype(F32)[None] for x in b.final)
    return (
        from_back(b.back_out),
        from_back(b.back_grad),
        *heads,
        up,
        gate,
        down,
        out_sqk,
        out_sup,
        out_sgate,
        out_rattn,
        out_rmlp,
    )


def solution(mesh):
    tok = P(("dp", "tensor"), None)
    mat = P(None, "dp", "tensor")
    vec = P(None, "tensor")
    in_specs = (tok, tok, P(), P()) + (mat,) * 7 + (vec,) * 3 + (P(), P())
    out_specs = (tok, tok) + (mat,) * 7 + (vec,) * 3 + (P(), P())
    return jax.shard_map(body, mesh=mesh, in_specs=in_specs, out_specs=out_specs, check_vma=False)
```
